32 devices in a mesh: pass: 2 (over y), rows: 16 (over z, x, core).
Axes of the slice: x: 2, y: 2, z: 4, core: 2. Of those that a mesh axis runs over, the one named last changes fastest.
Arguments:
- stream: bfloat16 [2, 16, 1024, 768], P('pass', 'rows'), may hold values from -6 to 6
- lengths: int32 [16], P('rows'), may hold values from 256 to 1024, as said below
- pass_embed: bfloat16 [2, 768], replicated, may hold values from -3 to 3
- first_gain: bfloat16 [2, 768], replicated, may hold values from 0.5 to 1.5
- first_bias: bfloat16 [2, 768], replicated, may hold values from -1.5 to 1.5
- triple_weight: bfloat16 [2, 768, 2304], replicated, may hold values from -0.21875 to 0.21875
- merge_weight: bfloat16 [2, 768, 768], replicated, may hold values from -6 to 6
- second_gain: bfloat16 [2, 768], replicated, may hold values from 0.5 to 1.5
- second_bias: bfloat16 [2, 768], replicated, may hold values from -1.5 to 1.5
- up_weight: bfloat16 [2, 768, 3072], replicated, may hold values from -0.21875 to 0.21875
- down_weight: bfloat16 [2, 3072, 768], replicated, may hold values from -0.109375 to 0.109375
- cotangent: bfloat16 [2, 16, 1024, 768], P('pass', 'rows'), may hold values from -6 to 6
Outputs:
- output: bfloat16 [2, 16, 1024, 768], P('pass', 'rows')
- input_grad: bfloat16 [2, 16, 1024, 768], P('pass', 'rows')
- pass_embed_grad: float32 [2, 768], P(None, 'rows')
- first_gain_grad: float32 [2, 768], P(None, 'rows')
- first_bias_grad: float32 [2, 768], P(None, 'rows')
- triple_grad: float32 [2, 768, 2304], P(None, 'rows')
- merge_grad: float32 [2, 768, 768], P(None, 'rows')
- second_gain_grad: float32 [2, 768], P(None, 'rows')
- second_bias_grad: float32 [2, 768], P(None, 'rows')
- up_grad: float32 [2, 768, 3072], P(None, 'rows')
- down_grad: float32 [2, 3072, 768], P(None, 'rows')
The draws below stay inside these ranges and needn't reach their ends.
Inputs may be any that keep to these rules, and one draw needn't show every extreme that they name: `lengths`: each is at least 256; in every draw some sequence has exactly 1024.
All inputs are finite; a program needn't handle non-finite values.
Results may differ from the reference program's by a relative error of at most 0.015.
Values may be sent and summed in bfloat16 or wider, within the bound.
A program may use at most 320 MiB of HBM per device.

```python
import jax
import jax.numpy as jnp
from jax import lax

D = 768
HEAD_DIM = 64
FF = 3072
LAYERS = 2
PASSES = 2
LEN = 1024
SEQS = 16


def draw_lengths(key, part):
    key = jax.random.fold_in(key, 11)
    first_key, second_key = jax.random.split(key)
    drawn = jax.random.randint(first_key, (SEQS,), max(1, LEN // 4), LEN + 1)
    longest = jax.random.randint(second_key, (), 0, SEQS)
    return jnp.where(jnp.arange(SEQS) == longest, LEN, drawn).astype(jnp.int32)


def levels(key, dims, shards, smallest, high):
    factor_of = 1.0
    for position, shards_of in shards:
        draws = jax.random.uniform(jax.random.fold_in(jax.random.fold_in(key, 6), position), (shards_of,), jnp.float32, smallest / len(shards), high / len(shards))
        factor_of = factor_of * jnp.repeat(jnp.exp(draws), dims[position] // shards_of).reshape((-1,) + (1,) * (len(dims) - 1 - position))
    return factor_of


def noise(stream_key, dims, width, limit, shards=(), dtype=jnp.bfloat16):
    array = width * jax.random.normal(stream_key, dims, jnp.float32)
    if shards:
        array = array * levels(stream_key, dims, shards, -0.22, 0.18)
    return jnp.clip(array, -limit, limit).astype(dtype)


def setup_inputs(seed: int = 0) -> dict:
    key_of = jax.random.split(jax.random.key(seed), 13)
    stream = noise(key_of[0], (PASSES, SEQS, LEN, D), 1.0, 6.0, ((0, 2), (1, 16)))
    lengths = draw_lengths(jax.random.fold_in(key_of[12], 71), 0)
    pass_embed = noise(key_of[2], (PASSES, D), 0.5, 3.0)
    first_gain = jnp.clip(1.0 + 0.1 * jax.random.normal(key_of[3], (LAYERS, D), jnp.float32), 0.5, 1.5).astype(jnp.bfloat16)
    first_bias = noise(key_of[4], (LAYERS, D), 0.3, 1.5)
    triple_weight = noise(key_of[5], (LAYERS, D, 3 * D), D ** -0.5, 0.21875)
    merge_weight = noise(key_of[6], (LAYERS, D, D), (max(1, 2 * D // LEN)) ** -0.5, 6.0)
    second_gain = jnp.clip(1.0 + 0.1 * jax.random.normal(key_of[7], (LAYERS, D), jnp.float32), 0.5, 1.5).astype(jnp.bfloat16)
    second_bias = noise(key_of[8], (LAYERS, D), 0.3, 1.5)
    up_weight = noise(key_of[9], (LAYERS, D, FF), D ** -0.5, 0.21875)
    down_weight = noise(key_of[10], (LAYERS, FF, D), FF ** -0.5, 0.109375)
    cotangent = noise(key_of[11], (PASSES, SEQS, LEN, D), 1.0, 6.0, ((0, 2), (1, 16)))
    return dict(stream=stream, lengths=lengths, pass_embed=pass_embed, first_gain=first_gain, first_bias=first_bias, triple_weight=triple_weight, merge_weight=merge_weight, second_gain=second_gain, second_bias=second_bias, up_weight=up_weight, down_weight=down_weight, cotangent=cotangent)


epsilon = 1e-05
highest = lax.Precision.HIGHEST

@jax.custom_vjp
def low(v):
    return lax.optimization_barrier(v.astype(jnp.bfloat16)).astype(jnp.float32)

@jax.custom_vjp
def low_back(v):
    return v

def low_keep(v):
    return (low(v), None)

def low_pass(kept, grad):
    return (grad,)

def back_keep(v):
    return (v, None)

def back_low(kept, grad):
    return (low(grad),)
low.defvjp(low_keep, low_pass)
low_back.defvjp(back_keep, back_low)

def layer_norm(hidden, gain, bias):
    row_mean = lax.optimization_barrier(jnp.mean(hidden, -1, keepdims=True))
    centred = hidden - row_mean
    variance = lax.optimization_barrier(jnp.mean(centred * centred, -1, keepdims=True))
    return centred * lax.rsqrt(variance + epsilon) * gain + bias

def product(left, right):
    return jnp.einsum('pnd,de->pne', left, right, precision=highest)

def attention(triple, row_length):
    passes, slot_count, triple_width = triple.shape
    model_width = triple_width // 3
    head_count = model_width // HEAD_DIM
    flat = triple.reshape(passes * slot_count, 3, head_count, HEAD_DIM)
    queries, key_rows, value_rows = (flat[:, 0], flat[:, 1], flat[:, 2])
    positions = jnp.tile(jnp.arange(slot_count), passes)
    pass_ids = jnp.repeat(jnp.arange(passes), slot_count)
    earlier = positions[None, :] < positions[:, None]
    same_step = (positions[None, :] == positions[:, None]) & (pass_ids[None, :] <= pass_ids[:, None])
    allowed = (earlier | same_step) & (positions[None, :] < row_length)
    raw_score = jnp.einsum('qhd,khd->hqk', queries, key_rows, precision=highest) * HEAD_DIM ** (-0.5)
    masked = jnp.where(allowed[None], low_back(raw_score), -jnp.inf)
    row_max = lax.optimization_barrier(jnp.max(masked, -1, keepdims=True))
    exponent = jnp.exp(masked - row_max)
    softmax = exponent / lax.optimization_barrier(jnp.sum(exponent, -1, keepdims=True))
    mixed_out = jnp.einsum('hqk,khd->qhd', low(softmax), value_rows, precision=highest)
    return mixed_out.reshape(passes, slot_count, model_width)

def sequence_forward(seq_input, row_length, weights):
    pass_embed, first_gain, first_bias, triple_weight, merge_weight, second_gain, second_bias, up_weight, down_weight = weights
    slot_count = seq_input.shape[1]
    valid_rows = (jnp.arange(slot_count) < row_length).astype(jnp.float32)
    hidden = seq_input + pass_embed[:, None, :]
    for depth in range(LAYERS):
        normed = low(layer_norm(hidden, first_gain[depth], first_bias[depth]))
        triple = low_back(low(product(normed, triple_weight[depth])))
        mixed_out = low_back(low(attention(triple, row_length)))
        hidden = hidden + low_back(product(mixed_out, merge_weight[depth]))
        normed_two = low(layer_norm(hidden, second_gain[depth], second_bias[depth]))
        pre_act = low_back(product(normed_two, up_weight[depth]))
        activation = low(jax.nn.gelu(pre_act, approximate=True))
        hidden = hidden + low_back(product(activation, down_weight[depth]))
    return hidden * valid_rows[None, :, None]

def reference(stream, lengths, pass_embed, first_gain, first_bias, triple_weight, merge_weight, second_gain, second_bias, up_weight, down_weight, cotangent):
    weights = tuple((item.astype(jnp.float32) for item in (pass_embed, first_gain, first_bias, triple_weight, merge_weight, second_gain, second_bias, up_weight, down_weight)))
    inputs = stream.astype(jnp.float32)

    def whole(input_all, weight_all):

        def per_sequence(operands):
            seq_input, row_length = operands
            return sequence_forward(seq_input, row_length, weight_all)
        stacked = lax.map(jax.checkpoint(per_sequence), (jnp.swapaxes(input_all, 0, 1), lengths))
        return jnp.swapaxes(stacked, 0, 1)
    result, pullback = jax.vjp(whole, inputs, weights)
    grad_input, grad_weights = pullback(cotangent.astype(jnp.float32))
    return (result.astype(jnp.bfloat16), grad_input.astype(jnp.bfloat16), grad_weights[0], grad_weights[1], grad_weights[2], grad_weights[3], grad_weights[4], grad_weights[5], grad_weights[6], grad_weights[7], grad_weights[8])
```

```python
import functools
import math

import jax
import jax.numpy as jnp
from jax import lax
from jax.experimental import pallas as pl
from jax.experimental.pallas import tpu as pltpu
from jax.sharding import PartitionSpec as P

HEAD_DIM = 64
EPSILON = 1e-05
SCALE = HEAD_DIM**-0.5
MESH = pl.DeviceIdType.MESH
NN = (((1,), (0,)), ((), ()))
NT = (((1,), (1,)), ((), ()))
TN = (((0,), (0,)), ((), ()))
BLOCK = 256
LANES = 128
BF16 = jnp.bfloat16
F32 = jnp.float32
VMEM_LIMIT = 60 * 2**20
ANY = pl.BlockSpec(memory_space=pl.ANY)


def dot(left, right, dims=NN):
    return lax.dot_general(left, right, dims, preferred_element_type=F32)


def sds(shape, dtype):
    return jax.ShapeDtypeStruct(shape, dtype)


def params(collective_id=None):
    return pltpu.CompilerParams(
        vmem_limit_bytes=VMEM_LIMIT,
        collective_id=collective_id,
        has_side_effects=collective_id is not None,
    )


def whole(shape):
    zeros = (0,) * len(shape)
    return pl.BlockSpec(shape, lambda *_: zeros, pipeline_mode=pl.Buffered(1))


def norm(hidden, gain, bias):
    centred = hidden - jnp.mean(hidden, -1, keepdims=True)
    inverse = lax.rsqrt(jnp.mean(centred * centred, -1, keepdims=True) + EPSILON)
    scaled = centred * inverse
    return (scaled * gain + bias).astype(BF16), scaled, inverse


def norm_back(grad, scaled, inverse, gain):
    e = grad * gain
    return inverse * (
        e - jnp.mean(e, -1, keepdims=True) - scaled * jnp.mean(e * scaled, -1, keepdims=True)
    )


def partner():
    rows = lax.axis_index("rows")
    return rows + 1 - 2 * (rows % 2)


def greet():
    barrier = pltpu.get_barrier_semaphore()
    pl.semaphore_signal(barrier, inc=1, device_id={"rows": partner()}, device_id_type=MESH)
    pl.semaphore_wait(barrier, 1)


def qkv_kernel(
    hidden_ref, embed_ref, gain_ref, bias_ref, weight_ref,
    full_ref, normed_ref, scaled_ref, inverse_ref, query_ref, kv_ref,
    held, local_sem, send_sem, recv_sem,
):
    step = pl.program_id(0)
    own = lax.axis_index("rows") % 2
    width = hidden_ref.shape[1]
    rows = hidden_ref.shape[0]

    @pl.when(step == 0)
    def _():
        greet()

    hidden = hidden_ref[...].astype(F32) + embed_ref[...]
    full_ref[...] = hidden
    normed, scaled, inverse = norm(hidden, gain_ref[...], bias_ref[...])
    normed_ref[...] = normed
    scaled_ref[...] = scaled.astype(BF16)
    inverse_ref[...] = inverse
    keys = dot(normed, weight_ref[:, width:])
    held[step] = keys.astype(BF16)

    def copies(i):
        there = pltpu.make_async_remote_copy(
            src_ref=held.at[i], dst_ref=kv_ref.at[i, own],
            send_sem=send_sem.at[i], recv_sem=recv_sem.at[i],
            device_id={"rows": partner()}, device_id_type=MESH,
        )
        here = pltpu.make_async_copy(held.at[i], kv_ref.at[i, own], local_sem.at[i])
        return there, here

    there, here = copies(step)
    there.start()
    here.start()
    queries = dot(normed, weight_ref[:, :width])
    query_ref[...] = (queries.astype(BF16).astype(F32) * SCALE).astype(BF16)

    @pl.when(step == pl.num_programs(0) - 1)
    def _():
        for i in range(held.shape[0]):
            there, here = copies(i)
            there.wait()
            here.wait()


def qkv(hidden, embed, gain, bias, weight, collective_id):
    tokens, width = hidden.shape
    steps = tokens // BLOCK
    tile = pl.BlockSpec((BLOCK, width), lambda i: (i, 0))
    return pl.pallas_call(
        qkv_kernel,
        grid=(steps,),
        in_specs=[tile, whole((1, width)), whole((1, width)), whole((1, width)), whole(weight.shape)],
        out_specs=[tile, tile, tile, pl.BlockSpec((BLOCK, 1), lambda i: (i, 0)), tile, ANY],
        out_shape=[
            sds((tokens, width), F32),
            sds((tokens, width), BF16),
            sds((tokens, width), BF16),
            sds((tokens, 1), F32),
            sds((tokens, width), BF16),
            sds((steps, 2, BLOCK, 2 * width), BF16),
        ],
        scratch_shapes=[
            pltpu.VMEM((steps, BLOCK, 2 * width), BF16),
            pltpu.SemaphoreType.DMA((steps,)),
            pltpu.SemaphoreType.DMA((steps,)),
            pltpu.SemaphoreType.DMA((steps,)),
        ],
        compiler_params=params(collective_id),
        name="qkv",
    )(hidden, embed, gain, bias, weight)


def tile_index(blocks, key_block, query_block):
    return key_block * blocks - key_block * (key_block - 1) // 2 + query_block - key_block


def attend_kernel(length_ref, query_ref, key_ref, value_ref, mixed_ref, total_ref, exp_ref):
    own = lax.axis_index("rows") % 2
    tokens = query_ref.shape[0]
    blocks = tokens // BLOCK
    pair = 2 * BLOCK
    lane = lax.broadcasted_iota(jnp.int32, (BLOCK, LANES), 1)
    query_at = lax.broadcasted_iota(jnp.int32, (BLOCK, pair), 0)
    column = lax.broadcasted_iota(jnp.int32, (BLOCK, pair), 1)
    key_pass = column // BLOCK
    key_at = column - key_pass * BLOCK
    causal = (key_at < query_at) | ((key_at == query_at) & (key_pass <= own))
    length = length_ref[0]
    ones = jnp.ones((tokens * 2, LANES), BF16)
    values = jnp.concatenate([value_ref[...], ones], 1)
    for block in range(blocks):
        rows = pl.ds(block * BLOCK, BLOCK)

        @pl.when(block * BLOCK < length)
        def _():
            allowed = causal & (key_at < length - block * BLOCK)
            query = query_ref[rows, :]
            outs = []
            for head in range(2):
                chosen = jnp.where(lane // HEAD_DIM == head, query, jnp.zeros_like(query))
                raw = dot(chosen, key_ref[: (block + 1) * pair, :], NT)
                last = jnp.where(allowed, raw[:, block * pair :], -jnp.inf)
                top = jnp.max(last, -1, keepdims=True)
                if block:
                    top = jnp.maximum(top, jnp.max(raw[:, : block * pair], -1, keepdims=True))
                parts = [jnp.exp(raw[:, k * pair : (k + 1) * pair] - top).astype(BF16) for k in range(block)]
                parts.append(jnp.exp(last - top).astype(BF16))
                for k, part in enumerate(parts):
                    exp_ref[head, tile_index(blocks, k, block)] = part
                mixed = dot(jnp.concatenate(parts, 1), values[: (block + 1) * pair])
                inverse = 1.0 / mixed[:, LANES : LANES + 1]
                total_ref[0, rows, head : head + 1] = inverse
                outs.append(mixed[:, :LANES] * inverse)
            mixed_ref[rows, :] = jnp.where(lane < HEAD_DIM, outs[0], outs[1]).astype(BF16)

        @pl.when(block * BLOCK >= length)
        def _():
            mixed_ref[rows, :] = jnp.zeros((BLOCK, LANES), BF16)
            total_ref[0, rows, :] = jnp.zeros((BLOCK, 2), F32)
            for head in range(2):
                for k in range(block + 1):
                    exp_ref[head, tile_index(blocks, k, block)] = jnp.zeros((BLOCK, pair), BF16)


def attend(length, query, kv):
    tokens, width = query.shape
    blocks = tokens // BLOCK
    tiles = blocks * (blocks + 1) // 2
    pairs = width // LANES
    column = pl.BlockSpec((tokens, LANES), lambda h: (0, h))
    return pl.pallas_call(
        attend_kernel,
        grid=(pairs,),
        in_specs=[
            pl.BlockSpec(memory_space=pltpu.SMEM),
            column,
            pl.BlockSpec((2 * tokens, LANES), lambda h: (0, h)),
            pl.BlockSpec((2 * tokens, LANES), lambda h: (0, h + pairs)),
        ],
        out_specs=[
            column,
            pl.BlockSpec((1, tokens, 2), lambda h: (h, 0, 0)),
            pl.BlockSpec((2, tiles, BLOCK, 2 * BLOCK), lambda h: (h, 0, 0, 0)),
        ],
        out_shape=[
            sds((tokens, width), BF16),
            sds((pairs, tokens, 2), F32),
            sds((2 * pairs, tiles, BLOCK, 2 * BLOCK), BF16),
        ],
        compiler_params=params(),
        name="attend",
    )(length, query, kv, kv)


def attend_back_kernel(
    query_ref, key_ref, value_ref, grad_ref, mixed_ref, total_ref, exp_ref,
    grad_query_ref, own_ref, recv_ref,
    query_sum, held, send_sem, recv_sem,
):
    step = pl.program_id(0)
    own = lax.axis_index("rows") % 2
    tokens = query_ref.shape[0]
    blocks = tokens // BLOCK
    pair = 2 * BLOCK
    lane = lax.broadcasted_iota(jnp.int32, (tokens, LANES), 1)

    @pl.when(step == 0)
    def _():
        greet()

    grad = grad_ref[...].astype(F32)
    product = grad * mixed_ref[...].astype(F32)
    query = query_ref[...]
    zero = jnp.zeros_like(query)
    sums = []
    for head in range(2):
        mine = lane // HEAD_DIM == head
        inverse = total_ref[0, :, head : head + 1]
        scaled = jnp.where(mine, grad * inverse, 0.0).astype(BF16)
        inner = jnp.sum(jnp.where(mine, product, 0.0), -1, keepdims=True) * inverse
        chosen = jnp.where(mine, query, zero)
        for block in range(blocks):
            first = block * BLOCK
            keys = pl.ds(block * pair, pair)
            start = tile_index(blocks, block, block)
            prob = exp_ref[head, start : start + blocks - block].reshape(tokens - first, pair)
            grad_prob = dot(scaled[first:], value_ref[keys, :], NT)
            score = (prob.astype(F32) * (grad_prob - inner[first:])).astype(BF16)
            grad_value = dot(prob, scaled[first:], TN)
            grad_key = dot(score, chosen[first:], TN)
            grad_query = dot(score, key_ref[keys, :])
            if block == 0:
                query_sum[head] = grad_query
            else:
                query_sum[head, first:, :] += grad_query
            sums.append((grad_key, grad_value))
    for block in range(blocks):
        for which in range(2):
            total = (sums[block][which] + sums[blocks + block][which]).astype(BF16)
            for p in range(2):
                held[step % 2, p, which, pl.ds(block * BLOCK, BLOCK), :] = total[p * BLOCK : (p + 1) * BLOCK]
    grad_query_ref[...] = (jnp.where(lane < HEAD_DIM, query_sum[0], query_sum[1]) * SCALE).astype(BF16)
    own_ref[0] = held[step % 2, own, 0]
    own_ref[1] = held[step % 2, own, 1]

    def copy(i):
        return pltpu.make_async_remote_copy(
            src_ref=held.at[i % 2, 1 - own], dst_ref=recv_ref.at[i],
            send_sem=send_sem.at[i], recv_sem=recv_sem.at[i],
            device_id={"rows": partner()}, device_id_type=MESH,
        )

    copy(step).start()

    @pl.when(step > 0)
    def _():
        copy(step - 1).wait_send()

    @pl.when(step == pl.num_programs(0) - 1)
    def _():
        copy(step).wait_send()
        for i in range(recv_ref.shape[0]):
            copy(i).wait_recv()


def attend_back(query, kv, grad_mixed, mixed, total, exps, collective_id):
    tokens, width = query.shape
    pairs = width // LANES
    tiles = exps.shape[1]
    column = pl.BlockSpec((tokens, LANES), lambda h: (0, h))
    return pl.pallas_call(
        attend_back_kernel,
        grid=(pairs,),
        in_specs=[
            column,
            pl.BlockSpec((2 * tokens, LANES), lambda h: (0, h)),
            pl.BlockSpec((2 * tokens, LANES), lambda h: (0, h + pairs)),
            column,
            column,
            pl.BlockSpec((1, tokens, 2), lambda h: (h, 0, 0)),
            pl.BlockSpec((2, tiles, BLOCK, 2 * BLOCK), lambda h: (h, 0, 0, 0)),
        ],
        out_specs=[column, pl.BlockSpec((2, tokens, LANES), lambda h: (0, 0, h)), ANY],
        out_shape=[
            sds((tokens, width), BF16),
            sds((2, tokens, width), BF16),
            sds((pairs, 2, tokens, LANES), BF16),
        ],
        scratch_shapes=[
            pltpu.VMEM((2, tokens, LANES), F32),
            pltpu.VMEM((2, 2, 2, tokens, LANES), BF16),
            pltpu.SemaphoreType.DMA((pairs,)),
            pltpu.SemaphoreType.DMA((pairs,)),
        ],
        compiler_params=params(collective_id),
        name="attend_back",
    )(query, kv, kv, grad_mixed, mixed, total, exps)


def gelu_both(v):
    root = math.sqrt(2.0 / math.pi)
    square = v * v
    t = jnp.tanh(v * (root + (root * 0.044715) * square))
    half = 0.5 * (1.0 + t)
    slope = half + 0.5 * v * (1.0 - t * t) * (root + (3.0 * root * 0.044715) * square)
    return v * half, slope


def ffn_kernel(
    hidden_ref, mixed_ref, merge_ref, gain_ref, bias_ref, up_ref, down_ref,
    next_ref, normed_ref, scaled_ref, inverse_ref, act_ref, slope_ref,
):
    mid = hidden_ref[...] + dot(mixed_ref[...], merge_ref[...])
    normed, scaled, inverse = norm(mid, gain_ref[...], bias_ref[...])
    normed_ref[...] = normed
    scaled_ref[...] = scaled.astype(BF16)
    inverse_ref[...] = inverse
    total = mid
    hidden_units = up_ref.shape[1]
    part = mid.shape[1]
    for first in range(0, hidden_units, part):
        act, slope = gelu_both(dot(normed, up_ref[:, first : first + part]))
        act = act.astype(BF16)
        act_ref[:, first : first + part] = act
        slope_ref[:, first : first + part] = slope.astype(BF16)
        total = total + dot(act, down_ref[first : first + part, :])
    next_ref[...] = total


def ffn(hidden, mixed, merge, gain, bias, up, down):
    tokens, width = hidden.shape
    units = up.shape[1]
    tile = pl.BlockSpec((BLOCK, width), lambda i: (i, 0))
    wide = pl.BlockSpec((BLOCK, units), lambda i: (i, 0))
    return pl.pallas_call(
        ffn_kernel,
        grid=(tokens // BLOCK,),
        in_specs=[
            tile, tile, whole(merge.shape), whole((1, width)), whole((1, width)),
            whole(up.shape), whole(down.shape),
        ],
        out_specs=[tile, tile, tile, pl.BlockSpec((BLOCK, 1), lambda i: (i, 0)), wide, wide],
        out_shape=[
            sds((tokens, width), F32),
            sds((tokens, width), BF16),
            sds((tokens, width), BF16),
            sds((tokens, 1), F32),
            sds((tokens, units), BF16),
            sds((tokens, units), BF16),
        ],
        compiler_params=params(),
        name="ffn",
    )(hidden, mixed, merge, gain, bias, up, down)


def ffn_back_kernel(
    grad_ref, act_ref, slope_ref, normed_ref, scaled_ref, inverse_ref, mixed_ref,
    gain_ref, up_ref, down_ref, merge_ref,
    down_grad_ref, up_grad_ref, merge_grad_ref, mid_ref, grad_mixed_ref, small_ref,
    total, low, branch,
):
    step = pl.program_id(0)
    tokens = grad_ref.shape[0]

    @pl.when(step == 0)
    def _():
        low[...] = grad_ref[...].astype(BF16)
        total[...] = jnp.zeros_like(total)

    grad_low = low[...]
    down_grad_ref[...] = dot(act_ref[...], grad_low, TN).astype(BF16)
    grad_act = dot(grad_low, down_ref[...], NT)
    grad_pre = (slope_ref[...].astype(F32) * grad_act).astype(BF16)
    up_grad_ref[...] = dot(normed_ref[...], grad_pre, TN).astype(BF16)
    total[...] += dot(grad_pre, up_ref[...], NT)

    @pl.when(step == pl.num_programs(0) - 1)
    def _():
        def rows(i, sums):
            at = pl.ds(pl.multiple_of(i * BLOCK, BLOCK), BLOCK)
            grad = total[at, :]
            scaled = scaled_ref[at, :].astype(F32)
            mid = grad_ref[at, :] + norm_back(grad, scaled, inverse_ref[at, :], gain_ref[...])
            mid_ref[at, :] = mid
            low_mid = mid.astype(BF16)
            branch[at, :] = low_mid
            grad_mixed_ref[at, :] = dot(low_mid, merge_ref[...], NT).astype(BF16)
            return (
                sums[0] + jnp.sum(grad * scaled, 0, keepdims=True),
                sums[1] + jnp.sum(grad, 0, keepdims=True),
            )

        empty = jnp.zeros((1, grad_ref.shape[1]), F32)
        gain_sum, bias_sum = lax.fori_loop(0, tokens // BLOCK, rows, (empty, empty))
        small_ref[0:1, :] = gain_sum
        small_ref[1:2, :] = bias_sum
        merge_grad_ref[...] = dot(mixed_ref[...], branch[...], TN).astype(BF16)


def ffn_back(grad, act, slope, normed, scaled, inverse, mixed, gain, up, down, merge):
    tokens, width = grad.shape
    units = up.shape[1]
    part = 512
    full = whole((tokens, width))
    return pl.pallas_call(
        ffn_back_kernel,
        grid=(units // part,),
        in_specs=[
            full,
            pl.BlockSpec((tokens, part), lambda i: (0, i)),
            pl.BlockSpec((tokens, part), lambda i: (0, i)),
            full, full, whole((tokens, 1)), full, whole((1, width)),
            pl.BlockSpec((width, part), lambda i: (0, i)),
            pl.BlockSpec((part, width), lambda i: (i, 0)),
            whole(merge.shape),
        ],
        out_specs=[
            pl.BlockSpec((part, width), lambda i: (i, 0)),
            pl.BlockSpec((width, part), lambda i: (0, i)),
            whole(merge.shape), full, full, whole((2, width)),
        ],
        out_shape=[
            sds(down.shape, BF16),
            sds(up.shape, BF16),
            sds(merge.shape, BF16),
            sds((tokens, width), F32),
            sds((tokens, width), BF16),
            sds((2, width), F32),
        ],
        scratch_shapes=[
            pltpu.VMEM((tokens, width), F32),
            pltpu.VMEM((tokens, width), BF16),
            pltpu.VMEM((tokens, width), BF16),
        ],
        compiler_params=params(),
        name="ffn_back",
    )(grad, act, slope, normed, scaled, inverse, mixed, gain, up, down, merge)


def qkv_back_kernel(
    grad_query_ref, own_ref, recv_ref, normed_ref, scaled_ref, inverse_ref, mid_ref, gain_ref, weight_ref,
    weight_grad_ref, hidden_ref, small_ref,
    total, grads,
):
    step = pl.program_id(0)
    tokens, width = mid_ref.shape

    @pl.when(step == 0)
    def _():
        grads[...] = grad_query_ref[...]
        total[...] = jnp.zeros_like(total)

    @pl.when(step > 0)
    def _():
        for pair in range(width // LANES):
            lanes = slice(pair * LANES, (pair + 1) * LANES)
            grads[:, lanes] = (
                own_ref[0, :, lanes].astype(F32) + recv_ref[pair, 0].astype(F32)
            ).astype(BF16)

    weight_grad_ref[...] = dot(normed_ref[...], grads[...], TN).astype(BF16)
    total[...] += dot(grads[...], weight_ref[...], NT)

    @pl.when(step == pl.num_programs(0) - 1)
    def _():
        def rows(i, sums):
            at = pl.ds(pl.multiple_of(i * BLOCK, BLOCK), BLOCK)
            grad = total[at, :]
            scaled = scaled_ref[at, :].astype(F32)
            hidden = mid_ref[at, :] + norm_back(grad, scaled, inverse_ref[at, :], gain_ref[...])
            hidden_ref[at, :] = hidden
            return (
                sums[0] + jnp.sum(grad * scaled, 0, keepdims=True),
                sums[1] + jnp.sum(grad, 0, keepdims=True),
                sums[2] + jnp.sum(hidden, 0, keepdims=True),
            )

        empty = jnp.zeros((1, width), F32)
        sums = lax.fori_loop(0, tokens // BLOCK, rows, (empty, empty, empty))
        for i in range(3):
            small_ref[i : i + 1, :] = sums[i]


def qkv_back(grad_query, own, recv, normed, scaled, inverse, mid, gain, weight):
    tokens, width = mid.shape
    pairs = width // LANES
    full = whole((tokens, width))
    which = lambda i: jnp.maximum(i - 1, 0)
    return pl.pallas_call(
        qkv_back_kernel,
        grid=(3,),
        in_specs=[
            full,
            pl.BlockSpec((1, tokens, width), lambda i: (which(i), 0, 0)),
            pl.BlockSpec((pairs, 1, tokens, LANES), lambda i: (0, which(i), 0, 0)),
            full, full, whole((tokens, 1)), full, whole((1, width)),
            pl.BlockSpec((width, width), lambda i: (0, i)),
        ],
        out_specs=[pl.BlockSpec((width, width), lambda i: (0, i)), full, whole((3, width))],
        out_shape=[sds(weight.shape, BF16), sds((tokens, width), F32), sds((3, width), F32)],
        scratch_shapes=[pltpu.VMEM((tokens, width), F32), pltpu.VMEM((tokens, width), BF16)],
        compiler_params=params(),
        name="qkv_back",
    )(grad_query, own, recv, normed, scaled, inverse, mid, gain, weight)


def local(
    stream, lengths, pass_embed, first_gain, first_bias, triple_weight, merge_weight,
    second_gain, second_bias, up_weight, down_weight, cotangent,
):
    row_count = lax.axis_size("rows")
    own_row = lax.axis_index("rows")
    core = own_row % 2
    tokens, width = stream.shape[2], stream.shape[3]
    layers = triple_weight.shape[0]

    def holder(p, r):
        return p * row_count + r if p == r % 2 else (1 - p) * row_count + (r ^ 1)

    swaps = [(p * row_count + r, holder(p, r)) for p in range(2) for r in range(row_count)]

    def swap(x):
        return lax.ppermute(x, ("pass", "rows"), swaps)

    valid = (jnp.arange(tokens) < lengths[0]).astype(F32)[:, None]
    hidden = swap(stream.reshape(tokens, width))
    length = swap(lengths)
    grad_hidden = swap((cotangent.reshape(tokens, width).astype(F32) * valid).astype(BF16))
    embed = jnp.where(core == 0, pass_embed[0:1], pass_embed[1:2]).astype(F32)
    nothing = jnp.zeros_like(embed)

    def vector(array, depth):
        return array[depth : depth + 1].astype(F32)

    kept = []
    for depth in range(layers):
        hidden, normed, scaled, inverse, query, kv = qkv(
            hidden, nothing if depth else embed, vector(first_gain, depth), vector(first_bias, depth),
            triple_weight[depth], depth,
        )
        kv = kv.reshape(2 * tokens, 2 * width)
        mixed, total, exps = attend(length, query, kv)
        hidden, normed_two, scaled_two, inverse_two, act, slope = ffn(
            hidden, mixed, merge_weight[depth], vector(second_gain, depth), vector(second_bias, depth),
            up_weight[depth], down_weight[depth],
        )
        kept.append(
            (normed, scaled, inverse, query, kv, mixed, total, exps, normed_two, scaled_two, inverse_two, act, slope)
        )
    output = (swap(hidden.astype(BF16)).astype(F32) * valid).astype(BF16).reshape(stream.shape)

    grad_hidden = grad_hidden.astype(F32)
    grads = [None] * layers
    smalls = [None] * layers
    for depth in reversed(range(layers)):
        (normed, scaled, inverse, query, kv, mixed, total, exps, normed_two, scaled_two, inverse_two, act, slope) = kept[depth]
        down_grad, up_grad, merge_grad, mid, grad_mixed, small_two = ffn_back(
            grad_hidden, act, slope, normed_two, scaled_two, inverse_two, mixed, vector(second_gain, depth),
            up_weight[depth], down_weight[depth], merge_weight[depth],
        )
        grad_query, own, recv = attend_back(
            query, kv, grad_mixed, mixed, total, exps, layers + depth
        )
        triple_grad, grad_hidden, small_one = qkv_back(
            grad_query, own, recv, normed, scaled, inverse, mid, vector(first_gain, depth), triple_weight[depth],
        )
        grads[depth] = (triple_grad, merge_grad, up_grad, down_grad)
        smalls[depth] = jnp.concatenate([small_one[:2], small_two], 0)
    input_grad = swap(grad_hidden.astype(BF16)).reshape(stream.shape)

    def reduce(per_layer):
        shares = [
            lax.psum_scatter(g, "rows", scatter_dimension=0, tiled=True) for g in per_layer
        ]
        return lax.psum(jnp.stack(shares), "pass").astype(F32)

    weight_grads = [reduce([grads[depth][i] for depth in range(layers)]) for i in range(4)]
    hidden_sum = small_one[2:3]
    pass_rows = jnp.where(jnp.arange(2)[:, None] == core, hidden_sum, 0.0)
    small = jnp.concatenate([pass_rows, *smalls], 0)
    small = lax.psum(small, ("pass", "rows"))
    share = width // row_count
    small = lax.dynamic_slice_in_dim(small, own_row * share, share, 1)
    pass_grad = small[:2]
    by_layer = small[2:].reshape(layers, 4, share)
    return (
        output, input_grad, pass_grad, by_layer[:, 0], by_layer[:, 1], weight_grads[0], weight_grads[1],
        by_layer[:, 2], by_layer[:, 3], weight_grads[2], weight_grads[3],
    )


def solution(mesh):
    token = P("pass", "rows", None, None)
    matrix = P(None, "rows", None)
    rows = P(None, "rows")
    in_specs = (token, P("rows")) + (P(),) * 9 + (token,)
    out_specs = (token, token, rows, rows, rows, matrix, matrix, rows, rows, matrix, matrix)
    return jax.shard_map(local, mesh=mesh, in_specs=in_specs, out_specs=out_specs, check_vma=False)
```

```python
import functools
import math

import jax
import jax.numpy as jnp
from jax import lax
from jax.experimental import pallas as pl
from jax.experimental.pallas import tpu as pltpu
from jax.sharding import PartitionSpec as P

HEAD_DIM = 64
EPSILON = 1e-05
SCALE = HEAD_DIM**-0.5
MESH = pl.DeviceIdType.MESH
NN = (((1,), (0,)), ((), ()))
NT = (((1,), (1,)), ((), ()))
TN = (((0,), (0,)), ((), ()))
BLOCK = 256
LANES = 128
BF16 = jnp.bfloat16
F32 = jnp.float32
VMEM_LIMIT = 62 * 2**20
ANY = pl.BlockSpec(memory_space=pl.ANY)


def dot(left, right, dims=NN):
    return lax.dot_general(left, right, dims, preferred_element_type=F32)


def sds(shape, dtype):
    return jax.ShapeDtypeStruct(shape, dtype)


def params(collective_id=None):
    return pltpu.CompilerParams(
        vmem_limit_bytes=VMEM_LIMIT,
        collective_id=collective_id,
        has_side_effects=collective_id is not None,
    )


def whole(shape):
    zeros = (0,) * len(shape)
    return pl.BlockSpec(shape, lambda *_: zeros, pipeline_mode=pl.Buffered(1))


def norm(hidden, gain, bias):
    centred = hidden - jnp.mean(hidden, -1, keepdims=True)
    inverse = lax.rsqrt(jnp.mean(centred * centred, -1, keepdims=True) + EPSILON)
    scaled = centred * inverse
    return (scaled * gain + bias).astype(BF16), scaled, inverse


def norm_back(grad, scaled, inverse, gain):
    e = grad * gain
    return inverse * (
        e - jnp.mean(e, -1, keepdims=True) - scaled * jnp.mean(e * scaled, -1, keepdims=True)
    )


def partner():
    rows = lax.axis_index("rows")
    return rows + 1 - 2 * (rows % 2)


def greet():
    barrier = pltpu.get_barrier_semaphore()
    pl.semaphore_signal(barrier, inc=1, device_id={"rows": partner()}, device_id_type=MESH)
    pl.semaphore_wait(barrier, 1)


def bits():
    row = lax.axis_index("rows")
    return row, row % 2, (row // 2) % 2, (row // 4) % 2, (row // 8) % 2, lax.axis_index("pass")


def send(src, dst, send_sem, recv_sem, device):
    return pltpu.make_async_remote_copy(
        src_ref=src, dst_ref=dst, send_sem=send_sem, recv_sem=recv_sem,
        device_id=device, device_id_type=MESH,
    )


def qkv_kernel(
    depth, kept, hidden_ref, embed_ref, gain_ref, bias_ref, weight_ref, *refs,
):
    full_ref, normed_ref, scaled_ref, inverse_ref, query_ref, kv_ref = refs[kept : kept + 6]
    held, local_sem, send_sem, recv_sem = refs[kept + 6 :]
    step = pl.program_id(0)
    own = lax.axis_index("rows") % 2
    width = hidden_ref.shape[1]

    @pl.when(step == 0)
    def _():
        greet()

    hidden = hidden_ref[...].astype(F32) + embed_ref[...]
    full_ref[...] = hidden
    normed, scaled, inverse = norm(hidden, gain_ref[...], bias_ref[...])
    normed_ref[0, 0] = normed
    scaled_ref[0, 0] = scaled.astype(BF16)
    inverse_ref[0, 0] = inverse
    keys = dot(normed, weight_ref[0, :, width:])
    held[step] = keys.astype(BF16)

    def copies(i):
        there = send(held.at[i], kv_ref.at[depth, i, own], send_sem.at[i], recv_sem.at[i], {"rows": partner()})
        here = pltpu.make_async_copy(held.at[i], kv_ref.at[depth, i, own], local_sem.at[i])
        return there, here

    there, here = copies(step)
    there.start()
    here.start()
    queries = dot(normed, weight_ref[0, :, :width])
    query_ref[0] = (queries.astype(BF16).astype(F32) * SCALE).astype(BF16)

    @pl.when(step == pl.num_programs(0) - 1)
    def _():
        for i in range(held.shape[0]):
            there, here = copies(i)
            there.wait()
            here.wait()


def qkv(depth, layers, hidden, embed, gain, bias, weight, kept):
    tokens, width = hidden.shape
    steps = tokens // BLOCK
    tile = pl.BlockSpec((BLOCK, width), lambda i: (i, 0))
    own = pl.BlockSpec((1, 1, BLOCK, width), lambda i: (depth, 1, i, 0))
    return pl.pallas_call(
        functools.partial(qkv_kernel, depth, len(kept)),
        grid=(steps,),
        in_specs=[
            tile, whole((1, width)), whole((1, width)), whole((1, width)),
            pl.BlockSpec((1,) + weight.shape[1:], lambda i: (depth, 0, 0), pipeline_mode=pl.Buffered(1)),
        ] + [ANY] * len(kept),
        out_specs=[
            tile, own, own,
            pl.BlockSpec((1, 1, BLOCK, 1), lambda i: (depth, 1, i, 0)),
            pl.BlockSpec((1, BLOCK, width), lambda i: (depth, i, 0)),
            ANY,
        ],
        out_shape=[
            sds((tokens, width), F32),
            sds((layers, 2, tokens, width), BF16),
            sds((layers, 2, tokens, width), BF16),
            sds((layers, 2, tokens, 1), F32),
            sds((layers, tokens, width), BF16),
            sds((layers, steps, 2, BLOCK, 2 * width), BF16),
        ],
        input_output_aliases={5 + i: 1 + i for i in range(len(kept))},
        scratch_shapes=[
            pltpu.VMEM((steps, BLOCK, 2 * width), BF16),
            pltpu.SemaphoreType.DMA((steps,)),
            pltpu.SemaphoreType.DMA((steps,)),
            pltpu.SemaphoreType.DMA((steps,)),
        ],
        compiler_params=params(depth),
        name="qkv",
    )(hidden, embed, gain, bias, weight, *kept)


def tile_index(blocks, key_block, query_block):
    return key_block * blocks - key_block * (key_block - 1) // 2 + query_block - key_block


def attend_kernel(kept, length_ref, query_ref, key_ref, value_ref, *refs):
    mixed_ref, total_ref, exp_ref = refs[kept:]
    own = lax.axis_index("rows") % 2
    tokens = query_ref.shape[1]
    blocks = tokens // BLOCK
    pair = 2 * BLOCK
    lane = lax.broadcasted_iota(jnp.int32, (BLOCK, LANES), 1)
    query_at = lax.broadcasted_iota(jnp.int32, (BLOCK, pair), 0)
    column = lax.broadcasted_iota(jnp.int32, (BLOCK, pair), 1)
    key_pass = column // BLOCK
    key_at = column - key_pass * BLOCK
    causal = (key_at < query_at) | ((key_at == query_at) & (key_pass <= own))
    length = length_ref[0]
    ones = jnp.ones((tokens * 2, LANES), BF16)
    values = jnp.concatenate([value_ref[0], ones], 1)
    for block in range(blocks):
        rows = pl.ds(block * BLOCK, BLOCK)

        @pl.when(block * BLOCK < length)
        def _():
            allowed = causal & (key_at < length - block * BLOCK)
            query = query_ref[0, rows, :]
            outs = []
            for head in range(2):
                chosen = jnp.where(lane // HEAD_DIM == head, query, jnp.zeros_like(query))
                raw = dot(chosen, key_ref[0, : (block + 1) * pair, :], NT)
                last = jnp.where(allowed, raw[:, block * pair :], -jnp.inf)
                top = jnp.max(last, -1, keepdims=True)
                if block:
                    top = jnp.maximum(top, jnp.max(raw[:, : block * pair], -1, keepdims=True))
                parts = [jnp.exp(raw[:, k * pair : (k + 1) * pair] - top).astype(BF16) for k in range(block)]
                parts.append(jnp.exp(last - top).astype(BF16))
                for k, part in enumerate(parts):
                    exp_ref[0, head, tile_index(blocks, k, block)] = part
                mixed = dot(jnp.concatenate(parts, 1), values[: (block + 1) * pair])
                inverse = 1.0 / mixed[:, LANES : LANES + 1]
                total_ref[0, 0, rows, head : head + 1] = inverse
                outs.append(mixed[:, :LANES] * inverse)
            mixed_ref[0, rows, :] = jnp.where(lane < HEAD_DIM, outs[0], outs[1]).astype(BF16)

        @pl.when(block * BLOCK >= length)
        def _():
            mixed_ref[0, rows, :] = jnp.zeros((BLOCK, LANES), BF16)
            total_ref[0, 0, rows, :] = jnp.zeros((BLOCK, 2), F32)
            for head in range(2):
                for k in range(block + 1):
                    exp_ref[0, head, tile_index(blocks, k, block)] = jnp.zeros((BLOCK, pair), BF16)


def attend(depth, length, query, kv, kept):
    layers, tokens, width = query.shape
    blocks = tokens // BLOCK
    tiles = blocks * (blocks + 1) // 2
    pairs = width // LANES
    column = pl.BlockSpec((1, tokens, LANES), lambda h: (depth, 0, h))
    return pl.pallas_call(
        functools.partial(attend_kernel, len(kept)),
        grid=(pairs,),
        in_specs=[
            pl.BlockSpec(memory_space=pltpu.SMEM),
            column,
            pl.BlockSpec((1, 2 * tokens, LANES), lambda h: (depth, 0, h)),
            pl.BlockSpec((1, 2 * tokens, LANES), lambda h: (depth, 0, h + pairs)),
        ] + [ANY] * len(kept),
        out_specs=[
            column,
            pl.BlockSpec((1, 1, tokens, 2), lambda h: (depth, h, 0, 0)),
            pl.BlockSpec((1, 2, tiles, BLOCK, 2 * BLOCK), lambda h: (depth, h, 0, 0, 0)),
        ],
        out_shape=[
            sds((layers, tokens, width), BF16),
            sds((layers, pairs, tokens, 2), F32),
            sds((layers, 2 * pairs, tiles, BLOCK, 2 * BLOCK), BF16),
        ],
        input_output_aliases={4 + i: i for i in range(len(kept))},
        compiler_params=params(),
        name="attend",
    )(length, query, kv, kv, *kept)


def gelu_both(v):
    root = math.sqrt(2.0 / math.pi)
    square = v * v
    t = jnp.tanh(v * (root + (root * 0.044715) * square))
    half = 0.5 * (1.0 + t)
    slope = half + 0.5 * v * (1.0 - t * t) * (root + (3.0 * root * 0.044715) * square)
    return v * half, slope


def ffn_kernel(
    kept, hidden_ref, mixed_ref, merge_ref, gain_ref, bias_ref, up_ref, down_ref, *refs,
):
    next_ref, normed_ref, scaled_ref, inverse_ref, act_ref, slope_ref = refs[kept:]
    mid = hidden_ref[...] + dot(mixed_ref[0], merge_ref[0])
    normed, scaled, inverse = norm(mid, gain_ref[...], bias_ref[...])
    normed_ref[0, 0] = normed
    scaled_ref[0, 0] = scaled.astype(BF16)
    inverse_ref[0, 0] = inverse
    total = mid
    hidden_units = up_ref.shape[2]
    part = mid.shape[1]
    for first in range(0, hidden_units, part):
        act, slope = gelu_both(dot(normed, up_ref[0, :, first : first + part]))
        act = act.astype(BF16)
        act_ref[0, :, first : first + part] = act
        slope_ref[0, :, first : first + part] = slope.astype(BF16)
        total = total + dot(act, down_ref[0, first : first + part, :])
    next_ref[...] = total


def ffn(depth, hidden, mixed, merge, gain, bias, up, down, kept):
    tokens, width = hidden.shape
    layers, _, units = up.shape
    tile = pl.BlockSpec((BLOCK, width), lambda i: (i, 0))
    own = pl.BlockSpec((1, 1, BLOCK, width), lambda i: (depth, 0, i, 0))
    wide = pl.BlockSpec((1, BLOCK, units), lambda i: (depth, i, 0))

    def layer(weight):
        return pl.BlockSpec((1,) + weight.shape[1:], lambda i: (depth, 0, 0), pipeline_mode=pl.Buffered(1))

    return pl.pallas_call(
        functools.partial(ffn_kernel, len(kept)),
        grid=(tokens // BLOCK,),
        in_specs=[
            tile, pl.BlockSpec((1, BLOCK, width), lambda i: (depth, i, 0)), layer(merge),
            whole((1, width)), whole((1, width)), layer(up), layer(down),
        ] + [ANY] * len(kept),
        out_specs=[tile, own, own, pl.BlockSpec((1, 1, BLOCK, 1), lambda i: (depth, 0, i, 0)), wide, wide],
        out_shape=[
            sds((tokens, width), F32),
            sds((layers, 2, tokens, width), BF16),
            sds((layers, 2, tokens, width), BF16),
            sds((layers, 2, tokens, 1), F32),
            sds((layers, tokens, units), BF16),
            sds((layers, tokens, units), BF16),
        ],
        input_output_aliases={7 + i: 1 + i for i in range(len(kept))},
        compiler_params=params(),
        name="ffn",
    )(hidden, mixed, merge, gain, bias, up, down, *kept)


FFN_STEPS = 4
PAIRS = 6
STEPS = FFN_STEPS + PAIRS + 3
NO_PIECE = 9
STAGES = 5
ROWS = 16
SHARE = 48
SMALL = 16


def back_kernel(
    layers, hosted,
    cot_ref, act_ref, slope_ref, normed_ref, scaled_ref, inverse_ref, mixed_ref, up_ref, down_ref, merge_ref,
    first_gain_ref, second_gain_ref, query_ref, key_ref, value_ref, total_ref, exp_ref, weight_ref,
    out_ref, small_ref, input_ref,
    grad, low, total, grads, pending, landing, exps,
    staged, sums0, sums1, sums2, sums3, got0, got1, got2, got3, got4, final, small, small_got,
    exp_sem, cot_sem, kv_send, kv_recv, stage_send, stage_recv, out_sem, small_send, small_recv, swap_send, swap_recv,
    here_sem,
):
    t = pl.program_id(0)
    j = t % STEPS
    layer = layers - 1 - t // STEPS
    row, core, x, z0, z1, own_pass = bits()
    tokens, width = grad.shape
    blocks = tokens // BLOCK
    pair = 2 * BLOCK
    busy = t < layers * STEPS
    core_mate = {"rows": row + 1 - 2 * core}
    mates = [
        core_mate, {"rows": row + 2 - 4 * x}, {"rows": row + 4 - 8 * z0}, {"rows": row + 8 - 16 * z1},
        {"pass": 1 - own_pass},
    ]
    diagonal = {"pass": 1 - own_pass, "rows": row + 1 - 2 * core}
    swapped = own_pass != core

    @pl.when(t == 0)
    def _():
        barrier = pltpu.get_barrier_semaphore()
        greeted = mates if hosted else mates[:1]
        for mate in greeted:
            pl.semaphore_signal(barrier, inc=1, device_id=mate, device_id_type=MESH)

        @pl.when(swapped)
        def _():
            pl.semaphore_signal(barrier, inc=1, device_id=diagonal, device_id_type=MESH)

        pl.semaphore_wait(barrier, len(greeted) + jnp.where(swapped, 1, 0))
        load = pltpu.make_async_copy(cot_ref, low, cot_sem)
        load.start()
        load.wait()
        grad[...] = low[...].astype(F32)
        small[...] = jnp.zeros_like(small)


    def exp_copy(head):
        return pltpu.make_async_copy(exp_ref.at[layer, head], exps.at[head % 2], exp_sem.at[head % 2])

    def put(slot, r, value):
        staged[slot, r % 2, (r // 2) % 2, (r // 4) % 2, (r // 8) % 2] = value

    @pl.when(busy & (j < FFN_STEPS))
    def _():
        @pl.when(j == 0)
        def _():
            total[...] = jnp.zeros_like(total)

        grad_low = low[...]
        down_grad = dot(act_ref[0], grad_low, TN).astype(BF16)
        for q in range(4):
            for i in range(4):
                first = q * 4 * SHARE + i * SHARE
                staged[i, q % 2, q // 2, j % 2, (j // 2) % 2] = down_grad[first : first + SHARE]
        grad_act = dot(grad_low, down_ref[0], NT)
        grad_pre = (slope_ref[0].astype(F32) * grad_act).astype(BF16)
        up_grad = dot(normed_ref[0, 0], grad_pre, TN).astype(BF16)
        for r in range(ROWS):
            put(4 + j % 2, r, up_grad[r * SHARE : (r + 1) * SHARE])
        total[...] += dot(grad_pre, up_ref[0], NT)

        @pl.when(j == FFN_STEPS - 1)
        def _():
            exp_copy(0).start()

            def rows(i, sums):
                at = pl.ds(pl.multiple_of(i * BLOCK, BLOCK), BLOCK)
                part = total[at, :]
                scaled = scaled_ref[0, 0, at, :].astype(F32)
                mid = grad[at, :] + norm_back(part, scaled, inverse_ref[0, 0, at, :], second_gain_ref[0])
                grad[at, :] = mid
                low_mid = mid.astype(BF16)
                low[at, :] = low_mid
                grads[0, at, :] = dot(low_mid, merge_ref[0], NT).astype(BF16)
                return (
                    sums[0] + jnp.sum(part * scaled, 0, keepdims=True),
                    sums[1] + jnp.sum(part, 0, keepdims=True),
                )

            empty = jnp.zeros((1, width), F32)
            gain_sum, bias_sum = lax.fori_loop(0, blocks, rows, (empty, empty))
            small[pl.ds(4 + 4 * layer, 1), :] = gain_sum
            small[pl.ds(5 + 4 * layer, 1), :] = bias_sum
            merge_grad = dot(mixed_ref[0], low[...], TN).astype(BF16)
            for r in range(ROWS):
                put(6, r, merge_grad[r * SHARE : (r + 1) * SHARE])


    def kv_copy(p):
        return send(
            pending.at[p % 2], landing.at[p % 2], kv_send.at[p % 2], kv_recv.at[p % 2], core_mate,
        )

    def take(p):
        kv_copy(p).wait()
        lanes = pl.ds(pl.multiple_of(p * LANES, LANES), LANES)
        for which in range(2):
            grads[1 + which, :, lanes] = (
                grads[1 + which, :, lanes].astype(F32) + landing[p % 2, which].astype(F32)
            ).astype(BF16)

    @pl.when(busy & (j >= FFN_STEPS) & (j < FFN_STEPS + PAIRS))
    def _():
        p = j - FFN_STEPS
        lanes = pl.ds(pl.multiple_of(p * LANES, LANES), LANES)
        lane = lax.broadcasted_iota(jnp.int32, (tokens, LANES), 1)
        out_grad = grads[0, :, lanes].astype(F32)
        product = out_grad * mixed_ref[0, :, lanes].astype(F32)
        query = query_ref[0]
        sums = []
        for head in range(2):
            if head:
                @pl.when(p < PAIRS - 1)
                def _():
                    exp_copy(2 * p + 2).start()
            else:
                exp_copy(2 * p + 1).start()
            exp_copy(2 * p + head).wait()
            mine = lane // HEAD_DIM == head
            inverse = total_ref[0, 0, :, head : head + 1]
            scaled = jnp.where(mine, out_grad * inverse, 0.0).astype(BF16)
            inner = jnp.sum(jnp.where(mine, product, 0.0), -1, keepdims=True) * inverse
            chosen = jnp.where(mine, query, jnp.zeros_like(query))
            mine_lanes = slice(head * LANES, (head + 1) * LANES)
            for block in range(blocks):
                first = block * BLOCK
                keys = pl.ds(block * pair, pair)
                start = tile_index(blocks, block, block)
                prob = exps[head, start : start + blocks - block].reshape(tokens - first, pair)
                grad_prob = dot(scaled[first:], value_ref[0, keys, :], NT)
                score = (prob.astype(F32) * (grad_prob - inner[first:])).astype(BF16)
                grad_value = dot(prob, scaled[first:], TN)
                grad_key = dot(score, chosen[first:], TN)
                grad_query = dot(score, key_ref[0, keys, :])
                if block == 0:
                    total[:, mine_lanes] = grad_query
                else:
                    total[first:, mine_lanes] += grad_query
                if head == 0:
                    sums.append((grad_key, grad_value))
                else:
                    for which, value in enumerate((grad_key, grad_value)):
                        both = sums[block][which] + value
                        zero, one = both[:BLOCK], both[BLOCK:]
                        at = pl.ds(first, BLOCK)
                        grads[1 + which, at, lanes] = jnp.where(core == 0, zero, one).astype(BF16)
                        pending[p % 2, which, at, :] = jnp.where(core == 0, one, zero).astype(BF16)
        grads[0, :, lanes] = (
            jnp.where(lane < HEAD_DIM, total[:, :LANES], total[:, LANES : 2 * LANES]) * SCALE
        ).astype(BF16)

        @pl.when(p > 0)
        def _():
            take(p - 1)

        kv_copy(p).start()


    @pl.when(busy & (j >= FFN_STEPS + PAIRS))
    def _():
        n = j - FFN_STEPS - PAIRS

        @pl.when(n == 0)
        def _():
            total[...] = jnp.zeros_like(total)

        @pl.when(n == 0)
        def _():
            take(PAIRS - 1)

        part = grads[n]
        triple_grad = dot(normed_ref[0, 0], part, TN).astype(BF16)
        for r in range(ROWS):
            put(4 + n, r, triple_grad[r * SHARE : (r + 1) * SHARE])
        total[...] += dot(part, weight_ref[0], NT)

        @pl.when(n == 2)
        def _():
            def rows(i, sums):
                at = pl.ds(pl.multiple_of(i * BLOCK, BLOCK), BLOCK)
                part = total[at, :]
                scaled = scaled_ref[0, 0, at, :].astype(F32)
                hidden = grad[at, :] + norm_back(part, scaled, inverse_ref[0, 0, at, :], first_gain_ref[0])
                grad[at, :] = hidden
                low[at, :] = hidden.astype(BF16)
                return (
                    sums[0] + jnp.sum(part * scaled, 0, keepdims=True),
                    sums[1] + jnp.sum(part, 0, keepdims=True),
                    sums[2] + jnp.sum(hidden, 0, keepdims=True),
                )

            empty = jnp.zeros((1, width), F32)
            gain_sum, bias_sum, hidden_sum = lax.fori_loop(0, blocks, rows, (empty, empty, empty))
            small[pl.ds(2 + 4 * layer, 1), :] = gain_sum
            small[pl.ds(3 + 4 * layer, 1), :] = bias_sum

            @pl.when(layer == 0)
            def _():
                small[pl.ds(core, 1), :] = hidden_sum


    last = layers * STEPS - 1

    def slot(v):
        i = v % STEPS
        return jnp.where(
            i < 4, 4 + i % 2, jnp.where(i < 8, i - 4, jnp.where(i == 8, 6, i - FFN_STEPS - PAIRS + 4))
        )

    def whether(v):
        return (v >= 0) & (v <= last) & (v % STEPS != NO_PIECE)

    def half(v):
        return (v - v // STEPS - jnp.where(v % STEPS > NO_PIECE, 1, 0)) % 2

    def out_copy(v):
        h = half(v)
        return pltpu.make_async_copy(final.at[h], out_ref.at[v], out_sem.at[h])

    def stage(s, v):
        h = half(v)
        src = (staged.at[slot(v), 1 - core], sums0.at[h, 1 - x], sums1.at[h, 1 - z0], sums2.at[h, 1 - z1], sums3.at[h])[s]
        dst = (got0, got1, got2, got3, got4)[s].at[h]
        return send(src, dst, stage_send.at[s, h], stage_recv.at[s, h], mates[s])

    def add(a, b):
        return (a.astype(F32) + b.astype(F32)).astype(BF16)

    if hosted:
        @pl.when(whether(t - 6))
        def _():
            out_copy(t - 6).wait()

        @pl.when(whether(t - 5))
        def _():
            v = t - 5
            h = half(v)
            stage(4, v).wait()
            final[h] = sums3[h].astype(F32) + got4[h].astype(F32)
            out_copy(v).start()

        @pl.when(whether(t - 4))
        def _():
            v = t - 4
            h = half(v)
            stage(3, v).wait()
            sums3[h] = add(sums2[h, z1], got3[h])
            stage(4, v).start()

        @pl.when(whether(t - 3))
        def _():
            v = t - 3
            h = half(v)
            stage(2, v).wait()
            sums2[h] = add(sums1[h, z0], got2[h])
            stage(3, v).start()

        @pl.when(whether(t - 2))
        def _():
            v = t - 2
            h = half(v)
            stage(1, v).wait()
            sums1[h] = add(sums0[h, x], got1[h])
            stage(2, v).start()

        @pl.when(whether(t - 1))
        def _():
            v = t - 1
            h = half(v)
            stage(0, v).wait()
            sums0[h] = add(staged[slot(v), core], got0[h])
            stage(1, v).start()

        @pl.when(whether(t))
        def _():
            stage(0, t).start()

        for s in range(STAGES + 1):
            def small_copy(s):
                return send(small, small_got.at[s], small_send.at[s], small_recv.at[s], mates[s])

            @pl.when(t == last + s)
            def _():
                if s:
                    small_copy(s - 1).wait()
                    small[...] += small_got[s - 1]
                if s < STAGES:
                    small_copy(s).start()
    else:
        def piece_copy(v):
            return pltpu.make_async_copy(staged.at[slot(v)], out_ref.at[v], out_sem.at[v % 2])

        @pl.when(whether(t - 1))
        def _():
            piece_copy(t - 1).wait()

        @pl.when(whether(t))
        def _():
            piece_copy(t).start()


    def swap_copy():
        return send(low, input_ref, swap_send, swap_recv, diagonal)

    def here_copy():
        return pltpu.make_async_copy(low, input_ref, here_sem)

    @pl.when((t == last) & swapped)
    def _():
        swap_copy().start()

    @pl.when((t == last) & jnp.logical_not(swapped))
    def _():
        here_copy().start()

    @pl.when(t == pl.num_programs(0) - 1)
    def _():
        @pl.when(swapped)
        def _():
            swap_copy().wait()

        @pl.when(jnp.logical_not(swapped))
        def _():
            here_copy().wait()

        small_ref[...] = small[...]


def back(cotangent, act, slope, normeds, scaleds, inverses, mixed, up, down, merge, first_gain, second_gain, query, kv,
         total, exps, weight, hosted):
    layers, tokens, width = query.shape
    tiles = exps.shape[2]
    steps = layers * STEPS + (STAGES + 2 if hosted else 1)
    piece = (2, 2, 2, 2, SHARE, width)

    def at(t):
        t = jnp.minimum(t, layers * STEPS - 1)
        return layers - 1 - t // STEPS, t % STEPS

    def tile_of(t):
        layer, j = at(t)
        return layer, jnp.minimum(j, FFN_STEPS - 1)

    def head_of(t):
        layer, j = at(t)
        return layer, jnp.clip(j - FFN_STEPS, 0, PAIRS - 1)

    def part_of(t):
        layer, j = at(t)
        return layer, jnp.clip(j - FFN_STEPS - PAIRS, 0, 2)

    def kind_of(t):
        layer, j = at(t)
        return layer, (j >= FFN_STEPS).astype(jnp.int32), 0, 0

    once = dict(pipeline_mode=pl.Buffered(1))

    def of_layer(shape):
        return pl.BlockSpec((1,) + shape, lambda t: (at(t)[0],) + (0,) * len(shape), **once)

    units = pl.BlockSpec((1, tokens, width), lambda t: (tile_of(t)[0], 0, tile_of(t)[1]))
    in_specs = [
        ANY, units, units,
        pl.BlockSpec((1, 1, tokens, width), kind_of, **once),
        pl.BlockSpec((1, 1, tokens, width), kind_of, **once),
        pl.BlockSpec((1, 1, tokens, 1), kind_of, **once),
        of_layer((tokens, width)),
        pl.BlockSpec((1, width, width), lambda t: (tile_of(t)[0], 0, tile_of(t)[1])),
        pl.BlockSpec((1, width, width), lambda t: (tile_of(t)[0], tile_of(t)[1], 0)),
        of_layer((width, width)),
        of_layer((1, width)), of_layer((1, width)),
        pl.BlockSpec((1, tokens, LANES), lambda t: (head_of(t)[0], 0, head_of(t)[1])),
        pl.BlockSpec((1, 2 * tokens, LANES), lambda t: (head_of(t)[0], 0, head_of(t)[1])),
        pl.BlockSpec((1, 2 * tokens, LANES), lambda t: (head_of(t)[0], 0, head_of(t)[1] + PAIRS)),
        pl.BlockSpec((1, 1, tokens, 2), lambda t: (head_of(t)[0], head_of(t)[1], 0, 0)),
        ANY,
        pl.BlockSpec((1, width, width), lambda t: (part_of(t)[0], 0, part_of(t)[1]), **once),
    ]
    out_piece = sds((layers * STEPS, SHARE, width), F32) if hosted else sds((layers * STEPS,) + piece, BF16)
    dma = pltpu.SemaphoreType.DMA

    def some(*shape):
        return pltpu.VMEM(shape, BF16)

    return pl.pallas_call(
        functools.partial(back_kernel, layers, hosted),
        grid=(steps,),
        in_specs=in_specs,
        out_specs=[ANY, whole((SMALL, width)), ANY],
        out_shape=[out_piece, sds((SMALL, width), F32), sds((tokens, width), BF16)],
        scratch_shapes=[
            pltpu.VMEM((tokens, width), F32),
            some(tokens, width),
            pltpu.VMEM((tokens, width), F32),
            some(3, tokens, width),
            some(2, 2, tokens, LANES),
            some(2, 2, tokens, LANES),
            some(2, tiles, BLOCK, 2 * BLOCK),
            some(7, *piece),
            some(2, *piece[1:]), some(2, *piece[2:]), some(2, *piece[3:]), some(2, *piece[4:]),
            some(2, *piece[1:]), some(2, *piece[2:]), some(2, *piece[3:]), some(2, *piece[4:]), some(2, *piece[4:]),
            pltpu.VMEM((2, SHARE, width), F32),
            pltpu.VMEM((SMALL, width), F32),
            pltpu.VMEM((STAGES, SMALL, width), F32),
            dma((2,)), dma, dma((2,)), dma((2,)), dma((STAGES, 2)), dma((STAGES, 2)), dma((2,)),
            dma((STAGES,)), dma((STAGES,)), dma, dma, dma,
        ],
        compiler_params=params(layers),
        name="back",
    )(cotangent, act, slope, normeds, scaleds, inverses, mixed, up, down, merge, first_gain, second_gain, query, kv, kv,
      total, exps, weight)


def local(
    stream, lengths, pass_embed, first_gain, first_bias, triple_weight, merge_weight,
    second_gain, second_bias, up_weight, down_weight, cotangent,
):
    row_count = lax.axis_size("rows")
    own_row = lax.axis_index("rows")
    core = own_row % 2
    tokens, width = stream.shape[2], stream.shape[3]
    layers = triple_weight.shape[0]
    hosted = row_count == ROWS

    def holder(p, r):
        return p * row_count + r if p == r % 2 else (1 - p) * row_count + (r ^ 1)

    swaps = [(p * row_count + r, holder(p, r)) for p in range(2) for r in range(row_count)]

    def swap(x):
        return lax.ppermute(x, ("pass", "rows"), swaps)

    valid = (jnp.arange(tokens) < lengths[0]).astype(F32)[:, None]
    hidden = swap(stream.reshape(tokens, width))
    length = swap(lengths)
    cotangent = swap((cotangent.reshape(tokens, width).astype(F32) * valid).astype(BF16))
    embed = jnp.where(core == 0, pass_embed[0:1], pass_embed[1:2]).astype(F32)
    nothing = jnp.zeros_like(embed)

    def vector(array, depth):
        return array[depth : depth + 1].astype(F32)

    qkv_kept, attend_kept, ffn_kept = [], [], []
    for depth in range(layers):
        hidden, *qkv_kept = qkv(
            depth, layers, hidden, nothing if depth else embed, vector(first_gain, depth), vector(first_bias, depth),
            triple_weight, qkv_kept,
        )
        normeds, scaleds, inverses, query, kv_blocks = qkv_kept
        kv = kv_blocks.reshape(layers, 2 * tokens, 2 * width)
        attend_kept = attend(depth, length, query, kv, attend_kept)
        hidden, *ffn_kept = ffn(
            depth, hidden, attend_kept[0], merge_weight, vector(second_gain, depth), vector(second_bias, depth),
            up_weight, down_weight, [normeds, scaleds, inverses, *ffn_kept[3:]],
        )
        qkv_kept = [*ffn_kept[:3], query, kv_blocks]
    normeds, scaleds, inverses, act, slope = ffn_kept
    mixed, total, exps = attend_kept
    output = (swap(hidden.astype(BF16)).astype(F32) * valid).astype(BF16).reshape(stream.shape)

    pieces, small, input_grad = back(
        cotangent, act, slope, normeds, scaleds, inverses, mixed, up_weight, down_weight, merge_weight,
        first_gain.astype(F32)[:, None], second_gain.astype(F32)[:, None], query, kv, total, exps, triple_weight, hosted,
    )
    input_grad = input_grad.reshape(stream.shape)
    if hosted:
        pieces = pieces.reshape(layers, STEPS, SHARE, width)
    else:
        pieces = pieces.reshape(layers, STEPS, 2, 2, 2, 2, SHARE, width).transpose(0, 1, 5, 4, 3, 2, 6, 7)
    pieces = pieces[::-1]

    def columns(first, last):
        some = pieces[:, first:last]
        some = some.reshape(layers, last - first, -1, width)
        return some.transpose(0, 2, 1, 3).reshape(layers, -1, (last - first) * width)

    up_grad = columns(0, 4)
    merge_grad = columns(8, 9)
    triple_grad = columns(10, 13)
    down_grad = pieces[:, 4:8]
    if hosted:
        down_grad = down_grad.reshape(layers, 4 * SHARE, width)
    else:
        down_grad = down_grad.reshape(layers, 4, ROWS, SHARE, width).transpose(0, 2, 1, 3, 4).reshape(layers, -1, width)

        def reduce(gradient):
            share = lax.psum_scatter(gradient, "rows", scatter_dimension=1, tiled=True)
            return lax.psum(share, "pass").astype(F32)

        up_grad, merge_grad, triple_grad, down_grad = map(reduce, (up_grad, merge_grad, triple_grad, down_grad))
        small = lax.psum(small, ("pass", "rows"))
    share = width // row_count
    small = lax.dynamic_slice_in_dim(small, own_row * share, share, 1)
    by_layer = small[2 : 2 + 4 * layers].reshape(layers, 4, share)
    return (
        output, input_grad, small[:2], by_layer[:, 0], by_layer[:, 1], triple_grad, merge_grad,
        by_layer[:, 2], by_layer[:, 3], up_grad, down_grad,
    )


def solution(mesh):
    token = P("pass", "rows", None, None)
    matrix = P(None, "rows", None)
    rows = P(None, "rows")
    in_specs = (token, P("rows")) + (P(),) * 9 + (token,)
    out_specs = (token, token, rows, rows, rows, matrix, matrix, rows, rows, matrix, matrix)
    return jax.shard_map(local, mesh=mesh, in_specs=in_specs, out_specs=out_specs, check_vma=False)
```

```python
import functools
import math

import jax
import jax.numpy as jnp
from jax import lax
from jax.experimental import pallas as pl
from jax.experimental.pallas import tpu as pltpu
from jax.sharding import PartitionSpec as P

HEAD_DIM = 64
EPSILON = 1e-05
SCALE = HEAD_DIM**-0.5
MESH = pl.DeviceIdType.MESH
NN = (((1,), (0,)), ((), ()))
NT = (((1,), (1,)), ((), ()))
TN = (((0,), (0,)), ((), ()))
BLOCK = 128
TILE = 256
LANES = 128
BF16 = jnp.bfloat16
F32 = jnp.float32
VMEM_LIMIT = 62 * 2**20
ANY = pl.BlockSpec(memory_space=pl.ANY)


def dot(left, right, dims=NN):
    return lax.dot_general(left, right, dims, preferred_element_type=F32)


def sds(shape, dtype):
    return jax.ShapeDtypeStruct(shape, dtype)


def params(collective_id=None):
    return pltpu.CompilerParams(
        vmem_limit_bytes=VMEM_LIMIT,
        collective_id=collective_id,
        has_side_effects=collective_id is not None,
    )


def whole(shape):
    zeros = (0,) * len(shape)
    return pl.BlockSpec(shape, lambda *_: zeros, pipeline_mode=pl.Buffered(1))


def norm(hidden, gain, bias):
    centred = hidden - jnp.mean(hidden, -1, keepdims=True)
    inverse = lax.rsqrt(jnp.mean(centred * centred, -1, keepdims=True) + EPSILON)
    scaled = centred * inverse
    return (scaled * gain + bias).astype(BF16), scaled, inverse


def norm_back(grad, scaled, inverse, gain):
    e = grad * gain
    return inverse * (
        e - jnp.mean(e, -1, keepdims=True) - scaled * jnp.mean(e * scaled, -1, keepdims=True)
    )


def bits():
    row = lax.axis_index("rows")
    return row, row % 2, (row // 2) % 2, (row // 4) % 2, (row // 8) % 2, lax.axis_index("pass")


def send(src, dst, send_sem, recv_sem, device):
    return pltpu.make_async_remote_copy(
        src_ref=src, dst_ref=dst, send_sem=send_sem, recv_sem=recv_sem,
        device_id=device, device_id_type=MESH,
    )


QKV_STEPS = 4
PAIRS = 6
FFN_TILES = 4
FORWARD = QKV_STEPS + PAIRS + FFN_TILES


def tile_index(blocks, key_block, query_block):
    return key_block * blocks - key_block * (key_block - 1) // 2 + query_block - key_block


def gelu_both(v):
    root = math.sqrt(2.0 / math.pi)
    cube = (root * 0.044715) * (v * v)
    half = 0.5 + 0.5 * jnp.tanh(v * (root + cube))
    act = v * half
    return act, half + (act - act * half) * (2.0 * root + 6.0 * cube)


def forward_kernel(
    layers,
    stream_ref, cot_ref, length_ref, embed_ref, first_gain_ref, first_bias_ref, second_gain_ref, second_bias_ref,
    triple_ref, merge_ref, up_ref, down_ref,
    normed_ref, scaled_ref, inverse_ref, query_ref, mixed_ref, total_ref, exp_ref, act_ref, slope_ref, kv_ref,
    out_ref, cot_out_ref, length_out_ref,
    hidden, arrived, length_here, queries, kv, values, mixes, triple, merge, up, down,
    weight_sem, kv_sem, kv_send, kv_recv, free_sem, swap_send, swap_recv, here_sem,
):
    t = pl.program_id(0)
    layer = t // FORWARD
    j = t % FORWARD
    row, core, _, _, _, own_pass = bits()
    tokens, width = hidden.shape
    blocks = tokens // BLOCK
    pair = 2 * BLOCK
    core_mate = {"rows": row + 1 - 2 * core}
    diagonal = {"pass": 1 - own_pass, "rows": row + 1 - 2 * core}
    swapped = own_pass != core


    def moves(i):
        if i < QKV_STEPS:
            rows = pl.ds(i * TILE, TILE)
            ends = stream_ref.at[rows, :], arrived.at[rows, :]
        else:
            ends = ((cot_ref, cot_out_ref), (length_ref, length_here))[i - QKV_STEPS]
        return (
            send(*ends, swap_send.at[i], swap_recv.at[i], diagonal),
            pltpu.make_async_copy(*ends, here_sem.at[i]),
        )

    def move(i, act):
        there, here = moves(i)

        @pl.when(swapped)
        def _():
            getattr(there, act)()

        @pl.when(jnp.logical_not(swapped))
        def _():
            getattr(here, act)()


    def weight_copies(which, of_layer):
        refs = ((triple_ref, triple), (merge_ref, merge), (up_ref, up), (down_ref, down))
        source, target = refs[which]
        return pltpu.make_async_copy(source.at[of_layer], target, weight_sem.at[which])

    @pl.when(t == 0)
    def _():
        barrier = pltpu.get_barrier_semaphore()
        pl.semaphore_signal(barrier, inc=1, device_id=core_mate, device_id_type=MESH)

        @pl.when(swapped)
        def _():
            pl.semaphore_signal(barrier, inc=1, device_id=diagonal, device_id_type=MESH)

        pl.semaphore_wait(barrier, 1 + jnp.where(swapped, 1, 0))
        move(QKV_STEPS + 1, "start")
        for i in range(QKV_STEPS):
            move(i, "start")
        for which in range(4):
            weight_copies(which, 0).start()
        move(QKV_STEPS + 1, "wait")
        length_out_ref[...] = length_here[...]

    for i in range(QKV_STEPS):
        @pl.when(t == i)
        def _():
            move(i, "wait")
            if i == QKV_STEPS - 1:
                move(QKV_STEPS, "start")


    def kv_copy(i):
        part = kv.at[pl.ds(i * (TILE // BLOCK), TILE // BLOCK), core]
        return send(part, part, kv_send.at[i], kv_recv.at[i], core_mate)

    def kv_keep(of_layer):
        return pltpu.make_async_copy(kv, kv_ref.at[of_layer], kv_sem)

    @pl.when(j < QKV_STEPS)
    def _():
        rows = pl.ds(pl.multiple_of(j * TILE, TILE), TILE)

        @pl.when(layer == 0)
        def _():
            hidden[rows, :] = arrived[rows, :].astype(F32) + embed_ref[...]

        @pl.when(j == 0)
        def _():
            weight_copies(0, layer).wait()

        @pl.when((j == 0) & (layer > 0))
        def _():
            pl.semaphore_wait(free_sem, 1)

        normed, scaled, inverse = norm(hidden[rows, :], first_gain_ref[0], first_bias_ref[0])
        normed_ref[0, 0] = normed
        scaled_ref[0, 0] = scaled.astype(BF16)
        inverse_ref[0, 0] = inverse
        keys = dot(normed, triple[:, width:]).astype(BF16)
        for b in range(TILE // BLOCK):
            kv[j * (TILE // BLOCK) + b, core] = keys[b * BLOCK : (b + 1) * BLOCK]
        kv_copy(j).start()
        query = (dot(normed, triple[:, :width]).astype(BF16).astype(F32) * SCALE).astype(BF16)
        queries[rows, :] = query
        query_ref[0] = query


    @pl.when((j >= QKV_STEPS) & (j < QKV_STEPS + PAIRS))
    def _():
        p = j - QKV_STEPS
        lanes = pl.ds(pl.multiple_of(p * LANES, LANES), LANES)
        value_lanes = pl.ds(pl.multiple_of(width + p * LANES, LANES), LANES)

        @pl.when(p == 0)
        def _():
            for i in range(QKV_STEPS):
                kv_copy(i).wait()
            kv_keep(layer).start()

        @pl.when((p == 0) & (layer < layers - 1))
        def _():
            weight_copies(0, layer + 1).start()

        values[:, :LANES] = kv[:, :, :, value_lanes].reshape(2 * tokens, LANES)
        values[:, LANES:] = jnp.ones((2 * tokens, LANES), BF16)
        lane = lax.broadcasted_iota(jnp.int32, (BLOCK, LANES), 1)
        query_at = lax.broadcasted_iota(jnp.int32, (BLOCK, pair), 0)
        column = lax.broadcasted_iota(jnp.int32, (BLOCK, pair), 1)
        key_pass = column // BLOCK
        key_at = column - key_pass * BLOCK
        causal = (key_at < query_at) | ((key_at == query_at) & (key_pass <= core))
        length = length_here[0:1, 0:1]

        def scores(block, head):
            query = queries[pl.ds(block * BLOCK, BLOCK), lanes]
            chosen = jnp.where(lane // HEAD_DIM == head, query, jnp.zeros_like(query))
            keys = kv[: block + 1, :, :, lanes].reshape((block + 1) * pair, LANES)
            return dot(chosen, keys, NT)

        def exponentials(block, head, raw):
            allowed = causal & (key_at + block * BLOCK < length)
            last = jnp.where(allowed, raw[:, block * pair :], -jnp.inf)
            top = jnp.max(last, -1, keepdims=True)
            if block:
                top = jnp.maximum(top, jnp.max(raw[:, : block * pair], -1, keepdims=True))
            parts = []
            for k in range(block + 1):
                source = last if k == block else raw[:, k * pair : (k + 1) * pair]
                part = jnp.exp(source - top).astype(BF16)
                exp_ref[0, head, tile_index(blocks, k, block)] = part
                parts.append(part)
            return jnp.concatenate(parts, 1) if block else parts[0]

        outs = {}

        def mix(block, head, exps):
            both = dot(exps, values[: (block + 1) * pair, :])
            inverse = jnp.where(block * BLOCK < length, 1.0 / both[:, LANES : LANES + 1], 0.0)
            rows = pl.ds(block * BLOCK, BLOCK)
            total_ref[0, 0, rows, head : head + 1] = inverse
            outs[head] = both[:, :LANES] * inverse
            if head == 1:
                value = jnp.where(lane < HEAD_DIM, outs[0], outs[1]).astype(BF16)
                mixes[rows, lanes] = value
                mixed_ref[0, rows, :] = value

        items = [(block, head) for block in range(blocks) for head in range(2)]
        ahead = scores(*items[0])
        behind = None
        for n, item in enumerate(items):
            raw = ahead
            if n + 1 < len(items):
                ahead = scores(*items[n + 1])
            exps = exponentials(*item, raw)
            if behind is not None:
                mix(*behind)
            behind = (*item, exps)
        mix(*behind)

        @pl.when(p == PAIRS - 1)
        def _():
            kv_keep(layer).wait()

        @pl.when((p == PAIRS - 1) & (layer < layers - 1))
        def _():
            pl.semaphore_signal(free_sem, inc=1, device_id=core_mate, device_id_type=MESH)


    @pl.when(j >= QKV_STEPS + PAIRS)
    def _():
        i = j - QKV_STEPS - PAIRS
        rows = pl.ds(pl.multiple_of(i * TILE, TILE), TILE)

        @pl.when(i == 0)
        def _():
            for which in range(1, 4):
                weight_copies(which, layer).wait()

        mid = hidden[rows, :] + dot(mixes[rows, :], merge[...])
        normed, scaled, inverse = norm(mid, second_gain_ref[0], second_bias_ref[0])
        normed_ref[0, 0] = normed
        scaled_ref[0, 0] = scaled.astype(BF16)
        inverse_ref[0, 0] = inverse
        parts = up.shape[1] // width
        sum_next = mid
        ahead = dot(normed, up[:, :width])
        for part in range(parts):
            at = slice(part * width, (part + 1) * width)
            now = ahead
            if part + 1 < parts:
                ahead = dot(normed, up[:, (part + 1) * width : (part + 2) * width])
            act, slope = gelu_both(now)
            act = act.astype(BF16)
            act_ref[0, :, at] = act
            slope_ref[0, :, at] = slope.astype(BF16)
            sum_next = sum_next + dot(act, down[at, :])
        hidden[rows, :] = sum_next

        @pl.when(layer == layers - 1)
        def _():
            position = lax.broadcasted_iota(jnp.int32, (TILE, 1), 0) + i * TILE
            valid = (position < length_here[0:1, 0:1]).astype(F32)
            out_ref[...] = (sum_next * valid).astype(BF16)

        @pl.when((i == FFN_TILES - 1) & (layer < layers - 1))
        def _():
            for which in range(1, 4):
                weight_copies(which, layer + 1).start()

    @pl.when(t == pl.num_programs(0) - 1)
    def _():
        move(QKV_STEPS, "wait")


def forward(stream, cotangent, length, embed, first_gain, first_bias, second_gain, second_bias, triple, merge, up, down):
    tokens, width = stream.shape
    layers, _, units = up.shape
    blocks = tokens // BLOCK
    tiles = blocks * (blocks + 1) // 2

    def phase(t):
        return t // FORWARD, t % FORWARD

    def row_tile(t):
        layer, j = phase(t)
        late = j >= QKV_STEPS + PAIRS
        kind = jnp.where(late, 0, 1)
        return layer, kind, jnp.where(late, j - QKV_STEPS - PAIRS, jnp.minimum(j, QKV_STEPS - 1)), 0

    def query_tile(t):
        layer, j = phase(t)
        return layer, jnp.minimum(j, QKV_STEPS - 1), 0

    def head(t):
        layer, j = phase(t)
        return layer, jnp.clip(j - QKV_STEPS, 0, PAIRS - 1)

    def ffn_tile(t):
        layer, j = phase(t)
        return layer, jnp.maximum(j - QKV_STEPS - PAIRS, 0), 0

    vector = pl.BlockSpec((1, 1, width), lambda t: (t // FORWARD, 0, 0))
    rows = pl.BlockSpec((1, 1, TILE, width), row_tile)
    dma = pltpu.SemaphoreType.DMA
    return pl.pallas_call(
        functools.partial(forward_kernel, layers),
        grid=(layers * FORWARD,),
        in_specs=[ANY, ANY, whole(length.shape), whole((1, width)), vector, vector, vector, vector, ANY, ANY, ANY, ANY],
        out_specs=[
            rows, rows, pl.BlockSpec((1, 1, TILE, 1), row_tile),
            pl.BlockSpec((1, TILE, width), query_tile),
            pl.BlockSpec((1, tokens, LANES), lambda t: (head(t)[0], 0, head(t)[1])),
            pl.BlockSpec((1, 1, tokens, 2), lambda t: (*head(t), 0, 0)),
            pl.BlockSpec((1, 2, tiles, BLOCK, 2 * BLOCK), lambda t: (*head(t), 0, 0, 0)),
            pl.BlockSpec((1, TILE, units), ffn_tile), pl.BlockSpec((1, TILE, units), ffn_tile),
            ANY,
            pl.BlockSpec((TILE, width), lambda t: (jnp.where(phase(t)[0] == layers - 1, ffn_tile(t)[1], 0), 0)),
            ANY, whole(length.shape),
        ],
        out_shape=[
            sds((layers, 2, tokens, width), BF16),
            sds((layers, 2, tokens, width), BF16),
            sds((layers, 2, tokens, 1), F32),
            sds((layers, tokens, width), BF16),
            sds((layers, tokens, width), BF16),
            sds((layers, PAIRS, tokens, 2), F32),
            sds((layers, 2 * PAIRS, tiles, BLOCK, 2 * BLOCK), BF16),
            sds((layers, tokens, units), BF16),
            sds((layers, tokens, units), BF16),
            sds((layers, blocks, 2, BLOCK, 2 * width), BF16),
            sds((tokens, width), BF16),
            sds((tokens, width), BF16),
            sds(length.shape, jnp.int32),
        ],
        scratch_shapes=[
            pltpu.VMEM((tokens, width), F32),
            pltpu.VMEM((tokens, width), BF16),
            pltpu.VMEM(length.shape, jnp.int32),
            pltpu.VMEM((tokens, width), BF16),
            pltpu.VMEM((blocks, 2, BLOCK, 2 * width), BF16),
            pltpu.VMEM((2 * tokens, 2 * LANES), BF16),
            pltpu.VMEM((tokens, width), BF16),
            pltpu.VMEM(triple.shape[1:], BF16),
            pltpu.VMEM(merge.shape[1:], BF16),
            pltpu.VMEM(up.shape[1:], BF16),
            pltpu.VMEM(down.shape[1:], BF16),
            dma((4,)), dma, dma((QKV_STEPS,)), dma((QKV_STEPS,)), pltpu.SemaphoreType.REGULAR,
            dma((QKV_STEPS + 2,)), dma((QKV_STEPS + 2,)), dma((QKV_STEPS + 2,)),
        ],
        compiler_params=params(0),
        name="forward",
    )(stream, cotangent, length, embed, first_gain, first_bias, second_gain, second_bias, triple, merge, up, down)


FFN_STEPS = 4
STEPS = FFN_STEPS + PAIRS + 3
NO_PIECE = 9
STAGES = 5
ROWS = 16
SHARE = 48
SMALL = 16


def back_kernel(
    layers, hosted,
    cot_ref, done_ref, length_ref, act_ref, slope_ref, normed_ref, scaled_ref, inverse_ref, mixed_ref, up_ref, down_ref, merge_ref,
    first_gain_ref, second_gain_ref, query_ref, key_ref, value_ref, total_ref, exp_ref, weight_ref,
    out_ref, small_ref, input_ref, output_ref,
    grad, low, total, grads, pending, landing, exps,
    staged, sums0, sums1, sums2, sums3, got0, got1, got2, got3, got4, final, small, small_got,
    exp_sem, cot_sem, kv_send, kv_recv, stage_send, stage_recv, out_sem, small_send, small_recv, swap_send, swap_recv,
    here_sem,
):
    t = pl.program_id(0)
    j = t % STEPS
    layer = layers - 1 - t // STEPS
    row, core, x, z0, z1, own_pass = bits()
    tokens, width = grad.shape
    blocks = tokens // BLOCK
    pair = 2 * BLOCK
    busy = t < layers * STEPS
    core_mate = {"rows": row + 1 - 2 * core}
    mates = [
        core_mate, {"rows": row + 2 - 4 * x}, {"rows": row + 4 - 8 * z0}, {"rows": row + 8 - 16 * z1},
        {"pass": 1 - own_pass},
    ]
    diagonal = {"pass": 1 - own_pass, "rows": row + 1 - 2 * core}
    swapped = own_pass != core

    @pl.when(t == 0)
    def _():
        barrier = pltpu.get_barrier_semaphore()
        greeted = mates if hosted else mates[:1]
        for mate in greeted:
            pl.semaphore_signal(barrier, inc=1, device_id=mate, device_id_type=MESH)

        @pl.when(swapped)
        def _():
            pl.semaphore_signal(barrier, inc=1, device_id=diagonal, device_id_type=MESH)

        pl.semaphore_wait(barrier, len(greeted) + jnp.where(swapped, 1, 0))
        load = pltpu.make_async_copy(cot_ref, low, cot_sem)
        load.start()
        load.wait()
        position = lax.broadcasted_iota(jnp.int32, (tokens, 1), 0)
        valid = (position < length_ref[0:1, 0:1]).astype(F32)
        masked = low[...].astype(F32) * valid
        grad[...] = masked
        low[...] = masked.astype(BF16)
        small[...] = jnp.zeros_like(small)


    def exp_copy(head):
        return pltpu.make_async_copy(exp_ref.at[layer, head], exps.at[head % 2], exp_sem.at[head % 2])

    def put(slot, r, value):
        staged[slot, r % 2, (r // 2) % 2, (r // 4) % 2, (r // 8) % 2] = value

    @pl.when(busy & (j < FFN_STEPS))
    def _():
        @pl.when(j == 0)
        def _():
            total[...] = jnp.zeros_like(total)

        grad_low = low[...]
        down_grad = dot(act_ref[0], grad_low, TN).astype(BF16)
        for q in range(4):
            for i in range(4):
                first = q * 4 * SHARE + i * SHARE
                staged[i, q % 2, q // 2, j % 2, (j // 2) % 2] = down_grad[first : first + SHARE]
        grad_act = dot(grad_low, down_ref[0], NT)
        grad_pre = (slope_ref[0].astype(F32) * grad_act).astype(BF16)
        up_grad = dot(normed_ref[0, 0], grad_pre, TN).astype(BF16)
        for r in range(ROWS):
            put(4 + j % 2, r, up_grad[r * SHARE : (r + 1) * SHARE])
        total[...] += dot(grad_pre, up_ref[0], NT)

        @pl.when(j == FFN_STEPS - 1)
        def _():
            exp_copy(0).start()

            def rows(i, sums):
                at = pl.ds(pl.multiple_of(i * TILE, TILE), TILE)
                part = total[at, :]
                scaled = scaled_ref[0, 0, at, :].astype(F32)
                mid = grad[at, :] + norm_back(part, scaled, inverse_ref[0, 0, at, :], second_gain_ref[0])
                grad[at, :] = mid
                low_mid = mid.astype(BF16)
                low[at, :] = low_mid
                grads[0, at, :] = dot(low_mid, merge_ref[0], NT).astype(BF16)
                return (
                    sums[0] + jnp.sum(part * scaled, 0, keepdims=True),
                    sums[1] + jnp.sum(part, 0, keepdims=True),
                )

            empty = jnp.zeros((1, width), F32)
            gain_sum, bias_sum = lax.fori_loop(0, tokens // TILE, rows, (empty, empty))
            small[pl.ds(4 + 4 * layer, 1), :] = gain_sum
            small[pl.ds(5 + 4 * layer, 1), :] = bias_sum
            merge_grad = dot(mixed_ref[0], low[...], TN).astype(BF16)
            for r in range(ROWS):
                put(6, r, merge_grad[r * SHARE : (r + 1) * SHARE])


    def kv_copy(p):
        return send(
            pending.at[p % 2], landing.at[p % 2], kv_send.at[p % 2], kv_recv.at[p % 2], core_mate,
        )

    def take(p):
        kv_copy(p).wait()
        lanes = pl.ds(pl.multiple_of(p * LANES, LANES), LANES)
        for which in range(2):
            grads[1 + which, :, lanes] = (
                grads[1 + which, :, lanes].astype(F32) + landing[p % 2, which].astype(F32)
            ).astype(BF16)

    @pl.when(busy & (j >= FFN_STEPS) & (j < FFN_STEPS + PAIRS))
    def _():
        p = j - FFN_STEPS
        lanes = pl.ds(pl.multiple_of(p * LANES, LANES), LANES)
        lane = lax.broadcasted_iota(jnp.int32, (tokens, LANES), 1)
        out_grad = grads[0, :, lanes].astype(F32)
        product = out_grad * mixed_ref[0, :, lanes].astype(F32)
        query = query_ref[0]
        scaled, scaled_across, inner, chosen_across = [], [], [], []
        for head in range(2):
            mine = lane // HEAD_DIM == head
            inverse = total_ref[0, 0, :, head : head + 1]
            part = jnp.where(mine, out_grad * inverse, 0.0)
            scaled.append(part.astype(BF16))
            scaled_across.append(part.T.astype(BF16))
            inner.append(jnp.sum(jnp.where(mine, product, 0.0), -1, keepdims=True) * inverse)
            chosen_across.append(jnp.where(mine, query, jnp.zeros_like(query)).astype(F32).T.astype(BF16))

        def probs_grad(head, block):
            return dot(scaled[head][block * BLOCK :], value_ref[0, block * pair : (block + 1) * pair, :], NT)

        def score_grad(head, block, grad_prob):
            start = tile_index(blocks, block, block)
            prob = exps[head, start : start + blocks - block].reshape(tokens - block * BLOCK, pair)
            return prob, (prob.astype(F32) * (grad_prob - inner[head][block * BLOCK :])).astype(BF16)

        sums = {}

        def products(head, block, prob, score):
            first = block * BLOCK
            pairs = dot(chosen_across[head][:, first:], score), dot(scaled_across[head][:, first:], prob)
            grad_query = dot(score, key_ref[0, block * pair : (block + 1) * pair, :])
            mine_lanes = slice(head * LANES, (head + 1) * LANES)
            if block == 0:
                total[:, mine_lanes] = grad_query
            else:
                total[first:, mine_lanes] += grad_query
            if head == 0:
                sums[block] = pairs
                return
            at = pl.ds(first, BLOCK)
            for which in range(2):
                both = (sums[block][which] + pairs[which]).T
                zero, one = both[:BLOCK], both[BLOCK:]
                grads[1 + which, at, lanes] = jnp.where(core == 0, zero, one).astype(BF16)
                pending[p % 2, which, at, :] = jnp.where(core == 0, one, zero).astype(BF16)

        exp_copy(2 * p + 1).start()
        exp_copy(2 * p).wait()
        exp_copy(2 * p + 1).wait()
        items = [(head, block) for head in range(2) for block in range(blocks)]
        ahead = probs_grad(*items[0])
        behind = None
        for n, item in enumerate(items):
            now = ahead
            if n + 1 < len(items):
                ahead = probs_grad(*items[n + 1])
            both = score_grad(*item, now)
            if behind is not None:
                products(*behind)
            behind = (*item, *both)
        products(*behind)

        @pl.when(p < PAIRS - 1)
        def _():
            exp_copy(2 * p + 2).start()

        grads[0, :, lanes] = (
            jnp.where(lane < HEAD_DIM, total[:, :LANES], total[:, LANES : 2 * LANES]) * SCALE
        ).astype(BF16)

        @pl.when(p > 0)
        def _():
            take(p - 1)

        kv_copy(p).start()


    @pl.when(busy & (j >= FFN_STEPS + PAIRS))
    def _():
        n = j - FFN_STEPS - PAIRS

        @pl.when(n == 0)
        def _():
            total[...] = jnp.zeros_like(total)

        @pl.when(n == 0)
        def _():
            take(PAIRS - 1)

        part = grads[n]
        triple_grad = dot(normed_ref[0, 0], part, TN).astype(BF16)
        for r in range(ROWS):
            put(4 + n, r, triple_grad[r * SHARE : (r + 1) * SHARE])
        total[...] += dot(part, weight_ref[0], NT)

        @pl.when(n == 2)
        def _():
            def rows(i, sums):
                at = pl.ds(pl.multiple_of(i * TILE, TILE), TILE)
                part = total[at, :]
                scaled = scaled_ref[0, 0, at, :].astype(F32)
                hidden = grad[at, :] + norm_back(part, scaled, inverse_ref[0, 0, at, :], first_gain_ref[0])
                grad[at, :] = hidden
                low[at, :] = hidden.astype(BF16)
                return (
                    sums[0] + jnp.sum(part * scaled, 0, keepdims=True),
                    sums[1] + jnp.sum(part, 0, keepdims=True),
                    sums[2] + jnp.sum(hidden, 0, keepdims=True),
                )

            empty = jnp.zeros((1, width), F32)
            gain_sum, bias_sum, hidden_sum = lax.fori_loop(0, tokens // TILE, rows, (empty, empty, empty))
            small[pl.ds(2 + 4 * layer, 1), :] = gain_sum
            small[pl.ds(3 + 4 * layer, 1), :] = bias_sum

            @pl.when(layer == 0)
            def _():
                small[pl.ds(core, 1), :] = hidden_sum


    last = layers * STEPS - 1

    def slot(v):
        i = v % STEPS
        return jnp.where(
            i < 4, 4 + i % 2, jnp.where(i < 8, i - 4, jnp.where(i == 8, 6, i - FFN_STEPS - PAIRS + 4))
        )

    def whether(v):
        return (v >= 0) & (v <= last) & (v % STEPS != NO_PIECE)

    def half(v):
        return (v - v // STEPS - jnp.where(v % STEPS > NO_PIECE, 1, 0)) % 2

    def out_copy(v):
        h = half(v)
        return pltpu.make_async_copy(final.at[h], out_ref.at[v], out_sem.at[h])

    def stage(s, v):
        h = half(v)
        src = (staged.at[slot(v), 1 - core], sums0.at[h, 1 - x], sums1.at[h, 1 - z0], sums2.at[h, 1 - z1], sums3.at[h])[s]
        dst = (got0, got1, got2, got3, got4)[s].at[h]
        return send(src, dst, stage_send.at[s, h], stage_recv.at[s, h], mates[s])

    def add(a, b):
        return (a.astype(F32) + b.astype(F32)).astype(BF16)

    if hosted:
        @pl.when(whether(t - 6))
        def _():
            out_copy(t - 6).wait()

        @pl.when(whether(t - 5))
        def _():
            v = t - 5
            h = half(v)
            stage(4, v).wait()
            final[h] = sums3[h].astype(F32) + got4[h].astype(F32)
            out_copy(v).start()

        @pl.when(whether(t - 4))
        def _():
            v = t - 4
            h = half(v)
            stage(3, v).wait()
            sums3[h] = add(sums2[h, z1], got3[h])
            stage(4, v).start()

        @pl.when(whether(t - 3))
        def _():
            v = t - 3
            h = half(v)
            stage(2, v).wait()
            sums2[h] = add(sums1[h, z0], got2[h])
            stage(3, v).start()

        @pl.when(whether(t - 2))
        def _():
            v = t - 2
            h = half(v)
            stage(1, v).wait()
            sums1[h] = add(sums0[h, x], got1[h])
            stage(2, v).start()

        @pl.when(whether(t - 1))
        def _():
            v = t - 1
            h = half(v)
            stage(0, v).wait()
            sums0[h] = add(staged[slot(v), core], got0[h])
            stage(1, v).start()

        @pl.when(whether(t))
        def _():
            stage(0, t).start()

        for s in range(STAGES + 1):
            def small_copy(s):
                return send(small, small_got.at[s], small_send.at[s], small_recv.at[s], mates[s])

            @pl.when(t == last + s)
            def _():
                if s:
                    small_copy(s - 1).wait()
                    small[...] += small_got[s - 1]
                if s < STAGES:
                    small_copy(s).start()
    else:
        def piece_copy(v):
            return pltpu.make_async_copy(staged.at[slot(v)], out_ref.at[v], out_sem.at[v % 2])

        @pl.when(whether(t - 1))
        def _():
            piece_copy(t - 1).wait()

        @pl.when(whether(t))
        def _():
            piece_copy(t).start()


    def swaps(i, act):
        source, target = ((done_ref, output_ref), (low, input_ref))[i]

        @pl.when(swapped)
        def _():
            getattr(send(source, target, swap_send.at[i], swap_recv.at[i], diagonal), act)()

        @pl.when(jnp.logical_not(swapped))
        def _():
            getattr(pltpu.make_async_copy(source, target, here_sem.at[i]), act)()

    @pl.when(t == 0)
    def _():
        swaps(0, "start")

    @pl.when(t == last)
    def _():
        swaps(1, "start")

    @pl.when(t == pl.num_programs(0) - 1)
    def _():
        swaps(0, "wait")
        swaps(1, "wait")
        small_ref[...] = small[...]


def back(cotangent, done, length, act, slope, normeds, scaleds, inverses, mixed, up, down, merge, first_gain, second_gain, query, kv,
         total, exps, weight, hosted):
    layers, tokens, width = query.shape
    tiles = exps.shape[2]
    steps = layers * STEPS + (STAGES + 2 if hosted else 1)
    piece = (2, 2, 2, 2, SHARE, width)

    def at(t):
        t = jnp.minimum(t, layers * STEPS - 1)
        return layers - 1 - t // STEPS, t % STEPS

    def tile_of(t):
        layer, j = at(t)
        return layer, jnp.minimum(j, FFN_STEPS - 1)

    def head_of(t):
        layer, j = at(t)
        return layer, jnp.clip(j - FFN_STEPS, 0, PAIRS - 1)

    def part_of(t):
        layer, j = at(t)
        return layer, jnp.clip(j - FFN_STEPS - PAIRS, 0, 2)

    def kind_of(t):
        layer, j = at(t)
        return layer, (j >= FFN_STEPS).astype(jnp.int32), 0, 0

    once = dict(pipeline_mode=pl.Buffered(1))

    def of_layer(shape):
        return pl.BlockSpec((1,) + shape, lambda t: (at(t)[0],) + (0,) * len(shape), **once)

    units = pl.BlockSpec((1, tokens, width), lambda t: (tile_of(t)[0], 0, tile_of(t)[1]))
    in_specs = [
        ANY, ANY, whole(length.shape), units, units,
        pl.BlockSpec((1, 1, tokens, width), kind_of, **once),
        pl.BlockSpec((1, 1, tokens, width), kind_of, **once),
        pl.BlockSpec((1, 1, tokens, 1), kind_of, **once),
        of_layer((tokens, width)),
        pl.BlockSpec((1, width, width), lambda t: (tile_of(t)[0], 0, tile_of(t)[1])),
        pl.BlockSpec((1, width, width), lambda t: (tile_of(t)[0], tile_of(t)[1], 0)),
        of_layer((width, width)),
        of_layer((1, width)), of_layer((1, width)),
        pl.BlockSpec((1, tokens, LANES), lambda t: (head_of(t)[0], 0, head_of(t)[1])),
        pl.BlockSpec((1, 2 * tokens, LANES), lambda t: (head_of(t)[0], 0, head_of(t)[1])),
        pl.BlockSpec((1, 2 * tokens, LANES), lambda t: (head_of(t)[0], 0, head_of(t)[1] + PAIRS)),
        pl.BlockSpec((1, 1, tokens, 2), lambda t: (head_of(t)[0], head_of(t)[1], 0, 0)),
        ANY,
        pl.BlockSpec((1, width, width), lambda t: (part_of(t)[0], 0, part_of(t)[1]), **once),
    ]
    out_piece = sds((layers * STEPS, SHARE, width), F32) if hosted else sds((layers * STEPS,) + piece, BF16)
    dma = pltpu.SemaphoreType.DMA

    def some(*shape):
        return pltpu.VMEM(shape, BF16)

    return pl.pallas_call(
        functools.partial(back_kernel, layers, hosted),
        grid=(steps,),
        in_specs=in_specs,
        out_specs=[ANY, whole((SMALL, width)), ANY, ANY],
        out_shape=[
            out_piece, sds((SMALL, width), F32), sds((tokens, width), BF16), sds((tokens, width), BF16),
        ],
        scratch_shapes=[
            pltpu.VMEM((tokens, width), F32),
            some(tokens, width),
            pltpu.VMEM((tokens, width), F32),
            some(3, tokens, width),
            some(2, 2, tokens, LANES),
            some(2, 2, tokens, LANES),
            some(2, tiles, BLOCK, 2 * BLOCK),
            some(7, *piece),
            some(2, *piece[1:]), some(2, *piece[2:]), some(2, *piece[3:]), some(2, *piece[4:]),
            some(2, *piece[1:]), some(2, *piece[2:]), some(2, *piece[3:]), some(2, *piece[4:]), some(2, *piece[4:]),
            pltpu.VMEM((2, SHARE, width), F32),
            pltpu.VMEM((SMALL, width), F32),
            pltpu.VMEM((STAGES, SMALL, width), F32),
            dma((2,)), dma, dma((2,)), dma((2,)), dma((STAGES, 2)), dma((STAGES, 2)), dma((2,)),
            dma((STAGES,)), dma((STAGES,)), dma((2,)), dma((2,)), dma((2,)),
        ],
        compiler_params=params(1),
        name="back",
    )(cotangent, done, length, act, slope, normeds, scaleds, inverses, mixed, up, down, merge, first_gain, second_gain, query, kv, kv,
      total, exps, weight)


def local(
    stream, lengths, pass_embed, first_gain, first_bias, triple_weight, merge_weight,
    second_gain, second_bias, up_weight, down_weight, cotangent,
):
    row_count = lax.axis_size("rows")
    own_row = lax.axis_index("rows")
    core = own_row % 2
    tokens, width = stream.shape[2], stream.shape[3]
    layers = triple_weight.shape[0]
    hosted = row_count == ROWS

    embed = jnp.where(core == 0, pass_embed[0:1], pass_embed[1:2]).astype(F32)
    first_gain, first_bias, second_gain, second_bias = (
        v.astype(F32)[:, None] for v in (first_gain, first_bias, second_gain, second_bias)
    )
    (normeds, scaleds, inverses, query, mixed, total, exps, act, slope, kv, done, cotangent, length) = forward(
        stream.reshape(tokens, width), cotangent.reshape(tokens, width),
        jnp.broadcast_to(lengths.reshape(1, 1), (8, LANES)), embed,
        first_gain, first_bias, second_gain, second_bias, triple_weight, merge_weight, up_weight, down_weight,
    )
    pieces, small, input_grad, output = back(
        cotangent, done, length, act, slope, normeds, scaleds, inverses, mixed, up_weight, down_weight, merge_weight,
        first_gain, second_gain, query, kv.reshape(layers, 2 * tokens, 2 * width), total, exps, triple_weight, hosted,
    )
    input_grad = input_grad.reshape(stream.shape)
    output = output.reshape(stream.shape)
    if hosted:
        pieces = pieces.reshape(layers, STEPS, SHARE, width)
    else:
        pieces = pieces.reshape(layers, STEPS, 2, 2, 2, 2, SHARE, width).transpose(0, 1, 5, 4, 3, 2, 6, 7)
    pieces = pieces[::-1]

    def columns(first, last):
        some = pieces[:, first:last]
        some = some.reshape(layers, last - first, -1, width)
        return some.transpose(0, 2, 1, 3).reshape(layers, -1, (last - first) * width)

    up_grad = columns(0, 4)
    merge_grad = columns(8, 9)
    triple_grad = columns(10, 13)
    down_grad = pieces[:, 4:8]
    if hosted:
        down_grad = down_grad.reshape(layers, 4 * SHARE, width)
    else:
        down_grad = down_grad.reshape(layers, 4, ROWS, SHARE, width).transpose(0, 2, 1, 3, 4).reshape(layers, -1, width)

        def reduce(gradient):
            share = lax.psum_scatter(gradient, "rows", scatter_dimension=1, tiled=True)
            return lax.psum(share, "pass").astype(F32)

        up_grad, merge_grad, triple_grad, down_grad = map(reduce, (up_grad, merge_grad, triple_grad, down_grad))
        small = lax.psum(small, ("pass", "rows"))
    share = width // row_count
    small = lax.dynamic_slice_in_dim(small, own_row * share, share, 1)
    by_layer = small[2 : 2 + 4 * layers].reshape(layers, 4, share)
    return (
        output, input_grad, small[:2], by_layer[:, 0], by_layer[:, 1], triple_grad, merge_grad,
        by_layer[:, 2], by_layer[:, 3], up_grad, down_grad,
    )


def solution(mesh):
    token = P("pass", "rows", None, None)
    matrix = P(None, "rows", None)
    rows = P(None, "rows")
    in_specs = (token, P("rows")) + (P(),) * 9 + (token,)
    out_specs = (token, token, rows, rows, rows, matrix, matrix, rows, rows, matrix, matrix)
    return jax.shard_map(local, mesh=mesh, in_specs=in_specs, out_specs=out_specs, check_vma=False)
```

```python
import functools
import math

import jax
import jax.numpy as jnp
from jax import lax
from jax.experimental import pallas as pl
from jax.experimental.pallas import tpu as pltpu
from jax.sharding import PartitionSpec as P

HEAD_DIM = 64
EPSILON = 1e-05
SCALE = HEAD_DIM**-0.5
MESH = pl.DeviceIdType.MESH
NN = (((1,), (0,)), ((), ()))
NT = (((1,), (1,)), ((), ()))
TN = (((0,), (0,)), ((), ()))
BLOCK = 128
TILE = 256
LANES = 128
BF16 = jnp.bfloat16
F32 = jnp.float32
VMEM_LIMIT = 63 * 2**20 + 3 * 2**18
ANY = pl.BlockSpec(memory_space=pl.ANY)


def dot(left, right, dims=NN):
    return lax.dot_general(left, right, dims, preferred_element_type=F32)


def sds(shape, dtype):
    return jax.ShapeDtypeStruct(shape, dtype)


def params(collective_id=None):
    return pltpu.CompilerParams(
        vmem_limit_bytes=VMEM_LIMIT,
        collective_id=collective_id,
        has_side_effects=collective_id is not None,
    )


def whole(shape):
    zeros = (0,) * len(shape)
    return pl.BlockSpec(shape, lambda *_: zeros, pipeline_mode=pl.Buffered(1))


def pick(ref, which):
    return jnp.where(which == 0, ref[0:1, :], ref[1:2, :]).astype(F32)


def norm(hidden, gain, bias):
    centred = hidden - jnp.mean(hidden, -1, keepdims=True)
    inverse = lax.rsqrt(jnp.mean(centred * centred, -1, keepdims=True) + EPSILON)
    scaled = centred * inverse
    return (scaled * gain + bias).astype(BF16), scaled, inverse


def norm_back(grad, scaled, inverse, gain):
    e = grad * gain
    return inverse * (
        e - jnp.mean(e, -1, keepdims=True) - scaled * jnp.mean(e * scaled, -1, keepdims=True)
    )


def bits():
    row = lax.axis_index("rows")
    return row, row % 2, (row // 2) % 2, (row // 4) % 2, (row // 8) % 2, lax.axis_index("pass")


def send(src, dst, send_sem, recv_sem, device):
    return pltpu.make_async_remote_copy(
        src_ref=src, dst_ref=dst, send_sem=send_sem, recv_sem=recv_sem,
        device_id=device, device_id_type=MESH,
    )


QKV_STEPS = 4
PAIRS = 6
FFN_TILES = 4
FORWARD = QKV_STEPS + PAIRS + FFN_TILES


def tile_index(blocks, key_block, query_block):
    return key_block * blocks - key_block * (key_block - 1) // 2 + query_block - key_block


def gelu_both(v):
    root = math.sqrt(2.0 / math.pi)
    cube = (root * 0.044715) * (v * v)
    half = 0.5 + 0.5 * jnp.tanh(v * (root + cube))
    act = v * half
    return act, half + (act - act * half) * (2.0 * root + 6.0 * cube)


def forward_kernel(
    layers,
    stream_ref, cot_ref, length_ref, embed_ref, first_gain_ref, first_bias_ref, second_gain_ref, second_bias_ref,
    triple_ref, merge_ref, up_ref, down_ref,
    normed_ref, scaled_ref, inverse_ref, query_ref, mixed_ref, total_ref, exp_ref, act_ref, slope_ref, kv_ref,
    out_ref, cot_out_ref, length_out_ref,
    hidden, arrived, length_mine, length_here, queries, kv, values, mixes, triple, merge, up, down,
    weight_sem, kv_sem, kv_send, kv_recv, free_sem, swap_send, swap_recv, here_sem,
):
    t = pl.program_id(0)
    layer = t // FORWARD
    j = t % FORWARD
    row, core, _, _, _, own_pass = bits()
    tokens, width = hidden.shape
    blocks = tokens // BLOCK
    pair = 2 * BLOCK
    core_mate = {"rows": row + 1 - 2 * core}
    diagonal = {"pass": 1 - own_pass, "rows": row + 1 - 2 * core}
    swapped = own_pass != core


    def moves(i):
        if i < QKV_STEPS:
            rows = pl.ds(i * TILE, TILE)
            ends = stream_ref.at[rows, :], arrived.at[rows, :]
        else:
            ends = ((cot_ref, cot_out_ref), (length_mine, length_here))[i - QKV_STEPS]
        return (
            send(*ends, swap_send.at[i], swap_recv.at[i], diagonal),
            pltpu.make_async_copy(*ends, here_sem.at[i]),
        )

    def move(i, act):
        there, here = moves(i)

        @pl.when(swapped)
        def _():
            getattr(there, act)()

        @pl.when(jnp.logical_not(swapped))
        def _():
            getattr(here, act)()


    def weight_copies(which, of_layer):
        refs = ((triple_ref, triple), (merge_ref, merge), (up_ref, up), (down_ref, down))
        source, target = refs[which]
        return pltpu.make_async_copy(source.at[of_layer], target, weight_sem.at[which])

    @pl.when(t == 0)
    def _():
        barrier = pltpu.get_barrier_semaphore()
        pl.semaphore_signal(barrier, inc=1, device_id=core_mate, device_id_type=MESH)

        @pl.when(swapped)
        def _():
            pl.semaphore_signal(barrier, inc=1, device_id=diagonal, device_id_type=MESH)

        pl.semaphore_wait(barrier, 1 + jnp.where(swapped, 1, 0))
        length_mine[...] = jnp.full(length_mine.shape, length_ref[0], jnp.int32)
        move(QKV_STEPS + 1, "start")
        for i in range(QKV_STEPS):
            move(i, "start")
        for which in range(4):
            weight_copies(which, 0).start()
        move(QKV_STEPS + 1, "wait")
        length_out_ref[...] = length_here[...]

    for i in range(QKV_STEPS):
        @pl.when(t == i)
        def _():
            move(i, "wait")
            if i == QKV_STEPS - 1:
                move(QKV_STEPS, "start")


    def kv_copy(i):
        part = kv.at[pl.ds(i * (TILE // BLOCK), TILE // BLOCK), core]
        return send(part, part, kv_send.at[i], kv_recv.at[i], core_mate)

    def kv_keep(of_layer):
        return pltpu.make_async_copy(kv, kv_ref.at[of_layer], kv_sem)

    @pl.when(j < QKV_STEPS)
    def _():
        rows = pl.ds(pl.multiple_of(j * TILE, TILE), TILE)

        @pl.when(layer == 0)
        def _():
            hidden[rows, :] = arrived[rows, :].astype(F32) + pick(embed_ref, core)

        @pl.when(j == 0)
        def _():
            weight_copies(0, layer).wait()

        @pl.when((j == 0) & (layer > 0))
        def _():
            pl.semaphore_wait(free_sem, 1)

        normed, scaled, inverse = norm(
            hidden[rows, :], pick(first_gain_ref, layer), pick(first_bias_ref, layer)
        )
        normed_ref[0, 0] = normed
        scaled_ref[0, 0] = scaled.astype(BF16)
        inverse_ref[0, 0] = inverse
        keys = dot(normed, triple[:, width:]).astype(BF16)
        for b in range(TILE // BLOCK):
            kv[j * (TILE // BLOCK) + b, core] = keys[b * BLOCK : (b + 1) * BLOCK]
        kv_copy(j).start()
        query = (dot(normed, triple[:, :width]).astype(BF16).astype(F32) * SCALE).astype(BF16)
        queries[rows, :] = query
        query_ref[0] = query


    @pl.when((j >= QKV_STEPS) & (j < QKV_STEPS + PAIRS))
    def _():
        p = j - QKV_STEPS
        lanes = pl.ds(pl.multiple_of(p * LANES, LANES), LANES)
        value_lanes = pl.ds(pl.multiple_of(width + p * LANES, LANES), LANES)

        @pl.when(p == 0)
        def _():
            for i in range(QKV_STEPS):
                kv_copy(i).wait()
            kv_keep(layer).start()

        @pl.when((p == 0) & (layer < layers - 1))
        def _():
            weight_copies(0, layer + 1).start()

        values[:, :LANES] = kv[:, :, :, value_lanes].reshape(2 * tokens, LANES)
        values[:, LANES:] = jnp.ones((2 * tokens, LANES), BF16)
        lane = lax.broadcasted_iota(jnp.int32, (BLOCK, LANES), 1)
        query_at = lax.broadcasted_iota(jnp.int32, (BLOCK, pair), 0)
        column = lax.broadcasted_iota(jnp.int32, (BLOCK, pair), 1)
        key_pass = column // BLOCK
        key_at = column - key_pass * BLOCK
        causal = (key_at < query_at) | ((key_at == query_at) & (key_pass <= core))
        length = length_here[0:1, 0:1]

        def scores(block, head):
            query = queries[pl.ds(block * BLOCK, BLOCK), lanes]
            chosen = jnp.where(lane // HEAD_DIM == head, query, jnp.zeros_like(query))
            keys = kv[: block + 1, :, :, lanes].reshape((block + 1) * pair, LANES)
            return dot(chosen, keys, NT)

        def exponentials(block, head, raw):
            allowed = causal & (key_at + block * BLOCK < length)
            last = jnp.where(allowed, raw[:, block * pair :], -jnp.inf)
            top = jnp.max(last, -1, keepdims=True)
            if block:
                top = jnp.maximum(top, jnp.max(raw[:, : block * pair], -1, keepdims=True))
            parts = []
            for k in range(block + 1):
                source = last if k == block else raw[:, k * pair : (k + 1) * pair]
                part = jnp.exp(source - top).astype(BF16)
                exp_ref[0, head, tile_index(blocks, k, block)] = part
                parts.append(part)
            return jnp.concatenate(parts, 1) if block else parts[0]

        outs = {}

        def mix(block, head, exps):
            both = dot(exps, values[: (block + 1) * pair, :])
            inverse = jnp.where(block * BLOCK < length, 1.0 / both[:, LANES : LANES + 1], 0.0)
            rows = pl.ds(block * BLOCK, BLOCK)
            total_ref[0, 0, rows, head : head + 1] = inverse
            outs[head] = both[:, :LANES] * inverse
            if head == 1:
                value = jnp.where(lane < HEAD_DIM, outs[0], outs[1]).astype(BF16)
                mixes[rows, lanes] = value
                mixed_ref[0, rows, :] = value

        items = [(block, head) for block in range(blocks) for head in range(2)]
        ahead = scores(*items[0])
        behind = None
        for n, item in enumerate(items):
            raw = ahead
            if n + 1 < len(items):
                ahead = scores(*items[n + 1])
            exps = exponentials(*item, raw)
            if behind is not None:
                mix(*behind)
            behind = (*item, exps)
        mix(*behind)

        @pl.when(p == PAIRS - 1)
        def _():
            kv_keep(layer).wait()

        @pl.when((p == PAIRS - 1) & (layer < layers - 1))
        def _():
            pl.semaphore_signal(free_sem, inc=1, device_id=core_mate, device_id_type=MESH)


    @pl.when(j >= QKV_STEPS + PAIRS)
    def _():
        i = j - QKV_STEPS - PAIRS
        rows = pl.ds(pl.multiple_of(i * TILE, TILE), TILE)

        @pl.when(i == 0)
        def _():
            for which in range(1, 4):
                weight_copies(which, layer).wait()

        mid = hidden[rows, :] + dot(mixes[rows, :], merge[...])
        normed, scaled, inverse = norm(mid, pick(second_gain_ref, layer), pick(second_bias_ref, layer))
        normed_ref[0, 0] = normed
        scaled_ref[0, 0] = scaled.astype(BF16)
        inverse_ref[0, 0] = inverse
        parts = up.shape[1] // width
        sum_next = mid
        ahead = dot(normed, up[:, :width])
        for part in range(parts):
            at = slice(part * width, (part + 1) * width)
            now = ahead
            if part + 1 < parts:
                ahead = dot(normed, up[:, (part + 1) * width : (part + 2) * width])
            act, slope = gelu_both(now)
            act = act.astype(BF16)
            act_ref[0, :, at] = act
            slope_ref[0, :, at] = slope.astype(BF16)
            sum_next = sum_next + dot(act, down[at, :])
        hidden[rows, :] = sum_next

        @pl.when(layer == layers - 1)
        def _():
            position = lax.broadcasted_iota(jnp.int32, (TILE, 1), 0) + i * TILE
            valid = (position < length_here[0:1, 0:1]).astype(F32)
            out_ref[...] = (sum_next * valid).astype(BF16)

        @pl.when((i == FFN_TILES - 1) & (layer < layers - 1))
        def _():
            for which in range(1, 4):
                weight_copies(which, layer + 1).start()

    @pl.when(t == pl.num_programs(0) - 1)
    def _():
        move(QKV_STEPS, "wait")


def forward(stream, cotangent, length, embed, first_gain, first_bias, second_gain, second_bias, triple, merge, up, down):
    tokens, width = stream.shape
    layers, _, units = up.shape
    blocks = tokens // BLOCK
    tiles = blocks * (blocks + 1) // 2

    def phase(t):
        return t // FORWARD, t % FORWARD

    def row_tile(t):
        layer, j = phase(t)
        late = j >= QKV_STEPS + PAIRS
        kind = jnp.where(late, 0, 1)
        return layer, kind, jnp.where(late, j - QKV_STEPS - PAIRS, jnp.minimum(j, QKV_STEPS - 1)), 0

    def query_tile(t):
        layer, j = phase(t)
        return layer, jnp.minimum(j, QKV_STEPS - 1), 0

    def head(t):
        layer, j = phase(t)
        return layer, jnp.clip(j - QKV_STEPS, 0, PAIRS - 1)

    def ffn_tile(t):
        layer, j = phase(t)
        return layer, jnp.maximum(j - QKV_STEPS - PAIRS, 0), 0

    vector = whole((layers, width))
    rows = pl.BlockSpec((1, 1, TILE, width), row_tile)
    dma = pltpu.SemaphoreType.DMA
    return pl.pallas_call(
        functools.partial(forward_kernel, layers),
        grid=(layers * FORWARD,),
        in_specs=[ANY, ANY, pl.BlockSpec(memory_space=pltpu.SMEM), whole(embed.shape), vector, vector, vector, vector, ANY, ANY, ANY, ANY],
        out_specs=[
            rows, rows, pl.BlockSpec((1, 1, TILE, 1), row_tile),
            pl.BlockSpec((1, TILE, width), query_tile),
            pl.BlockSpec((1, tokens, LANES), lambda t: (head(t)[0], 0, head(t)[1])),
            pl.BlockSpec((1, 1, tokens, 2), lambda t: (*head(t), 0, 0)),
            pl.BlockSpec((1, 2, tiles, BLOCK, 2 * BLOCK), lambda t: (*head(t), 0, 0, 0)),
            pl.BlockSpec((1, TILE, units), ffn_tile), pl.BlockSpec((1, TILE, units), ffn_tile),
            ANY,
            pl.BlockSpec((TILE, width), lambda t: (jnp.where(phase(t)[0] == layers - 1, ffn_tile(t)[1], 0), 0)),
            ANY, whole((8, LANES)),
        ],
        out_shape=[
            sds((layers, 2, tokens, width), BF16),
            sds((layers, 2, tokens, width), BF16),
            sds((layers, 2, tokens, 1), F32),
            sds((layers, tokens, width), BF16),
            sds((layers, tokens, width), BF16),
            sds((layers, PAIRS, tokens, 2), F32),
            sds((layers, 2 * PAIRS, tiles, BLOCK, 2 * BLOCK), BF16),
            sds((layers, tokens, units), BF16),
            sds((layers, tokens, units), BF16),
            sds((layers, blocks, 2, BLOCK, 2 * width), BF16),
            sds((tokens, width), BF16),
            sds((tokens, width), BF16),
            sds((8, LANES), jnp.int32),
        ],
        scratch_shapes=[
            pltpu.VMEM((tokens, width), F32),
            pltpu.VMEM((tokens, width), BF16),
            pltpu.VMEM((8, LANES), jnp.int32),
            pltpu.VMEM((8, LANES), jnp.int32),
            pltpu.VMEM((tokens, width), BF16),
            pltpu.VMEM((blocks, 2, BLOCK, 2 * width), BF16),
            pltpu.VMEM((2 * tokens, 2 * LANES), BF16),
            pltpu.VMEM((tokens, width), BF16),
            pltpu.VMEM(triple.shape[1:], BF16),
            pltpu.VMEM(merge.shape[1:], BF16),
            pltpu.VMEM(up.shape[1:], BF16),
            pltpu.VMEM(down.shape[1:], BF16),
            dma((4,)), dma, dma((QKV_STEPS,)), dma((QKV_STEPS,)), pltpu.SemaphoreType.REGULAR,
            dma((QKV_STEPS + 2,)), dma((QKV_STEPS + 2,)), dma((QKV_STEPS + 2,)),
        ],
        compiler_params=params(0),
        name="forward",
    )(stream, cotangent, length, embed, first_gain, first_bias, second_gain, second_bias, triple, merge, up, down)


FFN_STEPS = 4
STEPS = FFN_STEPS + PAIRS + 4
PIECES = STEPS - 2
STAGES = 5
ROWS = 16
SHARE = 48
SMALL = 16


def back_kernel(
    layers, hosted,
    cot_ref, done_ref, length_ref, act_ref, slope_ref, normed_ref, scaled_ref, inverse_ref, mixed_ref, up_ref, down_ref, merge_ref,
    first_gain_ref, second_gain_ref, query_ref, key_ref, value_ref, total_ref, exp_ref, weight_ref,
    *refs,
):
    outs = refs[: 4 if hosted else 1]
    (
        small_ref, input_ref, output_ref,
        grad, total, grads, pending, landing, exps,
        staged, left0, left1, left2, left3, right0, right1, right2, right3, got0,
        got_left1, got_left2, got_left3, got_left4, got_right1, got_right2, got_right3, got_late,
        final, small, small_got,
        exp_sem, cot_sem, kv_send, kv_recv, core_send, core_recv, left_send, left_recv, right_send, right_recv,
        late_send, late_recv, out_sem, small_send, small_recv, swap_send, swap_recv, here_sem,
    ) = refs[len(outs) :]
    low = grads.at[1]
    t = pl.program_id(0)
    j = t % STEPS
    layer = layers - 1 - t // STEPS
    row, core, x, z0, z1, own_pass = bits()
    tokens, width = grad.shape
    blocks = tokens // BLOCK
    pair = 2 * BLOCK
    busy = t < layers * STEPS
    core_mate = {"rows": row + 1 - 2 * core}
    mates = [
        core_mate, {"rows": row + 2 - 4 * x}, {"rows": row + 4 - 8 * z0}, {"rows": row + 8 - 16 * z1},
        {"pass": 1 - own_pass},
    ]
    diagonal = {"pass": 1 - own_pass, "rows": row + 1 - 2 * core}
    swapped = own_pass != core

    @pl.when(t == 0)
    def _():
        barrier = pltpu.get_barrier_semaphore()
        greeted = mates if hosted else mates[:1]
        for mate in greeted:
            pl.semaphore_signal(barrier, inc=1, device_id=mate, device_id_type=MESH)

        @pl.when(swapped)
        def _():
            pl.semaphore_signal(barrier, inc=1, device_id=diagonal, device_id_type=MESH)

        pl.semaphore_wait(barrier, len(greeted) + jnp.where(swapped, 1, 0))
        load = pltpu.make_async_copy(cot_ref, low, cot_sem)
        load.start()
        load.wait()
        position = lax.broadcasted_iota(jnp.int32, (tokens, 1), 0)
        valid = (position < length_ref[0:1, 0:1]).astype(F32)
        masked = low[...].astype(F32) * valid
        grad[...] = masked
        low[...] = masked.astype(BF16)
        small[...] = jnp.zeros_like(small)


    def exp_copy(head):
        at = (head // 2) % 2, head % 2
        return pltpu.make_async_copy(exp_ref.at[layer, head], exps.at[at], exp_sem.at[at])

    def put(slot, r, value):
        staged[slot, r % 2, (r // 2) % 2, (r // 4) % 2, (r // 8) % 2] = value

    @pl.when(busy & (j < FFN_STEPS))
    def _():
        @pl.when(j == 0)
        def _():
            total[...] = jnp.zeros_like(total)

        grad_low = low[...]
        down_grad = dot(act_ref[0], grad_low, TN).astype(BF16)
        for q in range(4):
            for i in range(4):
                first = q * 4 * SHARE + i * SHARE
                staged[i, q % 2, q // 2, j % 2, (j // 2) % 2] = down_grad[first : first + SHARE]
        grad_act = dot(grad_low, down_ref[0], NT)
        grad_pre = (slope_ref[0].astype(F32) * grad_act).astype(BF16)
        up_grad = dot(normed_ref[0, 0], grad_pre, TN).astype(BF16)
        for r in range(ROWS):
            put(4 + j % 2, r, up_grad[r * SHARE : (r + 1) * SHARE])
        total[...] += dot(grad_pre, up_ref[0], NT)

        @pl.when(j == FFN_STEPS - 1)
        def _():
            exp_copy(0).start()
            exp_copy(1).start()

            def rows(i, sums):
                at = pl.ds(pl.multiple_of(i * TILE, TILE), TILE)
                part = total[at, :]
                scaled = scaled_ref[0, 0, at, :].astype(F32)
                mid = grad[at, :] + norm_back(part, scaled, inverse_ref[0, 0, at, :], pick(second_gain_ref, layer))
                grad[at, :] = mid
                low_mid = mid.astype(BF16)
                low[at, :] = low_mid
                grads[0, at, :] = dot(low_mid, merge_ref[0], NT).astype(BF16)
                return (
                    sums[0] + jnp.sum(part * scaled, 0, keepdims=True),
                    sums[1] + jnp.sum(part, 0, keepdims=True),
                )

            empty = jnp.zeros((1, width), F32)
            gain_sum, bias_sum = lax.fori_loop(0, tokens // TILE, rows, (empty, empty))
            small[pl.ds(4 + 4 * layer, 1), :] = gain_sum
            small[pl.ds(5 + 4 * layer, 1), :] = bias_sum
            merge_grad = dot(mixed_ref[0], low[...], TN).astype(BF16)
            for r in range(ROWS):
                put(6, r, merge_grad[r * SHARE : (r + 1) * SHARE])


    def kv_copy(p):
        return send(
            pending.at[p % 2], landing.at[p % 2], kv_send.at[p % 2], kv_recv.at[p % 2], core_mate,
        )

    def take(p):
        kv_copy(p).wait()
        lanes = pl.ds(pl.multiple_of(p * LANES, LANES), LANES)
        for which in range(2):
            grads[1 + which, :, lanes] = (
                grads[1 + which, :, lanes].astype(F32) + landing[p % 2, which].astype(F32)
            ).astype(BF16)

    @pl.when(busy & (j >= FFN_STEPS) & (j < FFN_STEPS + PAIRS))
    def _():
        p = j - FFN_STEPS
        lanes = pl.ds(pl.multiple_of(p * LANES, LANES), LANES)
        lane = lax.broadcasted_iota(jnp.int32, (tokens, LANES), 1)
        out_grad = grads[0, :, lanes].astype(F32)
        product = out_grad * mixed_ref[0, :, lanes].astype(F32)
        query = query_ref[0]
        scaled, scaled_across, inner, chosen_across = [], [], [], []
        for head in range(2):
            mine = lane // HEAD_DIM == head
            inverse = total_ref[0, 0, :, head : head + 1]
            part = jnp.where(mine, out_grad * inverse, 0.0)
            scaled.append(part.astype(BF16))
            scaled_across.append(part.T.astype(BF16))
            inner.append(jnp.sum(jnp.where(mine, product, 0.0), -1, keepdims=True) * inverse)
            chosen_across.append(jnp.where(mine, query, jnp.zeros_like(query)).astype(F32).T.astype(BF16))

        def probs_grad(head, block):
            return dot(scaled[head][block * BLOCK :], value_ref[0, block * pair : (block + 1) * pair, :], NT)

        def score_grad(head, block, grad_prob):
            start = tile_index(blocks, block, block)
            prob = exps[p % 2, head, start : start + blocks - block].reshape(tokens - block * BLOCK, pair)
            return prob, (prob.astype(F32) * (grad_prob - inner[head][block * BLOCK :])).astype(BF16)

        sums = {}

        def products(head, block, prob, score):
            first = block * BLOCK
            pairs = dot(chosen_across[head][:, first:], score), dot(scaled_across[head][:, first:], prob)
            grad_query = dot(score, key_ref[0, block * pair : (block + 1) * pair, :])
            mine_lanes = slice(head * LANES, (head + 1) * LANES)
            if block == 0:
                total[:, mine_lanes] = grad_query
            else:
                total[first:, mine_lanes] += grad_query
            if head == 0:
                sums[block] = pairs
                return
            at = pl.ds(first, BLOCK)
            for which in range(2):
                both = (sums[block][which] + pairs[which]).T
                zero, one = both[:BLOCK], both[BLOCK:]
                grads[1 + which, at, lanes] = jnp.where(core == 0, zero, one).astype(BF16)
                pending[p % 2, which, at, :] = jnp.where(core == 0, one, zero).astype(BF16)

        exp_copy(2 * p).wait()
        exp_copy(2 * p + 1).wait()

        @pl.when(p < PAIRS - 1)
        def _():
            exp_copy(2 * p + 2).start()
            exp_copy(2 * p + 3).start()

        items = [(head, block) for block in range(blocks) for head in range(2)]
        ahead = probs_grad(*items[0])
        behind = None
        for n, item in enumerate(items):
            now = ahead
            if n + 1 < len(items):
                ahead = probs_grad(*items[n + 1])
            both = score_grad(*item, now)
            if behind is not None:
                products(*behind)
            behind = (*item, *both)
        products(*behind)

        grads[0, :, lanes] = (
            jnp.where(lane < HEAD_DIM, total[:, :LANES], total[:, LANES : 2 * LANES]) * SCALE
        ).astype(BF16)

        @pl.when(p > 0)
        def _():
            take(p - 1)

        kv_copy(p).start()


    @pl.when(busy & (j == FFN_STEPS + PAIRS))
    def _():
        total[...] = jnp.zeros_like(total)
        take(PAIRS - 1)

    @pl.when(busy & (j >= FFN_STEPS + PAIRS))
    def _():
        n = j - FFN_STEPS - PAIRS

        @pl.when(n < 3)
        def _():
            triple_grad = dot(normed_ref[0, 0], grads[n], TN).astype(BF16)
            for r in range(ROWS):
                put(4 + n, r, triple_grad[r * SHARE : (r + 1) * SHARE])

        @pl.when(n > 0)
        def _():
            total[...] += dot(grads[n - 1], weight_ref[0], NT)

        @pl.when(n == 3)
        def _():
            def rows(i, sums):
                at = pl.ds(pl.multiple_of(i * TILE, TILE), TILE)
                part = total[at, :]
                scaled = scaled_ref[0, 0, at, :].astype(F32)
                hidden = grad[at, :] + norm_back(part, scaled, inverse_ref[0, 0, at, :], pick(first_gain_ref, layer))
                grad[at, :] = hidden
                low[at, :] = hidden.astype(BF16)
                return (
                    sums[0] + jnp.sum(part * scaled, 0, keepdims=True),
                    sums[1] + jnp.sum(part, 0, keepdims=True),
                    sums[2] + jnp.sum(hidden, 0, keepdims=True),
                )

            empty = jnp.zeros((1, width), F32)
            gain_sum, bias_sum, hidden_sum = lax.fori_loop(0, tokens // TILE, rows, (empty, empty, empty))
            small[pl.ds(2 + 4 * layer, 1), :] = gain_sum
            small[pl.ds(3 + 4 * layer, 1), :] = bias_sum

            @pl.when(layer == 0)
            def _():
                small[pl.ds(core, 1), :] = hidden_sum


    last = layers * STEPS - 1
    half_width = width // 2

    def slot(v):
        i = v % STEPS
        return jnp.where(
            i < 4, 4 + i % 2, jnp.where(i < 8, i - 4, jnp.where(i == 8, 6, i - FFN_STEPS - PAIRS + 4))
        )

    def whether(v):
        return (v >= 0) & (v <= last) & (v % STEPS != FFN_STEPS + PAIRS - 1) & (v % STEPS != STEPS - 1)

    def order(v):
        i = v % STEPS
        return v // STEPS * PIECES + i - jnp.where(i >= FFN_STEPS + PAIRS, 1, 0)

    def add(a, b):
        return (a.astype(F32) + b.astype(F32)).astype(BF16)

    def core_stage(v):
        h = order(v) % 2
        return send(staged.at[slot(v), 1 - core], got0.at[h], core_send.at[h], core_recv.at[h], mates[0])

    def left_stage(s, v):
        h = order(v) % 2
        src = (left0.at[h, 1 - x], left1.at[h, 1 - z0], left2.at[h, 1 - z1], left3.at[h])[s - 1]
        dst = (got_left1, got_left2, got_left3, got_left4)[s - 1].at[h]
        return send(src, dst, left_send.at[s - 1, h], left_recv.at[s - 1, h], mates[s])

    def right_stage(s, v):
        h = order(v) % 2
        src = (right0.at[h, 1 - own_pass], right1.at[h, 1 - z0], right2.at[h, 1 - z1])[s - 1]
        dst = (got_right1, got_right2, got_right3)[s - 1].at[h]
        return send(src, dst, right_send.at[s - 1, h], right_recv.at[s - 1, h], (mates[4], mates[2], mates[3])[s - 1])

    def late_stage(s, v):
        k = order(v)
        return send(right3.at[k % 2], got_late.at[k], late_send.at[s - 4, k], late_recv.at[s - 4, k], (mates[1], mates[4])[s - 4])

    keeps = x == own_pass

    def late_start(s, v):
        @pl.when(keeps == (s == 5))
        def _():
            late_stage(s, v).start()

    def late_wait(s, v, receive):
        @pl.when(keeps == (s == 5))
        def _():
            late_stage(s, v).wait_send()

        @pl.when(keeps != (s == 5))
        def _():
            late_stage(s, v).wait_recv()
            receive()

    def out_copies(v, act):
        h = order(v) % 2
        i = v % STEPS
        at_layer = layers - 1 - v // STEPS
        triple_out, merge_out, up_out, down_out = outs

        def columns(n):
            return pl.ds(pl.multiple_of(n * width, width), width)

        def go(target):
            getattr(pltpu.make_async_copy(final.at[h], target, out_sem.at[h]), act)()

        @pl.when(i < 4)
        def _():
            go(up_out.at[at_layer, :, columns(i)])

        @pl.when((i >= 4) & (i < 8))
        def _():
            go(down_out.at[at_layer, pl.ds(pl.multiple_of((i - 4) * SHARE, SHARE), SHARE), :])

        @pl.when(i == 8)
        def _():
            go(merge_out.at[at_layer])

        @pl.when(i >= FFN_STEPS + PAIRS)
        def _():
            go(triple_out.at[at_layer, :, columns(i - FFN_STEPS - PAIRS)])

    if hosted:
        @pl.when(whether(t - 7))
        def _():
            out_copies(t - 7, "wait")

        @pl.when(whether(t - 6))
        def _():
            v = t - 6
            h = order(v) % 2

            def receive():
                right3[h] = got_late[order(v)]

            late_wait(5, v, receive)
            final[h, :, half_width:] = right3[h].astype(F32)
            out_copies(v, "start")

        @pl.when(whether(t - 5))
        def _():
            v = t - 5
            h = order(v) % 2

            def receive():
                right3[h] = add(right3[h], got_late[order(v)])

            late_wait(4, v, receive)
            late_start(5, v)
            left_stage(4, v).wait()
            final[h, :, :half_width] = left3[h].astype(F32) + got_left4[h].astype(F32)

        @pl.when(whether(t - 4))
        def _():
            v = t - 4
            h = order(v) % 2
            right_stage(3, v).wait()
            right3[h] = add(right2[h, z1], got_right3[h])
            late_start(4, v)
            left_stage(3, v).wait()
            left3[h] = add(left2[h, z1], got_left3[h])
            left_stage(4, v).start()

        @pl.when(whether(t - 3))
        def _():
            v = t - 3
            h = order(v) % 2
            right_stage(2, v).wait()
            right2[h] = add(right1[h, z0], got_right2[h])
            right_stage(3, v).start()
            left_stage(2, v).wait()
            left2[h] = add(left1[h, z0], got_left2[h])
            left_stage(3, v).start()

        @pl.when(whether(t - 2))
        def _():
            v = t - 2
            h = order(v) % 2
            right_stage(1, v).wait()
            right1[h] = add(right0[h, own_pass], got_right1[h])
            right_stage(2, v).start()
            left_stage(1, v).wait()
            left1[h] = add(left0[h, x], got_left1[h])
            left_stage(2, v).start()

        @pl.when(whether(t - 1))
        def _():
            v = t - 1
            h = order(v) % 2
            core_stage(v).wait()
            right0[h] = add(staged[slot(v), core, :, :, :, :, half_width:], got0[h, :, :, :, :, half_width:])
            right_stage(1, v).start()
            left0[h] = add(staged[slot(v), core, :, :, :, :, :half_width], got0[h, :, :, :, :, :half_width])
            left_stage(1, v).start()

        @pl.when(whether(t))
        def _():
            core_stage(t).start()

        for s in range(STAGES + 1):
            def small_copy(s):
                return send(small, small_got.at[s], small_send.at[s], small_recv.at[s], mates[s])

            @pl.when(t == last + s)
            def _():
                if s:
                    small_copy(s - 1).wait()
                    small[...] += small_got[s - 1]
                if s < STAGES:
                    small_copy(s).start()
    else:
        def piece_copy(v):
            return pltpu.make_async_copy(staged.at[slot(v)], outs[0].at[v], out_sem.at[v % 2])

        @pl.when(whether(t - 1))
        def _():
            piece_copy(t - 1).wait()

        @pl.when(whether(t))
        def _():
            piece_copy(t).start()


    def swaps(i, act):
        source, target = ((done_ref, output_ref), (low, input_ref))[i]

        @pl.when(swapped)
        def _():
            getattr(send(source, target, swap_send.at[i], swap_recv.at[i], diagonal), act)()

        @pl.when(jnp.logical_not(swapped))
        def _():
            getattr(pltpu.make_async_copy(source, target, here_sem.at[i]), act)()

    @pl.when(t == 0)
    def _():
        swaps(0, "start")

    @pl.when(t == last)
    def _():
        swaps(1, "start")

    @pl.when(t == pl.num_programs(0) - 1)
    def _():
        swaps(0, "wait")
        swaps(1, "wait")
        small_ref[...] = small[...]


def back(cotangent, done, length, act, slope, normeds, scaleds, inverses, mixed, up, down, merge, first_gain, second_gain, query, kv,
         total, exps, weight, hosted):
    layers, tokens, width = query.shape
    tiles = exps.shape[2]
    steps = layers * STEPS + (STAGES + 1 if hosted else 1)
    piece = (2, 2, 2, 2, SHARE, width)
    part = (2, 2, 2, SHARE, width // 2)
    count = layers * PIECES

    def at(t):
        t = jnp.minimum(t, layers * STEPS - 1)
        return layers - 1 - t // STEPS, t % STEPS

    def tile_of(t):
        layer, j = at(t)
        return layer, jnp.minimum(j, FFN_STEPS - 1)

    def head_of(t):
        layer, j = at(t)
        return layer, jnp.clip(j - FFN_STEPS, 0, PAIRS - 1)

    def part_of(t):
        layer, j = at(t)
        return layer, jnp.clip(j - FFN_STEPS - PAIRS - 1, 0, 2)

    def kind_of(t):
        layer, j = at(t)
        return layer, (j >= FFN_STEPS).astype(jnp.int32), 0, 0

    once = dict(pipeline_mode=pl.Buffered(1))

    def of_layer(shape):
        return pl.BlockSpec((1,) + shape, lambda t: (at(t)[0],) + (0,) * len(shape), **once)

    units = pl.BlockSpec((1, tokens, width), lambda t: (tile_of(t)[0], 0, tile_of(t)[1]))
    in_specs = [
        ANY, ANY, whole(length.shape), units, units,
        pl.BlockSpec((1, 1, tokens, width), kind_of, **once),
        pl.BlockSpec((1, 1, tokens, width), kind_of, **once),
        pl.BlockSpec((1, 1, tokens, 1), kind_of, **once),
        of_layer((tokens, width)),
        pl.BlockSpec((1, width, width), lambda t: (tile_of(t)[0], 0, tile_of(t)[1])),
        pl.BlockSpec((1, width, width), lambda t: (tile_of(t)[0], tile_of(t)[1], 0)),
        of_layer((width, width)),
        whole((layers, width)), whole((layers, width)),
        pl.BlockSpec((1, tokens, LANES), lambda t: (head_of(t)[0], 0, head_of(t)[1])),
        pl.BlockSpec((1, 2 * tokens, LANES), lambda t: (head_of(t)[0], 0, head_of(t)[1])),
        pl.BlockSpec((1, 2 * tokens, LANES), lambda t: (head_of(t)[0], 0, head_of(t)[1] + PAIRS)),
        pl.BlockSpec((1, 1, tokens, 2), lambda t: (head_of(t)[0], head_of(t)[1], 0, 0)),
        ANY,
        pl.BlockSpec((1, width, width), lambda t: (part_of(t)[0], 0, part_of(t)[1]), **once),
    ]
    if hosted:
        shapes = [
            sds((layers, SHARE, 3 * width), F32), sds((layers, SHARE, width), F32),
            sds((layers, SHARE, FFN_STEPS * width), F32), sds((layers, 4 * SHARE, width), F32),
        ]
    else:
        shapes = [sds((layers * STEPS,) + piece, BF16)]
    dma = pltpu.SemaphoreType.DMA

    def some(*shape):
        return pltpu.VMEM(shape, BF16)

    return pl.pallas_call(
        functools.partial(back_kernel, layers, hosted),
        grid=(steps,),
        in_specs=in_specs,
        out_specs=[ANY] * len(shapes) + [whole((SMALL, width)), ANY, ANY],
        out_shape=shapes + [
            sds((SMALL, width), F32), sds((tokens, width), BF16), sds((tokens, width), BF16),
        ],
        scratch_shapes=[
            pltpu.VMEM((tokens, width), F32),
            pltpu.VMEM((tokens, width), F32),
            some(3, tokens, width),
            some(2, 2, tokens, LANES),
            some(2, 2, tokens, LANES),
            some(2, 2, tiles, BLOCK, 2 * BLOCK),
            some(7, *piece),
            some(2, *part), some(2, *part[1:]), some(2, *part[2:]), some(2, *part[3:]),
            some(2, *part), some(2, *part[1:]), some(2, *part[2:]), some(2, *part[3:]),
            some(2, *piece[1:]),
            some(2, *part[1:]), some(2, *part[2:]), some(2, *part[3:]), some(2, *part[3:]),
            some(2, *part[1:]), some(2, *part[2:]), some(2, *part[3:]), some(count, *part[3:]),
            pltpu.VMEM((2, SHARE, width), F32),
            pltpu.VMEM((SMALL, width), F32),
            pltpu.VMEM((STAGES, SMALL, width), F32),
            dma((2, 2)), dma, dma((2,)), dma((2,)), dma((2,)), dma((2,)), dma((4, 2)), dma((4, 2)), dma((3, 2)), dma((3, 2)),
            dma((2, count)), dma((2, count)), dma((2,)),
            dma((STAGES,)), dma((STAGES,)), dma((2,)), dma((2,)), dma((2,)),
        ],
        compiler_params=params(1),
        name="back",
    )(cotangent, done, length, act, slope, normeds, scaleds, inverses, mixed, up, down, merge, first_gain, second_gain, query, kv, kv,
      total, exps, weight)


def local(
    stream, lengths, pass_embed, first_gain, first_bias, triple_weight, merge_weight,
    second_gain, second_bias, up_weight, down_weight, cotangent,
):
    row_count = lax.axis_size("rows")
    own_row = lax.axis_index("rows")
    tokens, width = stream.shape[2], stream.shape[3]
    layers = triple_weight.shape[0]
    hosted = row_count == ROWS

    (normeds, scaleds, inverses, query, mixed, total, exps, act, slope, kv, done, cotangent, length) = forward(
        stream.reshape(tokens, width), cotangent.reshape(tokens, width), lengths, pass_embed,
        first_gain, first_bias, second_gain, second_bias, triple_weight, merge_weight, up_weight, down_weight,
    )
    *weight_grads, small, input_grad, output = back(
        cotangent, done, length, act, slope, normeds, scaleds, inverses, mixed, up_weight, down_weight, merge_weight,
        first_gain, second_gain, query, kv.reshape(layers, 2 * tokens, 2 * width), total, exps, triple_weight, hosted,
    )
    input_grad = input_grad.reshape(stream.shape)
    output = output.reshape(stream.shape)
    if hosted:
        triple_grad, merge_grad, up_grad, down_grad = weight_grads
    else:
        pieces = weight_grads[0].transpose(0, 4, 3, 2, 1, 5, 6).reshape(layers, STEPS, -1, width)[::-1]

        def columns(first, last):
            return pieces[:, first:last].transpose(0, 2, 1, 3).reshape(layers, -1, (last - first) * width)

        def reduce(gradient):
            share = lax.psum_scatter(gradient, "rows", scatter_dimension=1, tiled=True)
            return lax.psum(share, "pass").astype(F32)

        down_grad = pieces[:, 4:8].reshape(layers, 4, ROWS, SHARE, width).transpose(0, 2, 1, 3, 4)
        triple_grad, merge_grad, up_grad, down_grad = map(
            reduce, (columns(10, 13), columns(8, 9), columns(0, 4), down_grad.reshape(layers, -1, width))
        )
        small = lax.psum(small, ("pass", "rows"))
    share = width // row_count
    small = lax.dynamic_slice_in_dim(small, own_row * share, share, 1)
    by_layer = small[2 : 2 + 4 * layers].reshape(layers, 4, share)
    return (
        output, input_grad, small[:2], by_layer[:, 0], by_layer[:, 1], triple_grad, merge_grad,
        by_layer[:, 2], by_layer[:, 3], up_grad, down_grad,
    )


def solution(mesh):
    token = P("pass", "rows", None, None)
    matrix = P(None, "rows", None)
    rows = P(None, "rows")
    in_specs = (token, P("rows")) + (P(),) * 9 + (token,)
    out_specs = (token, token, rows, rows, rows, matrix, matrix, rows, rows, matrix, matrix)
    return jax.shard_map(local, mesh=mesh, in_specs=in_specs, out_specs=out_specs, check_vma=False)
```

```python
import functools
import math

import jax
import jax.numpy as jnp
from jax import lax
from jax.experimental import pallas as pl
from jax.experimental.pallas import tpu as pltpu
from jax.sharding import PartitionSpec as P

HEAD_DIM = 64
EPSILON = 1e-05
SCALE = HEAD_DIM**-0.5
MESH = pl.DeviceIdType.MESH
NN = (((1,), (0,)), ((), ()))
NT = (((1,), (1,)), ((), ()))
TN = (((0,), (0,)), ((), ()))
BLOCK = 128
TILE = 256
LANES = 128
BF16 = jnp.bfloat16
F32 = jnp.float32
VMEM_LIMIT = 63 * 2**20 + 3 * 2**18
ANY = pl.BlockSpec(memory_space=pl.ANY)


def dot(left, right, dims=NN):
    return lax.dot_general(left, right, dims, preferred_element_type=F32)


def sds(shape, dtype):
    return jax.ShapeDtypeStruct(shape, dtype)


def params(collective_id=None):
    return pltpu.CompilerParams(
        vmem_limit_bytes=VMEM_LIMIT,
        collective_id=collective_id,
        has_side_effects=collective_id is not None,
    )


def whole(shape):
    zeros = (0,) * len(shape)
    return pl.BlockSpec(shape, lambda *_: zeros, pipeline_mode=pl.Buffered(1))


def pick(ref, which):
    return jnp.where(which == 0, ref[0:1, :], ref[1:2, :]).astype(F32)


def norm(hidden, gain, bias):
    centred = hidden - jnp.mean(hidden, -1, keepdims=True)
    inverse = lax.rsqrt(jnp.mean(centred * centred, -1, keepdims=True) + EPSILON)
    scaled = centred * inverse
    return (scaled * gain + bias).astype(BF16), scaled, inverse


def norm_back(grad, scaled, inverse, gain):
    e = grad * gain
    return inverse * (
        e - jnp.mean(e, -1, keepdims=True) - scaled * jnp.mean(e * scaled, -1, keepdims=True)
    )


def bits():
    row = lax.axis_index("rows")
    return row, row % 2, (row // 2) % 2, (row // 4) % 2, (row // 8) % 2, lax.axis_index("pass")


def send(src, dst, send_sem, recv_sem, device):
    return pltpu.make_async_remote_copy(
        src_ref=src, dst_ref=dst, send_sem=send_sem, recv_sem=recv_sem,
        device_id=device, device_id_type=MESH,
    )


QKV_STEPS = 4
PAIRS = 6
FFN_TILES = 4
FORWARD = QKV_STEPS + PAIRS + FFN_TILES


def tile_index(blocks, key_block, query_block):
    return key_block * blocks - key_block * (key_block - 1) // 2 + query_block - key_block


def gelu_both(v):
    root = math.sqrt(2.0 / math.pi)
    cube = (root * 0.044715) * (v * v)
    half = 0.5 + 0.5 * jnp.tanh(v * (root + cube))
    act = v * half
    return act, half + (act - act * half) * (2.0 * root + 6.0 * cube)


def forward_kernel(
    layers,
    stream_ref, cot_ref, length_ref, embed_ref, first_gain_ref, first_bias_ref, second_gain_ref, second_bias_ref,
    triple_ref, merge_ref, up_ref, down_ref,
    normed_ref, scaled_ref, inverse_ref, query_ref, mixed_ref, total_ref, exp_ref, act_ref, slope_ref, kv_ref,
    out_ref, cot_out_ref, length_out_ref,
    hidden, arrived, length_mine, length_here, queries, kv, values, mixes, triple, merge, up, down,
    weight_sem, kv_sem, kv_send, kv_recv, free_sem, swap_send, swap_recv, here_sem,
):
    t = pl.program_id(0)
    layer = t // FORWARD
    j = t % FORWARD
    row, core, _, _, _, own_pass = bits()
    tokens, width = hidden.shape
    blocks = tokens // BLOCK
    pair = 2 * BLOCK
    core_mate = {"rows": row + 1 - 2 * core}
    diagonal = {"pass": 1 - own_pass, "rows": row + 1 - 2 * core}
    swapped = own_pass != core


    def moves(i):
        if i < QKV_STEPS:
            rows = pl.ds(i * TILE, TILE)
            ends = stream_ref.at[rows, :], arrived.at[rows, :]
        else:
            ends = ((cot_ref, cot_out_ref), (length_mine, length_here))[i - QKV_STEPS]
        return (
            send(*ends, swap_send.at[i], swap_recv.at[i], diagonal),
            pltpu.make_async_copy(*ends, here_sem.at[i]),
        )

    def move(i, act):
        there, here = moves(i)

        @pl.when(swapped)
        def _():
            getattr(there, act)()

        @pl.when(jnp.logical_not(swapped))
        def _():
            getattr(here, act)()


    def weight_copies(which, of_layer):
        refs = ((triple_ref, triple), (merge_ref, merge), (up_ref, up), (down_ref, down))
        source, target = refs[which]
        return pltpu.make_async_copy(source.at[of_layer], target, weight_sem.at[which])

    @pl.when(t == 0)
    def _():
        barrier = pltpu.get_barrier_semaphore()
        pl.semaphore_signal(barrier, inc=1, device_id=core_mate, device_id_type=MESH)

        @pl.when(swapped)
        def _():
            pl.semaphore_signal(barrier, inc=1, device_id=diagonal, device_id_type=MESH)

        pl.semaphore_wait(barrier, 1 + jnp.where(swapped, 1, 0))
        length_mine[...] = jnp.full(length_mine.shape, length_ref[0], jnp.int32)
        move(QKV_STEPS + 1, "start")
        for i in range(QKV_STEPS):
            move(i, "start")
        for which in range(4):
            weight_copies(which, 0).start()
        move(QKV_STEPS + 1, "wait")
        length_out_ref[...] = length_here[...]

    for i in range(QKV_STEPS):
        @pl.when(t == i)
        def _():
            move(i, "wait")
            if i == QKV_STEPS - 1:
                move(QKV_STEPS, "start")


    def kv_copy(i):
        part = kv.at[pl.ds(i * (TILE // BLOCK), TILE // BLOCK), core]
        return send(part, part, kv_send.at[i], kv_recv.at[i], core_mate)

    def kv_keep(of_layer):
        return pltpu.make_async_copy(kv, kv_ref.at[of_layer], kv_sem)

    @pl.when(j < QKV_STEPS)
    def _():
        rows = pl.ds(pl.multiple_of(j * TILE, TILE), TILE)

        @pl.when(layer == 0)
        def _():
            hidden[rows, :] = arrived[rows, :].astype(F32) + pick(embed_ref, core)

        @pl.when(j == 0)
        def _():
            weight_copies(0, layer).wait()

        @pl.when((j == 0) & (layer > 0))
        def _():
            pl.semaphore_wait(free_sem, 1)

        normed, scaled, inverse = norm(
            hidden[rows, :], pick(first_gain_ref, layer), pick(first_bias_ref, layer)
        )
        normed_ref[0, 0] = normed
        scaled_ref[0, 0] = scaled.astype(BF16)
        inverse_ref[0, 0] = inverse
        keys = dot(normed, triple[:, width:]).astype(BF16)
        for b in range(TILE // BLOCK):
            kv[j * (TILE // BLOCK) + b, core] = keys[b * BLOCK : (b + 1) * BLOCK]
        kv_copy(j).start()
        query = (dot(normed, triple[:, :width]).astype(BF16).astype(F32) * SCALE).astype(BF16)
        queries[rows, :] = query
        query_ref[0] = query


    @pl.when((j >= QKV_STEPS) & (j < QKV_STEPS + PAIRS))
    def _():
        p = j - QKV_STEPS
        lanes = pl.ds(pl.multiple_of(p * LANES, LANES), LANES)
        value_lanes = pl.ds(pl.multiple_of(width + p * LANES, LANES), LANES)

        @pl.when(p == 0)
        def _():
            for i in range(QKV_STEPS):
                kv_copy(i).wait()
            kv_keep(layer).start()

        @pl.when((p == 0) & (layer < layers - 1))
        def _():
            weight_copies(0, layer + 1).start()

        values[:, :LANES] = kv[:, :, :, value_lanes].reshape(2 * tokens, LANES)
        values[:, LANES:] = jnp.ones((2 * tokens, LANES), BF16)
        lane = lax.broadcasted_iota(jnp.int32, (BLOCK, LANES), 1)
        query_at = lax.broadcasted_iota(jnp.int32, (BLOCK, pair), 0)
        column = lax.broadcasted_iota(jnp.int32, (BLOCK, pair), 1)
        key_pass = column // BLOCK
        key_at = column - key_pass * BLOCK
        causal = (key_at < query_at) | ((key_at == query_at) & (key_pass <= core))
        length = length_here[0:1, 0:1]

        def scores(block, head):
            query = queries[pl.ds(block * BLOCK, BLOCK), lanes]
            chosen = jnp.where(lane // HEAD_DIM == head, query, jnp.zeros_like(query))
            keys = kv[: block + 1, :, :, lanes].reshape((block + 1) * pair, LANES)
            return dot(chosen, keys, NT)

        def exponentials(block, head, raw):
            allowed = causal & (key_at + block * BLOCK < length)
            last = jnp.where(allowed, raw[:, block * pair :], -jnp.inf)
            top = jnp.max(last, -1, keepdims=True)
            if block:
                top = jnp.maximum(top, jnp.max(raw[:, : block * pair], -1, keepdims=True))
            parts = []
            for k in range(block + 1):
                source = last if k == block else raw[:, k * pair : (k + 1) * pair]
                part = jnp.exp(source - top).astype(BF16)
                exp_ref[0, head, tile_index(blocks, k, block)] = part
                parts.append(part)
            return jnp.concatenate(parts, 1) if block else parts[0]

        outs = {}

        def mix(block, head, exps):
            both = dot(exps, values[: (block + 1) * pair, :])
            inverse = jnp.where(block * BLOCK < length, 1.0 / both[:, LANES:], 0.0)
            rows = pl.ds(block * BLOCK, BLOCK)
            total_ref[0, 0, head : head + 1, rows] = inverse.T[:1]
            outs[head] = both[:, :LANES] * inverse
            if head == 1:
                value = jnp.where(lane < HEAD_DIM, outs[0], outs[1]).astype(BF16)
                mixes[rows, lanes] = value
                mixed_ref[0, rows, :] = value

        items = [(block, head) for block in range(blocks) for head in range(2)]
        ahead = scores(*items[0])
        behind = None
        for n, item in enumerate(items):
            raw = ahead
            if n + 1 < len(items):
                ahead = scores(*items[n + 1])
            exps = exponentials(*item, raw)
            if behind is not None:
                mix(*behind)
            behind = (*item, exps)
        mix(*behind)

        @pl.when(p == PAIRS - 1)
        def _():
            kv_keep(layer).wait()

        @pl.when((p == PAIRS - 1) & (layer < layers - 1))
        def _():
            pl.semaphore_signal(free_sem, inc=1, device_id=core_mate, device_id_type=MESH)


    @pl.when(j >= QKV_STEPS + PAIRS)
    def _():
        i = j - QKV_STEPS - PAIRS
        rows = pl.ds(pl.multiple_of(i * TILE, TILE), TILE)

        @pl.when(i == 0)
        def _():
            for which in range(1, 4):
                weight_copies(which, layer).wait()

        mid = hidden[rows, :] + dot(mixes[rows, :], merge[...])
        normed, scaled, inverse = norm(mid, pick(second_gain_ref, layer), pick(second_bias_ref, layer))
        normed_ref[0, 0] = normed
        scaled_ref[0, 0] = scaled.astype(BF16)
        inverse_ref[0, 0] = inverse
        parts = up.shape[1] // width
        sum_next = mid
        ahead = dot(normed, up[:, :width])
        for part in range(parts):
            at = slice(part * width, (part + 1) * width)
            now = ahead
            if part + 1 < parts:
                ahead = dot(normed, up[:, (part + 1) * width : (part + 2) * width])
            act, slope = gelu_both(now)
            act = act.astype(BF16)
            act_ref[0, :, at] = act
            slope_ref[0, :, at] = slope.astype(BF16)
            sum_next = sum_next + dot(act, down[at, :])
        hidden[rows, :] = sum_next

        @pl.when(layer == layers - 1)
        def _():
            position = lax.broadcasted_iota(jnp.int32, (TILE, 1), 0) + i * TILE
            valid = (position < length_here[0:1, 0:1]).astype(F32)
            out_ref[...] = (sum_next * valid).astype(BF16)

        @pl.when((i == FFN_TILES - 1) & (layer < layers - 1))
        def _():
            for which in range(1, 4):
                weight_copies(which, layer + 1).start()

    @pl.when(t == pl.num_programs(0) - 1)
    def _():
        move(QKV_STEPS, "wait")


def forward(stream, cotangent, length, embed, first_gain, first_bias, second_gain, second_bias, triple, merge, up, down):
    tokens, width = stream.shape
    layers, _, units = up.shape
    blocks = tokens // BLOCK
    tiles = blocks * (blocks + 1) // 2

    def phase(t):
        return t // FORWARD, t % FORWARD

    def row_tile(t):
        layer, j = phase(t)
        late = j >= QKV_STEPS + PAIRS
        kind = jnp.where(late, 0, 1)
        return layer, kind, jnp.where(late, j - QKV_STEPS - PAIRS, jnp.minimum(j, QKV_STEPS - 1)), 0

    def query_tile(t):
        layer, j = phase(t)
        return layer, jnp.minimum(j, QKV_STEPS - 1), 0

    def head(t):
        layer, j = phase(t)
        return layer, jnp.clip(j - QKV_STEPS, 0, PAIRS - 1)

    def ffn_tile(t):
        layer, j = phase(t)
        return layer, jnp.maximum(j - QKV_STEPS - PAIRS, 0), 0

    vector = whole((layers, width))
    rows = pl.BlockSpec((1, 1, TILE, width), row_tile)
    dma = pltpu.SemaphoreType.DMA
    return pl.pallas_call(
        functools.partial(forward_kernel, layers),
        grid=(layers * FORWARD,),
        in_specs=[ANY, ANY, pl.BlockSpec(memory_space=pltpu.SMEM), whole(embed.shape), vector, vector, vector, vector, ANY, ANY, ANY, ANY],
        out_specs=[
            rows, rows, pl.BlockSpec((1, 1, TILE, 1), row_tile),
            pl.BlockSpec((1, TILE, width), query_tile),
            pl.BlockSpec((1, tokens, LANES), lambda t: (head(t)[0], 0, head(t)[1])),
            pl.BlockSpec((1, 1, 8, tokens), lambda t: (*head(t), 0, 0)),
            pl.BlockSpec((1, 2, tiles, BLOCK, 2 * BLOCK), lambda t: (*head(t), 0, 0, 0)),
            pl.BlockSpec((1, TILE, units), ffn_tile), pl.BlockSpec((1, TILE, units), ffn_tile),
            ANY,
            pl.BlockSpec((TILE, width), lambda t: (jnp.where(phase(t)[0] == layers - 1, ffn_tile(t)[1], 0), 0)),
            ANY, whole((8, LANES)),
        ],
        out_shape=[
            sds((layers, 2, tokens, width), BF16),
            sds((layers, 2, tokens, width), BF16),
            sds((layers, 2, tokens, 1), F32),
            sds((layers, tokens, width), BF16),
            sds((layers, tokens, width), BF16),
            sds((layers, PAIRS, 8, tokens), F32),
            sds((layers, 2 * PAIRS, tiles, BLOCK, 2 * BLOCK), BF16),
            sds((layers, tokens, units), BF16),
            sds((layers, tokens, units), BF16),
            sds((layers, blocks, 2, BLOCK, 2 * width), BF16),
            sds((tokens, width), BF16),
            sds((tokens, width), BF16),
            sds((8, LANES), jnp.int32),
        ],
        scratch_shapes=[
            pltpu.VMEM((tokens, width), F32),
            pltpu.VMEM((tokens, width), BF16),
            pltpu.VMEM((8, LANES), jnp.int32),
            pltpu.VMEM((8, LANES), jnp.int32),
            pltpu.VMEM((tokens, width), BF16),
            pltpu.VMEM((blocks, 2, BLOCK, 2 * width), BF16),
            pltpu.VMEM((2 * tokens, 2 * LANES), BF16),
            pltpu.VMEM((tokens, width), BF16),
            pltpu.VMEM(triple.shape[1:], BF16),
            pltpu.VMEM(merge.shape[1:], BF16),
            pltpu.VMEM(up.shape[1:], BF16),
            pltpu.VMEM(down.shape[1:], BF16),
            dma((4,)), dma, dma((QKV_STEPS,)), dma((QKV_STEPS,)), pltpu.SemaphoreType.REGULAR,
            dma((QKV_STEPS + 2,)), dma((QKV_STEPS + 2,)), dma((QKV_STEPS + 2,)),
        ],
        compiler_params=params(0),
        name="forward",
    )(stream, cotangent, length, embed, first_gain, first_bias, second_gain, second_bias, triple, merge, up, down)


FFN_STEPS = 4
STEPS = FFN_STEPS + PAIRS + 4
PIECES = STEPS - 2
STAGES = 5
ROWS = 16
SHARE = 48
SMALL = 16


def back_kernel(
    layers, hosted,
    cot_ref, done_ref, length_ref, act_ref, slope_ref, normeds_ref, scaleds_ref, inverses_ref, mixes_ref, up_ref, down_ref,
    merges_ref,
    first_gain_ref, second_gain_ref, query_ref, key_ref, value_ref, total_ref, exp_ref, triples_ref,
    *refs,
):
    outs = refs[: 4 if hosted else 1]
    (
        small_ref, input_ref, output_ref,
        normed_ref, scaled_ref, inverse_ref, mixed_ref, weights, grad, total, grads, pending, landing, exps,
        staged, left0, left1, left2, left3, right0, right1, right2, right3, got0,
        got_left1, got_left2, got_left3, got_left4, got_right1, got_right2, got_right3, got_late,
        final, small, small_got,
        load_sem, exp_sem, cot_sem, kv_send, kv_recv, core_send, core_recv, left_send, left_recv, right_send, right_recv,
        late_send, late_recv, out_sem, small_send, small_recv, swap_send, swap_recv, here_sem,
    ) = refs[len(outs) :]
    low = grads.at[1]
    t = pl.program_id(0)
    j = t % STEPS
    layer = layers - 1 - t // STEPS
    row, core, x, z0, z1, own_pass = bits()
    tokens, width = grad.shape
    blocks = tokens // BLOCK
    pair = 2 * BLOCK
    busy = t < layers * STEPS
    core_mate = {"rows": row + 1 - 2 * core}
    mates = [
        core_mate, {"rows": row + 2 - 4 * x}, {"rows": row + 4 - 8 * z0}, {"rows": row + 8 - 16 * z1},
        {"pass": 1 - own_pass},
    ]
    diagonal = {"pass": 1 - own_pass, "rows": row + 1 - 2 * core}
    swapped = own_pass != core

    @pl.when(t == 0)
    def _():
        barrier = pltpu.get_barrier_semaphore()
        greeted = mates if hosted else mates[:1]
        for mate in greeted:
            pl.semaphore_signal(barrier, inc=1, device_id=mate, device_id_type=MESH)

        @pl.when(swapped)
        def _():
            pl.semaphore_signal(barrier, inc=1, device_id=diagonal, device_id_type=MESH)

        pl.semaphore_wait(barrier, len(greeted) + jnp.where(swapped, 1, 0))
        load = pltpu.make_async_copy(cot_ref, low, cot_sem)
        load.start()
        load.wait()
        position = lax.broadcasted_iota(jnp.int32, (tokens, 1), 0)
        valid = (position < length_ref[0:1, 0:1]).astype(F32)
        masked = low[...].astype(F32) * valid
        grad[...] = masked
        low[...] = masked.astype(BF16)
        small[...] = jnp.zeros_like(small)


    def load(what, of_layer):
        def weight_part(n):
            return triples_ref.at[of_layer, :, n * width : (n + 1) * width]

        source, target, sem = (
            (normeds_ref.at[of_layer, 0], normed_ref, 0), (scaleds_ref.at[of_layer, 0], scaled_ref, 1),
            (inverses_ref.at[of_layer, 0], inverse_ref, 2), (mixes_ref.at[of_layer], mixed_ref, 3),
            (normeds_ref.at[of_layer, 1], normed_ref, 0), (scaleds_ref.at[of_layer, 1], scaled_ref, 1),
            (inverses_ref.at[of_layer, 1], inverse_ref, 2), (merges_ref.at[of_layer], weights.at[0], 4),
            (weight_part(0), weights.at[1], 5), (weight_part(1), weights.at[0], 4), (weight_part(2), weights.at[1], 5),
        )[what]
        return pltpu.make_async_copy(source, target, load_sem.at[sem])

    def fetch(*which, of_layer=layer, when=True):
        @pl.when(when)
        def _():
            for what in which:
                load(what, of_layer).start()

    def have(*which):
        for what in which:
            load(what, layer).wait()

    more = layer > 0
    fetch(0, 1, 2, 3, 7, when=t == 0)


    def exp_copy(head):
        at = (head // 2) % 2, head % 2
        return pltpu.make_async_copy(exp_ref.at[layer, head], exps.at[at], exp_sem.at[at])

    def put(slot, r, value):
        staged[slot, r % 2, (r // 2) % 2, (r // 4) % 2, (r // 8) % 2] = value

    @pl.when(busy & (j < FFN_STEPS))
    def _():
        @pl.when(j == 0)
        def _():
            total[...] = jnp.zeros_like(total)
            have(0)

        grad_low = low[...]
        down_grad = dot(act_ref[0], grad_low, TN).astype(BF16)
        for q in range(4):
            for i in range(4):
                first = q * 4 * SHARE + i * SHARE
                staged[i, q % 2, q // 2, j % 2, (j // 2) % 2] = down_grad[first : first + SHARE]
        grad_act = dot(grad_low, down_ref[0], NT)
        grad_pre = (slope_ref[0].astype(F32) * grad_act).astype(BF16)
        up_grad = dot(normed_ref[...], grad_pre, TN).astype(BF16)
        for r in range(ROWS):
            put(4 + j % 2, r, up_grad[r * SHARE : (r + 1) * SHARE])
        total[...] += dot(grad_pre, up_ref[0], NT)

        @pl.when(j == FFN_STEPS - 1)
        def _():
            exp_copy(0).start()
            exp_copy(1).start()
            have(1, 2, 3, 7)

            def rows(i, sums):
                at = pl.ds(pl.multiple_of(i * TILE, TILE), TILE)
                part = total[at, :]
                scaled = scaled_ref[at, :].astype(F32)
                mid = grad[at, :] + norm_back(part, scaled, inverse_ref[at, :], pick(second_gain_ref, layer))
                grad[at, :] = mid
                low_mid = mid.astype(BF16)
                low[at, :] = low_mid
                grads[0, at, :] = dot(low_mid, weights[0], NT).astype(BF16)
                return (
                    sums[0] + jnp.sum(part * scaled, 0, keepdims=True),
                    sums[1] + jnp.sum(part, 0, keepdims=True),
                )

            empty = jnp.zeros((1, width), F32)
            gain_sum, bias_sum = lax.fori_loop(0, tokens // TILE, rows, (empty, empty))
            small[pl.ds(4 + 4 * layer, 1), :] = gain_sum
            small[pl.ds(5 + 4 * layer, 1), :] = bias_sum
            merge_grad = dot(mixed_ref[...], low[...], TN).astype(BF16)
            for r in range(ROWS):
                put(6, r, merge_grad[r * SHARE : (r + 1) * SHARE])
            fetch(4, 5, 6, 8, 9)


    def kv_copy(p):
        return send(
            pending.at[p % 2], landing.at[p % 2], kv_send.at[p % 2], kv_recv.at[p % 2], core_mate,
        )

    def take(p):
        kv_copy(p).wait()
        lanes = pl.ds(pl.multiple_of(p * LANES, LANES), LANES)
        for which in range(2):
            grads[1 + which, :, lanes] = (
                grads[1 + which, :, lanes].astype(F32) + landing[p % 2, which].astype(F32)
            ).astype(BF16)

    @pl.when(busy & (j >= FFN_STEPS) & (j < FFN_STEPS + PAIRS))
    def _():
        p = j - FFN_STEPS
        lanes = pl.ds(pl.multiple_of(p * LANES, LANES), LANES)
        lane = lax.broadcasted_iota(jnp.int32, (tokens, LANES), 1)
        out_grad = grads[0, :, lanes].astype(F32)
        product = out_grad * mixed_ref[:, lanes].astype(F32)
        query = query_ref[0]
        inverses = total_ref[0, 0].T
        weighted = out_grad * jnp.where(lane < HEAD_DIM, inverses[:, :1], inverses[:, 1:2])
        weighted_across = weighted.T.astype(BF16)
        weighted = weighted.astype(BF16)
        query_across = query.astype(F32).T.astype(BF16)
        across = lax.broadcasted_iota(jnp.int32, (LANES, tokens), 0)
        scaled, scaled_across, inner, chosen_across = [], [], [], []
        for head in range(2):
            mine = lane // HEAD_DIM == head
            mine_across = across // HEAD_DIM == head
            scaled.append(jnp.where(mine, weighted, jnp.zeros_like(weighted)))
            scaled_across.append(jnp.where(mine_across, weighted_across, jnp.zeros_like(weighted_across)))
            chosen_across.append(jnp.where(mine_across, query_across, jnp.zeros_like(query_across)))
            inner.append(jnp.sum(jnp.where(mine, product, 0.0), -1, keepdims=True) * inverses[:, head : head + 1])

        def probs_grad(head, block):
            return dot(scaled[head][block * BLOCK :], value_ref[0, block * pair : (block + 1) * pair, :], NT)

        def score_grad(head, block, grad_prob):
            start = tile_index(blocks, block, block)
            prob = exps[p % 2, head, start : start + blocks - block].reshape(tokens - block * BLOCK, pair)
            return prob, (prob.astype(F32) * (grad_prob - inner[head][block * BLOCK :])).astype(BF16)

        sums = {}

        def products(head, block, prob, score):
            first = block * BLOCK
            pairs = dot(chosen_across[head][:, first:], score), dot(scaled_across[head][:, first:], prob)
            grad_query = dot(score, key_ref[0, block * pair : (block + 1) * pair, :])
            mine_lanes = slice(head * LANES, (head + 1) * LANES)
            if block == 0:
                total[:, mine_lanes] = grad_query
            else:
                total[first:, mine_lanes] += grad_query
            if head == 0:
                sums[block] = pairs
                return
            at = pl.ds(first, BLOCK)
            for which in range(2):
                both = (sums[block][which] + pairs[which]).T
                zero, one = both[:BLOCK], both[BLOCK:]
                grads[1 + which, at, lanes] = jnp.where(core == 0, zero, one).astype(BF16)
                pending[p % 2, which, at, :] = jnp.where(core == 0, one, zero).astype(BF16)

        exp_copy(2 * p).wait()
        exp_copy(2 * p + 1).wait()

        @pl.when(p < PAIRS - 1)
        def _():
            exp_copy(2 * p + 2).start()
            exp_copy(2 * p + 3).start()

        items = [(head, block) for block in range(blocks) for head in range(2)]
        ahead = probs_grad(*items[0])
        behind = None
        for n, item in enumerate(items):
            now = ahead
            if n + 1 < len(items):
                ahead = probs_grad(*items[n + 1])
            both = score_grad(*item, now)
            if behind is not None:
                products(*behind)
            behind = (*item, *both)
        products(*behind)

        grads[0, :, lanes] = (
            jnp.where(lane < HEAD_DIM, total[:, :LANES], total[:, LANES : 2 * LANES]) * SCALE
        ).astype(BF16)

        @pl.when(p > 0)
        def _():
            take(p - 1)

        kv_copy(p).start()


    @pl.when(busy & (j == FFN_STEPS + PAIRS))
    def _():
        total[...] = jnp.zeros_like(total)
        take(PAIRS - 1)
        have(4)
        fetch(3, of_layer=layer - 1, when=more)

    @pl.when(busy & (j >= FFN_STEPS + PAIRS))
    def _():
        n = j - FFN_STEPS - PAIRS

        @pl.when(n < 3)
        def _():
            triple_grad = dot(normed_ref[...], grads[n], TN).astype(BF16)
            for r in range(ROWS):
                put(4 + n, r, triple_grad[r * SHARE : (r + 1) * SHARE])

        for part in range(3):
            @pl.when(n == part + 1)
            def _():
                have(8 + part)

        @pl.when(n > 0)
        def _():
            total[...] += dot(grads[n - 1], weights[n % 2], NT)

        @pl.when(n == 1)
        def _():
            fetch(10)

        fetch(7, 0, of_layer=layer - 1, when=more & (n == 2))

        @pl.when(n == 3)
        def _():
            have(5, 6)
            def rows(i, sums):
                at = pl.ds(pl.multiple_of(i * TILE, TILE), TILE)
                part = total[at, :]
                scaled = scaled_ref[at, :].astype(F32)
                hidden = grad[at, :] + norm_back(part, scaled, inverse_ref[at, :], pick(first_gain_ref, layer))
                grad[at, :] = hidden
                low[at, :] = hidden.astype(BF16)
                return (
                    sums[0] + jnp.sum(part * scaled, 0, keepdims=True),
                    sums[1] + jnp.sum(part, 0, keepdims=True),
                    sums[2] + jnp.sum(hidden, 0, keepdims=True),
                )

            empty = jnp.zeros((1, width), F32)
            gain_sum, bias_sum, hidden_sum = lax.fori_loop(0, tokens // TILE, rows, (empty, empty, empty))
            small[pl.ds(2 + 4 * layer, 1), :] = gain_sum
            small[pl.ds(3 + 4 * layer, 1), :] = bias_sum

            @pl.when(layer == 0)
            def _():
                small[pl.ds(core, 1), :] = hidden_sum

            fetch(1, 2, of_layer=layer - 1, when=more)


    last = layers * STEPS - 1
    half_width = width // 2

    def slot(v):
        i = v % STEPS
        return jnp.where(
            i < 4, 4 + i % 2, jnp.where(i < 8, i - 4, jnp.where(i == 8, 6, i - FFN_STEPS - PAIRS + 4))
        )

    def whether(v):
        return (v >= 0) & (v <= last) & (v % STEPS != FFN_STEPS + PAIRS - 1) & (v % STEPS != STEPS - 1)

    def order(v):
        i = v % STEPS
        return v // STEPS * PIECES + i - jnp.where(i >= FFN_STEPS + PAIRS, 1, 0)

    def add(a, b):
        return (a.astype(F32) + b.astype(F32)).astype(BF16)

    def core_stage(v):
        h = order(v) % 2
        return send(staged.at[slot(v), 1 - core], got0.at[h], core_send.at[h], core_recv.at[h], mates[0])

    def left_stage(s, v):
        h = order(v) % 2
        src = (left0.at[h, 1 - x], left1.at[h, 1 - z0], left2.at[h, 1 - z1], left3.at[h])[s - 1]
        d = order(v) % 4 if s == 1 else h
        dst = (got_left1, got_left2, got_left3, got_left4)[s - 1].at[d]
        return send(src, dst, left_send.at[s - 1, h], left_recv.at[s - 1, d], mates[s])

    def right_stage(s, v):
        h = order(v) % 2
        src = (right0.at[h, 1 - own_pass], right1.at[h, 1 - z0], right2.at[h, 1 - z1])[s - 1]
        d = order(v) % 4 if s == 1 else h
        dst = (got_right1, got_right2, got_right3)[s - 1].at[d]
        return send(src, dst, right_send.at[s - 1, h], right_recv.at[s - 1, d], (mates[4], mates[2], mates[3])[s - 1])

    def late_stage(s, v):
        k = order(v)
        return send(right3.at[k % 2], got_late.at[k], late_send.at[s - 4, k], late_recv.at[s - 4, k], (mates[1], mates[4])[s - 4])

    keeps = x == own_pass

    def late_start(s, v):
        @pl.when(keeps == (s == 5))
        def _():
            late_stage(s, v).start()

    def late_wait(s, v, receive):
        @pl.when(keeps == (s == 5))
        def _():
            late_stage(s, v).wait_send()

        @pl.when(keeps != (s == 5))
        def _():
            late_stage(s, v).wait_recv()
            receive()

    def out_copies(v, act):
        h = order(v) % 2
        i = v % STEPS
        at_layer = layers - 1 - v // STEPS
        triple_out, merge_out, up_out, down_out = outs

        def columns(n):
            return pl.ds(pl.multiple_of(n * width, width), width)

        def go(target):
            getattr(pltpu.make_async_copy(final.at[h], target, out_sem.at[h]), act)()

        @pl.when(i < 4)
        def _():
            go(up_out.at[at_layer, :, columns(i)])

        @pl.when((i >= 4) & (i < 8))
        def _():
            go(down_out.at[at_layer, pl.ds(pl.multiple_of((i - 4) * SHARE, SHARE), SHARE), :])

        @pl.when(i == 8)
        def _():
            go(merge_out.at[at_layer])

        @pl.when(i >= FFN_STEPS + PAIRS)
        def _():
            go(triple_out.at[at_layer, :, columns(i - FFN_STEPS - PAIRS)])

    if hosted:
        @pl.when(whether(t - 8))
        def _():
            out_copies(t - 8, "wait")

        @pl.when(whether(t - 7))
        def _():
            v = t - 7
            h = order(v) % 2

            def receive():
                right3[h] = got_late[order(v)]

            late_wait(5, v, receive)
            final[h, :, half_width:] = right3[h].astype(F32)
            out_copies(v, "start")

        @pl.when(whether(t - 6))
        def _():
            v = t - 6
            h = order(v) % 2

            def receive():
                right3[h] = add(right3[h], got_late[order(v)])

            late_wait(4, v, receive)
            late_start(5, v)
            left_stage(4, v).wait()
            final[h, :, :half_width] = left3[h].astype(F32) + got_left4[h].astype(F32)

        @pl.when(whether(t - 5))
        def _():
            v = t - 5
            h = order(v) % 2
            right_stage(3, v).wait()
            right3[h] = add(right2[h, z1], got_right3[h])
            late_start(4, v)
            left_stage(3, v).wait()
            left3[h] = add(left2[h, z1], got_left3[h])
            left_stage(4, v).start()

        @pl.when(whether(t - 4))
        def _():
            v = t - 4
            h = order(v) % 2
            right_stage(2, v).wait()
            right2[h] = add(right1[h, z0], got_right2[h])
            right_stage(3, v).start()
            left_stage(2, v).wait()
            left2[h] = add(left1[h, z0], got_left2[h])
            left_stage(3, v).start()

        @pl.when(whether(t - 3))
        def _():
            v = t - 3
            h = order(v) % 2
            right_stage(1, v).wait()
            right1[h] = add(right0[h, own_pass], got_right1[order(v) % 4])
            right_stage(2, v).start()
            left_stage(1, v).wait()
            left1[h] = add(left0[h, x], got_left1[order(v) % 4])
            left_stage(2, v).start()

        @pl.when(whether(t - 1))
        def _():
            v = t - 1
            h = order(v) % 2
            core_stage(v).wait()
            right0[h] = add(staged[slot(v), core, :, :, :, :, half_width:], got0[h, :, :, :, :, half_width:])
            right_stage(1, v).start()
            left0[h] = add(staged[slot(v), core, :, :, :, :, :half_width], got0[h, :, :, :, :, :half_width])
            left_stage(1, v).start()

        @pl.when(whether(t))
        def _():
            core_stage(t).start()

        for s in range(STAGES + 1):
            def small_copy(s):
                return send(small, small_got.at[s], small_send.at[s], small_recv.at[s], mates[s])

            @pl.when(t == last + s)
            def _():
                if s:
                    small_copy(s - 1).wait()
                    small[...] += small_got[s - 1]
                if s < STAGES:
                    small_copy(s).start()
    else:
        def piece_copy(v):
            return pltpu.make_async_copy(staged.at[slot(v)], outs[0].at[v], out_sem.at[v % 2])

        @pl.when(whether(t - 1))
        def _():
            piece_copy(t - 1).wait()

        @pl.when(whether(t))
        def _():
            piece_copy(t).start()


    def swaps(i, act):
        source, target = ((done_ref, output_ref), (low, input_ref))[i]

        @pl.when(swapped)
        def _():
            getattr(send(source, target, swap_send.at[i], swap_recv.at[i], diagonal), act)()

        @pl.when(jnp.logical_not(swapped))
        def _():
            getattr(pltpu.make_async_copy(source, target, here_sem.at[i]), act)()

    @pl.when(t == 0)
    def _():
        swaps(0, "start")

    @pl.when(t == last)
    def _():
        swaps(1, "start")

    @pl.when(t == pl.num_programs(0) - 1)
    def _():
        swaps(0, "wait")
        swaps(1, "wait")
        small_ref[...] = small[...]


def back(cotangent, done, length, act, slope, normeds, scaleds, inverses, mixed, up, down, merge, first_gain, second_gain, query, kv,
         total, exps, weight, hosted):
    layers, tokens, width = query.shape
    tiles = exps.shape[2]
    steps = layers * STEPS + (STAGES + 2 if hosted else 1)
    piece = (2, 2, 2, 2, SHARE, width)
    part = (2, 2, 2, SHARE, width // 2)
    count = layers * PIECES

    def at(t):
        t = jnp.minimum(t, layers * STEPS - 1)
        return layers - 1 - t // STEPS, t % STEPS

    def tile_of(t):
        layer, j = at(t)
        return layer, jnp.minimum(j, FFN_STEPS - 1)

    def head_of(t):
        layer, j = at(t)
        return layer, jnp.clip(j - FFN_STEPS, 0, PAIRS - 1)

    units = pl.BlockSpec((1, tokens, width), lambda t: (tile_of(t)[0], 0, tile_of(t)[1]))
    in_specs = [
        ANY, ANY, whole(length.shape), units, units,
        ANY, ANY, ANY, ANY,
        pl.BlockSpec((1, width, width), lambda t: (tile_of(t)[0], 0, tile_of(t)[1])),
        pl.BlockSpec((1, width, width), lambda t: (tile_of(t)[0], tile_of(t)[1], 0)),
        ANY,
        whole((layers, width)), whole((layers, width)),
        pl.BlockSpec((1, tokens, LANES), lambda t: (head_of(t)[0], 0, head_of(t)[1])),
        pl.BlockSpec((1, 2 * tokens, LANES), lambda t: (head_of(t)[0], 0, head_of(t)[1])),
        pl.BlockSpec((1, 2 * tokens, LANES), lambda t: (head_of(t)[0], 0, head_of(t)[1] + PAIRS)),
        pl.BlockSpec((1, 1, 8, tokens), lambda t: (head_of(t)[0], head_of(t)[1], 0, 0)),
        ANY, ANY,
    ]
    if hosted:
        shapes = [
            sds((layers, SHARE, 3 * width), F32), sds((layers, SHARE, width), F32),
            sds((layers, SHARE, FFN_STEPS * width), F32), sds((layers, 4 * SHARE, width), F32),
        ]
    else:
        shapes = [sds((layers * STEPS,) + piece, BF16)]
    dma = pltpu.SemaphoreType.DMA

    def some(*shape):
        return pltpu.VMEM(shape, BF16)

    return pl.pallas_call(
        functools.partial(back_kernel, layers, hosted),
        grid=(steps,),
        in_specs=in_specs,
        out_specs=[ANY] * len(shapes) + [whole((SMALL, width)), ANY, ANY],
        out_shape=shapes + [
            sds((SMALL, width), F32), sds((tokens, width), BF16), sds((tokens, width), BF16),
        ],
        scratch_shapes=[
            some(tokens, width), some(tokens, width), pltpu.VMEM((tokens, 1), F32), some(tokens, width),
            some(2, width, width),
            pltpu.VMEM((tokens, width), F32),
            pltpu.VMEM((tokens, width), F32),
            some(3, tokens, width),
            some(2, 2, tokens, LANES),
            some(2, 2, tokens, LANES),
            some(2, 2, tiles, BLOCK, 2 * BLOCK),
            some(7, *piece),
            some(2, *part), some(2, *part[1:]), some(2, *part[2:]), some(2, *part[3:]),
            some(2, *part), some(2, *part[1:]), some(2, *part[2:]), some(2, *part[3:]),
            some(2, *piece[1:]),
            some(4, *part[1:]), some(2, *part[2:]), some(2, *part[3:]), some(2, *part[3:]),
            some(4, *part[1:]), some(2, *part[2:]), some(2, *part[3:]), some(count, *part[3:]),
            pltpu.VMEM((2, SHARE, width), F32),
            pltpu.VMEM((SMALL, width), F32),
            pltpu.VMEM((STAGES, SMALL, width), F32),
            dma((6,)), dma((2, 2)), dma, dma((2,)), dma((2,)), dma((2,)), dma((2,)), dma((4, 2)), dma((4, 4)), dma((3, 2)), dma((3, 4)),
            dma((2, count)), dma((2, count)), dma((2,)),
            dma((STAGES,)), dma((STAGES,)), dma((2,)), dma((2,)), dma((2,)),
        ],
        compiler_params=params(1),
        name="back",
    )(cotangent, done, length, act, slope, normeds, scaleds, inverses, mixed, up, down, merge, first_gain, second_gain, query, kv, kv,
      total, exps, weight)


def local(
    stream, lengths, pass_embed, first_gain, first_bias, triple_weight, merge_weight,
    second_gain, second_bias, up_weight, down_weight, cotangent,
):
    row_count = lax.axis_size("rows")
    own_row = lax.axis_index("rows")
    tokens, width = stream.shape[2], stream.shape[3]
    layers = triple_weight.shape[0]
    hosted = row_count == ROWS

    (normeds, scaleds, inverses, query, mixed, total, exps, act, slope, kv, done, cotangent, length) = forward(
        stream.reshape(tokens, width), cotangent.reshape(tokens, width), lengths, pass_embed,
        first_gain, first_bias, second_gain, second_bias, triple_weight, merge_weight, up_weight, down_weight,
    )
    *weight_grads, small, input_grad, output = back(
        cotangent, done, length, act, slope, normeds, scaleds, inverses, mixed, up_weight, down_weight, merge_weight,
        first_gain, second_gain, query, kv.reshape(layers, 2 * tokens, 2 * width), total, exps, triple_weight, hosted,
    )
    input_grad = input_grad.reshape(stream.shape)
    output = output.reshape(stream.shape)
    if hosted:
        triple_grad, merge_grad, up_grad, down_grad = weight_grads
    else:
        pieces = weight_grads[0].transpose(0, 4, 3, 2, 1, 5, 6).reshape(layers, STEPS, -1, width)[::-1]

        def columns(first, last):
            return pieces[:, first:last].transpose(0, 2, 1, 3).reshape(layers, -1, (last - first) * width)

        def reduce(gradient):
            share = lax.psum_scatter(gradient, "rows", scatter_dimension=1, tiled=True)
            return lax.psum(share, "pass").astype(F32)

        down_grad = pieces[:, 4:8].reshape(layers, 4, ROWS, SHARE, width).transpose(0, 2, 1, 3, 4)
        triple_grad, merge_grad, up_grad, down_grad = map(
            reduce, (columns(10, 13), columns(8, 9), columns(0, 4), down_grad.reshape(layers, -1, width))
        )
        small = lax.psum(small, ("pass", "rows"))
    share = width // row_count
    small = lax.dynamic_slice_in_dim(small, own_row * share, share, 1)
    by_layer = small[2 : 2 + 4 * layers].reshape(layers, 4, share)
    return (
        output, input_grad, small[:2], by_layer[:, 0], by_layer[:, 1], triple_grad, merge_grad,
        by_layer[:, 2], by_layer[:, 3], up_grad, down_grad,
    )


def solution(mesh):
    token = P("pass", "rows", None, None)
    matrix = P(None, "rows", None)
    rows = P(None, "rows")
    in_specs = (token, P("rows")) + (P(),) * 9 + (token,)
    out_specs = (token, token, rows, rows, rows, matrix, matrix, rows, rows, matrix, matrix)
    return jax.shard_map(local, mesh=mesh, in_specs=in_specs, out_specs=out_specs, check_vma=False)
```

```python
import functools
import math

import jax
import jax.numpy as jnp
from jax import lax
from jax.experimental import pallas as pl
from jax.experimental.pallas import tpu as pltpu
from jax.sharding import PartitionSpec as P

HEAD_DIM = 64
EPSILON = 1e-05
SCALE = HEAD_DIM**-0.5
MESH = pl.DeviceIdType.MESH
NN = (((1,), (0,)), ((), ()))
NT = (((1,), (1,)), ((), ()))
TN = (((0,), (0,)), ((), ()))
BLOCK = 128
TILE = 256
LANES = 128
BF16 = jnp.bfloat16
F32 = jnp.float32
VMEM_LIMIT = 63 * 2**20 + 3 * 2**18
ANY = pl.BlockSpec(memory_space=pl.ANY)


def dot(left, right, dims=NN):
    return lax.dot_general(left, right, dims, preferred_element_type=F32)


def sds(shape, dtype):
    return jax.ShapeDtypeStruct(shape, dtype)


def params(collective_id=None):
    return pltpu.CompilerParams(
        vmem_limit_bytes=VMEM_LIMIT,
        collective_id=collective_id,
        has_side_effects=collective_id is not None,
    )


def whole(shape):
    zeros = (0,) * len(shape)
    return pl.BlockSpec(shape, lambda *_: zeros, pipeline_mode=pl.Buffered(1))


def pick(ref, which):
    return jnp.where(which == 0, ref[0:1, :], ref[1:2, :]).astype(F32)


def norm(hidden, gain, bias):
    centred = hidden - jnp.mean(hidden, -1, keepdims=True)
    inverse = lax.rsqrt(jnp.mean(centred * centred, -1, keepdims=True) + EPSILON)
    scaled = centred * inverse
    return (scaled * gain + bias).astype(BF16), scaled, inverse


def norm_back(grad, scaled, inverse, gain):
    e = grad * gain
    return inverse * (
        e - jnp.mean(e, -1, keepdims=True) - scaled * jnp.mean(e * scaled, -1, keepdims=True)
    )


def bits():
    row = lax.axis_index("rows")
    return row, row % 2, (row // 2) % 2, (row // 4) % 2, (row // 8) % 2, lax.axis_index("pass")


def send(src, dst, send_sem, recv_sem, device):
    return pltpu.make_async_remote_copy(
        src_ref=src, dst_ref=dst, send_sem=send_sem, recv_sem=recv_sem,
        device_id=device, device_id_type=MESH,
    )


QKV_STEPS = 4
PAIRS = 6
FFN_TILES = 4
FORWARD = QKV_STEPS + PAIRS + FFN_TILES


def tile_index(blocks, key_block, query_block):
    return key_block * blocks - key_block * (key_block - 1) // 2 + query_block - key_block


def gelu_both(v):
    root = math.sqrt(2.0 / math.pi)
    cube = (root * 0.044715) * (v * v)
    half = 0.5 + 0.5 * jnp.tanh(v * (root + cube))
    act = v * half
    return act, half + (act - act * half) * (2.0 * root + 6.0 * cube)


def forward_kernel(
    layers,
    stream_ref, cot_ref, length_ref, embed_ref, first_gain_ref, first_bias_ref, second_gain_ref, second_bias_ref,
    triple_ref, merge_ref, up_ref, down_ref,
    normed_ref, scaled_ref, inverse_ref, query_ref, mixed_ref, total_ref, exp_ref, act_ref, slope_ref, kv_ref,
    out_ref, cot_out_ref, length_out_ref,
    hidden, arrived, length_mine, length_here, queries, kv, values, mixes, triple, merge, up, down,
    weight_sem, kv_sem, kv_send, kv_recv, free_sem, swap_send, swap_recv, here_sem,
):
    t = pl.program_id(0)
    layer = t // FORWARD
    j = t % FORWARD
    row, core, _, _, _, own_pass = bits()
    tokens, width = hidden.shape
    blocks = tokens // BLOCK
    pair = 2 * BLOCK
    core_mate = {"rows": row + 1 - 2 * core}
    diagonal = {"pass": 1 - own_pass, "rows": row + 1 - 2 * core}
    swapped = own_pass != core


    def moves(i):
        if i < QKV_STEPS:
            rows = pl.ds(i * TILE, TILE)
            ends = stream_ref.at[rows, :], arrived.at[rows, :]
        else:
            ends = ((cot_ref, cot_out_ref), (length_mine, length_here))[i - QKV_STEPS]
        return (
            send(*ends, swap_send.at[i], swap_recv.at[i], diagonal),
            pltpu.make_async_copy(*ends, here_sem.at[i]),
        )

    def move(i, act):
        there, here = moves(i)

        @pl.when(swapped)
        def _():
            getattr(there, act)()

        @pl.when(jnp.logical_not(swapped))
        def _():
            getattr(here, act)()


    def weight_copies(which, of_layer):
        refs = ((triple_ref, triple), (merge_ref, merge), (up_ref, up), (down_ref, down))
        source, target = refs[which]
        return pltpu.make_async_copy(source.at[of_layer], target, weight_sem.at[which])

    @pl.when(t == 0)
    def _():
        barrier = pltpu.get_barrier_semaphore()
        pl.semaphore_signal(barrier, inc=1, device_id=core_mate, device_id_type=MESH)

        @pl.when(swapped)
        def _():
            pl.semaphore_signal(barrier, inc=1, device_id=diagonal, device_id_type=MESH)

        pl.semaphore_wait(barrier, 1 + jnp.where(swapped, 1, 0))
        length_mine[...] = jnp.full(length_mine.shape, length_ref[0], jnp.int32)
        move(QKV_STEPS + 1, "start")
        for i in range(QKV_STEPS):
            move(i, "start")
        for which in range(4):
            weight_copies(which, 0).start()
        move(QKV_STEPS + 1, "wait")
        length_out_ref[...] = length_here[...]

    for i in range(QKV_STEPS):
        @pl.when(t == i)
        def _():
            move(i, "wait")
            if i == QKV_STEPS - 1:
                move(QKV_STEPS, "start")


    def kv_copy(i):
        part = kv.at[pl.ds(i * (TILE // BLOCK), TILE // BLOCK), core]
        return send(part, part, kv_send.at[i], kv_recv.at[i], core_mate)

    def kv_keep(of_layer):
        return pltpu.make_async_copy(kv, kv_ref.at[of_layer], kv_sem)

    @pl.when(j < QKV_STEPS)
    def _():
        rows = pl.ds(pl.multiple_of(j * TILE, TILE), TILE)

        @pl.when(layer == 0)
        def _():
            hidden[rows, :] = arrived[rows, :].astype(F32) + pick(embed_ref, core)

        @pl.when(j == 0)
        def _():
            weight_copies(0, layer).wait()

        @pl.when((j == 0) & (layer > 0))
        def _():
            pl.semaphore_wait(free_sem, 1)

        normed, scaled, inverse = norm(
            hidden[rows, :], pick(first_gain_ref, layer), pick(first_bias_ref, layer)
        )
        normed_ref[0, 0] = normed
        scaled_ref[0, 0] = scaled.astype(BF16)
        inverse_ref[0, 0] = inverse
        keys = dot(normed, triple[:, width:]).astype(BF16)
        for b in range(TILE // BLOCK):
            kv[j * (TILE // BLOCK) + b, core] = keys[b * BLOCK : (b + 1) * BLOCK]
        kv_copy(j).start()
        query = (dot(normed, triple[:, :width]).astype(BF16).astype(F32) * SCALE).astype(BF16)
        queries[rows, :] = query
        query_ref[0] = query


    @pl.when((j >= QKV_STEPS) & (j < QKV_STEPS + PAIRS))
    def _():
        p = j - QKV_STEPS
        lanes = pl.ds(pl.multiple_of(p * LANES, LANES), LANES)
        value_lanes = pl.ds(pl.multiple_of(width + p * LANES, LANES), LANES)

        @pl.when(p == 0)
        def _():
            for i in range(QKV_STEPS):
                kv_copy(i).wait()
            kv_keep(layer).start()

        @pl.when((p == 0) & (layer < layers - 1))
        def _():
            weight_copies(0, layer + 1).start()

        values[:, :LANES] = kv[:, :, :, value_lanes].reshape(2 * tokens, LANES)
        values[:, LANES:] = jnp.ones((2 * tokens, LANES), BF16)
        lane = lax.broadcasted_iota(jnp.int32, (BLOCK, LANES), 1)
        query_at = lax.broadcasted_iota(jnp.int32, (BLOCK, pair), 0)
        column = lax.broadcasted_iota(jnp.int32, (BLOCK, pair), 1)
        key_pass = column // BLOCK
        key_at = column - key_pass * BLOCK
        causal = (key_at < query_at) | ((key_at == query_at) & (key_pass <= core))
        length = length_here[0:1, 0:1]

        def scores(block, head):
            query = queries[pl.ds(block * BLOCK, BLOCK), lanes]
            chosen = jnp.where(lane // HEAD_DIM == head, query, jnp.zeros_like(query))
            keys = kv[: block + 1, :, :, lanes].reshape((block + 1) * pair, LANES)
            return dot(chosen, keys, NT)

        def exponentials(block, head, raw):
            allowed = causal & (key_at + block * BLOCK < length)
            last = jnp.where(allowed, raw[:, block * pair :], -jnp.inf)
            top = jnp.max(last, -1, keepdims=True)
            if block:
                top = jnp.maximum(top, jnp.max(raw[:, : block * pair], -1, keepdims=True))
            parts = []
            for k in range(block + 1):
                source = last if k == block else raw[:, k * pair : (k + 1) * pair]
                part = jnp.exp(source - top).astype(BF16)
                exp_ref[0, head, tile_index(blocks, k, block)] = part
                parts.append(part)
            return jnp.concatenate(parts, 1) if block else parts[0]

        outs = {}

        def mix(block, head, exps):
            both = dot(exps, values[: (block + 1) * pair, :])
            inverse = jnp.where(block * BLOCK < length, 1.0 / both[:, LANES:], 0.0)
            rows = pl.ds(block * BLOCK, BLOCK)
            total_ref[0, 0, head : head + 1, rows] = inverse.T[:1]
            outs[head] = both[:, :LANES] * inverse
            if head == 1:
                value = jnp.where(lane < HEAD_DIM, outs[0], outs[1]).astype(BF16)
                mixes[rows, lanes] = value
                mixed_ref[0, rows, :] = value

        items = [(block, head) for block in range(blocks) for head in range(2)]
        ahead = scores(*items[0])
        behind = None
        for n, item in enumerate(items):
            raw = ahead
            if n + 1 < len(items):
                ahead = scores(*items[n + 1])
            exps = exponentials(*item, raw)
            if behind is not None:
                mix(*behind)
            behind = (*item, exps)
        mix(*behind)

        @pl.when(p == PAIRS - 1)
        def _():
            kv_keep(layer).wait()

        @pl.when((p == PAIRS - 1) & (layer < layers - 1))
        def _():
            pl.semaphore_signal(free_sem, inc=1, device_id=core_mate, device_id_type=MESH)


    @pl.when(j >= QKV_STEPS + PAIRS)
    def _():
        i = j - QKV_STEPS - PAIRS
        rows = pl.ds(pl.multiple_of(i * TILE, TILE), TILE)

        @pl.when(i == 0)
        def _():
            for which in range(1, 4):
                weight_copies(which, layer).wait()

        mid = hidden[rows, :] + dot(mixes[rows, :], merge[...])
        normed, scaled, inverse = norm(mid, pick(second_gain_ref, layer), pick(second_bias_ref, layer))
        normed_ref[0, 0] = normed
        scaled_ref[0, 0] = scaled.astype(BF16)
        inverse_ref[0, 0] = inverse
        parts = up.shape[1] // width
        sum_next = mid
        ahead = dot(normed, up[:, :width])
        for part in range(parts):
            at = slice(part * width, (part + 1) * width)
            now = ahead
            if part + 1 < parts:
                ahead = dot(normed, up[:, (part + 1) * width : (part + 2) * width])
            act, slope = gelu_both(now)
            act = act.astype(BF16)
            act_ref[0, :, at] = act
            slope_ref[0, :, at] = slope.astype(BF16)
            sum_next = sum_next + dot(act, down[at, :])
        hidden[rows, :] = sum_next

        @pl.when(layer == layers - 1)
        def _():
            position = lax.broadcasted_iota(jnp.int32, (TILE, 1), 0) + i * TILE
            valid = (position < length_here[0:1, 0:1]).astype(F32)
            out_ref[...] = (sum_next * valid).astype(BF16)

        @pl.when((i == FFN_TILES - 1) & (layer < layers - 1))
        def _():
            for which in range(1, 4):
                weight_copies(which, layer + 1).start()

    @pl.when(t == pl.num_programs(0) - 1)
    def _():
        move(QKV_STEPS, "wait")


def forward(stream, cotangent, length, embed, first_gain, first_bias, second_gain, second_bias, triple, merge, up, down):
    tokens, width = stream.shape
    layers, _, units = up.shape
    blocks = tokens // BLOCK
    tiles = blocks * (blocks + 1) // 2

    def phase(t):
        return t // FORWARD, t % FORWARD

    def row_tile(t):
        layer, j = phase(t)
        late = j >= QKV_STEPS + PAIRS
        kind = jnp.where(late, 0, 1)
        return layer, kind, jnp.where(late, j - QKV_STEPS - PAIRS, jnp.minimum(j, QKV_STEPS - 1)), 0

    def query_tile(t):
        layer, j = phase(t)
        return layer, jnp.minimum(j, QKV_STEPS - 1), 0

    def head(t):
        layer, j = phase(t)
        return layer, jnp.clip(j - QKV_STEPS, 0, PAIRS - 1)

    def ffn_tile(t):
        layer, j = phase(t)
        return layer, jnp.maximum(j - QKV_STEPS - PAIRS, 0), 0

    vector = whole((layers, width))
    rows = pl.BlockSpec((1, 1, TILE, width), row_tile)
    dma = pltpu.SemaphoreType.DMA
    return pl.pallas_call(
        functools.partial(forward_kernel, layers),
        grid=(layers * FORWARD,),
        in_specs=[ANY, ANY, pl.BlockSpec(memory_space=pltpu.SMEM), whole(embed.shape), vector, vector, vector, vector, ANY, ANY, ANY, ANY],
        out_specs=[
            rows, rows, pl.BlockSpec((1, 1, TILE, 1), row_tile),
            pl.BlockSpec((1, TILE, width), query_tile),
            pl.BlockSpec((1, tokens, LANES), lambda t: (head(t)[0], 0, head(t)[1])),
            pl.BlockSpec((1, 1, 8, tokens), lambda t: (*head(t), 0, 0)),
            pl.BlockSpec((1, 2, tiles, BLOCK, 2 * BLOCK), lambda t: (*head(t), 0, 0, 0)),
            pl.BlockSpec((1, TILE, units), ffn_tile), pl.BlockSpec((1, TILE, units), ffn_tile),
            ANY,
            pl.BlockSpec((TILE, width), lambda t: (jnp.where(phase(t)[0] == layers - 1, ffn_tile(t)[1], 0), 0)),
            ANY, whole((8, LANES)),
        ],
        out_shape=[
            sds((layers, 2, tokens, width), BF16),
            sds((layers, 2, tokens, width), BF16),
            sds((layers, 2, tokens, 1), F32),
            sds((layers, tokens, width), BF16),
            sds((layers, tokens, width), BF16),
            sds((layers, PAIRS, 8, tokens), F32),
            sds((layers, 2 * PAIRS, tiles, BLOCK, 2 * BLOCK), BF16),
            sds((layers, tokens, units), BF16),
            sds((layers, tokens, units), BF16),
            sds((layers, blocks, 2, BLOCK, 2 * width), BF16),
            sds((tokens, width), BF16),
            sds((tokens, width), BF16),
            sds((8, LANES), jnp.int32),
        ],
        scratch_shapes=[
            pltpu.VMEM((tokens, width), F32),
            pltpu.VMEM((tokens, width), BF16),
            pltpu.VMEM((8, LANES), jnp.int32),
            pltpu.VMEM((8, LANES), jnp.int32),
            pltpu.VMEM((tokens, width), BF16),
            pltpu.VMEM((blocks, 2, BLOCK, 2 * width), BF16),
            pltpu.VMEM((2 * tokens, 2 * LANES), BF16),
            pltpu.VMEM((tokens, width), BF16),
            pltpu.VMEM(triple.shape[1:], BF16),
            pltpu.VMEM(merge.shape[1:], BF16),
            pltpu.VMEM(up.shape[1:], BF16),
            pltpu.VMEM(down.shape[1:], BF16),
            dma((4,)), dma, dma((QKV_STEPS,)), dma((QKV_STEPS,)), pltpu.SemaphoreType.REGULAR,
            dma((QKV_STEPS + 2,)), dma((QKV_STEPS + 2,)), dma((QKV_STEPS + 2,)),
        ],
        compiler_params=params(0),
        name="forward",
    )(stream, cotangent, length, embed, first_gain, first_bias, second_gain, second_bias, triple, merge, up, down)


FFN_STEPS = 4
STEPS = FFN_STEPS + PAIRS + 4
PIECES = STEPS - 2
STAGES = 5
ROWS = 16
SHARE = 48
SMALL = 16


def back_kernel(
    layers, hosted,
    cot_ref, done_ref, length_ref, act_ref, slope_ref, normeds_ref, scaleds_ref, inverses_ref, mixes_ref, up_ref, down_ref,
    merges_ref,
    first_gain_ref, second_gain_ref, query_ref, key_ref, value_ref, total_ref, exp_ref, triples_ref,
    *refs,
):
    outs = refs[: 4 if hosted else 1]
    (
        small_ref, input_ref, output_ref,
        normed_ref, scaled_ref, inverse_ref, mixed_ref, weights, grad, total, grads, pending, landing, exps,
        staged, left0, left1, left2, left3, right0, right1, right2, right3, right4, got0,
        got_left1, got_left2, got_left3, got_left4, got_right1, got_right2, got_right3, got_late,
        final, small, small_got,
        load_sem, exp_sem, cot_sem, kv_send, kv_recv, core_send, core_recv, left_send, left_recv, right_send, right_recv,
        late_send, late_recv, out_sem, small_send, small_recv, swap_send, swap_recv, here_sem,
    ) = refs[len(outs) :]
    low = grads.at[1]
    t = pl.program_id(0)
    j = t % STEPS
    layer = layers - 1 - t // STEPS
    row, core, x, z0, z1, own_pass = bits()
    tokens, width = grad.shape
    blocks = tokens // BLOCK
    pair = 2 * BLOCK
    busy = t < layers * STEPS
    core_mate = {"rows": row + 1 - 2 * core}
    mates = [
        core_mate, {"rows": row + 2 - 4 * x}, {"rows": row + 4 - 8 * z0}, {"rows": row + 8 - 16 * z1},
        {"pass": 1 - own_pass},
    ]
    diagonal = {"pass": 1 - own_pass, "rows": row + 1 - 2 * core}
    swapped = own_pass != core

    @pl.when(t == 0)
    def _():
        barrier = pltpu.get_barrier_semaphore()
        greeted = mates if hosted else mates[:1]
        for mate in greeted:
            pl.semaphore_signal(barrier, inc=1, device_id=mate, device_id_type=MESH)

        @pl.when(swapped)
        def _():
            pl.semaphore_signal(barrier, inc=1, device_id=diagonal, device_id_type=MESH)

        pl.semaphore_wait(barrier, len(greeted) + jnp.where(swapped, 1, 0))
        load = pltpu.make_async_copy(cot_ref, low, cot_sem)
        load.start()
        load.wait()
        position = lax.broadcasted_iota(jnp.int32, (tokens, 1), 0)
        valid = (position < length_ref[0:1, 0:1]).astype(F32)
        masked = low[...].astype(F32) * valid
        grad[...] = masked
        low[...] = masked.astype(BF16)
        small[...] = jnp.zeros_like(small)


    def load(what, of_layer):
        def weight_part(n):
            return triples_ref.at[of_layer, :, n * width : (n + 1) * width]

        source, target, sem = (
            (normeds_ref.at[of_layer, 0], normed_ref, 0), (scaleds_ref.at[of_layer, 0], scaled_ref, 1),
            (inverses_ref.at[of_layer, 0], inverse_ref, 2), (mixes_ref.at[of_layer], mixed_ref, 3),
            (normeds_ref.at[of_layer, 1], normed_ref, 0), (scaleds_ref.at[of_layer, 1], scaled_ref, 1),
            (inverses_ref.at[of_layer, 1], inverse_ref, 2), (merges_ref.at[of_layer], weights.at[0], 4),
            (weight_part(0), weights.at[1], 5), (weight_part(1), weights.at[0], 4), (weight_part(2), weights.at[1], 5),
        )[what]
        return pltpu.make_async_copy(source, target, load_sem.at[sem])

    def fetch(*which, of_layer=layer, when=True):
        @pl.when(when)
        def _():
            for what in which:
                load(what, of_layer).start()

    def have(*which):
        for what in which:
            load(what, layer).wait()

    more = layer > 0
    fetch(0, 1, 2, 3, 7, when=t == 0)


    def exp_copy(head):
        at = (head // 2) % 2, head % 2
        return pltpu.make_async_copy(exp_ref.at[layer, head], exps.at[at], exp_sem.at[at])

    def put(slot, r, value):
        staged[slot, r % 2, (r // 2) % 2, (r // 4) % 2, (r // 8) % 2] = value

    @pl.when(busy & (j < FFN_STEPS))
    def _():
        @pl.when(j == 0)
        def _():
            total[...] = jnp.zeros_like(total)
            have(0)

        grad_low = low[...]
        down_grad = dot(act_ref[0], grad_low, TN).astype(BF16)
        for q in range(4):
            for i in range(4):
                first = q * 4 * SHARE + i * SHARE
                staged[i, q % 2, q // 2, j % 2, (j // 2) % 2] = down_grad[first : first + SHARE]
        grad_act = dot(grad_low, down_ref[0], NT)
        grad_pre = (slope_ref[0].astype(F32) * grad_act).astype(BF16)
        up_grad = dot(normed_ref[...], grad_pre, TN).astype(BF16)
        for r in range(ROWS):
            put(4 + j % 2, r, up_grad[r * SHARE : (r + 1) * SHARE])
        total[...] += dot(grad_pre, up_ref[0], NT)

        @pl.when(j == FFN_STEPS - 1)
        def _():
            exp_copy(0).start()
            exp_copy(1).start()
            have(1, 2, 3, 7)

            def rows(i, sums):
                at = pl.ds(pl.multiple_of(i * TILE, TILE), TILE)
                part = total[at, :]
                scaled = scaled_ref[at, :].astype(F32)
                mid = grad[at, :] + norm_back(part, scaled, inverse_ref[at, :], pick(second_gain_ref, layer))
                grad[at, :] = mid
                low_mid = mid.astype(BF16)
                low[at, :] = low_mid
                grads[0, at, :] = dot(low_mid, weights[0], NT).astype(BF16)
                return (
                    sums[0] + jnp.sum(part * scaled, 0, keepdims=True),
                    sums[1] + jnp.sum(part, 0, keepdims=True),
                )

            empty = jnp.zeros((1, width), F32)
            gain_sum, bias_sum = lax.fori_loop(0, tokens // TILE, rows, (empty, empty))
            small[pl.ds(4 + 4 * layer, 1), :] = gain_sum
            small[pl.ds(5 + 4 * layer, 1), :] = bias_sum
            merge_grad = dot(mixed_ref[...], low[...], TN).astype(BF16)
            for r in range(ROWS):
                put(6, r, merge_grad[r * SHARE : (r + 1) * SHARE])
            fetch(4, 5, 6, 8, 9)


    def kv_copy(p):
        return send(
            pending.at[p % 2], landing.at[p % 2], kv_send.at[p % 2], kv_recv.at[p % 2], core_mate,
        )

    def take(p):
        kv_copy(p).wait()
        lanes = pl.ds(pl.multiple_of(p * LANES, LANES), LANES)
        for which in range(2):
            grads[1 + which, :, lanes] = (
                grads[1 + which, :, lanes].astype(F32) + landing[p % 2, which].astype(F32)
            ).astype(BF16)

    @pl.when(busy & (j >= FFN_STEPS) & (j < FFN_STEPS + PAIRS))
    def _():
        p = j - FFN_STEPS
        lanes = pl.ds(pl.multiple_of(p * LANES, LANES), LANES)
        lane = lax.broadcasted_iota(jnp.int32, (tokens, LANES), 1)
        out_grad = grads[0, :, lanes].astype(F32)
        product = out_grad * mixed_ref[:, lanes].astype(F32)
        query = query_ref[0]
        inverses = total_ref[0, 0].T
        weighted = out_grad * jnp.where(lane < HEAD_DIM, inverses[:, :1], inverses[:, 1:2])
        weighted_across = weighted.T.astype(BF16)
        weighted = weighted.astype(BF16)
        query_across = query.astype(F32).T.astype(BF16)
        across = lax.broadcasted_iota(jnp.int32, (LANES, tokens), 0)
        scaled, scaled_across, inner, chosen_across = [], [], [], []
        for head in range(2):
            mine = lane // HEAD_DIM == head
            mine_across = across // HEAD_DIM == head
            scaled.append(jnp.where(mine, weighted, jnp.zeros_like(weighted)))
            scaled_across.append(jnp.where(mine_across, weighted_across, jnp.zeros_like(weighted_across)))
            chosen_across.append(jnp.where(mine_across, query_across, jnp.zeros_like(query_across)))
            inner.append(jnp.sum(jnp.where(mine, product, 0.0), -1, keepdims=True) * inverses[:, head : head + 1])

        def probs_grad(head, block):
            return dot(scaled[head][block * BLOCK :], value_ref[0, block * pair : (block + 1) * pair, :], NT)

        def score_grad(head, block, grad_prob):
            start = tile_index(blocks, block, block)
            prob = exps[p % 2, head, start : start + blocks - block].reshape(tokens - block * BLOCK, pair)
            return prob, (prob.astype(F32) * (grad_prob - inner[head][block * BLOCK :])).astype(BF16)

        sums = {}

        def products(head, block, prob, score):
            first = block * BLOCK
            pairs = dot(chosen_across[head][:, first:], score), dot(scaled_across[head][:, first:], prob)
            grad_query = dot(score, key_ref[0, block * pair : (block + 1) * pair, :])
            mine_lanes = slice(head * LANES, (head + 1) * LANES)
            if block == 0:
                total[:, mine_lanes] = grad_query
            else:
                total[first:, mine_lanes] += grad_query
            if head == 0:
                sums[block] = pairs
                return
            at = pl.ds(first, BLOCK)
            for which in range(2):
                both = (sums[block][which] + pairs[which]).T
                zero, one = both[:BLOCK], both[BLOCK:]
                grads[1 + which, at, lanes] = jnp.where(core == 0, zero, one).astype(BF16)
                pending[p % 2, which, at, :] = jnp.where(core == 0, one, zero).astype(BF16)

        exp_copy(2 * p).wait()
        exp_copy(2 * p + 1).wait()

        @pl.when(p < PAIRS - 1)
        def _():
            exp_copy(2 * p + 2).start()
            exp_copy(2 * p + 3).start()

        items = [(head, block) for block in range(blocks) for head in range(2)]
        ahead = probs_grad(*items[0])
        behind = None
        for n, item in enumerate(items):
            now = ahead
            if n + 1 < len(items):
                ahead = probs_grad(*items[n + 1])
            both = score_grad(*item, now)
            if behind is not None:
                products(*behind)
            behind = (*item, *both)
        products(*behind)

        grads[0, :, lanes] = (
            jnp.where(lane < HEAD_DIM, total[:, :LANES], total[:, LANES : 2 * LANES]) * SCALE
        ).astype(BF16)

        @pl.when(p > 0)
        def _():
            take(p - 1)

        kv_copy(p).start()


    @pl.when(busy & (j == FFN_STEPS + PAIRS))
    def _():
        total[...] = jnp.zeros_like(total)
        take(PAIRS - 1)
        have(4)
        fetch(3, of_layer=layer - 1, when=more)

    @pl.when(busy & (j >= FFN_STEPS + PAIRS))
    def _():
        n = j - FFN_STEPS - PAIRS

        @pl.when(n < 3)
        def _():
            triple_grad = dot(normed_ref[...], grads[n], TN).astype(BF16)
            for r in range(ROWS):
                put(4 + n, r, triple_grad[r * SHARE : (r + 1) * SHARE])

        for part in range(3):
            @pl.when(n == part + 1)
            def _():
                have(8 + part)

        @pl.when(n > 0)
        def _():
            total[...] += dot(grads[n - 1], weights[n % 2], NT)

        @pl.when(n == 1)
        def _():
            fetch(10)

        fetch(7, 0, of_layer=layer - 1, when=more & (n == 2))

        @pl.when(n == 3)
        def _():
            have(5, 6)
            def rows(i, sums):
                at = pl.ds(pl.multiple_of(i * TILE, TILE), TILE)
                part = total[at, :]
                scaled = scaled_ref[at, :].astype(F32)
                hidden = grad[at, :] + norm_back(part, scaled, inverse_ref[at, :], pick(first_gain_ref, layer))
                grad[at, :] = hidden
                low[at, :] = hidden.astype(BF16)
                return (
                    sums[0] + jnp.sum(part * scaled, 0, keepdims=True),
                    sums[1] + jnp.sum(part, 0, keepdims=True),
                    sums[2] + jnp.sum(hidden, 0, keepdims=True),
                )

            empty = jnp.zeros((1, width), F32)
            gain_sum, bias_sum, hidden_sum = lax.fori_loop(0, tokens // TILE, rows, (empty, empty, empty))
            small[pl.ds(2 + 4 * layer, 1), :] = gain_sum
            small[pl.ds(3 + 4 * layer, 1), :] = bias_sum

            @pl.when(layer == 0)
            def _():
                small[pl.ds(core, 1), :] = hidden_sum

            fetch(1, 2, of_layer=layer - 1, when=more)


    last = layers * STEPS - 1
    half_width = width // 2

    def slot(v):
        i = v % STEPS
        return jnp.where(
            i < 4, 4 + i % 2, jnp.where(i < 8, i - 4, jnp.where(i == 8, 6, i - FFN_STEPS - PAIRS + 4))
        )

    def whether(v):
        return (v >= 0) & (v <= last) & (v % STEPS != FFN_STEPS + PAIRS - 1) & (v % STEPS != STEPS - 1)

    def order(v):
        i = v % STEPS
        return v // STEPS * PIECES + i - jnp.where(i >= FFN_STEPS + PAIRS, 1, 0)

    def add(a, b):
        return (a.astype(F32) + b.astype(F32)).astype(BF16)

    def core_stage(v):
        h = order(v) % 2
        return send(staged.at[slot(v), 1 - core], got0.at[h], core_send.at[h], core_recv.at[h], mates[0])

    def left_stage(s, v):
        h, d = order(v) % 2, order(v) % 4
        src = (left0.at[h, 1 - x], left1.at[h, 1 - z0], left2.at[h, 1 - z1], left3.at[h])[s - 1]
        dst = (got_left1, got_left2, got_left3, got_left4)[s - 1].at[d]
        return send(src, dst, left_send.at[s - 1, h], left_recv.at[s - 1, d], mates[s])

    def right_stage(s, v):
        h, d = order(v) % 2, order(v) % 4
        src = (right0.at[h, 1 - own_pass], right1.at[h, 1 - z0], right2.at[h, 1 - z1])[s - 1]
        dst = (got_right1, got_right2, got_right3)[s - 1].at[d]
        return send(src, dst, right_send.at[s - 1, h], right_recv.at[s - 1, d], (mates[4], mates[2], mates[3])[s - 1])

    def late_stage(s, v):
        k = order(v)
        src = (right3, right4)[s - 4].at[k % 2]
        return send(src, got_late.at[k], late_send.at[s - 4, k], late_recv.at[s - 4, k], (mates[1], mates[4])[s - 4])

    keeps = x == own_pass

    def late_start(s, v):
        @pl.when(keeps == (s == 5))
        def _():
            late_stage(s, v).start()

    def late_wait(s, v, receive):
        @pl.when(keeps == (s == 5))
        def _():
            late_stage(s, v).wait_send()

        @pl.when(keeps != (s == 5))
        def _():
            late_stage(s, v).wait_recv()
            receive()

    def out_copies(v, act):
        h = order(v) % 4
        i = v % STEPS
        at_layer = layers - 1 - v // STEPS
        triple_out, merge_out, up_out, down_out = outs

        def columns(n):
            return pl.ds(pl.multiple_of(n * width, width), width)

        def go(target):
            getattr(pltpu.make_async_copy(final.at[h], target, out_sem.at[h]), act)()

        @pl.when(i < 4)
        def _():
            go(up_out.at[at_layer, :, columns(i)])

        @pl.when((i >= 4) & (i < 8))
        def _():
            go(down_out.at[at_layer, pl.ds(pl.multiple_of((i - 4) * SHARE, SHARE), SHARE), :])

        @pl.when(i == 8)
        def _():
            go(merge_out.at[at_layer])

        @pl.when(i >= FFN_STEPS + PAIRS)
        def _():
            go(triple_out.at[at_layer, :, columns(i - FFN_STEPS - PAIRS)])


    if hosted:
        @pl.when(whether(t - 12))
        def _():
            out_copies(t - 12, "wait")

        @pl.when(whether(t - 11))
        def _():
            v = t - 11
            h, d = order(v) % 2, order(v) % 4

            def receive():
                right4[h] = got_late[order(v)]

            late_wait(5, v, receive)
            final[d, :, half_width:] = right4[h].astype(F32)
            out_copies(v, "start")

        @pl.when(whether(t - 9))
        def _():
            v = t - 9
            h, d = order(v) % 2, order(v) % 4

            def receive():
                right4[h] = add(right3[h], got_late[order(v)])

            late_wait(4, v, receive)
            late_start(5, v)
            left_stage(4, v).wait()
            final[d, :, :half_width] = left3[h].astype(F32) + got_left4[d].astype(F32)

        @pl.when(whether(t - 7))
        def _():
            v = t - 7
            h, d = order(v) % 2, order(v) % 4
            right_stage(3, v).wait()
            right3[h] = add(right2[h, z1], got_right3[d])
            late_start(4, v)
            left_stage(3, v).wait()
            left3[h] = add(left2[h, z1], got_left3[d])
            left_stage(4, v).start()

        @pl.when(whether(t - 5))
        def _():
            v = t - 5
            h, d = order(v) % 2, order(v) % 4
            right_stage(2, v).wait()
            right2[h] = add(right1[h, z0], got_right2[d])
            right_stage(3, v).start()
            left_stage(2, v).wait()
            left2[h] = add(left1[h, z0], got_left2[d])
            left_stage(3, v).start()

        @pl.when(whether(t - 3))
        def _():
            v = t - 3
            h, d = order(v) % 2, order(v) % 4
            right_stage(1, v).wait()
            right1[h] = add(right0[h, own_pass], got_right1[d])
            right_stage(2, v).start()
            left_stage(1, v).wait()
            left1[h] = add(left0[h, x], got_left1[d])
            left_stage(2, v).start()

        @pl.when(whether(t - 1))
        def _():
            v = t - 1
            h = order(v) % 2
            core_stage(v).wait()
            right0[h] = add(staged[slot(v), core, :, :, :, :, half_width:], got0[h, :, :, :, :, half_width:])
            right_stage(1, v).start()
            left0[h] = add(staged[slot(v), core, :, :, :, :, :half_width], got0[h, :, :, :, :, :half_width])
            left_stage(1, v).start()

        @pl.when(whether(t))
        def _():
            core_stage(t).start()

        for s in range(STAGES + 1):
            def small_copy(s):
                return send(small, small_got.at[s], small_send.at[s], small_recv.at[s], mates[s])

            @pl.when(t == last + s)
            def _():
                if s:
                    small_copy(s - 1).wait()
                    small[...] += small_got[s - 1]
                if s < STAGES:
                    small_copy(s).start()
    else:
        def piece_copy(v):
            return pltpu.make_async_copy(staged.at[slot(v)], outs[0].at[v], out_sem.at[v % 2])

        @pl.when(whether(t - 1))
        def _():
            piece_copy(t - 1).wait()

        @pl.when(whether(t))
        def _():
            piece_copy(t).start()


    def swaps(i, act):
        source, target = ((done_ref, output_ref), (low, input_ref))[i]

        @pl.when(swapped)
        def _():
            getattr(send(source, target, swap_send.at[i], swap_recv.at[i], diagonal), act)()

        @pl.when(jnp.logical_not(swapped))
        def _():
            getattr(pltpu.make_async_copy(source, target, here_sem.at[i]), act)()

    @pl.when(t == 0)
    def _():
        swaps(0, "start")

    @pl.when(t == last)
    def _():
        swaps(1, "start")

    @pl.when(t == pl.num_programs(0) - 1)
    def _():
        swaps(0, "wait")
        swaps(1, "wait")
        small_ref[...] = small[...]


def back(cotangent, done, length, act, slope, normeds, scaleds, inverses, mixed, up, down, merge, first_gain, second_gain, query, kv,
         total, exps, weight, hosted):
    layers, tokens, width = query.shape
    tiles = exps.shape[2]
    steps = layers * STEPS + (2 * STAGES + 1 if hosted else 1)
    piece = (2, 2, 2, 2, SHARE, width)
    part = (2, 2, 2, SHARE, width // 2)
    count = layers * PIECES

    def at(t):
        t = jnp.minimum(t, layers * STEPS - 1)
        return layers - 1 - t // STEPS, t % STEPS

    def tile_of(t):
        layer, j = at(t)
        return layer, jnp.minimum(j, FFN_STEPS - 1)

    def head_of(t):
        layer, j = at(t)
        return layer, jnp.clip(j - FFN_STEPS, 0, PAIRS - 1)

    units = pl.BlockSpec((1, tokens, width), lambda t: (tile_of(t)[0], 0, tile_of(t)[1]))
    in_specs = [
        ANY, ANY, whole(length.shape), units, units,
        ANY, ANY, ANY, ANY,
        pl.BlockSpec((1, width, width), lambda t: (tile_of(t)[0], 0, tile_of(t)[1])),
        pl.BlockSpec((1, width, width), lambda t: (tile_of(t)[0], tile_of(t)[1], 0)),
        ANY,
        whole((layers, width)), whole((layers, width)),
        pl.BlockSpec((1, tokens, LANES), lambda t: (head_of(t)[0], 0, head_of(t)[1])),
        pl.BlockSpec((1, 2 * tokens, LANES), lambda t: (head_of(t)[0], 0, head_of(t)[1])),
        pl.BlockSpec((1, 2 * tokens, LANES), lambda t: (head_of(t)[0], 0, head_of(t)[1] + PAIRS)),
        pl.BlockSpec((1, 1, 8, tokens), lambda t: (head_of(t)[0], head_of(t)[1], 0, 0)),
        ANY, ANY,
    ]
    if hosted:
        shapes = [
            sds((layers, SHARE, 3 * width), F32), sds((layers, SHARE, width), F32),
            sds((layers, SHARE, FFN_STEPS * width), F32), sds((layers, 4 * SHARE, width), F32),
        ]
    else:
        shapes = [sds((layers * STEPS,) + piece, BF16)]
    dma = pltpu.SemaphoreType.DMA

    def some(*shape):
        return pltpu.VMEM(shape, BF16)

    return pl.pallas_call(
        functools.partial(back_kernel, layers, hosted),
        grid=(steps,),
        in_specs=in_specs,
        out_specs=[ANY] * len(shapes) + [whole((SMALL, width)), ANY, ANY],
        out_shape=shapes + [
            sds((SMALL, width), F32), sds((tokens, width), BF16), sds((tokens, width), BF16),
        ],
        scratch_shapes=[
            some(tokens, width), some(tokens, width), pltpu.VMEM((tokens, 1), F32), some(tokens, width),
            some(2, width, width),
            pltpu.VMEM((tokens, width), F32),
            pltpu.VMEM((tokens, width), F32),
            some(3, tokens, width),
            some(2, 2, tokens, LANES),
            some(2, 2, tokens, LANES),
            some(2, 2, tiles, BLOCK, 2 * BLOCK),
            some(7, *piece),
            some(2, *part), some(2, *part[1:]), some(2, *part[2:]), some(2, *part[3:]),
            some(2, *part), some(2, *part[1:]), some(2, *part[2:]), some(2, *part[3:]), some(2, *part[3:]),
            some(2, *piece[1:]),
            some(4, *part[1:]), some(4, *part[2:]), some(4, *part[3:]), some(4, *part[3:]),
            some(4, *part[1:]), some(4, *part[2:]), some(4, *part[3:]), some(count, *part[3:]),
            pltpu.VMEM((4, SHARE, width), F32),
            pltpu.VMEM((SMALL, width), F32),
            pltpu.VMEM((STAGES, SMALL, width), F32),
            dma((6,)), dma((2, 2)), dma, dma((2,)), dma((2,)), dma((2,)), dma((2,)), dma((4, 2)), dma((4, 4)), dma((3, 2)), dma((3, 4)),
            dma((2, count)), dma((2, count)), dma((4,)),
            dma((STAGES,)), dma((STAGES,)), dma((2,)), dma((2,)), dma((2,)),
        ],
        compiler_params=params(1),
        name="back",
    )(cotangent, done, length, act, slope, normeds, scaleds, inverses, mixed, up, down, merge, first_gain, second_gain, query, kv, kv,
      total, exps, weight)


def local(
    stream, lengths, pass_embed, first_gain, first_bias, triple_weight, merge_weight,
    second_gain, second_bias, up_weight, down_weight, cotangent,
):
    row_count = lax.axis_size("rows")
    own_row = lax.axis_index("rows")
    tokens, width = stream.shape[2], stream.shape[3]
    layers = triple_weight.shape[0]
    hosted = row_count == ROWS

    (normeds, scaleds, inverses, query, mixed, total, exps, act, slope, kv, done, cotangent, length) = forward(
        stream.reshape(tokens, width), cotangent.reshape(tokens, width), lengths, pass_embed,
        first_gain, first_bias, second_gain, second_bias, triple_weight, merge_weight, up_weight, down_weight,
    )
    *weight_grads, small, input_grad, output = back(
        cotangent, done, length, act, slope, normeds, scaleds, inverses, mixed, up_weight, down_weight, merge_weight,
        first_gain, second_gain, query, kv.reshape(layers, 2 * tokens, 2 * width), total, exps, triple_weight, hosted,
    )
    input_grad = input_grad.reshape(stream.shape)
    output = output.reshape(stream.shape)
    if hosted:
        triple_grad, merge_grad, up_grad, down_grad = weight_grads
    else:
        pieces = weight_grads[0].transpose(0, 4, 3, 2, 1, 5, 6).reshape(layers, STEPS, -1, width)[::-1]

        def columns(first, last):
            return pieces[:, first:last].transpose(0, 2, 1, 3).reshape(layers, -1, (last - first) * width)

        def reduce(gradient):
            share = lax.psum_scatter(gradient, "rows", scatter_dimension=1, tiled=True)
            return lax.psum(share, "pass").astype(F32)

        down_grad = pieces[:, 4:8].reshape(layers, 4, ROWS, SHARE, width).transpose(0, 2, 1, 3, 4)
        triple_grad, merge_grad, up_grad, down_grad = map(
            reduce, (columns(10, 13), columns(8, 9), columns(0, 4), down_grad.reshape(layers, -1, width))
        )
        small = lax.psum(small, ("pass", "rows"))
    share = width // row_count
    small = lax.dynamic_slice_in_dim(small, own_row * share, share, 1)
    by_layer = small[2 : 2 + 4 * layers].reshape(layers, 4, share)
    return (
        output, input_grad, small[:2], by_layer[:, 0], by_layer[:, 1], triple_grad, merge_grad,
        by_layer[:, 2], by_layer[:, 3], up_grad, down_grad,
    )


def solution(mesh):
    token = P("pass", "rows", None, None)
    matrix = P(None, "rows", None)
    rows = P(None, "rows")
    in_specs = (token, P("rows")) + (P(),) * 9 + (token,)
    out_specs = (token, token, rows, rows, rows, matrix, matrix, rows, rows, matrix, matrix)
    return jax.shard_map(local, mesh=mesh, in_specs=in_specs, out_specs=out_specs, check_vma=False)
```

```python
import functools
import math

import jax
import jax.numpy as jnp
from jax import lax
from jax.experimental import pallas as pl
from jax.experimental.pallas import tpu as pltpu
from jax.sharding import PartitionSpec as P

HEAD_DIM = 64
EPSILON = 1e-05
SCALE = HEAD_DIM**-0.5
MESH = pl.DeviceIdType.MESH
NN = (((1,), (0,)), ((), ()))
NT = (((1,), (1,)), ((), ()))
TN = (((0,), (0,)), ((), ()))
BLOCK = 128
TILE = 256
LANES = 128
BF16 = jnp.bfloat16
F32 = jnp.float32
VMEM_LIMIT = 63 * 2**20 + 3 * 2**18
ANY = pl.BlockSpec(memory_space=pl.ANY)


def dot(left, right, dims=NN):
    return lax.dot_general(left, right, dims, preferred_element_type=F32)


def sds(shape, dtype):
    return jax.ShapeDtypeStruct(shape, dtype)


def params(collective_id=None):
    return pltpu.CompilerParams(
        vmem_limit_bytes=VMEM_LIMIT,
        collective_id=collective_id,
        has_side_effects=collective_id is not None,
    )


def whole(shape):
    zeros = (0,) * len(shape)
    return pl.BlockSpec(shape, lambda *_: zeros, pipeline_mode=pl.Buffered(1))


def pick(ref, which):
    return jnp.where(which == 0, ref[0:1, :], ref[1:2, :]).astype(F32)


def norm(hidden, gain, bias):
    centred = hidden - jnp.mean(hidden, -1, keepdims=True)
    inverse = lax.rsqrt(jnp.mean(centred * centred, -1, keepdims=True) + EPSILON)
    scaled = centred * inverse
    return (scaled * gain + bias).astype(BF16), scaled, inverse


def norm_back(grad, scaled, inverse, gain):
    e = grad * gain
    return inverse * (
        e - jnp.mean(e, -1, keepdims=True) - scaled * jnp.mean(e * scaled, -1, keepdims=True)
    )


def bits():
    row = lax.axis_index("rows")
    x, z0, z1 = (lax.rem(lax.div(row, 2**n), 2) for n in (1, 2, 3))
    return row, lax.rem(row, 2), x, z0, z1, lax.axis_index("pass")


def send(src, dst, send_sem, recv_sem, device):
    return pltpu.make_async_remote_copy(
        src_ref=src, dst_ref=dst, send_sem=send_sem, recv_sem=recv_sem,
        device_id=device, device_id_type=MESH,
    )


QKV_STEPS = 4
PAIRS = 6
FFN_TILES = 4
FORWARD = QKV_STEPS + PAIRS + FFN_TILES


def tile_index(blocks, key_block, query_block):
    return key_block * blocks - key_block * (key_block - 1) // 2 + query_block - key_block


def gelu_both(v):
    root = math.sqrt(2.0 / math.pi)
    cube = (root * 0.044715) * (v * v)
    half = 0.5 + 0.5 * jnp.tanh(v * (root + cube))
    act = v * half
    return act, half + (act - act * half) * (2.0 * root + 6.0 * cube)


def forward_kernel(
    layers,
    stream_ref, cot_ref, length_ref, embed_ref, first_gain_ref, first_bias_ref, second_gain_ref, second_bias_ref,
    triple_ref, merge_ref, up_ref, down_ref,
    normed_ref, scaled_ref, inverse_ref, query_ref, mixed_ref, total_ref, exp_ref, act_ref, slope_ref, kv_ref,
    out_ref, cot_out_ref, length_out_ref,
    hidden, arrived, length_mine, length_here, queries, kv, values, mixes, triple, merge, up, down,
    weight_sem, kv_sem, kv_send, kv_recv, free_sem, swap_send, swap_recv, here_sem,
):
    layer, j = pl.program_id(0), pl.program_id(1)
    t = layer * FORWARD + j
    row, core, _, _, _, own_pass = bits()
    tokens, width = hidden.shape
    blocks = tokens // BLOCK
    pair = 2 * BLOCK
    core_mate = {"rows": row + 1 - 2 * core}
    diagonal = {"pass": 1 - own_pass, "rows": row + 1 - 2 * core}
    swapped = own_pass != core


    def moves(i):
        if i < QKV_STEPS:
            rows = pl.ds(i * TILE, TILE)
            ends = stream_ref.at[rows, :], arrived.at[rows, :]
        else:
            ends = ((cot_ref, cot_out_ref), (length_mine, length_here))[i - QKV_STEPS]
        return (
            send(*ends, swap_send.at[i], swap_recv.at[i], diagonal),
            pltpu.make_async_copy(*ends, here_sem.at[i]),
        )

    def move(i, act):
        there, here = moves(i)

        @pl.when(swapped)
        def _():
            getattr(there, act)()

        @pl.when(jnp.logical_not(swapped))
        def _():
            getattr(here, act)()


    def weight_copies(which, of_layer):
        refs = ((triple_ref, triple), (merge_ref, merge), (up_ref, up), (down_ref, down))
        source, target = refs[which]
        return pltpu.make_async_copy(source.at[of_layer], target, weight_sem.at[which])

    @pl.when(t == 0)
    def _():
        barrier = pltpu.get_barrier_semaphore()
        pl.semaphore_signal(barrier, inc=1, device_id=core_mate, device_id_type=MESH)

        @pl.when(swapped)
        def _():
            pl.semaphore_signal(barrier, inc=1, device_id=diagonal, device_id_type=MESH)

        pl.semaphore_wait(barrier, 1 + jnp.where(swapped, 1, 0))
        length_mine[...] = jnp.full(length_mine.shape, length_ref[0], jnp.int32)
        move(QKV_STEPS + 1, "start")
        for i in range(QKV_STEPS):
            move(i, "start")
        for which in range(4):
            weight_copies(which, 0).start()
        move(QKV_STEPS + 1, "wait")
        length_out_ref[...] = length_here[...]

    for i in range(QKV_STEPS):
        @pl.when(t == i)
        def _():
            move(i, "wait")
            if i == QKV_STEPS - 1:
                move(QKV_STEPS, "start")


    def kv_copy(i):
        part = kv.at[pl.ds(i * (TILE // BLOCK), TILE // BLOCK), core]
        return send(part, part, kv_send.at[i], kv_recv.at[i], core_mate)

    def kv_keep(of_layer):
        return pltpu.make_async_copy(kv, kv_ref.at[of_layer], kv_sem)

    @pl.when(j < QKV_STEPS)
    def _():
        rows = pl.ds(pl.multiple_of(j * TILE, TILE), TILE)

        @pl.when(layer == 0)
        def _():
            hidden[rows, :] = arrived[rows, :].astype(F32) + pick(embed_ref, core)

        @pl.when(j == 0)
        def _():
            weight_copies(0, layer).wait()

        @pl.when((j == 0) & (layer > 0))
        def _():
            pl.semaphore_wait(free_sem, 1)

        normed, scaled, inverse = norm(
            hidden[rows, :], pick(first_gain_ref, layer), pick(first_bias_ref, layer)
        )
        normed_ref[0, 0] = normed
        scaled_ref[0, 0] = scaled.astype(BF16)
        inverse_ref[0, 0] = inverse
        keys = dot(normed, triple[:, width:]).astype(BF16)
        for b in range(TILE // BLOCK):
            kv[j * (TILE // BLOCK) + b, core] = keys[b * BLOCK : (b + 1) * BLOCK]
        kv_copy(j).start()
        query = (dot(normed, triple[:, :width]).astype(BF16).astype(F32) * SCALE).astype(BF16)
        queries[rows, :] = query
        query_ref[0] = query


    @pl.when((j >= QKV_STEPS) & (j < QKV_STEPS + PAIRS))
    def _():
        p = j - QKV_STEPS
        lanes = pl.ds(pl.multiple_of(p * LANES, LANES), LANES)
        value_lanes = pl.ds(pl.multiple_of(width + p * LANES, LANES), LANES)

        @pl.when(p == 0)
        def _():
            for i in range(QKV_STEPS):
                kv_copy(i).wait()
            kv_keep(layer).start()

        @pl.when((p == 0) & (layer < layers - 1))
        def _():
            weight_copies(0, layer + 1).start()

        values[:, :LANES] = kv[:, :, :, value_lanes].reshape(2 * tokens, LANES)
        values[:, LANES:] = jnp.ones((2 * tokens, LANES), BF16)
        lane = lax.broadcasted_iota(jnp.int32, (BLOCK, LANES), 1)
        query_at = lax.broadcasted_iota(jnp.int32, (BLOCK, pair), 0)
        column = lax.broadcasted_iota(jnp.int32, (BLOCK, pair), 1)
        key_pass = column // BLOCK
        key_at = column - key_pass * BLOCK
        causal = (key_at < query_at) | ((key_at == query_at) & (key_pass <= core))
        length = length_here[0:1, 0:1]

        def scores(block, head):
            query = queries[pl.ds(block * BLOCK, BLOCK), lanes]
            chosen = jnp.where(lane // HEAD_DIM == head, query, jnp.zeros_like(query))
            keys = kv[: block + 1, :, :, lanes].reshape((block + 1) * pair, LANES)
            return dot(chosen, keys, NT)

        def exponentials(block, head, raw):
            allowed = causal & (key_at + block * BLOCK < length)
            last = jnp.where(allowed, raw[:, block * pair :], -jnp.inf)
            top = jnp.max(last, -1, keepdims=True)
            if block:
                top = jnp.maximum(top, jnp.max(raw[:, : block * pair], -1, keepdims=True))
            parts = []
            for k in range(block + 1):
                source = last if k == block else raw[:, k * pair : (k + 1) * pair]
                part = jnp.exp(source - top).astype(BF16)
                exp_ref[0, head, tile_index(blocks, k, block)] = part
                parts.append(part)
            return jnp.concatenate(parts, 1) if block else parts[0]

        outs = {}

        def mix(block, head, exps):
            both = dot(exps, values[: (block + 1) * pair, :])
            inverse = jnp.where(block * BLOCK < length, 1.0 / both[:, LANES:], 0.0)
            rows = pl.ds(block * BLOCK, BLOCK)
            total_ref[0, 0, head : head + 1, rows] = inverse.T[:1]
            outs[head] = both[:, :LANES] * inverse
            if head == 1:
                value = jnp.where(lane < HEAD_DIM, outs[0], outs[1]).astype(BF16)
                mixes[rows, lanes] = value
                mixed_ref[0, rows, :] = value

        items = [(block, head) for block in range(blocks) for head in range(2)]
        ahead = scores(*items[0])
        behind = None
        for n, item in enumerate(items):
            raw = ahead
            if n + 1 < len(items):
                ahead = scores(*items[n + 1])
            exps = exponentials(*item, raw)
            if behind is not None:
                mix(*behind)
            behind = (*item, exps)
        mix(*behind)

        @pl.when(p == PAIRS - 1)
        def _():
            kv_keep(layer).wait()

        @pl.when((p == PAIRS - 1) & (layer < layers - 1))
        def _():
            pl.semaphore_signal(free_sem, inc=1, device_id=core_mate, device_id_type=MESH)


    @pl.when(j >= QKV_STEPS + PAIRS)
    def _():
        i = j - QKV_STEPS - PAIRS
        rows = pl.ds(pl.multiple_of(i * TILE, TILE), TILE)

        @pl.when(i == 0)
        def _():
            for which in range(1, 4):
                weight_copies(which, layer).wait()

        mid = hidden[rows, :] + dot(mixes[rows, :], merge[...])
        normed, scaled, inverse = norm(mid, pick(second_gain_ref, layer), pick(second_bias_ref, layer))
        normed_ref[0, 0] = normed
        scaled_ref[0, 0] = scaled.astype(BF16)
        inverse_ref[0, 0] = inverse
        parts = up.shape[1] // width
        sum_next = mid
        ahead = dot(normed, up[:, :width])
        for part in range(parts):
            at = slice(part * width, (part + 1) * width)
            now = ahead
            if part + 1 < parts:
                ahead = dot(normed, up[:, (part + 1) * width : (part + 2) * width])
            act, slope = gelu_both(now)
            act = act.astype(BF16)
            act_ref[0, :, at] = act
            slope_ref[0, :, at] = slope.astype(BF16)
            sum_next = sum_next + dot(act, down[at, :])
        hidden[rows, :] = sum_next

        @pl.when(layer == layers - 1)
        def _():
            position = lax.broadcasted_iota(jnp.int32, (TILE, 1), 0) + i * TILE
            valid = (position < length_here[0:1, 0:1]).astype(F32)
            out_ref[...] = (sum_next * valid).astype(BF16)

        @pl.when((i == FFN_TILES - 1) & (layer < layers - 1))
        def _():
            for which in range(1, 4):
                weight_copies(which, layer + 1).start()

    @pl.when(t == layers * FORWARD - 1)
    def _():
        move(QKV_STEPS, "wait")


def forward(stream, cotangent, length, embed, first_gain, first_bias, second_gain, second_bias, triple, merge, up, down):
    tokens, width = stream.shape
    layers, _, units = up.shape
    blocks = tokens // BLOCK
    tiles = blocks * (blocks + 1) // 2

    def row_tile(layer, j):
        late = j >= QKV_STEPS + PAIRS
        kind = jnp.where(late, 0, 1)
        return layer, kind, jnp.where(late, j - QKV_STEPS - PAIRS, jnp.minimum(j, QKV_STEPS - 1)), 0

    def query_tile(layer, j):
        return layer, jnp.minimum(j, QKV_STEPS - 1), 0

    def head(j):
        return jnp.clip(j - QKV_STEPS, 0, PAIRS - 1)

    def ffn_tile(layer, j):
        return layer, jnp.maximum(j - QKV_STEPS - PAIRS, 0), 0

    vector = whole((layers, width))
    rows = pl.BlockSpec((1, 1, TILE, width), row_tile)
    dma = pltpu.SemaphoreType.DMA
    return pl.pallas_call(
        functools.partial(forward_kernel, layers),
        grid=(layers, FORWARD),
        in_specs=[ANY, ANY, pl.BlockSpec(memory_space=pltpu.SMEM), whole(embed.shape), vector, vector, vector, vector, ANY, ANY, ANY, ANY],
        out_specs=[
            rows, rows, pl.BlockSpec((1, 1, TILE, 1), row_tile),
            pl.BlockSpec((1, TILE, width), query_tile),
            pl.BlockSpec((1, tokens, LANES), lambda layer, j: (layer, 0, head(j))),
            pl.BlockSpec((1, 1, 8, tokens), lambda layer, j: (layer, head(j), 0, 0)),
            pl.BlockSpec((1, 2, tiles, BLOCK, 2 * BLOCK), lambda layer, j: (layer, head(j), 0, 0, 0)),
            pl.BlockSpec((1, TILE, units), ffn_tile), pl.BlockSpec((1, TILE, units), ffn_tile),
            ANY,
            pl.BlockSpec((TILE, width), lambda layer, j: (jnp.where(layer == layers - 1, ffn_tile(layer, j)[1], 0), 0)),
            ANY, whole((8, LANES)),
        ],
        out_shape=[
            sds((layers, 2, tokens, width), BF16),
            sds((layers, 2, tokens, width), BF16),
            sds((layers, 2, tokens, 1), F32),
            sds((layers, tokens, width), BF16),
            sds((layers, tokens, width), BF16),
            sds((layers, PAIRS, 8, tokens), F32),
            sds((layers, 2 * PAIRS, tiles, BLOCK, 2 * BLOCK), BF16),
            sds((layers, tokens, units), BF16),
            sds((layers, tokens, units), BF16),
            sds((layers, blocks, 2, BLOCK, 2 * width), BF16),
            sds((tokens, width), BF16),
            sds((tokens, width), BF16),
            sds((8, LANES), jnp.int32),
        ],
        scratch_shapes=[
            pltpu.VMEM((tokens, width), F32),
            pltpu.VMEM((tokens, width), BF16),
            pltpu.VMEM((8, LANES), jnp.int32),
            pltpu.VMEM((8, LANES), jnp.int32),
            pltpu.VMEM((tokens, width), BF16),
            pltpu.VMEM((blocks, 2, BLOCK, 2 * width), BF16),
            pltpu.VMEM((2 * tokens, 2 * LANES), BF16),
            pltpu.VMEM((tokens, width), BF16),
            pltpu.VMEM(triple.shape[1:], BF16),
            pltpu.VMEM(merge.shape[1:], BF16),
            pltpu.VMEM(up.shape[1:], BF16),
            pltpu.VMEM(down.shape[1:], BF16),
            dma((4,)), dma, dma((QKV_STEPS,)), dma((QKV_STEPS,)), pltpu.SemaphoreType.REGULAR,
            dma((QKV_STEPS + 2,)), dma((QKV_STEPS + 2,)), dma((QKV_STEPS + 2,)),
        ],
        compiler_params=params(0),
        name="forward",
    )(stream, cotangent, length, embed, first_gain, first_bias, second_gain, second_bias, triple, merge, up, down)


FFN_STEPS = 4
STEPS = FFN_STEPS + PAIRS + 4
PIECES = STEPS - 2
STAGES = 5
ROWS = 16
SHARE = 48
SMALL = 16


def left_part(width):
    return 2 * width // 3


def back_kernel(
    layers, hosted,
    cot_ref, done_ref, length_ref, act_ref, slope_ref, normeds_ref, scaleds_ref, inverses_ref, mixes_ref, up_ref, down_ref,
    merges_ref,
    first_gain_ref, second_gain_ref, query_ref, key_ref, value_ref, total_ref, exp_ref, triples_ref,
    *refs,
):
    outs = refs[: 4 if hosted else 1]
    (
        small_ref, input_ref, output_ref,
        normed_ref, scaled_ref, inverse_ref, mixed_ref, weights, grad, total, grads, pending, landing, exps,
        staged, left0, left1, left2, left3, right0, right1, right2, right3, right4, got0,
        got_left1, got_left2, got_left3, got_left4, got_right1, got_right2, got_right3, got_late,
        final, small, small_got,
        load_sem, exp_sem, cot_sem, kv_send, kv_recv, core_send, core_recv, left_send, left_recv, right_send, right_recv,
        late_send, late_recv, out_sem, small_send, small_recv, swap_send, swap_recv, here_sem,
    ) = refs[len(outs) :]
    low = grads.at[1]
    turn, j = pl.program_id(0), pl.program_id(1)
    t = turn * STEPS + j
    layer = jnp.maximum(layers - 1 - turn, 0)
    row, core, x, z0, z1, own_pass = bits()
    tokens, width = grad.shape
    blocks = tokens // BLOCK
    pair = 2 * BLOCK
    busy = turn < layers
    core_mate = {"rows": row + 1 - 2 * core}
    mates = [
        core_mate, {"rows": row + 2 - 4 * x}, {"rows": row + 4 - 8 * z0}, {"rows": row + 8 - 16 * z1},
        {"pass": 1 - own_pass},
    ]
    diagonal = {"pass": 1 - own_pass, "rows": row + 1 - 2 * core}
    swapped = own_pass != core

    @pl.when(t == 0)
    def _():
        barrier = pltpu.get_barrier_semaphore()
        greeted = mates if hosted else mates[:1]
        for mate in greeted:
            pl.semaphore_signal(barrier, inc=1, device_id=mate, device_id_type=MESH)

        @pl.when(swapped)
        def _():
            pl.semaphore_signal(barrier, inc=1, device_id=diagonal, device_id_type=MESH)

        pl.semaphore_wait(barrier, len(greeted) + jnp.where(swapped, 1, 0))
        load = pltpu.make_async_copy(cot_ref, low, cot_sem)
        load.start()
        load.wait()
        position = lax.broadcasted_iota(jnp.int32, (tokens, 1), 0)
        valid = (position < length_ref[0:1, 0:1]).astype(F32)
        masked = low[...].astype(F32) * valid
        grad[...] = masked
        low[...] = masked.astype(BF16)
        small[...] = jnp.zeros_like(small)


    def load(what, of_layer):
        def weight_part(n):
            return triples_ref.at[of_layer, :, n * width : (n + 1) * width]

        source, target, sem = (
            (normeds_ref.at[of_layer, 0], normed_ref, 0), (scaleds_ref.at[of_layer, 0], scaled_ref, 1),
            (inverses_ref.at[of_layer, 0], inverse_ref, 2), (mixes_ref.at[of_layer], mixed_ref, 3),
            (normeds_ref.at[of_layer, 1], normed_ref, 0), (scaleds_ref.at[of_layer, 1], scaled_ref, 1),
            (inverses_ref.at[of_layer, 1], inverse_ref, 2), (merges_ref.at[of_layer], weights.at[0], 4),
            (weight_part(0), weights.at[1], 5), (weight_part(1), weights.at[0], 4), (weight_part(2), weights.at[1], 5),
        )[what]
        return pltpu.make_async_copy(source, target, load_sem.at[sem])

    def fetch(*which, of_layer=layer, when=True):
        @pl.when(when)
        def _():
            for what in which:
                load(what, of_layer).start()

    def have(*which):
        for what in which:
            load(what, layer).wait()

    more = layer > 0
    fetch(0, 1, 2, 3, 7, when=t == 0)


    def exp_copy(head):
        at = lax.rem(lax.div(head, 2), 2), lax.rem(head, 2)
        return pltpu.make_async_copy(exp_ref.at[layer, head], exps.at[at], exp_sem.at[at])

    def put(slot, r, value):
        staged[slot, r % 2, (r // 2) % 2, (r // 4) % 2, (r // 8) % 2] = value

    @pl.when(busy & (j < FFN_STEPS))
    def _():
        @pl.when(j == 0)
        def _():
            total[...] = jnp.zeros_like(total)
            have(0)

        grad_low = low[...]
        down_grad = dot(act_ref[0], grad_low, TN).astype(BF16)
        for q in range(4):
            for i in range(4):
                first = q * 4 * SHARE + i * SHARE
                staged[i, q % 2, q // 2, lax.rem(j, 2), lax.div(j, 2)] = down_grad[first : first + SHARE]
        grad_act = dot(grad_low, down_ref[0], NT)
        grad_pre = (slope_ref[0].astype(F32) * grad_act).astype(BF16)
        up_grad = dot(normed_ref[...], grad_pre, TN).astype(BF16)
        for r in range(ROWS):
            put(4 + lax.rem(j, 2), r, up_grad[r * SHARE : (r + 1) * SHARE])
        total[...] += dot(grad_pre, up_ref[0], NT)

        @pl.when(j == FFN_STEPS - 1)
        def _():
            exp_copy(jnp.int32(0)).start()
            exp_copy(jnp.int32(1)).start()
            have(1, 2, 3, 7)

            def rows(i, sums):
                at = pl.ds(pl.multiple_of(i * TILE, TILE), TILE)
                part = total[at, :]
                scaled = scaled_ref[at, :].astype(F32)
                mid = grad[at, :] + norm_back(part, scaled, inverse_ref[at, :], pick(second_gain_ref, layer))
                grad[at, :] = mid
                low_mid = mid.astype(BF16)
                low[at, :] = low_mid
                grads[0, at, :] = dot(low_mid, weights[0], NT).astype(BF16)
                return (
                    sums[0] + jnp.sum(part * scaled, 0, keepdims=True),
                    sums[1] + jnp.sum(part, 0, keepdims=True),
                )

            empty = jnp.zeros((1, width), F32)
            gain_sum, bias_sum = lax.fori_loop(0, tokens // TILE, rows, (empty, empty))
            small[pl.ds(4 + 4 * layer, 1), :] = gain_sum
            small[pl.ds(5 + 4 * layer, 1), :] = bias_sum
            merge_grad = dot(mixed_ref[...], low[...], TN).astype(BF16)
            for r in range(ROWS):
                put(6, r, merge_grad[r * SHARE : (r + 1) * SHARE])
            fetch(4, 5, 6, 8, 9)


    def kv_copy(p):
        return send(
            pending.at[lax.rem(p, 2)], landing.at[lax.rem(p, 2)], kv_send.at[lax.rem(p, 2)], kv_recv.at[lax.rem(p, 2)], core_mate,
        )

    def take(p):
        kv_copy(p).wait()
        lanes = pl.ds(pl.multiple_of(p * LANES, LANES), LANES)
        for which in range(2):
            grads[1 + which, :, lanes] = (
                grads[1 + which, :, lanes].astype(F32) + landing[lax.rem(p, 2), which].astype(F32)
            ).astype(BF16)

    @pl.when(busy & (j >= FFN_STEPS) & (j < FFN_STEPS + PAIRS))
    def _():
        p = j - FFN_STEPS
        lanes = pl.ds(pl.multiple_of(p * LANES, LANES), LANES)
        lane = lax.broadcasted_iota(jnp.int32, (tokens, LANES), 1)
        out_grad = grads[0, :, lanes].astype(F32)
        product = out_grad * mixed_ref[:, lanes].astype(F32)
        query = query_ref[0]
        inverses = total_ref[0, 0].T
        weighted = out_grad * jnp.where(lane < HEAD_DIM, inverses[:, :1], inverses[:, 1:2])
        weighted_across = weighted.T.astype(BF16)
        weighted = weighted.astype(BF16)
        query_across = query.astype(F32).T.astype(BF16)
        across = lax.broadcasted_iota(jnp.int32, (LANES, tokens), 0)
        scaled, scaled_across, inner, chosen_across = [], [], [], []
        for head in range(2):
            mine = lane // HEAD_DIM == head
            mine_across = across // HEAD_DIM == head
            scaled.append(jnp.where(mine, weighted, jnp.zeros_like(weighted)))
            scaled_across.append(jnp.where(mine_across, weighted_across, jnp.zeros_like(weighted_across)))
            chosen_across.append(jnp.where(mine_across, query_across, jnp.zeros_like(query_across)))
            inner.append(jnp.sum(jnp.where(mine, product, 0.0), -1, keepdims=True) * inverses[:, head : head + 1])

        def probs_grad(head, block):
            return dot(scaled[head][block * BLOCK :], value_ref[0, block * pair : (block + 1) * pair, :], NT)

        def score_grad(head, block, grad_prob):
            start = tile_index(blocks, block, block)
            prob = exps[lax.rem(p, 2), head, start : start + blocks - block].reshape(tokens - block * BLOCK, pair)
            return prob, (prob.astype(F32) * (grad_prob - inner[head][block * BLOCK :])).astype(BF16)

        sums = {}

        def products(head, block, prob, score):
            first = block * BLOCK
            pairs = dot(chosen_across[head][:, first:], score), dot(scaled_across[head][:, first:], prob)
            grad_query = dot(score, key_ref[0, block * pair : (block + 1) * pair, :])
            mine_lanes = slice(head * LANES, (head + 1) * LANES)
            if block == 0:
                total[:, mine_lanes] = grad_query
            else:
                total[first:, mine_lanes] += grad_query
            if head == 0:
                sums[block] = pairs
                return
            at = pl.ds(first, BLOCK)
            for which in range(2):
                both = (sums[block][which] + pairs[which]).T
                zero, one = both[:BLOCK], both[BLOCK:]
                grads[1 + which, at, lanes] = jnp.where(core == 0, zero, one).astype(BF16)
                pending[lax.rem(p, 2), which, at, :] = jnp.where(core == 0, one, zero).astype(BF16)

        exp_copy(2 * p).wait()
        exp_copy(2 * p + 1).wait()

        @pl.when(p < PAIRS - 1)
        def _():
            exp_copy(2 * p + 2).start()
            exp_copy(2 * p + 3).start()

        items = [(head, block) for block in range(blocks) for head in range(2)]
        ahead = probs_grad(*items[0])
        behind = None
        for n, item in enumerate(items):
            now = ahead
            if n + 1 < len(items):
                ahead = probs_grad(*items[n + 1])
            both = score_grad(*item, now)
            if behind is not None:
                products(*behind)
            behind = (*item, *both)
        products(*behind)

        grads[0, :, lanes] = (
            jnp.where(lane < HEAD_DIM, total[:, :LANES], total[:, LANES : 2 * LANES]) * SCALE
        ).astype(BF16)

        @pl.when(p > 0)
        def _():
            take(p - 1)

        kv_copy(p).start()


    @pl.when(busy & (j == FFN_STEPS + PAIRS))
    def _():
        total[...] = jnp.zeros_like(total)
        take(jnp.int32(PAIRS - 1))
        have(4)
        fetch(3, of_layer=layer - 1, when=more)

    @pl.when(busy & (j >= FFN_STEPS + PAIRS))
    def _():
        n = j - FFN_STEPS - PAIRS

        @pl.when(n < 3)
        def _():
            triple_grad = dot(normed_ref[...], grads[n], TN).astype(BF16)
            for r in range(ROWS):
                put(4 + n, r, triple_grad[r * SHARE : (r + 1) * SHARE])

        for part in range(3):
            @pl.when(n == part + 1)
            def _():
                have(8 + part)

        @pl.when(n > 0)
        def _():
            total[...] += dot(grads[n - 1], weights[lax.rem(n, 2)], NT)

        @pl.when(n == 1)
        def _():
            fetch(10)

        fetch(7, 0, of_layer=layer - 1, when=more & (n == 2))

        @pl.when(n == 3)
        def _():
            have(5, 6)
            def rows(i, sums):
                at = pl.ds(pl.multiple_of(i * TILE, TILE), TILE)
                part = total[at, :]
                scaled = scaled_ref[at, :].astype(F32)
                hidden = grad[at, :] + norm_back(part, scaled, inverse_ref[at, :], pick(first_gain_ref, layer))
                grad[at, :] = hidden
                low[at, :] = hidden.astype(BF16)
                return (
                    sums[0] + jnp.sum(part * scaled, 0, keepdims=True),
                    sums[1] + jnp.sum(part, 0, keepdims=True),
                    sums[2] + jnp.sum(hidden, 0, keepdims=True),
                )

            empty = jnp.zeros((1, width), F32)
            gain_sum, bias_sum, hidden_sum = lax.fori_loop(0, tokens // TILE, rows, (empty, empty, empty))
            small[pl.ds(2 + 4 * layer, 1), :] = gain_sum
            small[pl.ds(3 + 4 * layer, 1), :] = bias_sum

            @pl.when(layer == 0)
            def _():
                small[pl.ds(core, 1), :] = hidden_sum

            fetch(1, 2, of_layer=layer - 1, when=more)


    last = layers * STEPS - 1
    split = left_part(width)

    def piece(ago):
        before = j < ago
        return turn - jnp.where(before, 1, 0), j - ago + jnp.where(before, STEPS, 0)

    def slot(v):
        _, i = v
        return jnp.where(
            i < 4, 4 + lax.rem(i, 2), jnp.where(i < 8, i - 4, jnp.where(i == 8, 6, i - FFN_STEPS - PAIRS + 4))
        )

    def whether(ago):
        made, i = piece(ago)
        return (made >= 0) & (made < layers) & (i != FFN_STEPS + PAIRS - 1) & (i != STEPS - 1)

    def order(v):
        made, i = v
        return made * PIECES + i - jnp.where(i >= FFN_STEPS + PAIRS, 1, 0)

    def turns(v, count):
        return lax.rem(order(v), count)

    def add(a, b):
        return a + b

    def core_stage(v):
        h = turns(v, 2)
        return send(staged.at[slot(v), 1 - core], got0.at[h], core_send.at[h], core_recv.at[h], mates[0])

    def left_stage(s, v):
        h, d = turns(v, 2), turns(v, 4)
        src = (left0.at[h, 1 - x], left1.at[h, 1 - z0], left2.at[h, 1 - z1], left3.at[h])[s - 1]
        dst = (got_left1, got_left2, got_left3, got_left4)[s - 1].at[d]
        return send(src, dst, left_send.at[s - 1, h], left_recv.at[s - 1, d], mates[s])

    def right_stage(s, v):
        h, d = turns(v, 2), turns(v, 4)
        src = (right0.at[h, 1 - own_pass], right1.at[h, 1 - z0], right2.at[h, 1 - z1])[s - 1]
        dst = (got_right1, got_right2, got_right3)[s - 1].at[d]
        return send(src, dst, right_send.at[s - 1, h], right_recv.at[s - 1, d], (mates[4], mates[2], mates[3])[s - 1])

    def late_stage(s, v):
        k = order(v)
        src = (right3, right4)[s - 4].at[turns(v, 2)]
        return send(src, got_late.at[k], late_send.at[s - 4, k], late_recv.at[s - 4, k], (mates[1], mates[4])[s - 4])

    keeps = x == own_pass

    def late_start(s, v):
        @pl.when(keeps == (s == 5))
        def _():
            late_stage(s, v).start()

    def late_wait(s, v, receive):
        @pl.when(keeps == (s == 5))
        def _():
            late_stage(s, v).wait_send()

        @pl.when(keeps != (s == 5))
        def _():
            late_stage(s, v).wait_recv()
            receive()

    def out_copies(v, act):
        h = turns(v, 4)
        made, i = v
        at_layer = layers - 1 - made
        triple_out, merge_out, up_out, down_out = outs

        def columns(n):
            return pl.ds(pl.multiple_of(n * width, width), width)

        def go(target):
            getattr(pltpu.make_async_copy(final.at[h], target, out_sem.at[h]), act)()

        @pl.when(i < 4)
        def _():
            go(up_out.at[at_layer, :, columns(i)])

        @pl.when((i >= 4) & (i < 8))
        def _():
            go(down_out.at[at_layer, pl.ds(pl.multiple_of((i - 4) * SHARE, SHARE), SHARE), :])

        @pl.when(i == 8)
        def _():
            go(merge_out.at[at_layer])

        @pl.when(i >= FFN_STEPS + PAIRS)
        def _():
            go(triple_out.at[at_layer, :, columns(i - FFN_STEPS - PAIRS)])


    if hosted:
        @pl.when(whether(12))
        def _():
            out_copies(piece(12), "wait")

        @pl.when(whether(11))
        def _():
            v = piece(11)
            h, d = turns(v, 2), turns(v, 4)

            def receive():
                right4[h] = got_late[order(v)]

            late_wait(5, v, receive)
            final[d, :, split:] = right4[h].astype(F32)
            out_copies(v, "start")

        @pl.when(whether(9))
        def _():
            v = piece(9)
            h, d = turns(v, 2), turns(v, 4)

            def receive():
                right4[h] = add(right3[h], got_late[order(v)])

            late_wait(4, v, receive)
            late_start(5, v)
            left_stage(4, v).wait()
            final[d, :, :split] = left3[h].astype(F32) + got_left4[d].astype(F32)

        @pl.when(whether(7))
        def _():
            v = piece(7)
            h, d = turns(v, 2), turns(v, 4)
            right_stage(3, v).wait()
            right3[h] = add(right2[h, z1], got_right3[d])
            late_start(4, v)
            left_stage(3, v).wait()
            left3[h] = add(left2[h, z1], got_left3[d])
            left_stage(4, v).start()

        @pl.when(whether(5))
        def _():
            v = piece(5)
            h, d = turns(v, 2), turns(v, 4)
            right_stage(2, v).wait()
            right2[h] = add(right1[h, z0], got_right2[d])
            right_stage(3, v).start()
            left_stage(2, v).wait()
            left2[h] = add(left1[h, z0], got_left2[d])
            left_stage(3, v).start()

        @pl.when(whether(3))
        def _():
            v = piece(3)
            h, d = turns(v, 2), turns(v, 4)
            right_stage(1, v).wait()
            right1[h] = add(right0[h, own_pass], got_right1[d])
            right_stage(2, v).start()
            left_stage(1, v).wait()
            left1[h] = add(left0[h, x], got_left1[d])
            left_stage(2, v).start()

        @pl.when(whether(1))
        def _():
            v = piece(1)
            h = turns(v, 2)
            core_stage(v).wait()
            right0[h] = add(staged[slot(v), core, :, :, :, :, split:], got0[h, :, :, :, :, split:])
            right_stage(1, v).start()
            left0[h] = add(staged[slot(v), core, :, :, :, :, :split], got0[h, :, :, :, :, :split])
            left_stage(1, v).start()

        @pl.when(whether(0))
        def _():
            core_stage(piece(0)).start()

        for s in range(STAGES + 1):
            def small_copy(s):
                return send(small, small_got.at[s], small_send.at[s], small_recv.at[s], mates[s])

            @pl.when(t == last + s)
            def _():
                if s:
                    small_copy(s - 1).wait()
                    small[...] += small_got[s - 1]
                if s < STAGES:
                    small_copy(s).start()
    else:
        def piece_copy(v):
            return pltpu.make_async_copy(staged.at[slot(v)], outs[0].at[v[0] * STEPS + v[1]], out_sem.at[turns(v, 2)])

        @pl.when(whether(1))
        def _():
            piece_copy(piece(1)).wait()

        @pl.when(whether(0))
        def _():
            piece_copy(piece(0)).start()


    def swaps(i, act):
        source, target = ((done_ref, output_ref), (low, input_ref))[i]

        @pl.when(swapped)
        def _():
            getattr(send(source, target, swap_send.at[i], swap_recv.at[i], diagonal), act)()

        @pl.when(jnp.logical_not(swapped))
        def _():
            getattr(pltpu.make_async_copy(source, target, here_sem.at[i]), act)()

    @pl.when(t == 0)
    def _():
        swaps(0, "start")

    @pl.when(t == last)
    def _():
        swaps(1, "start")

    @pl.when(t == (layers + 1) * STEPS - 1)
    def _():
        swaps(0, "wait")
        swaps(1, "wait")
        small_ref[...] = small[...]


def back(cotangent, done, length, act, slope, normeds, scaleds, inverses, mixed, up, down, merge, first_gain, second_gain, query, kv,
         total, exps, weight, hosted):
    layers, tokens, width = query.shape
    tiles = exps.shape[2]
    piece = (2, 2, 2, 2, SHARE, width)
    left = (2, 2, 2, SHARE, left_part(width))
    right = (2, 2, 2, SHARE, width - left_part(width))
    count = layers * PIECES

    def at(turn, j):
        return jnp.maximum(layers - 1 - turn, 0), jnp.where(turn < layers, j, STEPS - 1)

    def tile(*step):
        layer, j = at(*step)
        return layer, jnp.minimum(j, FFN_STEPS - 1)

    def pair(*step):
        layer, j = at(*step)
        return layer, jnp.clip(j - FFN_STEPS, 0, PAIRS - 1)

    def spec(shape, place):
        return pl.BlockSpec(shape, lambda turn, j: place(turn, j))

    def across(*step):
        layer, n = tile(*step)
        return layer, 0, n

    def down_rows(*step):
        layer, n = tile(*step)
        return layer, n, 0

    def lanes(*step):
        layer, n = pair(*step)
        return layer, 0, n

    def value_lanes(*step):
        layer, n = pair(*step)
        return layer, 0, n + PAIRS

    def totals(*step):
        return (*pair(*step), 0, 0)

    units = spec((1, tokens, width), across)
    in_specs = [
        ANY, ANY, whole(length.shape), units, units,
        ANY, ANY, ANY, ANY,
        spec((1, width, width), across), spec((1, width, width), down_rows),
        ANY,
        whole((layers, width)), whole((layers, width)),
        spec((1, tokens, LANES), lanes), spec((1, 2 * tokens, LANES), lanes), spec((1, 2 * tokens, LANES), value_lanes),
        spec((1, 1, 8, tokens), totals),
        ANY, ANY,
    ]
    if hosted:
        shapes = [
            sds((layers, SHARE, 3 * width), F32), sds((layers, SHARE, width), F32),
            sds((layers, SHARE, FFN_STEPS * width), F32), sds((layers, 4 * SHARE, width), F32),
        ]
    else:
        shapes = [sds((layers * STEPS,) + piece, BF16)]
    dma = pltpu.SemaphoreType.DMA

    def some(*shape):
        return pltpu.VMEM(shape, BF16)

    return pl.pallas_call(
        functools.partial(back_kernel, layers, hosted),
        grid=(layers + 1, STEPS),
        in_specs=in_specs,
        out_specs=[ANY] * len(shapes) + [whole((SMALL, width)), ANY, ANY],
        out_shape=shapes + [
            sds((SMALL, width), F32), sds((tokens, width), BF16), sds((tokens, width), BF16),
        ],
        scratch_shapes=[
            some(tokens, width), some(tokens, width), pltpu.VMEM((tokens, 1), F32), some(tokens, width),
            some(2, width, width),
            pltpu.VMEM((tokens, width), F32),
            pltpu.VMEM((tokens, width), F32),
            some(3, tokens, width),
            some(2, 2, tokens, LANES),
            some(2, 2, tokens, LANES),
            some(2, 2, tiles, BLOCK, 2 * BLOCK),
            some(7, *piece),
            some(2, *left), some(2, *left[1:]), some(2, *left[2:]), some(2, *left[3:]),
            some(2, *right), some(2, *right[1:]), some(2, *right[2:]), some(2, *right[3:]), some(2, *right[3:]),
            some(2, *piece[1:]),
            some(4, *left[1:]), some(4, *left[2:]), some(4, *left[3:]), some(4, *left[3:]),
            some(4, *right[1:]), some(4, *right[2:]), some(4, *right[3:]), some(count, *right[3:]),
            pltpu.VMEM((4, SHARE, width), F32),
            pltpu.VMEM((SMALL, width), F32),
            pltpu.VMEM((STAGES, SMALL, width), F32),
            dma((6,)), dma((2, 2)), dma, dma((2,)), dma((2,)), dma((2,)), dma((2,)), dma((4, 2)), dma((4, 4)), dma((3, 2)), dma((3, 4)),
            dma((2, count)), dma((2, count)), dma((4,)),
            dma((STAGES,)), dma((STAGES,)), dma((2,)), dma((2,)), dma((2,)),
        ],
        compiler_params=params(1),
        name="back",
    )(cotangent, done, length, act, slope, normeds, scaleds, inverses, mixed, up, down, merge, first_gain, second_gain, query, kv, kv,
      total, exps, weight)


def local(
    stream, lengths, pass_embed, first_gain, first_bias, triple_weight, merge_weight,
    second_gain, second_bias, up_weight, down_weight, cotangent,
):
    row_count = lax.axis_size("rows")
    own_row = lax.axis_index("rows")
    tokens, width = stream.shape[2], stream.shape[3]
    layers = triple_weight.shape[0]
    hosted = row_count == ROWS

    (normeds, scaleds, inverses, query, mixed, total, exps, act, slope, kv, done, cotangent, length) = forward(
        stream.reshape(tokens, width), cotangent.reshape(tokens, width), lengths, pass_embed,
        first_gain, first_bias, second_gain, second_bias, triple_weight, merge_weight, up_weight, down_weight,
    )
    *weight_grads, small, input_grad, output = back(
        cotangent, done, length, act, slope, normeds, scaleds, inverses, mixed, up_weight, down_weight, merge_weight,
        first_gain, second_gain, query, kv.reshape(layers, 2 * tokens, 2 * width), total, exps, triple_weight, hosted,
    )
    input_grad = input_grad.reshape(stream.shape)
    output = output.reshape(stream.shape)
    if hosted:
        triple_grad, merge_grad, up_grad, down_grad = weight_grads
    else:
        pieces = weight_grads[0].transpose(0, 4, 3, 2, 1, 5, 6).reshape(layers, STEPS, -1, width)[::-1]

        def columns(first, last):
            return pieces[:, first:last].transpose(0, 2, 1, 3).reshape(layers, -1, (last - first) * width)

        def reduce(gradient):
            share = lax.psum_scatter(gradient, "rows", scatter_dimension=1, tiled=True)
            return lax.psum(share, "pass").astype(F32)

        down_grad = pieces[:, 4:8].reshape(layers, 4, ROWS, SHARE, width).transpose(0, 2, 1, 3, 4)
        triple_grad, merge_grad, up_grad, down_grad = map(
            reduce, (columns(10, 13), columns(8, 9), columns(0, 4), down_grad.reshape(layers, -1, width))
        )
        small = lax.psum(small, ("pass", "rows"))
    share = width // row_count
    small = lax.dynamic_slice_in_dim(small, own_row * share, share, 1)
    by_layer = small[2 : 2 + 4 * layers].reshape(layers, 4, share)
    return (
        output, input_grad, small[:2], by_layer[:, 0], by_layer[:, 1], triple_grad, merge_grad,
        by_layer[:, 2], by_layer[:, 3], up_grad, down_grad,
    )


def solution(mesh):
    token = P("pass", "rows", None, None)
    matrix = P(None, "rows", None)
    rows = P(None, "rows")
    in_specs = (token, P("rows")) + (P(),) * 9 + (token,)
    out_specs = (token, token, rows, rows, rows, matrix, matrix, rows, rows, matrix, matrix)
    return jax.shard_map(local, mesh=mesh, in_specs=in_specs, out_specs=out_specs, check_vma=False)
```

```python
import functools
import math

import jax
import jax.numpy as jnp
from jax import lax
from jax.experimental import pallas as pl
from jax.experimental.pallas import tpu as pltpu
from jax.sharding import PartitionSpec as P

HEAD_DIM = 64
EPSILON = 1e-05
SCALE = HEAD_DIM**-0.5
MESH = pl.DeviceIdType.MESH
NN = (((1,), (0,)), ((), ()))
NT = (((1,), (1,)), ((), ()))
TN = (((0,), (0,)), ((), ()))
BLOCK = 128
TILE = 256
LANES = 128
BF16 = jnp.bfloat16
F32 = jnp.float32
VMEM_LIMIT = 63 * 2**20 + 3 * 2**18
ANY = pl.BlockSpec(memory_space=pl.ANY)


def dot(left, right, dims=NN):
    return lax.dot_general(left, right, dims, preferred_element_type=F32)


def sds(shape, dtype):
    return jax.ShapeDtypeStruct(shape, dtype)


def params(collective_id=None):
    return pltpu.CompilerParams(
        vmem_limit_bytes=VMEM_LIMIT,
        collective_id=collective_id,
        has_side_effects=collective_id is not None,
    )


def whole(shape):
    zeros = (0,) * len(shape)
    return pl.BlockSpec(shape, lambda *_: zeros, pipeline_mode=pl.Buffered(1))


def pick(ref, which):
    return jnp.where(which == 0, ref[0:1, :], ref[1:2, :]).astype(F32)


def norm(hidden, gain, bias):
    centred = hidden - jnp.mean(hidden, -1, keepdims=True)
    inverse = lax.rsqrt(jnp.mean(centred * centred, -1, keepdims=True) + EPSILON)
    scaled = centred * inverse
    return (scaled * gain + bias).astype(BF16), scaled, inverse


def norm_back(grad, scaled, inverse, gain):
    e = grad * gain
    return inverse * (
        e - jnp.mean(e, -1, keepdims=True) - scaled * jnp.mean(e * scaled, -1, keepdims=True)
    )


def bits():
    row = lax.axis_index("rows")
    x, z0, z1 = (lax.rem(lax.div(row, 2**n), 2) for n in (1, 2, 3))
    return row, lax.rem(row, 2), x, z0, z1, lax.axis_index("pass")


def send(src, dst, send_sem, recv_sem, device):
    return pltpu.make_async_remote_copy(
        src_ref=src, dst_ref=dst, send_sem=send_sem, recv_sem=recv_sem,
        device_id=device, device_id_type=MESH,
    )


QKV_STEPS = 4
PAIRS = 6
FFN_TILES = 4
FORWARD = QKV_STEPS + PAIRS + FFN_TILES


def tile_index(blocks, key_block, query_block):
    return key_block * blocks - key_block * (key_block - 1) // 2 + query_block - key_block


def gelu_both(v):
    root = math.sqrt(2.0 / math.pi)
    cube = (root * 0.044715) * (v * v)
    half = 0.5 + 0.5 * jnp.tanh(v * (root + cube))
    act = v * half
    return act, half + (act - act * half) * (2.0 * root + 6.0 * cube)


def forward_kernel(
    layers,
    stream_ref, cot_ref, length_ref, embed_ref, first_gain_ref, first_bias_ref, second_gain_ref, second_bias_ref,
    triple_ref, merge_ref, up_ref, down_ref,
    normed_ref, scaled_ref, inverse_ref, query_ref, mixed_ref, total_ref, exp_ref, act_ref, slope_ref, kv_ref,
    out_ref, cot_out_ref, length_out_ref,
    hidden, arrived, length_mine, length_here, queries, kv, values, mixes, triple, merge, up, down,
    weight_sem, kv_sem, kv_send, kv_recv, free_sem, swap_send, swap_recv, here_sem,
):
    layer, j = pl.program_id(0), pl.program_id(1)
    t = layer * FORWARD + j
    row, core, _, _, _, own_pass = bits()
    tokens, width = hidden.shape
    blocks = tokens // BLOCK
    pair = 2 * BLOCK
    core_mate = {"rows": row + 1 - 2 * core}
    diagonal = {"pass": 1 - own_pass, "rows": row + 1 - 2 * core}
    swapped = own_pass != core


    def moves(i):
        if i < QKV_STEPS:
            rows = pl.ds(i * TILE, TILE)
            ends = stream_ref.at[rows, :], arrived.at[rows, :]
        else:
            ends = ((cot_ref, cot_out_ref), (length_mine, length_here))[i - QKV_STEPS]
        return (
            send(*ends, swap_send.at[i], swap_recv.at[i], diagonal),
            pltpu.make_async_copy(*ends, here_sem.at[i]),
        )

    def move(i, act):
        there, here = moves(i)

        @pl.when(swapped)
        def _():
            getattr(there, act)()

        @pl.when(jnp.logical_not(swapped))
        def _():
            getattr(here, act)()


    def weight_copies(which, of_layer):
        refs = ((triple_ref, triple), (merge_ref, merge), (up_ref, up), (down_ref, down))
        source, target = refs[which]
        return pltpu.make_async_copy(source.at[of_layer], target, weight_sem.at[which])

    @pl.when(t == 0)
    def _():
        barrier = pltpu.get_barrier_semaphore()
        pl.semaphore_signal(barrier, inc=1, device_id=core_mate, device_id_type=MESH)

        @pl.when(swapped)
        def _():
            pl.semaphore_signal(barrier, inc=1, device_id=diagonal, device_id_type=MESH)

        pl.semaphore_wait(barrier, 1 + jnp.where(swapped, 1, 0))
        length_mine[...] = jnp.full(length_mine.shape, length_ref[0], jnp.int32)
        move(QKV_STEPS + 1, "start")
        for i in range(QKV_STEPS):
            move(i, "start")
        for which in range(4):
            weight_copies(which, 0).start()
        move(QKV_STEPS + 1, "wait")
        length_out_ref[...] = length_here[...]

    for i in range(QKV_STEPS):
        @pl.when(t == i)
        def _():
            move(i, "wait")
            if i == QKV_STEPS - 1:
                move(QKV_STEPS, "start")


    def kv_copy(i):
        part = kv.at[pl.ds(i * (TILE // BLOCK), TILE // BLOCK), core]
        return send(part, part, kv_send.at[i], kv_recv.at[i], core_mate)

    def kv_keep(of_layer):
        return pltpu.make_async_copy(kv, kv_ref.at[of_layer], kv_sem)

    @pl.when(j < QKV_STEPS)
    def _():
        rows = pl.ds(pl.multiple_of(j * TILE, TILE), TILE)

        @pl.when(layer == 0)
        def _():
            hidden[rows, :] = arrived[rows, :].astype(F32) + pick(embed_ref, core)

        @pl.when(j == 0)
        def _():
            weight_copies(0, layer).wait()

        @pl.when((j == 0) & (layer > 0))
        def _():
            pl.semaphore_wait(free_sem, 1)

        normed, scaled, inverse = norm(
            hidden[rows, :], pick(first_gain_ref, layer), pick(first_bias_ref, layer)
        )
        normed_ref[0, 0] = normed
        scaled_ref[0, 0] = scaled.astype(BF16)
        inverse_ref[0, 0] = inverse
        keys = dot(normed, triple[:, width:]).astype(BF16)
        for b in range(TILE // BLOCK):
            kv[j * (TILE // BLOCK) + b, core] = keys[b * BLOCK : (b + 1) * BLOCK]
        kv_copy(j).start()
        query = (dot(normed, triple[:, :width]).astype(BF16).astype(F32) * SCALE).astype(BF16)
        queries[rows, :] = query
        query_ref[0] = query


    @pl.when((j >= QKV_STEPS) & (j < QKV_STEPS + PAIRS))
    def _():
        p = j - QKV_STEPS
        lanes = pl.ds(pl.multiple_of(p * LANES, LANES), LANES)
        value_lanes = pl.ds(pl.multiple_of(width + p * LANES, LANES), LANES)

        @pl.when(p == 0)
        def _():
            for i in range(QKV_STEPS):
                kv_copy(i).wait()
            kv_keep(layer).start()

        @pl.when((p == 0) & (layer < layers - 1))
        def _():
            weight_copies(0, layer + 1).start()

        values[:, :LANES] = kv[:, :, :, value_lanes].reshape(2 * tokens, LANES)
        values[:, LANES:] = jnp.ones((2 * tokens, LANES), BF16)
        lane = lax.broadcasted_iota(jnp.int32, (BLOCK, LANES), 1)
        query_at = lax.broadcasted_iota(jnp.int32, (BLOCK, pair), 0)
        column = lax.broadcasted_iota(jnp.int32, (BLOCK, pair), 1)
        key_pass = column // BLOCK
        key_at = column - key_pass * BLOCK
        causal = (key_at < query_at) | ((key_at == query_at) & (key_pass <= core))
        length = length_here[0:1, 0:1]

        def scores(block, head):
            query = queries[pl.ds(block * BLOCK, BLOCK), lanes]
            chosen = jnp.where(lane // HEAD_DIM == head, query, jnp.zeros_like(query))
            keys = kv[: block + 1, :, :, lanes].reshape((block + 1) * pair, LANES)
            return dot(chosen, keys, NT)

        def exponentials(block, head, raw):
            allowed = causal & (key_at + block * BLOCK < length)
            last = jnp.where(allowed, raw[:, block * pair :], -jnp.inf)
            top = jnp.max(last, -1, keepdims=True)
            if block:
                top = jnp.maximum(top, jnp.max(raw[:, : block * pair], -1, keepdims=True))
            parts = []
            for k in range(block + 1):
                source = last if k == block else raw[:, k * pair : (k + 1) * pair]
                part = jnp.exp(source - top).astype(BF16)
                exp_ref[0, head, tile_index(blocks, k, block)] = part
                parts.append(part)
            return jnp.concatenate(parts, 1) if block else parts[0]

        outs = {}

        def mix(block, head, exps):
            both = dot(exps, values[: (block + 1) * pair, :])
            inverse = jnp.where(block * BLOCK < length, 1.0 / both[:, LANES:], 0.0)
            rows = pl.ds(block * BLOCK, BLOCK)
            total_ref[0, 0, head : head + 1, rows] = inverse.T[:1]
            outs[head] = both[:, :LANES] * inverse
            if head == 1:
                value = jnp.where(lane < HEAD_DIM, outs[0], outs[1]).astype(BF16)
                mixes[rows, lanes] = value
                mixed_ref[0, rows, :] = value

        items = [(block, head) for block in range(blocks) for head in range(2)]
        ahead = scores(*items[0])
        behind = None
        for n, item in enumerate(items):
            raw = ahead
            if n + 1 < len(items):
                ahead = scores(*items[n + 1])
            exps = exponentials(*item, raw)
            if behind is not None:
                mix(*behind)
            behind = (*item, exps)
        mix(*behind)

        @pl.when(p == PAIRS - 1)
        def _():
            kv_keep(layer).wait()

        @pl.when((p == PAIRS - 1) & (layer < layers - 1))
        def _():
            pl.semaphore_signal(free_sem, inc=1, device_id=core_mate, device_id_type=MESH)


    @pl.when(j >= QKV_STEPS + PAIRS)
    def _():
        i = j - QKV_STEPS - PAIRS
        rows = pl.ds(pl.multiple_of(i * TILE, TILE), TILE)

        @pl.when(i == 0)
        def _():
            for which in range(1, 4):
                weight_copies(which, layer).wait()

        mid = hidden[rows, :] + dot(mixes[rows, :], merge[...])
        normed, scaled, inverse = norm(mid, pick(second_gain_ref, layer), pick(second_bias_ref, layer))
        normed_ref[0, 0] = normed
        scaled_ref[0, 0] = scaled.astype(BF16)
        inverse_ref[0, 0] = inverse
        parts = up.shape[1] // width
        sum_next = mid
        ahead = dot(normed, up[:, :width])
        for part in range(parts):
            at = slice(part * width, (part + 1) * width)
            now = ahead
            if part + 1 < parts:
                ahead = dot(normed, up[:, (part + 1) * width : (part + 2) * width])
            act, slope = gelu_both(now)
            act = act.astype(BF16)
            act_ref[0, :, at] = act
            slope_ref[0, :, at] = slope.astype(BF16)
            sum_next = sum_next + dot(act, down[at, :])
        hidden[rows, :] = sum_next

        @pl.when(layer == layers - 1)
        def _():
            position = lax.broadcasted_iota(jnp.int32, (TILE, 1), 0) + i * TILE
            valid = (position < length_here[0:1, 0:1]).astype(F32)
            out_ref[...] = (sum_next * valid).astype(BF16)

        @pl.when((i == FFN_TILES - 1) & (layer < layers - 1))
        def _():
            for which in range(1, 4):
                weight_copies(which, layer + 1).start()

    @pl.when(t == layers * FORWARD - 1)
    def _():
        move(QKV_STEPS, "wait")


def forward(stream, cotangent, length, embed, first_gain, first_bias, second_gain, second_bias, triple, merge, up, down):
    tokens, width = stream.shape
    layers, _, units = up.shape
    blocks = tokens // BLOCK
    tiles = blocks * (blocks + 1) // 2

    def row_tile(layer, j):
        late = j >= QKV_STEPS + PAIRS
        kind = jnp.where(late, 0, 1)
        return layer, kind, jnp.where(late, j - QKV_STEPS - PAIRS, jnp.minimum(j, QKV_STEPS - 1)), 0

    def query_tile(layer, j):
        return layer, jnp.minimum(j, QKV_STEPS - 1), 0

    def head(j):
        return jnp.clip(j - QKV_STEPS, 0, PAIRS - 1)

    def ffn_tile(layer, j):
        return layer, jnp.maximum(j - QKV_STEPS - PAIRS, 0), 0

    vector = whole((layers, width))
    rows = pl.BlockSpec((1, 1, TILE, width), row_tile)
    dma = pltpu.SemaphoreType.DMA
    return pl.pallas_call(
        functools.partial(forward_kernel, layers),
        grid=(layers, FORWARD),
        in_specs=[ANY, ANY, pl.BlockSpec(memory_space=pltpu.SMEM), whole(embed.shape), vector, vector, vector, vector, ANY, ANY, ANY, ANY],
        out_specs=[
            rows, rows, pl.BlockSpec((1, 1, TILE, 1), row_tile),
            pl.BlockSpec((1, TILE, width), query_tile),
            pl.BlockSpec((1, tokens, LANES), lambda layer, j: (layer, 0, head(j))),
            pl.BlockSpec((1, 1, 8, tokens), lambda layer, j: (layer, head(j), 0, 0)),
            pl.BlockSpec((1, 2, tiles, BLOCK, 2 * BLOCK), lambda layer, j: (layer, head(j), 0, 0, 0)),
            pl.BlockSpec((1, TILE, units), ffn_tile), pl.BlockSpec((1, TILE, units), ffn_tile),
            ANY,
            pl.BlockSpec((TILE, width), lambda layer, j: (jnp.where(layer == layers - 1, ffn_tile(layer, j)[1], 0), 0)),
            ANY, whole((8, LANES)),
        ],
        out_shape=[
            sds((layers, 2, tokens, width), BF16),
            sds((layers, 2, tokens, width), BF16),
            sds((layers, 2, tokens, 1), F32),
            sds((layers, tokens, width), BF16),
            sds((layers, tokens, width), BF16),
            sds((layers, PAIRS, 8, tokens), F32),
            sds((layers, 2 * PAIRS, tiles, BLOCK, 2 * BLOCK), BF16),
            sds((layers, tokens, units), BF16),
            sds((layers, tokens, units), BF16),
            sds((layers, blocks, 2, BLOCK, 2 * width), BF16),
            sds((tokens, width), BF16),
            sds((tokens, width), BF16),
            sds((8, LANES), jnp.int32),
        ],
        scratch_shapes=[
            pltpu.VMEM((tokens, width), F32),
            pltpu.VMEM((tokens, width), BF16),
            pltpu.VMEM((8, LANES), jnp.int32),
            pltpu.VMEM((8, LANES), jnp.int32),
            pltpu.VMEM((tokens, width), BF16),
            pltpu.VMEM((blocks, 2, BLOCK, 2 * width), BF16),
            pltpu.VMEM((2 * tokens, 2 * LANES), BF16),
            pltpu.VMEM((tokens, width), BF16),
            pltpu.VMEM(triple.shape[1:], BF16),
            pltpu.VMEM(merge.shape[1:], BF16),
            pltpu.VMEM(up.shape[1:], BF16),
            pltpu.VMEM(down.shape[1:], BF16),
            dma((4,)), dma, dma((QKV_STEPS,)), dma((QKV_STEPS,)), pltpu.SemaphoreType.REGULAR,
            dma((QKV_STEPS + 2,)), dma((QKV_STEPS + 2,)), dma((QKV_STEPS + 2,)),
        ],
        compiler_params=params(0),
        name="forward",
    )(stream, cotangent, length, embed, first_gain, first_bias, second_gain, second_bias, triple, merge, up, down)


FFN_STEPS = 4
STEPS = FFN_STEPS + PAIRS + 4
PIECES = STEPS - 2
STAGES = 5
ROWS = 16
SHARE = 48
SMALL = 16


def left_part(width):
    return 2 * width // 3


def back_kernel(
    layers, hosted,
    cot_ref, done_ref, length_ref, act_ref, slope_ref, normeds_ref, scaleds_ref, inverses_ref, mixes_ref, up_ref, down_ref,
    merges_ref,
    first_gain_ref, second_gain_ref, query_ref, key_ref, value_ref, total_ref, exp_ref, triples_ref,
    *refs,
):
    outs = refs[: 4 if hosted else 1]
    (
        small_ref, input_ref, output_ref,
        normed_ref, scaled_ref, inverse_ref, mixed_ref, weights, grad, total, grads, pending, landing, exps,
        staged, left0, left1, left2, left3, right0, right1, right2, right3, right4, got0,
        got_left1, got_left2, got_left3, got_left4, got_right1, got_right2, got_right3, got_late,
        final, small, small_got,
        load_sem, exp_sem, cot_sem, kv_send, kv_recv, core_send, core_recv, left_send, left_recv, right_send, right_recv,
        late_send, late_recv, out_sem, small_send, small_recv, swap_send, swap_recv, here_sem,
    ) = refs[len(outs) :]
    low = grads.at[0]
    turn, j = pl.program_id(0), pl.program_id(1)
    t = turn * STEPS + j
    layer = jnp.maximum(layers - 1 - turn, 0)
    row, core, x, z0, z1, own_pass = bits()
    tokens, width = grad.shape
    blocks = tokens // BLOCK
    pair = 2 * BLOCK
    busy = turn < layers
    core_mate = {"rows": row + 1 - 2 * core}
    mates = [
        core_mate, {"rows": row + 2 - 4 * x}, {"rows": row + 4 - 8 * z0}, {"rows": row + 8 - 16 * z1},
        {"pass": 1 - own_pass},
    ]
    diagonal = {"pass": 1 - own_pass, "rows": row + 1 - 2 * core}
    swapped = own_pass != core

    @pl.when(t == 0)
    def _():
        barrier = pltpu.get_barrier_semaphore()
        greeted = mates if hosted else mates[:1]
        for mate in greeted:
            pl.semaphore_signal(barrier, inc=1, device_id=mate, device_id_type=MESH)

        @pl.when(swapped)
        def _():
            pl.semaphore_signal(barrier, inc=1, device_id=diagonal, device_id_type=MESH)

        pl.semaphore_wait(barrier, len(greeted) + jnp.where(swapped, 1, 0))
        load = pltpu.make_async_copy(cot_ref, low, cot_sem)
        load.start()
        load.wait()
        position = lax.broadcasted_iota(jnp.int32, (tokens, 1), 0)
        valid = (position < length_ref[0:1, 0:1]).astype(F32)
        masked = low[...].astype(F32) * valid
        grad[...] = masked
        low[...] = masked.astype(BF16)
        small[...] = jnp.zeros_like(small)


    def swaps(i, act):
        if isinstance(i, int):
            source, target = done_ref, output_ref
        else:
            rows = pl.ds(pl.multiple_of((i - 1) * TILE, TILE), TILE)
            source, target = low.at[rows, :], input_ref.at[rows, :]

        @pl.when(swapped)
        def _():
            getattr(send(source, target, swap_send.at[i], swap_recv.at[i], diagonal), act)()

        @pl.when(jnp.logical_not(swapped))
        def _():
            getattr(pltpu.make_async_copy(source, target, here_sem.at[i]), act)()


    def load(what, of_layer):
        def weight_part(n):
            return triples_ref.at[of_layer, :, n * width : (n + 1) * width]

        source, target, sem = (
            (normeds_ref.at[of_layer, 0], normed_ref, 0), (scaleds_ref.at[of_layer, 0], scaled_ref, 1),
            (inverses_ref.at[of_layer, 0], inverse_ref, 2), (mixes_ref.at[of_layer], mixed_ref, 3),
            (normeds_ref.at[of_layer, 1], normed_ref, 0), (scaleds_ref.at[of_layer, 1], scaled_ref, 1),
            (inverses_ref.at[of_layer, 1], inverse_ref, 2), (merges_ref.at[of_layer], weights.at[0], 4),
            (weight_part(0), weights.at[1], 5), (weight_part(1), weights.at[0], 4), (weight_part(2), weights.at[1], 5),
        )[what]
        return pltpu.make_async_copy(source, target, load_sem.at[sem])

    def fetch(*which, of_layer=layer, when=True):
        @pl.when(when)
        def _():
            for what in which:
                load(what, of_layer).start()

    def have(*which):
        for what in which:
            load(what, layer).wait()

    more = layer > 0
    fetch(0, 1, 2, 3, 7, when=t == 0)


    def exp_copy(head):
        at = lax.rem(lax.div(head, 2), 2), lax.rem(head, 2)
        return pltpu.make_async_copy(exp_ref.at[layer, head], exps.at[at], exp_sem.at[at])

    def put(slot, r, value):
        staged[slot, r % 2, (r // 2) % 2, (r // 4) % 2, (r // 8) % 2] = value

    @pl.when(busy & (j < FFN_STEPS))
    def _():
        @pl.when(j == 0)
        def _():
            total[...] = jnp.zeros_like(total)

        grad_low = low[...]
        down_grad = dot(act_ref[0], grad_low, TN).astype(BF16)
        for q in range(4):
            for i in range(4):
                first = q * 4 * SHARE + i * SHARE
                staged[i, q % 2, q // 2, lax.rem(j, 2), lax.div(j, 2)] = down_grad[first : first + SHARE]
        grad_act = dot(grad_low, down_ref[0], NT)
        grad_pre = (slope_ref[0].astype(F32) * grad_act).astype(BF16)

        @pl.when(j == 0)
        def _():
            have(0)

        up_grad = dot(normed_ref[...], grad_pre, TN).astype(BF16)
        for r in range(ROWS):
            put(4 + lax.rem(j, 2), r, up_grad[r * SHARE : (r + 1) * SHARE])
        total[...] += dot(grad_pre, up_ref[0], NT)

        @pl.when(j == FFN_STEPS - 1)
        def _():
            exp_copy(jnp.int32(0)).start()
            exp_copy(jnp.int32(1)).start()
            have(1, 2, 3, 7)

            def rows(i, sums):
                at = pl.ds(pl.multiple_of(i * TILE, TILE), TILE)
                part = total[at, :]
                scaled = scaled_ref[at, :].astype(F32)
                mid = grad[at, :] + norm_back(part, scaled, inverse_ref[at, :], pick(second_gain_ref, layer))
                grad[at, :] = mid
                low_mid = mid.astype(BF16)
                grads[1, at, :] = low_mid
                grads[0, at, :] = dot(low_mid, weights[0], NT).astype(BF16)
                return (
                    sums[0] + jnp.sum(part * scaled, 0, keepdims=True),
                    sums[1] + jnp.sum(part, 0, keepdims=True),
                )

            empty = jnp.zeros((1, width), F32)
            gain_sum, bias_sum = lax.fori_loop(0, tokens // TILE, rows, (empty, empty))
            small[pl.ds(4 + 4 * layer, 1), :] = gain_sum
            small[pl.ds(5 + 4 * layer, 1), :] = bias_sum
            merge_grad = dot(mixed_ref[...], grads[1], TN).astype(BF16)
            for r in range(ROWS):
                put(6, r, merge_grad[r * SHARE : (r + 1) * SHARE])
            fetch(4, 5, 6, 8, 9)


    def kv_copy(p):
        return send(
            pending.at[lax.rem(p, 2)], landing.at[lax.rem(p, 2)], kv_send.at[lax.rem(p, 2)], kv_recv.at[lax.rem(p, 2)], core_mate,
        )

    def take(p):
        kv_copy(p).wait()
        lanes = pl.ds(pl.multiple_of(p * LANES, LANES), LANES)
        for which in range(2):
            grads[1 + which, :, lanes] = (
                grads[1 + which, :, lanes].astype(F32) + landing[lax.rem(p, 2), which].astype(F32)
            ).astype(BF16)

    @pl.when(busy & (j >= FFN_STEPS) & (j < FFN_STEPS + PAIRS))
    def _():
        p = j - FFN_STEPS
        lanes = pl.ds(pl.multiple_of(p * LANES, LANES), LANES)
        lane = lax.broadcasted_iota(jnp.int32, (tokens, LANES), 1)
        out_grad = grads[0, :, lanes].astype(F32)
        product = out_grad * mixed_ref[:, lanes].astype(F32)
        query = query_ref[0]
        inverses = total_ref[0, 0].T
        weighted = out_grad * jnp.where(lane < HEAD_DIM, inverses[:, :1], inverses[:, 1:2])
        weighted_across = weighted.T.astype(BF16)
        weighted = weighted.astype(BF16)
        query_across = query.astype(F32).T.astype(BF16)
        across = lax.broadcasted_iota(jnp.int32, (LANES, tokens), 0)
        scaled, scaled_across, inner, chosen_across = [], [], [], []
        for head in range(2):
            mine = lane // HEAD_DIM == head
            mine_across = across // HEAD_DIM == head
            scaled.append(jnp.where(mine, weighted, jnp.zeros_like(weighted)))
            scaled_across.append(jnp.where(mine_across, weighted_across, jnp.zeros_like(weighted_across)))
            chosen_across.append(jnp.where(mine_across, query_across, jnp.zeros_like(query_across)))
            inner.append(jnp.sum(jnp.where(mine, product, 0.0), -1, keepdims=True) * inverses[:, head : head + 1])

        def probs_grad(head, block):
            return dot(scaled[head][block * BLOCK :], value_ref[0, block * pair : (block + 1) * pair, :], NT)

        def score_grad(head, block, grad_prob):
            start = tile_index(blocks, block, block)
            prob = exps[lax.rem(p, 2), head, start : start + blocks - block].reshape(tokens - block * BLOCK, pair)
            return prob, (prob.astype(F32) * (grad_prob - inner[head][block * BLOCK :])).astype(BF16)

        sums = {}

        def products(head, block, prob, score):
            first = block * BLOCK
            pairs = dot(chosen_across[head][:, first:], score), dot(scaled_across[head][:, first:], prob)
            grad_query = dot(score, key_ref[0, block * pair : (block + 1) * pair, :])
            mine_lanes = slice(head * LANES, (head + 1) * LANES)
            if block == 0:
                total[:, mine_lanes] = grad_query
            else:
                total[first:, mine_lanes] += grad_query
            if head == 0:
                sums[block] = pairs
                return
            at = pl.ds(first, BLOCK)
            for which in range(2):
                both = (sums[block][which] + pairs[which]).T
                zero, one = both[:BLOCK], both[BLOCK:]
                grads[1 + which, at, lanes] = jnp.where(core == 0, zero, one).astype(BF16)
                pending[lax.rem(p, 2), which, at, :] = jnp.where(core == 0, one, zero).astype(BF16)

        exp_copy(2 * p).wait()
        exp_copy(2 * p + 1).wait()

        @pl.when(p < PAIRS - 1)
        def _():
            exp_copy(2 * p + 2).start()
            exp_copy(2 * p + 3).start()

        items = [(head, block) for block in range(blocks) for head in range(2)]
        ahead = probs_grad(*items[0])
        behind = None
        for n, item in enumerate(items):
            now = ahead
            if n + 1 < len(items):
                ahead = probs_grad(*items[n + 1])
            both = score_grad(*item, now)
            if behind is not None:
                products(*behind)
            behind = (*item, *both)
        products(*behind)

        grads[0, :, lanes] = (
            jnp.where(lane < HEAD_DIM, total[:, :LANES], total[:, LANES : 2 * LANES]) * SCALE
        ).astype(BF16)

        @pl.when(p > 0)
        def _():
            take(p - 1)

        kv_copy(p).start()


    @pl.when(busy & (j == FFN_STEPS + PAIRS))
    def _():
        take(jnp.int32(PAIRS - 1))
        have(8)
        total[...] = dot(grads[0], weights[1], NT)
        fetch(10)
        fetch(3, of_layer=layer - 1, when=more)
        have(4, 9)
        total[...] += dot(grads[1], weights[0], NT)
        fetch(7, of_layer=layer - 1, when=more)

    @pl.when(busy & (j > FFN_STEPS + PAIRS))
    def _():
        n = j - FFN_STEPS - PAIRS - 1

        triple_grad = dot(normed_ref[...], grads[n], TN).astype(BF16)
        for r in range(ROWS):
            put(4 + n, r, triple_grad[r * SHARE : (r + 1) * SHARE])

        fetch(0, of_layer=layer - 1, when=more & (n == 2))

        @pl.when(n == 0)
        def _():
            have(5, 6, 10)

            def rows(i, sums):
                at = pl.ds(pl.multiple_of(i * TILE, TILE), TILE)
                part = total[at, :] + dot(grads[2, at, :], weights[1], NT)
                scaled = scaled_ref[at, :].astype(F32)
                hidden = grad[at, :] + norm_back(part, scaled, inverse_ref[at, :], pick(first_gain_ref, layer))
                grad[at, :] = hidden
                low[at, :] = hidden.astype(BF16)

                @pl.when(turn == layers - 1)
                def _():
                    swaps(1 + i, "start")

                return (
                    sums[0] + jnp.sum(part * scaled, 0, keepdims=True),
                    sums[1] + jnp.sum(part, 0, keepdims=True),
                    sums[2] + jnp.sum(hidden, 0, keepdims=True),
                )

            empty = jnp.zeros((1, width), F32)
            gain_sum, bias_sum, hidden_sum = lax.fori_loop(0, tokens // TILE, rows, (empty, empty, empty))
            small[pl.ds(2 + 4 * layer, 1), :] = gain_sum
            small[pl.ds(3 + 4 * layer, 1), :] = bias_sum

            @pl.when(layer == 0)
            def _():
                small[pl.ds(core, 1), :] = hidden_sum

            fetch(1, 2, of_layer=layer - 1, when=more)


    last = layers * STEPS - 1
    split = left_part(width)

    def piece(ago):
        before = j < ago
        return turn - jnp.where(before, 1, 0), j - ago + jnp.where(before, STEPS, 0)

    def slot(v):
        _, i = v
        return jnp.where(
            i < 4, 4 + lax.rem(i, 2), jnp.where(i < 8, i - 4, jnp.where(i == 8, 6, i - FFN_STEPS - PAIRS + 3))
        )

    def whether(ago):
        made, i = piece(ago)
        return (made >= 0) & (made < layers) & ((i < FFN_STEPS + PAIRS - 1) | (i > FFN_STEPS + PAIRS))

    def order(v):
        made, i = v
        return made * PIECES + i - jnp.where(i > FFN_STEPS + PAIRS, 2, 0)

    def turns(v, count):
        return lax.rem(order(v), count)

    def add(a, b):
        return a + b

    def core_stage(v):
        h = turns(v, 2)
        return send(staged.at[slot(v), 1 - core], got0.at[h], core_send.at[h], core_recv.at[h], mates[0])

    def left_stage(s, v):
        h, d = turns(v, 2), turns(v, 4)
        src = (left0.at[h, 1 - x], left1.at[h, 1 - z0], left2.at[h, 1 - z1], left3.at[h])[s - 1]
        dst = (got_left1, got_left2, got_left3, got_left4)[s - 1].at[d]
        return send(src, dst, left_send.at[s - 1, h], left_recv.at[s - 1, d], mates[s])

    def right_stage(s, v):
        h, d = turns(v, 2), turns(v, 4)
        src = (right0.at[h, 1 - own_pass], right1.at[h, 1 - z0], right2.at[h, 1 - z1])[s - 1]
        dst = (got_right1, got_right2, got_right3)[s - 1].at[d]
        return send(src, dst, right_send.at[s - 1, h], right_recv.at[s - 1, d], (mates[4], mates[2], mates[3])[s - 1])

    def late_stage(s, v):
        k = order(v)
        src = (right3, right4)[s - 4].at[turns(v, 2)]
        return send(src, got_late.at[k], late_send.at[s - 4, k], late_recv.at[s - 4, k], (mates[1], mates[4])[s - 4])

    keeps = x == own_pass

    def late_start(s, v):
        @pl.when(keeps == (s == 5))
        def _():
            late_stage(s, v).start()

    def late_wait(s, v, receive):
        @pl.when(keeps == (s == 5))
        def _():
            late_stage(s, v).wait_send()

        @pl.when(keeps != (s == 5))
        def _():
            late_stage(s, v).wait_recv()
            receive()

    def out_copies(v, act):
        h = turns(v, 4)
        made, i = v
        at_layer = layers - 1 - made
        triple_out, merge_out, up_out, down_out = outs

        def columns(n):
            return pl.ds(pl.multiple_of(n * width, width), width)

        def go(target):
            getattr(pltpu.make_async_copy(final.at[h], target, out_sem.at[h]), act)()

        @pl.when(i < 4)
        def _():
            go(up_out.at[at_layer, :, columns(i)])

        @pl.when((i >= 4) & (i < 8))
        def _():
            go(down_out.at[at_layer, pl.ds(pl.multiple_of((i - 4) * SHARE, SHARE), SHARE), :])

        @pl.when(i == 8)
        def _():
            go(merge_out.at[at_layer])

        @pl.when(i > FFN_STEPS + PAIRS)
        def _():
            go(triple_out.at[at_layer, :, columns(i - FFN_STEPS - PAIRS - 1)])


    if hosted:
        @pl.when(whether(12))
        def _():
            out_copies(piece(12), "wait")

        @pl.when(whether(11))
        def _():
            v = piece(11)
            h, d = turns(v, 2), turns(v, 4)

            def receive():
                right4[h] = got_late[order(v)]

            late_wait(5, v, receive)
            final[d, :, split:] = right4[h].astype(F32)
            out_copies(v, "start")

        @pl.when(whether(9))
        def _():
            v = piece(9)
            h, d = turns(v, 2), turns(v, 4)

            def receive():
                right4[h] = add(right3[h], got_late[order(v)])

            late_wait(4, v, receive)
            late_start(5, v)
            left_stage(4, v).wait()
            final[d, :, :split] = left3[h].astype(F32) + got_left4[d].astype(F32)

        @pl.when(whether(7))
        def _():
            v = piece(7)
            h, d = turns(v, 2), turns(v, 4)
            right_stage(3, v).wait()
            right3[h] = add(right2[h, z1], got_right3[d])
            late_start(4, v)
            left_stage(3, v).wait()
            left3[h] = add(left2[h, z1], got_left3[d])
            left_stage(4, v).start()

        @pl.when(whether(5))
        def _():
            v = piece(5)
            h, d = turns(v, 2), turns(v, 4)
            right_stage(2, v).wait()
            right2[h] = add(right1[h, z0], got_right2[d])
            right_stage(3, v).start()
            left_stage(2, v).wait()
            left2[h] = add(left1[h, z0], got_left2[d])
            left_stage(3, v).start()

        @pl.when(whether(3))
        def _():
            v = piece(3)
            h, d = turns(v, 2), turns(v, 4)
            right_stage(1, v).wait()
            right1[h] = add(right0[h, own_pass], got_right1[d])
            right_stage(2, v).start()
            left_stage(1, v).wait()
            left1[h] = add(left0[h, x], got_left1[d])
            left_stage(2, v).start()

        @pl.when(whether(1))
        def _():
            v = piece(1)
            h = turns(v, 2)
            core_stage(v).wait()
            right0[h] = add(staged[slot(v), core, :, :, :, :, split:], got0[h, :, :, :, :, split:])
            right_stage(1, v).start()
            left0[h] = add(staged[slot(v), core, :, :, :, :, :split], got0[h, :, :, :, :, :split])
            left_stage(1, v).start()

        @pl.when(whether(0))
        def _():
            core_stage(piece(0)).start()

        for s in range(STAGES + 1):
            def small_copy(s):
                return send(small, small_got.at[s], small_send.at[s], small_recv.at[s], mates[s])

            @pl.when(t == last - 2 + s)
            def _():
                if s:
                    small_copy(s - 1).wait()
                    small[...] += small_got[s - 1]
                if s < STAGES:
                    small_copy(s).start()
    else:
        def piece_copy(v):
            return pltpu.make_async_copy(staged.at[slot(v)], outs[0].at[v[0] * STEPS + v[1]], out_sem.at[turns(v, 2)])

        @pl.when(whether(1))
        def _():
            piece_copy(piece(1)).wait()

        @pl.when(whether(0))
        def _():
            piece_copy(piece(0)).start()

    @pl.when(t == 0)
    def _():
        swaps(0, "start")

    @pl.when(t == (layers + 1) * STEPS - 1)
    def _():
        for i in range(1 + tokens // TILE):
            swaps(jnp.int32(i) if i else 0, "wait")
        small_ref[...] = small[...]


def back(cotangent, done, length, act, slope, normeds, scaleds, inverses, mixed, up, down, merge, first_gain, second_gain, query, kv,
         total, exps, weight, hosted):
    layers, tokens, width = query.shape
    tiles = exps.shape[2]
    piece = (2, 2, 2, 2, SHARE, width)
    left = (2, 2, 2, SHARE, left_part(width))
    right = (2, 2, 2, SHARE, width - left_part(width))
    count = layers * PIECES
    moved = 1 + tokens // TILE

    def at(turn, j):
        return jnp.maximum(layers - 1 - turn, 0), jnp.where(turn < layers, j, STEPS - 1)

    def tile(*step):
        layer, j = at(*step)
        return layer, jnp.minimum(j, FFN_STEPS - 1)

    def pair(*step):
        layer, j = at(*step)
        return layer, jnp.clip(j - FFN_STEPS, 0, PAIRS - 1)

    def spec(shape, place):
        return pl.BlockSpec(shape, lambda turn, j: place(turn, j))

    def across(*step):
        layer, n = tile(*step)
        return layer, 0, n

    def down_rows(*step):
        layer, n = tile(*step)
        return layer, n, 0

    def lanes(*step):
        layer, n = pair(*step)
        return layer, 0, n

    def value_lanes(*step):
        layer, n = pair(*step)
        return layer, 0, n + PAIRS

    def totals(*step):
        return (*pair(*step), 0, 0)

    units = spec((1, tokens, width), across)
    in_specs = [
        ANY, ANY, whole(length.shape), units, units,
        ANY, ANY, ANY, ANY,
        spec((1, width, width), across), spec((1, width, width), down_rows),
        ANY,
        whole((layers, width)), whole((layers, width)),
        spec((1, tokens, LANES), lanes), spec((1, 2 * tokens, LANES), lanes), spec((1, 2 * tokens, LANES), value_lanes),
        spec((1, 1, 8, tokens), totals),
        ANY, ANY,
    ]
    if hosted:
        shapes = [
            sds((layers, SHARE, 3 * width), F32), sds((layers, SHARE, width), F32),
            sds((layers, SHARE, FFN_STEPS * width), F32), sds((layers, 4 * SHARE, width), F32),
        ]
    else:
        shapes = [sds((layers * STEPS,) + piece, BF16)]
    dma = pltpu.SemaphoreType.DMA

    def some(*shape):
        return pltpu.VMEM(shape, BF16)

    return pl.pallas_call(
        functools.partial(back_kernel, layers, hosted),
        grid=(layers + 1, STEPS),
        in_specs=in_specs,
        out_specs=[ANY] * len(shapes) + [whole((SMALL, width)), ANY, ANY],
        out_shape=shapes + [
            sds((SMALL, width), F32), sds((tokens, width), BF16), sds((tokens, width), BF16),
        ],
        scratch_shapes=[
            some(tokens, width), some(tokens, width), pltpu.VMEM((tokens, 1), F32), some(tokens, width),
            some(2, width, width),
            pltpu.VMEM((tokens, width), F32),
            pltpu.VMEM((tokens, width), F32),
            some(3, tokens, width),
            some(2, 2, tokens, LANES),
            some(2, 2, tokens, LANES),
            some(2, 2, tiles, BLOCK, 2 * BLOCK),
            some(7, *piece),
            some(2, *left), some(2, *left[1:]), some(2, *left[2:]), some(2, *left[3:]),
            some(2, *right), some(2, *right[1:]), some(2, *right[2:]), some(2, *right[3:]), some(2, *right[3:]),
            some(2, *piece[1:]),
            some(4, *left[1:]), some(4, *left[2:]), some(4, *left[3:]), some(4, *left[3:]),
            some(4, *right[1:]), some(4, *right[2:]), some(4, *right[3:]), some(count, *right[3:]),
            pltpu.VMEM((4, SHARE, width), F32),
            pltpu.VMEM((SMALL, width), F32),
            pltpu.VMEM((STAGES, SMALL, width), F32),
            dma((6,)), dma((2, 2)), dma, dma((2,)), dma((2,)), dma((2,)), dma((2,)), dma((4, 2)), dma((4, 4)), dma((3, 2)), dma((3, 4)),
            dma((2, count)), dma((2, count)), dma((4,)),
            dma((STAGES,)), dma((STAGES,)), dma((moved,)), dma((moved,)), dma((moved,)),
        ],
        compiler_params=params(1),
        name="back",
    )(cotangent, done, length, act, slope, normeds, scaleds, inverses, mixed, up, down, merge, first_gain, second_gain, query, kv, kv,
      total, exps, weight)


def local(
    stream, lengths, pass_embed, first_gain, first_bias, triple_weight, merge_weight,
    second_gain, second_bias, up_weight, down_weight, cotangent,
):
    row_count = lax.axis_size("rows")
    own_row = lax.axis_index("rows")
    tokens, width = stream.shape[2], stream.shape[3]
    layers = triple_weight.shape[0]
    hosted = row_count == ROWS

    (normeds, scaleds, inverses, query, mixed, total, exps, act, slope, kv, done, cotangent, length) = forward(
        stream.reshape(tokens, width), cotangent.reshape(tokens, width), lengths, pass_embed,
        first_gain, first_bias, second_gain, second_bias, triple_weight, merge_weight, up_weight, down_weight,
    )
    *weight_grads, small, input_grad, output = back(
        cotangent, done, length, act, slope, normeds, scaleds, inverses, mixed, up_weight, down_weight, merge_weight,
        first_gain, second_gain, query, kv.reshape(layers, 2 * tokens, 2 * width), total, exps, triple_weight, hosted,
    )
    input_grad = input_grad.reshape(stream.shape)
    output = output.reshape(stream.shape)
    if hosted:
        triple_grad, merge_grad, up_grad, down_grad = weight_grads
    else:
        pieces = weight_grads[0].transpose(0, 4, 3, 2, 1, 5, 6).reshape(layers, STEPS, -1, width)[::-1]

        def columns(first, last):
            return pieces[:, first:last].transpose(0, 2, 1, 3).reshape(layers, -1, (last - first) * width)

        def reduce(gradient):
            share = lax.psum_scatter(gradient, "rows", scatter_dimension=1, tiled=True)
            return lax.psum(share, "pass").astype(F32)

        down_grad = pieces[:, 4:8].reshape(layers, 4, ROWS, SHARE, width).transpose(0, 2, 1, 3, 4)
        triple_grad, merge_grad, up_grad, down_grad = map(
            reduce, (columns(11, 14), columns(8, 9), columns(0, 4), down_grad.reshape(layers, -1, width))
        )
        small = lax.psum(small, ("pass", "rows"))
    share = width // row_count
    small = lax.dynamic_slice_in_dim(small, own_row * share, share, 1)
    by_layer = small[2 : 2 + 4 * layers].reshape(layers, 4, share)
    return (
        output, input_grad, small[:2], by_layer[:, 0], by_layer[:, 1], triple_grad, merge_grad,
        by_layer[:, 2], by_layer[:, 3], up_grad, down_grad,
    )


def solution(mesh):
    token = P("pass", "rows", None, None)
    matrix = P(None, "rows", None)
    rows = P(None, "rows")
    in_specs = (token, P("rows")) + (P(),) * 9 + (token,)
    out_specs = (token, token, rows, rows, rows, matrix, matrix, rows, rows, matrix, matrix)
    return jax.shard_map(local, mesh=mesh, in_specs=in_specs, out_specs=out_specs, check_vma=False)
```

```python
import functools
import math

import jax
import jax.numpy as jnp
from jax import lax
from jax.experimental import pallas as pl
from jax.experimental.pallas import tpu as pltpu
from jax.sharding import PartitionSpec as P

HEAD_DIM = 64
EPSILON = 1e-05
SCALE = HEAD_DIM**-0.5
MESH = pl.DeviceIdType.MESH
NN = (((1,), (0,)), ((), ()))
NT = (((1,), (1,)), ((), ()))
TN = (((0,), (0,)), ((), ()))
BLOCK = 128
TILE = 256
LANES = 128
BF16 = jnp.bfloat16
F32 = jnp.float32
VMEM_LIMIT = 63 * 2**20 + 3 * 2**18
ANY = pl.BlockSpec(memory_space=pl.ANY)


def dot(left, right, dims=NN):
    return lax.dot_general(left, right, dims, preferred_element_type=F32)


def sds(shape, dtype):
    return jax.ShapeDtypeStruct(shape, dtype)


def params(collective_id=None):
    return pltpu.CompilerParams(
        vmem_limit_bytes=VMEM_LIMIT,
        collective_id=collective_id,
        has_side_effects=collective_id is not None,
    )


def whole(shape):
    zeros = (0,) * len(shape)
    return pl.BlockSpec(shape, lambda *_: zeros, pipeline_mode=pl.Buffered(1))


def pick(ref, which):
    return jnp.where(which == 0, ref[0:1, :], ref[1:2, :]).astype(F32)


def norm(hidden, gain, bias):
    centred = hidden - jnp.mean(hidden, -1, keepdims=True)
    inverse = lax.rsqrt(jnp.mean(centred * centred, -1, keepdims=True) + EPSILON)
    scaled = centred * inverse
    return (scaled * gain + bias).astype(BF16), scaled, inverse


def norm_back(grad, scaled, inverse, gain):
    e = grad * gain
    return inverse * (
        e - jnp.mean(e, -1, keepdims=True) - scaled * jnp.mean(e * scaled, -1, keepdims=True)
    )


def bits():
    row = lax.axis_index("rows")
    x, z0, z1 = (lax.rem(lax.div(row, 2**n), 2) for n in (1, 2, 3))
    return row, lax.rem(row, 2), x, z0, z1, lax.axis_index("pass")


def send(src, dst, send_sem, recv_sem, device):
    return pltpu.make_async_remote_copy(
        src_ref=src, dst_ref=dst, send_sem=send_sem, recv_sem=recv_sem,
        device_id=device, device_id_type=MESH,
    )


QKV_STEPS = 4
PAIRS = 6
FFN_TILES = 4
FORWARD = QKV_STEPS + PAIRS + FFN_TILES


def tile_index(blocks, key_block, query_block):
    return key_block * blocks - key_block * (key_block - 1) // 2 + query_block - key_block


def gelu_both(v):
    root = math.sqrt(2.0 / math.pi)
    cube = (root * 0.044715) * (v * v)
    half = 0.5 + 0.5 * jnp.tanh(v * (root + cube))
    act = v * half
    return act, half + (act - act * half) * (2.0 * root + 6.0 * cube)


def forward_kernel(
    layers,
    stream_ref, cot_ref, length_ref, embed_ref, first_gain_ref, first_bias_ref, second_gain_ref, second_bias_ref,
    triple_ref, merge_ref, up_ref, down_ref,
    normed_ref, scaled_ref, inverse_ref, query_ref, mixed_ref, total_ref, exp_ref, act_ref, slope_ref, kv_ref,
    out_ref, cot_out_ref, length_out_ref,
    hidden, arrived, length_mine, length_here, queries, kv, values, mixes, triple, merge, up, down,
    weight_sem, kv_sem, kv_send, kv_recv, free_sem, swap_send, swap_recv, here_sem,
):
    layer, j = pl.program_id(0), pl.program_id(1)
    t = layer * FORWARD + j
    row, core, _, _, _, own_pass = bits()
    tokens, width = hidden.shape
    blocks = tokens // BLOCK
    pair = 2 * BLOCK
    core_mate = {"rows": row + 1 - 2 * core}
    diagonal = {"pass": 1 - own_pass, "rows": row + 1 - 2 * core}
    swapped = own_pass != core


    def moves(i):
        if i < QKV_STEPS:
            rows = pl.ds(i * TILE, TILE)
            ends = stream_ref.at[rows, :], arrived.at[rows, :]
        else:
            ends = ((cot_ref, cot_out_ref), (length_mine, length_here))[i - QKV_STEPS]
        return (
            send(*ends, swap_send.at[i], swap_recv.at[i], diagonal),
            pltpu.make_async_copy(*ends, here_sem.at[i]),
        )

    def move(i, act):
        there, here = moves(i)

        @pl.when(swapped)
        def _():
            getattr(there, act)()

        @pl.when(jnp.logical_not(swapped))
        def _():
            getattr(here, act)()


    def weight_copies(which, of_layer):
        refs = ((triple_ref, triple), (merge_ref, merge), (up_ref, up), (down_ref, down))
        source, target = refs[which]
        return pltpu.make_async_copy(source.at[of_layer], target, weight_sem.at[which])

    @pl.when(t == 0)
    def _():
        barrier = pltpu.get_barrier_semaphore()
        pl.semaphore_signal(barrier, inc=1, device_id=core_mate, device_id_type=MESH)

        @pl.when(swapped)
        def _():
            pl.semaphore_signal(barrier, inc=1, device_id=diagonal, device_id_type=MESH)

        pl.semaphore_wait(barrier, 1 + jnp.where(swapped, 1, 0))
        length_mine[...] = jnp.full(length_mine.shape, length_ref[0], jnp.int32)
        move(QKV_STEPS + 1, "start")
        for i in range(QKV_STEPS):
            move(i, "start")
        for which in range(4):
            weight_copies(which, 0).start()
        move(QKV_STEPS + 1, "wait")
        length_out_ref[...] = length_here[...]

    for i in range(QKV_STEPS):
        @pl.when(t == i)
        def _():
            move(i, "wait")
            if i == QKV_STEPS - 1:
                move(QKV_STEPS, "start")


    def kv_copy(i):
        part = kv.at[pl.ds(i * (TILE // BLOCK), TILE // BLOCK), core]
        return send(part, part, kv_send.at[i], kv_recv.at[i], core_mate)

    def kv_keep(of_layer):
        return pltpu.make_async_copy(kv, kv_ref.at[of_layer], kv_sem)

    @pl.when(j < QKV_STEPS)
    def _():
        rows = pl.ds(pl.multiple_of(j * TILE, TILE), TILE)

        @pl.when(layer == 0)
        def _():
            hidden[rows, :] = arrived[rows, :].astype(F32) + pick(embed_ref, core)

        @pl.when(j == 0)
        def _():
            weight_copies(0, layer).wait()

        @pl.when((j == 0) & (layer > 0))
        def _():
            pl.semaphore_wait(free_sem, 1)

        normed, scaled, inverse = norm(
            hidden[rows, :], pick(first_gain_ref, layer), pick(first_bias_ref, layer)
        )
        normed_ref[0, 0] = normed
        scaled_ref[0, 0] = scaled.astype(BF16)
        inverse_ref[0, 0] = inverse
        keys = dot(normed, triple[:, width:]).astype(BF16)
        for b in range(TILE // BLOCK):
            kv[j * (TILE // BLOCK) + b, core] = keys[b * BLOCK : (b + 1) * BLOCK]
        kv_copy(j).start()
        query = (dot(normed, triple[:, :width]).astype(BF16).astype(F32) * SCALE).astype(BF16)
        queries[rows, :] = query
        query_ref[0] = query


    @pl.when((j >= QKV_STEPS) & (j < QKV_STEPS + PAIRS))
    def _():
        p = j - QKV_STEPS
        lanes = pl.ds(pl.multiple_of(p * LANES, LANES), LANES)
        value_lanes = pl.ds(pl.multiple_of(width + p * LANES, LANES), LANES)

        @pl.when(p == 0)
        def _():
            for i in range(QKV_STEPS):
                kv_copy(i).wait()
            kv_keep(layer).start()

        @pl.when((p == 0) & (layer < layers - 1))
        def _():
            weight_copies(0, layer + 1).start()

        values[:, :LANES] = kv[:, :, :, value_lanes].reshape(2 * tokens, LANES)
        values[:, LANES:] = jnp.ones((2 * tokens, LANES), BF16)
        lane = lax.broadcasted_iota(jnp.int32, (BLOCK, LANES), 1)
        query_at = lax.broadcasted_iota(jnp.int32, (BLOCK, pair), 0)
        column = lax.broadcasted_iota(jnp.int32, (BLOCK, pair), 1)
        key_pass = column // BLOCK
        key_at = column - key_pass * BLOCK
        causal = (key_at < query_at) | ((key_at == query_at) & (key_pass <= core))
        length = length_here[0:1, 0:1]

        def scores(block, head):
            query = queries[pl.ds(block * BLOCK, BLOCK), lanes]
            chosen = jnp.where(lane // HEAD_DIM == head, query, jnp.zeros_like(query))
            keys = kv[: block + 1, :, :, lanes].reshape((block + 1) * pair, LANES)
            return dot(chosen, keys, NT)

        def exponentials(block, head, raw):
            allowed = causal & (key_at + block * BLOCK < length)
            last = jnp.where(allowed, raw[:, block * pair :], -jnp.inf)
            top = jnp.max(last, -1, keepdims=True)
            if block:
                top = jnp.maximum(top, jnp.max(raw[:, : block * pair], -1, keepdims=True))
            parts = []
            for k in range(block + 1):
                source = last if k == block else raw[:, k * pair : (k + 1) * pair]
                part = jnp.exp(source - top).astype(BF16)
                exp_ref[0, head, tile_index(blocks, k, block)] = part
                parts.append(part)
            return jnp.concatenate(parts, 1) if block else parts[0]

        outs = {}

        def mix(block, head, exps):
            both = dot(exps, values[: (block + 1) * pair, :])
            inverse = jnp.where(block * BLOCK < length, 1.0 / both[:, LANES:], 0.0)
            rows = pl.ds(block * BLOCK, BLOCK)
            total_ref[0, 0, head : head + 1, rows] = inverse.T[:1]
            outs[head] = both[:, :LANES] * inverse
            if head == 1:
                value = jnp.where(lane < HEAD_DIM, outs[0], outs[1]).astype(BF16)
                mixes[rows, lanes] = value
                mixed_ref[0, rows, :] = value

        items = [(block, head) for block in range(blocks) for head in range(2)]
        ahead = scores(*items[0])
        behind = None
        for n, item in enumerate(items):
            raw = ahead
            if n + 1 < len(items):
                ahead = scores(*items[n + 1])
            exps = exponentials(*item, raw)
            if behind is not None:
                mix(*behind)
            behind = (*item, exps)
        mix(*behind)

        @pl.when(p == PAIRS - 1)
        def _():
            kv_keep(layer).wait()

        @pl.when((p == PAIRS - 1) & (layer < layers - 1))
        def _():
            pl.semaphore_signal(free_sem, inc=1, device_id=core_mate, device_id_type=MESH)


    @pl.when(j >= QKV_STEPS + PAIRS)
    def _():
        i = j - QKV_STEPS - PAIRS
        rows = pl.ds(pl.multiple_of(i * TILE, TILE), TILE)

        @pl.when(i == 0)
        def _():
            for which in range(1, 4):
                weight_copies(which, layer).wait()

        mid = hidden[rows, :] + dot(mixes[rows, :], merge[...])
        normed, scaled, inverse = norm(mid, pick(second_gain_ref, layer), pick(second_bias_ref, layer))
        normed_ref[0, 0] = normed
        scaled_ref[0, 0] = scaled.astype(BF16)
        inverse_ref[0, 0] = inverse
        parts = up.shape[1] // width
        sum_next = mid
        ahead = dot(normed, up[:, :width])
        for part in range(parts):
            at = slice(part * width, (part + 1) * width)
            now = ahead
            if part + 1 < parts:
                ahead = dot(normed, up[:, (part + 1) * width : (part + 2) * width])
            act, slope = gelu_both(now)
            act = act.astype(BF16)
            act_ref[0, :, at] = act
            slope_ref[0, :, at] = slope.astype(BF16)
            sum_next = sum_next + dot(act, down[at, :])
        hidden[rows, :] = sum_next

        @pl.when(layer == layers - 1)
        def _():
            position = lax.broadcasted_iota(jnp.int32, (TILE, 1), 0) + i * TILE
            valid = (position < length_here[0:1, 0:1]).astype(F32)
            out_ref[...] = (sum_next * valid).astype(BF16)

        @pl.when((i == FFN_TILES - 1) & (layer < layers - 1))
        def _():
            for which in range(1, 4):
                weight_copies(which, layer + 1).start()

    @pl.when(t == layers * FORWARD - 1)
    def _():
        move(QKV_STEPS, "wait")


def forward(stream, cotangent, length, embed, first_gain, first_bias, second_gain, second_bias, triple, merge, up, down):
    tokens, width = stream.shape
    layers, _, units = up.shape
    blocks = tokens // BLOCK
    tiles = blocks * (blocks + 1) // 2

    def row_tile(layer, j):
        late = j >= QKV_STEPS + PAIRS
        kind = jnp.where(late, 0, 1)
        return layer, kind, jnp.where(late, j - QKV_STEPS - PAIRS, jnp.minimum(j, QKV_STEPS - 1)), 0

    def query_tile(layer, j):
        return layer, jnp.minimum(j, QKV_STEPS - 1), 0

    def head(j):
        return jnp.clip(j - QKV_STEPS, 0, PAIRS - 1)

    def ffn_tile(layer, j):
        return layer, jnp.maximum(j - QKV_STEPS - PAIRS, 0), 0

    vector = whole((layers, width))
    rows = pl.BlockSpec((1, 1, TILE, width), row_tile)
    dma = pltpu.SemaphoreType.DMA
    return pl.pallas_call(
        functools.partial(forward_kernel, layers),
        grid=(layers, FORWARD),
        in_specs=[ANY, ANY, pl.BlockSpec(memory_space=pltpu.SMEM), whole(embed.shape), vector, vector, vector, vector, ANY, ANY, ANY, ANY],
        out_specs=[
            rows, rows, pl.BlockSpec((1, 1, TILE, 1), row_tile),
            pl.BlockSpec((1, TILE, width), query_tile),
            pl.BlockSpec((1, tokens, LANES), lambda layer, j: (layer, 0, head(j))),
            pl.BlockSpec((1, 1, 8, tokens), lambda layer, j: (layer, head(j), 0, 0)),
            pl.BlockSpec((1, 2, tiles, BLOCK, 2 * BLOCK), lambda layer, j: (layer, head(j), 0, 0, 0)),
            pl.BlockSpec((1, TILE, units), ffn_tile), pl.BlockSpec((1, TILE, units), ffn_tile),
            ANY,
            pl.BlockSpec((TILE, width), lambda layer, j: (jnp.where(layer == layers - 1, ffn_tile(layer, j)[1], 0), 0)),
            ANY, whole((8, LANES)),
        ],
        out_shape=[
            sds((layers, 2, tokens, width), BF16),
            sds((layers, 2, tokens, width), BF16),
            sds((layers, 2, tokens, 1), F32),
            sds((layers, tokens, width), BF16),
            sds((layers, tokens, width), BF16),
            sds((layers, PAIRS, 8, tokens), F32),
            sds((layers, 2 * PAIRS, tiles, BLOCK, 2 * BLOCK), BF16),
            sds((layers, tokens, units), BF16),
            sds((layers, tokens, units), BF16),
            sds((layers, blocks, 2, BLOCK, 2 * width), BF16),
            sds((tokens, width), BF16),
            sds((tokens, width), BF16),
            sds((8, LANES), jnp.int32),
        ],
        scratch_shapes=[
            pltpu.VMEM((tokens, width), F32),
            pltpu.VMEM((tokens, width), BF16),
            pltpu.VMEM((8, LANES), jnp.int32),
            pltpu.VMEM((8, LANES), jnp.int32),
            pltpu.VMEM((tokens, width), BF16),
            pltpu.VMEM((blocks, 2, BLOCK, 2 * width), BF16),
            pltpu.VMEM((2 * tokens, 2 * LANES), BF16),
            pltpu.VMEM((tokens, width), BF16),
            pltpu.VMEM(triple.shape[1:], BF16),
            pltpu.VMEM(merge.shape[1:], BF16),
            pltpu.VMEM(up.shape[1:], BF16),
            pltpu.VMEM(down.shape[1:], BF16),
            dma((4,)), dma, dma((QKV_STEPS,)), dma((QKV_STEPS,)), pltpu.SemaphoreType.REGULAR,
            dma((QKV_STEPS + 2,)), dma((QKV_STEPS + 2,)), dma((QKV_STEPS + 2,)),
        ],
        compiler_params=params(0),
        name="forward",
    )(stream, cotangent, length, embed, first_gain, first_bias, second_gain, second_bias, triple, merge, up, down)


FFN_STEPS = 4
STEPS = FFN_STEPS + PAIRS + 3
PIECES = STEPS - 1
STAGES = 5
ROWS = 16
SHARE = 48
SMALL = 16


def left_part(width):
    return 2 * width // 3


def back_kernel(
    layers, hosted,
    cot_ref, done_ref, length_ref, act_ref, slope_ref, normeds_ref, scaleds_ref, inverses_ref, mixes_ref, up_ref, down_ref,
    merges_ref,
    first_gain_ref, second_gain_ref, query_ref, key_ref, value_ref, total_ref, exp_ref, triples_ref,
    *refs,
):
    outs = refs[: 4 if hosted else 1]
    (
        small_ref, input_ref, output_ref,
        normed_ref, scaled_ref, inverse_ref, mixed_ref, weights, grad, total, grads, pending, landing, exps,
        staged, left0, left1, left2, left3, right0, right1, right2, right3, right4, got0,
        got_left1, got_left2, got_left3, got_left4, got_right1, got_right2, got_right3, got_late,
        final, small, small_got,
        load_sem, exp_sem, cot_sem, kv_send, kv_recv, core_send, core_recv, left_send, left_recv, right_send, right_recv,
        late_send, late_recv, out_sem, small_send, small_recv, swap_send, swap_recv, here_sem,
    ) = refs[len(outs) :]
    low = grads.at[0]
    turn, j = pl.program_id(0), pl.program_id(1)
    t = turn * STEPS + j
    layer = jnp.maximum(layers - 1 - turn, 0)
    row, core, x, z0, z1, own_pass = bits()
    tokens, width = grad.shape
    blocks = tokens // BLOCK
    pair = 2 * BLOCK
    busy = turn < layers
    core_mate = {"rows": row + 1 - 2 * core}
    mates = [
        core_mate, {"rows": row + 2 - 4 * x}, {"rows": row + 4 - 8 * z0}, {"rows": row + 8 - 16 * z1},
        {"pass": 1 - own_pass},
    ]
    diagonal = {"pass": 1 - own_pass, "rows": row + 1 - 2 * core}
    swapped = own_pass != core

    @pl.when(t == 0)
    def _():
        barrier = pltpu.get_barrier_semaphore()
        greeted = mates if hosted else mates[:1]
        for mate in greeted:
            pl.semaphore_signal(barrier, inc=1, device_id=mate, device_id_type=MESH)

        @pl.when(swapped)
        def _():
            pl.semaphore_signal(barrier, inc=1, device_id=diagonal, device_id_type=MESH)

        pl.semaphore_wait(barrier, len(greeted) + jnp.where(swapped, 1, 0))
        load = pltpu.make_async_copy(cot_ref, low, cot_sem)
        load.start()
        load.wait()
        position = lax.broadcasted_iota(jnp.int32, (tokens, 1), 0)
        valid = (position < length_ref[0:1, 0:1]).astype(F32)
        masked = low[...].astype(F32) * valid
        grad[...] = masked
        low[...] = masked.astype(BF16)
        small[...] = jnp.zeros_like(small)


    def swaps(i, act):
        if isinstance(i, int):
            source, target = done_ref, output_ref
        else:
            rows = pl.ds(pl.multiple_of((i - 1) * TILE, TILE), TILE)
            source, target = low.at[rows, :], input_ref.at[rows, :]

        @pl.when(swapped)
        def _():
            getattr(send(source, target, swap_send.at[i], swap_recv.at[i], diagonal), act)()

        @pl.when(jnp.logical_not(swapped))
        def _():
            getattr(pltpu.make_async_copy(source, target, here_sem.at[i]), act)()


    def load(what, of_layer):
        def weight_part(n):
            return triples_ref.at[of_layer, :, n * width : (n + 1) * width]

        source, target, sem = (
            (normeds_ref.at[of_layer, 0], normed_ref, 0), (scaleds_ref.at[of_layer, 0], scaled_ref, 1),
            (inverses_ref.at[of_layer, 0], inverse_ref, 2), (mixes_ref.at[of_layer], mixed_ref, 3),
            (normeds_ref.at[of_layer, 1], normed_ref, 0), (scaleds_ref.at[of_layer, 1], scaled_ref, 1),
            (inverses_ref.at[of_layer, 1], inverse_ref, 2), (merges_ref.at[of_layer], weights.at[0], 4),
            (weight_part(0), weights.at[1], 5), (weight_part(1), weights.at[0], 4), (weight_part(2), weights.at[1], 5),
        )[what]
        return pltpu.make_async_copy(source, target, load_sem.at[sem])

    def fetch(*which, of_layer=layer, when=True):
        @pl.when(when)
        def _():
            for what in which:
                load(what, of_layer).start()

    def have(*which):
        for what in which:
            load(what, layer).wait()

    more = layer > 0
    fetch(0, 1, 2, 3, 7, when=t == 0)


    def exp_copy(head):
        at = lax.rem(lax.div(head, 2), 2), lax.rem(head, 2)
        return pltpu.make_async_copy(exp_ref.at[layer, head], exps.at[at], exp_sem.at[at])

    def put(slot, r, value):
        staged[slot, r % 2, (r // 2) % 2, (r // 4) % 2, (r // 8) % 2] = value

    @pl.when(busy & (j < FFN_STEPS))
    def _():
        @pl.when(j == 0)
        def _():
            total[...] = jnp.zeros_like(total)

        grad_low = low[...]
        down_grad = dot(act_ref[0], grad_low, TN).astype(BF16)
        for q in range(4):
            for i in range(4):
                first = q * 4 * SHARE + i * SHARE
                staged[i, q % 2, q // 2, lax.rem(j, 2), lax.div(j, 2)] = down_grad[first : first + SHARE]
        grad_act = dot(grad_low, down_ref[0], NT)
        grad_pre = (slope_ref[0].astype(F32) * grad_act).astype(BF16)

        @pl.when(j == 0)
        def _():
            have(0)

        up_grad = dot(normed_ref[...], grad_pre, TN).astype(BF16)
        for r in range(ROWS):
            put(4 + lax.rem(j, 2), r, up_grad[r * SHARE : (r + 1) * SHARE])
        total[...] += dot(grad_pre, up_ref[0], NT)

        @pl.when(j == FFN_STEPS - 1)
        def _():
            exp_copy(jnp.int32(0)).start()
            exp_copy(jnp.int32(1)).start()
            have(1, 2, 3, 7)

            def rows(i, sums):
                at = pl.ds(pl.multiple_of(i * TILE, TILE), TILE)
                part = total[at, :]
                scaled = scaled_ref[at, :].astype(F32)
                mid = grad[at, :] + norm_back(part, scaled, inverse_ref[at, :], pick(second_gain_ref, layer))
                grad[at, :] = mid
                low_mid = mid.astype(BF16)
                grads[1, at, :] = low_mid
                grads[0, at, :] = dot(low_mid, weights[0], NT).astype(BF16)
                return (
                    sums[0] + jnp.sum(part * scaled, 0, keepdims=True),
                    sums[1] + jnp.sum(part, 0, keepdims=True),
                )

            empty = jnp.zeros((1, width), F32)
            gain_sum, bias_sum = lax.fori_loop(0, tokens // TILE, rows, (empty, empty))
            small[pl.ds(4 + 4 * layer, 1), :] = gain_sum
            small[pl.ds(5 + 4 * layer, 1), :] = bias_sum
            merge_grad = dot(mixed_ref[...], grads[1], TN).astype(BF16)
            for r in range(ROWS):
                put(6, r, merge_grad[r * SHARE : (r + 1) * SHARE])
            fetch(4, 5, 6, 8, 9)


    def kv_copy(p):
        return send(
            pending.at[lax.rem(p, 2)], landing.at[lax.rem(p, 2)], kv_send.at[lax.rem(p, 2)], kv_recv.at[lax.rem(p, 2)], core_mate,
        )

    def take(p):
        kv_copy(p).wait()
        lanes = pl.ds(pl.multiple_of(p * LANES, LANES), LANES)
        for which in range(2):
            grads[1 + which, :, lanes] = (
                grads[1 + which, :, lanes].astype(F32) + landing[lax.rem(p, 2), which].astype(F32)
            ).astype(BF16)

    @pl.when(busy & (j >= FFN_STEPS) & (j < FFN_STEPS + PAIRS))
    def _():
        p = j - FFN_STEPS
        lanes = pl.ds(pl.multiple_of(p * LANES, LANES), LANES)
        lane = lax.broadcasted_iota(jnp.int32, (tokens, LANES), 1)
        out_grad = grads[0, :, lanes].astype(F32)
        product = out_grad * mixed_ref[:, lanes].astype(F32)
        query = query_ref[0]
        inverses = total_ref[0, 0].T
        weighted = out_grad * jnp.where(lane < HEAD_DIM, inverses[:, :1], inverses[:, 1:2])
        weighted_across = weighted.T.astype(BF16)
        weighted = weighted.astype(BF16)
        query_across = query.astype(F32).T.astype(BF16)
        across = lax.broadcasted_iota(jnp.int32, (LANES, tokens), 0)
        scaled, scaled_across, inner, chosen_across = [], [], [], []
        for head in range(2):
            mine = lane // HEAD_DIM == head
            mine_across = across // HEAD_DIM == head
            scaled.append(jnp.where(mine, weighted, jnp.zeros_like(weighted)))
            scaled_across.append(jnp.where(mine_across, weighted_across, jnp.zeros_like(weighted_across)))
            chosen_across.append(jnp.where(mine_across, query_across, jnp.zeros_like(query_across)))
            inner.append(jnp.sum(jnp.where(mine, product, 0.0), -1, keepdims=True) * inverses[:, head : head + 1])

        def probs_grad(head, block):
            return dot(scaled[head][block * BLOCK :], value_ref[0, block * pair : (block + 1) * pair, :], NT)

        def score_grad(head, block, grad_prob):
            start = tile_index(blocks, block, block)
            prob = exps[lax.rem(p, 2), head, start : start + blocks - block].reshape(tokens - block * BLOCK, pair)
            return prob, (prob.astype(F32) * (grad_prob - inner[head][block * BLOCK :])).astype(BF16)

        sums = {}

        def products(head, block, prob, score):
            first = block * BLOCK
            pairs = dot(chosen_across[head][:, first:], score), dot(scaled_across[head][:, first:], prob)
            grad_query = dot(score, key_ref[0, block * pair : (block + 1) * pair, :])
            mine_lanes = slice(head * LANES, (head + 1) * LANES)
            if block == 0:
                total[:, mine_lanes] = grad_query
            else:
                total[first:, mine_lanes] += grad_query
            if head == 0:
                sums[block] = pairs
                return
            at = pl.ds(first, BLOCK)
            for which in range(2):
                both = (sums[block][which] + pairs[which]).T
                zero, one = both[:BLOCK], both[BLOCK:]
                grads[1 + which, at, lanes] = jnp.where(core == 0, zero, one).astype(BF16)
                pending[lax.rem(p, 2), which, at, :] = jnp.where(core == 0, one, zero).astype(BF16)

        exp_copy(2 * p).wait()
        exp_copy(2 * p + 1).wait()

        @pl.when(p < PAIRS - 1)
        def _():
            exp_copy(2 * p + 2).start()
            exp_copy(2 * p + 3).start()

        items = [(head, block) for block in range(blocks) for head in range(2)]
        ahead = probs_grad(*items[0])
        behind = None
        for n, item in enumerate(items):
            now = ahead
            if n + 1 < len(items):
                ahead = probs_grad(*items[n + 1])
            both = score_grad(*item, now)
            if behind is not None:
                products(*behind)
            behind = (*item, *both)
        products(*behind)

        grads[0, :, lanes] = (
            jnp.where(lane < HEAD_DIM, total[:, :LANES], total[:, LANES : 2 * LANES]) * SCALE
        ).astype(BF16)

        @pl.when(p > 0)
        def _():
            take(p - 1)

        kv_copy(p).start()


    @pl.when(busy & (j == FFN_STEPS + PAIRS))
    def _():
        take(jnp.int32(PAIRS - 1))
        have(4, 8)
        total[...] = dot(grads[0], weights[1], NT)
        fetch(10)
        fetch(3, of_layer=layer - 1, when=more)
        have(9)
        total[...] += dot(grads[1], weights[0], NT)
        fetch(7, of_layer=layer - 1, when=more)

    @pl.when(busy & (j >= FFN_STEPS + PAIRS))
    def _():
        n = j - FFN_STEPS - PAIRS

        triple_grad = dot(normed_ref[...], grads[n], TN).astype(BF16)
        for r in range(ROWS):
            put(4 + n, r, triple_grad[r * SHARE : (r + 1) * SHARE])

        fetch(0, of_layer=layer - 1, when=more & (n == 2))

        @pl.when(n == 1)
        def _():
            have(5, 6, 10)

            def rows(i, sums):
                at = pl.ds(pl.multiple_of(i * TILE, TILE), TILE)
                part = total[at, :] + dot(grads[2, at, :], weights[1], NT)
                scaled = scaled_ref[at, :].astype(F32)
                hidden = grad[at, :] + norm_back(part, scaled, inverse_ref[at, :], pick(first_gain_ref, layer))
                grad[at, :] = hidden
                low[at, :] = hidden.astype(BF16)
                return (
                    sums[0] + jnp.sum(part * scaled, 0, keepdims=True),
                    sums[1] + jnp.sum(part, 0, keepdims=True),
                    sums[2] + jnp.sum(hidden, 0, keepdims=True),
                )

            empty = jnp.zeros((1, width), F32)
            gain_sum, bias_sum, hidden_sum = lax.fori_loop(0, tokens // TILE, rows, (empty, empty, empty))
            small[pl.ds(2 + 4 * layer, 1), :] = gain_sum
            small[pl.ds(3 + 4 * layer, 1), :] = bias_sum

            @pl.when(layer == 0)
            def _():
                small[pl.ds(core, 1), :] = hidden_sum

            fetch(1, 2, of_layer=layer - 1, when=more)


    last = layers * STEPS - 1
    split = left_part(width)

    def piece(ago):
        before = j < ago
        return turn - jnp.where(before, 1, 0), j - ago + jnp.where(before, STEPS, 0)

    def slot(v):
        _, i = v
        return jnp.where(
            i < 4, 4 + lax.rem(i, 2), jnp.where(i < 8, i - 4, jnp.where(i == 8, 6, i - FFN_STEPS - PAIRS + 4))
        )

    def whether(ago):
        made, i = piece(ago)
        return (made >= 0) & (made < layers) & (i != FFN_STEPS + PAIRS - 1)

    def order(v):
        made, i = v
        return made * PIECES + i - jnp.where(i >= FFN_STEPS + PAIRS, 1, 0)

    def turns(v, count):
        return lax.rem(order(v), count)

    def add(a, b):
        return a + b

    def core_stage(v):
        h = turns(v, 2)
        return send(staged.at[slot(v), 1 - core], got0.at[h], core_send.at[h], core_recv.at[h], mates[0])

    def left_stage(s, v):
        h, d = turns(v, 2), turns(v, 4)
        src = (left0.at[h, 1 - x], left1.at[h, 1 - z0], left2.at[h, 1 - z1], left3.at[h])[s - 1]
        dst = (got_left1, got_left2, got_left3, got_left4)[s - 1].at[d]
        return send(src, dst, left_send.at[s - 1, h], left_recv.at[s - 1, d], mates[s])

    def right_stage(s, v):
        h, d = turns(v, 2), turns(v, 4)
        src = (right0.at[h, 1 - own_pass], right1.at[h, 1 - z0], right2.at[h, 1 - z1])[s - 1]
        dst = (got_right1, got_right2, got_right3)[s - 1].at[d]
        return send(src, dst, right_send.at[s - 1, h], right_recv.at[s - 1, d], (mates[4], mates[2], mates[3])[s - 1])

    def late_stage(s, v):
        k = order(v)
        src = (right3, right4)[s - 4].at[turns(v, 2)]
        return send(src, got_late.at[k], late_send.at[s - 4, k], late_recv.at[s - 4, k], (mates[1], mates[4])[s - 4])

    keeps = x == own_pass

    def late_start(s, v):
        @pl.when(keeps == (s == 5))
        def _():
            late_stage(s, v).start()

    def late_wait(s, v, receive):
        @pl.when(keeps == (s == 5))
        def _():
            late_stage(s, v).wait_send()

        @pl.when(keeps != (s == 5))
        def _():
            late_stage(s, v).wait_recv()
            receive()

    def out_copies(v, act):
        h = turns(v, 4)
        made, i = v
        at_layer = layers - 1 - made
        triple_out, merge_out, up_out, down_out = outs

        def columns(n):
            return pl.ds(pl.multiple_of(n * width, width), width)

        def go(target):
            getattr(pltpu.make_async_copy(final.at[h], target, out_sem.at[h]), act)()

        @pl.when(i < 4)
        def _():
            go(up_out.at[at_layer, :, columns(i)])

        @pl.when((i >= 4) & (i < 8))
        def _():
            go(down_out.at[at_layer, pl.ds(pl.multiple_of((i - 4) * SHARE, SHARE), SHARE), :])

        @pl.when(i == 8)
        def _():
            go(merge_out.at[at_layer])

        @pl.when(i >= FFN_STEPS + PAIRS)
        def _():
            go(triple_out.at[at_layer, :, columns(i - FFN_STEPS - PAIRS)])


    if hosted:
        @pl.when(whether(12))
        def _():
            out_copies(piece(12), "wait")

        @pl.when(whether(11))
        def _():
            v = piece(11)
            h, d = turns(v, 2), turns(v, 4)

            def receive():
                right4[h] = got_late[order(v)]

            late_wait(5, v, receive)
            final[d, :, split:] = right4[h].astype(F32)
            out_copies(v, "start")

        @pl.when(whether(9))
        def _():
            v = piece(9)
            h, d = turns(v, 2), turns(v, 4)

            def receive():
                right4[h] = add(right3[h], got_late[order(v)])

            late_wait(4, v, receive)
            late_start(5, v)
            left_stage(4, v).wait()
            final[d, :, :split] = left3[h].astype(F32) + got_left4[d].astype(F32)

        @pl.when(whether(7))
        def _():
            v = piece(7)
            h, d = turns(v, 2), turns(v, 4)
            right_stage(3, v).wait()
            right3[h] = add(right2[h, z1], got_right3[d])
            late_start(4, v)
            left_stage(3, v).wait()
            left3[h] = add(left2[h, z1], got_left3[d])
            left_stage(4, v).start()

        @pl.when(whether(5))
        def _():
            v = piece(5)
            h, d = turns(v, 2), turns(v, 4)
            right_stage(2, v).wait()
            right2[h] = add(right1[h, z0], got_right2[d])
            right_stage(3, v).start()
            left_stage(2, v).wait()
            left2[h] = add(left1[h, z0], got_left2[d])
            left_stage(3, v).start()

        @pl.when(whether(3))
        def _():
            v = piece(3)
            h, d = turns(v, 2), turns(v, 4)
            right_stage(1, v).wait()
            right1[h] = add(right0[h, own_pass], got_right1[d])
            right_stage(2, v).start()
            left_stage(1, v).wait()
            left1[h] = add(left0[h, x], got_left1[d])
            left_stage(2, v).start()

        @pl.when(whether(1))
        def _():
            v = piece(1)
            h = turns(v, 2)
            core_stage(v).wait()
            right0[h] = add(staged[slot(v), core, :, :, :, :, split:], got0[h, :, :, :, :, split:])
            right_stage(1, v).start()
            left0[h] = add(staged[slot(v), core, :, :, :, :, :split], got0[h, :, :, :, :, :split])
            left_stage(1, v).start()

        @pl.when(whether(0))
        def _():
            core_stage(piece(0)).start()

        for s in range(STAGES + 1):
            def small_copy(s):
                return send(small, small_got.at[s], small_send.at[s], small_recv.at[s], mates[s])

            @pl.when(t == last - 1 + s)
            def _():
                if s:
                    small_copy(s - 1).wait()
                    small[...] += small_got[s - 1]
                if s < STAGES:
                    small_copy(s).start()
    else:
        def piece_copy(v):
            return pltpu.make_async_copy(staged.at[slot(v)], outs[0].at[v[0] * STEPS + v[1]], out_sem.at[turns(v, 2)])

        @pl.when(whether(1))
        def _():
            piece_copy(piece(1)).wait()

        @pl.when(whether(0))
        def _():
            piece_copy(piece(0)).start()

    @pl.when(t == 0)
    def _():
        swaps(0, "start")

    for i in range(tokens // TILE):
        @pl.when(t == last - 1 + i)
        def _():
            swaps(jnp.int32(1 + i), "start")

    @pl.when(t == (layers + 1) * STEPS - 1)
    def _():
        for i in range(1 + tokens // TILE):
            swaps(jnp.int32(i) if i else 0, "wait")
        small_ref[...] = small[...]


def back(cotangent, done, length, act, slope, normeds, scaleds, inverses, mixed, up, down, merge, first_gain, second_gain, query, kv,
         total, exps, weight, hosted):
    layers, tokens, width = query.shape
    tiles = exps.shape[2]
    piece = (2, 2, 2, 2, SHARE, width)
    left = (2, 2, 2, SHARE, left_part(width))
    right = (2, 2, 2, SHARE, width - left_part(width))
    count = layers * PIECES
    moved = 1 + tokens // TILE

    def at(turn, j):
        return jnp.maximum(layers - 1 - turn, 0), jnp.where(turn < layers, j, STEPS - 1)

    def tile(*step):
        layer, j = at(*step)
        return layer, jnp.minimum(j, FFN_STEPS - 1)

    def pair(*step):
        layer, j = at(*step)
        return layer, jnp.clip(j - FFN_STEPS, 0, PAIRS - 1)

    def spec(shape, place):
        return pl.BlockSpec(shape, lambda turn, j: place(turn, j))

    def across(*step):
        layer, n = tile(*step)
        return layer, 0, n

    def down_rows(*step):
        layer, n = tile(*step)
        return layer, n, 0

    def lanes(*step):
        layer, n = pair(*step)
        return layer, 0, n

    def value_lanes(*step):
        layer, n = pair(*step)
        return layer, 0, n + PAIRS

    def totals(*step):
        return (*pair(*step), 0, 0)

    units = spec((1, tokens, width), across)
    in_specs = [
        ANY, ANY, whole(length.shape), units, units,
        ANY, ANY, ANY, ANY,
        spec((1, width, width), across), spec((1, width, width), down_rows),
        ANY,
        whole((layers, width)), whole((layers, width)),
        spec((1, tokens, LANES), lanes), spec((1, 2 * tokens, LANES), lanes), spec((1, 2 * tokens, LANES), value_lanes),
        spec((1, 1, 8, tokens), totals),
        ANY, ANY,
    ]
    if hosted:
        shapes = [
            sds((layers, SHARE, 3 * width), F32), sds((layers, SHARE, width), F32),
            sds((layers, SHARE, FFN_STEPS * width), F32), sds((layers, 4 * SHARE, width), F32),
        ]
    else:
        shapes = [sds((layers * STEPS,) + piece, BF16)]
    dma = pltpu.SemaphoreType.DMA

    def some(*shape):
        return pltpu.VMEM(shape, BF16)

    return pl.pallas_call(
        functools.partial(back_kernel, layers, hosted),
        grid=(layers + 1, STEPS),
        in_specs=in_specs,
        out_specs=[ANY] * len(shapes) + [whole((SMALL, width)), ANY, ANY],
        out_shape=shapes + [
            sds((SMALL, width), F32), sds((tokens, width), BF16), sds((tokens, width), BF16),
        ],
        scratch_shapes=[
            some(tokens, width), some(tokens, width), pltpu.VMEM((tokens, 1), F32), some(tokens, width),
            some(2, width, width),
            pltpu.VMEM((tokens, width), F32),
            pltpu.VMEM((tokens, width), F32),
            some(3, tokens, width),
            some(2, 2, tokens, LANES),
            some(2, 2, tokens, LANES),
            some(2, 2, tiles, BLOCK, 2 * BLOCK),
            some(7, *piece),
            some(2, *left), some(2, *left[1:]), some(2, *left[2:]), some(2, *left[3:]),
            some(2, *right), some(2, *right[1:]), some(2, *right[2:]), some(2, *right[3:]), some(2, *right[3:]),
            some(2, *piece[1:]),
            some(4, *left[1:]), some(4, *left[2:]), some(4, *left[3:]), some(4, *left[3:]),
            some(4, *right[1:]), some(4, *right[2:]), some(4, *right[3:]), some(count, *right[3:]),
            pltpu.VMEM((4, SHARE, width), F32),
            pltpu.VMEM((SMALL, width), F32),
            pltpu.VMEM((STAGES, SMALL, width), F32),
            dma((6,)), dma((2, 2)), dma, dma((2,)), dma((2,)), dma((2,)), dma((2,)), dma((4, 2)), dma((4, 4)), dma((3, 2)), dma((3, 4)),
            dma((2, count)), dma((2, count)), dma((4,)),
            dma((STAGES,)), dma((STAGES,)), dma((moved,)), dma((moved,)), dma((moved,)),
        ],
        compiler_params=params(1),
        name="back",
    )(cotangent, done, length, act, slope, normeds, scaleds, inverses, mixed, up, down, merge, first_gain, second_gain, query, kv, kv,
      total, exps, weight)


def local(
    stream, lengths, pass_embed, first_gain, first_bias, triple_weight, merge_weight,
    second_gain, second_bias, up_weight, down_weight, cotangent,
):
    row_count = lax.axis_size("rows")
    own_row = lax.axis_index("rows")
    tokens, width = stream.shape[2], stream.shape[3]
    layers = triple_weight.shape[0]
    hosted = row_count == ROWS

    (normeds, scaleds, inverses, query, mixed, total, exps, act, slope, kv, done, cotangent, length) = forward(
        stream.reshape(tokens, width), cotangent.reshape(tokens, width), lengths, pass_embed,
        first_gain, first_bias, second_gain, second_bias, triple_weight, merge_weight, up_weight, down_weight,
    )
    *weight_grads, small, input_grad, output = back(
        cotangent, done, length, act, slope, normeds, scaleds, inverses, mixed, up_weight, down_weight, merge_weight,
        first_gain, second_gain, query, kv.reshape(layers, 2 * tokens, 2 * width), total, exps, triple_weight, hosted,
    )
    input_grad = input_grad.reshape(stream.shape)
    output = output.reshape(stream.shape)
    if hosted:
        triple_grad, merge_grad, up_grad, down_grad = weight_grads
    else:
        pieces = weight_grads[0].transpose(0, 4, 3, 2, 1, 5, 6).reshape(layers, STEPS, -1, width)[::-1]

        def columns(first, last):
            return pieces[:, first:last].transpose(0, 2, 1, 3).reshape(layers, -1, (last - first) * width)

        def reduce(gradient):
            share = lax.psum_scatter(gradient, "rows", scatter_dimension=1, tiled=True)
            return lax.psum(share, "pass").astype(F32)

        down_grad = pieces[:, 4:8].reshape(layers, 4, ROWS, SHARE, width).transpose(0, 2, 1, 3, 4)
        triple_grad, merge_grad, up_grad, down_grad = map(
            reduce, (columns(10, 13), columns(8, 9), columns(0, 4), down_grad.reshape(layers, -1, width))
        )
        small = lax.psum(small, ("pass", "rows"))
    share = width // row_count
    small = lax.dynamic_slice_in_dim(small, own_row * share, share, 1)
    by_layer = small[2 : 2 + 4 * layers].reshape(layers, 4, share)
    return (
        output, input_grad, small[:2], by_layer[:, 0], by_layer[:, 1], triple_grad, merge_grad,
        by_layer[:, 2], by_layer[:, 3], up_grad, down_grad,
    )


def solution(mesh):
    token = P("pass", "rows", None, None)
    matrix = P(None, "rows", None)
    rows = P(None, "rows")
    in_specs = (token, P("rows")) + (P(),) * 9 + (token,)
    out_specs = (token, token, rows, rows, rows, matrix, matrix, rows, rows, matrix, matrix)
    return jax.shard_map(local, mesh=mesh, in_specs=in_specs, out_specs=out_specs, check_vma=False)
```

```python
import functools
import math

import jax
import jax.numpy as jnp
from jax import lax
from jax.experimental import pallas as pl
from jax.experimental.pallas import tpu as pltpu
from jax.sharding import PartitionSpec as P

HEAD_DIM = 64
EPSILON = 1e-05
SCALE = HEAD_DIM**-0.5
MESH = pl.DeviceIdType.MESH
NN = (((1,), (0,)), ((), ()))
NT = (((1,), (1,)), ((), ()))
TN = (((0,), (0,)), ((), ()))
BLOCK = 128
TILE = 256
LANES = 128
BF16 = jnp.bfloat16
F32 = jnp.float32
VMEM_LIMIT = 63 * 2**20 + 3 * 2**18
ANY = pl.BlockSpec(memory_space=pl.ANY)


def dot(left, right, dims=NN):
    return lax.dot_general(left, right, dims, preferred_element_type=F32)


def sds(shape, dtype):
    return jax.ShapeDtypeStruct(shape, dtype)


def params(collective_id=None):
    return pltpu.CompilerParams(
        vmem_limit_bytes=VMEM_LIMIT,
        collective_id=collective_id,
        has_side_effects=collective_id is not None,
    )


def whole(shape):
    zeros = (0,) * len(shape)
    return pl.BlockSpec(shape, lambda *_: zeros, pipeline_mode=pl.Buffered(1))


def pick(ref, which):
    return jnp.where(which == 0, ref[0:1, :], ref[1:2, :]).astype(F32)


def norm(hidden, gain, bias):
    centred = hidden - jnp.mean(hidden, -1, keepdims=True)
    inverse = lax.rsqrt(jnp.mean(centred * centred, -1, keepdims=True) + EPSILON)
    scaled = centred * inverse
    return (scaled * gain + bias).astype(BF16), scaled, inverse


def norm_back(grad, scaled, inverse, gain):
    e = grad * gain
    return inverse * (
        e - jnp.mean(e, -1, keepdims=True) - scaled * jnp.mean(e * scaled, -1, keepdims=True)
    )


def bits():
    row = lax.axis_index("rows")
    x, z0, z1 = (lax.rem(lax.div(row, 2**n), 2) for n in (1, 2, 3))
    return row, lax.rem(row, 2), x, z0, z1, lax.axis_index("pass")


def send(src, dst, send_sem, recv_sem, device):
    return pltpu.make_async_remote_copy(
        src_ref=src, dst_ref=dst, send_sem=send_sem, recv_sem=recv_sem,
        device_id=device, device_id_type=MESH,
    )


QKV_STEPS = 4
PAIRS = 6
FFN_TILES = 4
FORWARD = QKV_STEPS + PAIRS + FFN_TILES


def tile_index(blocks, key_block, query_block):
    return key_block * blocks - key_block * (key_block - 1) // 2 + query_block - key_block


def gelu_both(v):
    root = math.sqrt(2.0 / math.pi)
    cube = (root * 0.044715) * (v * v)
    half = 0.5 + 0.5 * jnp.tanh(v * (root + cube))
    act = v * half
    return act, half + (act - act * half) * (2.0 * root + 6.0 * cube)


def forward_kernel(
    layers,
    stream_ref, cot_ref, length_ref, embed_ref, first_gain_ref, first_bias_ref, second_gain_ref, second_bias_ref,
    triple_ref, merge_ref, up_ref, down_ref,
    normed_ref, scaled_ref, inverse_ref, query_ref, mixed_ref, total_ref, exp_ref, act_ref, slope_ref, kv_ref,
    out_ref, cot_out_ref, length_out_ref,
    hidden, arrived, length_mine, length_here, queries, kv, values, mixes, triple, merge, up, down,
    weight_sem, kv_sem, kv_send, kv_recv, free_sem, swap_send, swap_recv, here_sem,
):
    layer, j = pl.program_id(0), pl.program_id(1)
    t = layer * FORWARD + j
    row, core, _, _, _, own_pass = bits()
    tokens, width = hidden.shape
    blocks = tokens // BLOCK
    pair = 2 * BLOCK
    core_mate = {"rows": row + 1 - 2 * core}
    diagonal = {"pass": 1 - own_pass, "rows": row + 1 - 2 * core}
    swapped = own_pass != core


    def moves(i):
        if i < QKV_STEPS:
            rows = pl.ds(i * TILE, TILE)
            ends = stream_ref.at[rows, :], arrived.at[rows, :]
        else:
            ends = ((cot_ref, cot_out_ref), (length_mine, length_here))[i - QKV_STEPS]
        return (
            send(*ends, swap_send.at[i], swap_recv.at[i], diagonal),
            pltpu.make_async_copy(*ends, here_sem.at[i]),
        )

    def move(i, act):
        there, here = moves(i)

        @pl.when(swapped)
        def _():
            getattr(there, act)()

        @pl.when(jnp.logical_not(swapped))
        def _():
            getattr(here, act)()


    def weight_copies(which, of_layer):
        refs = ((triple_ref, triple), (merge_ref, merge), (up_ref, up), (down_ref, down))
        source, target = refs[which]
        return pltpu.make_async_copy(source.at[of_layer], target, weight_sem.at[which])

    @pl.when(t == 0)
    def _():
        barrier = pltpu.get_barrier_semaphore()
        pl.semaphore_signal(barrier, inc=1, device_id=core_mate, device_id_type=MESH)

        @pl.when(swapped)
        def _():
            pl.semaphore_signal(barrier, inc=1, device_id=diagonal, device_id_type=MESH)

        pl.semaphore_wait(barrier, 1 + jnp.where(swapped, 1, 0))
        length_mine[...] = jnp.full(length_mine.shape, length_ref[0], jnp.int32)
        move(QKV_STEPS + 1, "start")
        for i in range(QKV_STEPS):
            move(i, "start")
        for which in range(4):
            weight_copies(which, 0).start()
        move(QKV_STEPS + 1, "wait")
        length_out_ref[...] = length_here[...]

    for i in range(QKV_STEPS):
        @pl.when(t == i)
        def _():
            move(i, "wait")
            if i == QKV_STEPS - 1:
                move(QKV_STEPS, "start")


    def kv_copy(i):
        part = kv.at[pl.ds(i * (TILE // BLOCK), TILE // BLOCK), core]
        return send(part, part, kv_send.at[i], kv_recv.at[i], core_mate)

    def kv_keep(of_layer):
        return pltpu.make_async_copy(kv, kv_ref.at[of_layer], kv_sem)

    @pl.when(j < QKV_STEPS)
    def _():
        rows = pl.ds(pl.multiple_of(j * TILE, TILE), TILE)

        @pl.when(layer == 0)
        def _():
            hidden[rows, :] = arrived[rows, :].astype(F32) + pick(embed_ref, core)

        @pl.when(j == 0)
        def _():
            weight_copies(0, layer).wait()

        @pl.when((j == 0) & (layer > 0))
        def _():
            pl.semaphore_wait(free_sem, 1)

        normed, scaled, inverse = norm(
            hidden[rows, :], pick(first_gain_ref, layer), pick(first_bias_ref, layer)
        )
        normed_ref[0, 0] = normed
        scaled_ref[0, 0] = scaled.astype(BF16)
        inverse_ref[0, 0] = inverse
        keys = dot(normed, triple[:, width:]).astype(BF16)
        for b in range(TILE // BLOCK):
            kv[j * (TILE // BLOCK) + b, core] = keys[b * BLOCK : (b + 1) * BLOCK]
        kv_copy(j).start()
        query = (dot(normed, triple[:, :width]).astype(BF16).astype(F32) * SCALE).astype(BF16)
        queries[rows, :] = query
        query_ref[0] = query


    @pl.when((j >= QKV_STEPS) & (j < QKV_STEPS + PAIRS))
    def _():
        p = j - QKV_STEPS
        lanes = pl.ds(pl.multiple_of(p * LANES, LANES), LANES)
        value_lanes = pl.ds(pl.multiple_of(width + p * LANES, LANES), LANES)

        @pl.when(p == 0)
        def _():
            for i in range(QKV_STEPS):
                kv_copy(i).wait()
            kv_keep(layer).start()

        @pl.when((p == 0) & (layer < layers - 1))
        def _():
            weight_copies(0, layer + 1).start()

        values[:, :LANES] = kv[:, :, :, value_lanes].reshape(2 * tokens, LANES)
        values[:, LANES:] = jnp.ones((2 * tokens, LANES), BF16)
        lane = lax.broadcasted_iota(jnp.int32, (BLOCK, LANES), 1)
        query_at = lax.broadcasted_iota(jnp.int32, (BLOCK, pair), 0)
        column = lax.broadcasted_iota(jnp.int32, (BLOCK, pair), 1)
        key_pass = column // BLOCK
        key_at = column - key_pass * BLOCK
        causal = (key_at < query_at) | ((key_at == query_at) & (key_pass <= core))
        length = length_here[0:1, 0:1]

        def scores(block, head):
            query = queries[pl.ds(block * BLOCK, BLOCK), lanes]
            chosen = jnp.where(lane // HEAD_DIM == head, query, jnp.zeros_like(query))
            keys = kv[: block + 1, :, :, lanes].reshape((block + 1) * pair, LANES)
            return dot(chosen, keys, NT)

        def exponentials(block, head, raw):
            allowed = causal & (key_at + block * BLOCK < length)
            last = jnp.where(allowed, raw[:, block * pair :], -jnp.inf)
            top = jnp.max(last, -1, keepdims=True)
            if block:
                top = jnp.maximum(top, jnp.max(raw[:, : block * pair], -1, keepdims=True))
            parts = []
            for k in range(block + 1):
                source = last if k == block else raw[:, k * pair : (k + 1) * pair]
                part = jnp.exp(source - top).astype(BF16)
                exp_ref[0, head, tile_index(blocks, k, block)] = part
                parts.append(part)
            return jnp.concatenate(parts, 1) if block else parts[0]

        outs = {}

        def mix(block, head, exps):
            both = dot(exps, values[: (block + 1) * pair, :])
            inverse = jnp.where(block * BLOCK < length, 1.0 / both[:, LANES:], 0.0)
            rows = pl.ds(block * BLOCK, BLOCK)
            total_ref[0, 0, head : head + 1, rows] = inverse.T[:1]
            outs[head] = both[:, :LANES] * inverse
            if head == 1:
                value = jnp.where(lane < HEAD_DIM, outs[0], outs[1]).astype(BF16)
                mixes[rows, lanes] = value
                mixed_ref[0, rows, :] = value

        items = [(block, head) for block in range(blocks) for head in range(2)]
        ahead = scores(*items[0])
        behind = None
        for n, item in enumerate(items):
            raw = ahead
            if n + 1 < len(items):
                ahead = scores(*items[n + 1])
            exps = exponentials(*item, raw)
            if behind is not None:
                mix(*behind)
            behind = (*item, exps)
        mix(*behind)

        @pl.when(p == PAIRS - 1)
        def _():
            kv_keep(layer).wait()

        @pl.when((p == PAIRS - 1) & (layer < layers - 1))
        def _():
            pl.semaphore_signal(free_sem, inc=1, device_id=core_mate, device_id_type=MESH)


    @pl.when(j >= QKV_STEPS + PAIRS)
    def _():
        i = j - QKV_STEPS - PAIRS
        rows = pl.ds(pl.multiple_of(i * TILE, TILE), TILE)

        @pl.when(i == 0)
        def _():
            for which in range(1, 4):
                weight_copies(which, layer).wait()

        mid = hidden[rows, :] + dot(mixes[rows, :], merge[...])
        normed, scaled, inverse = norm(mid, pick(second_gain_ref, layer), pick(second_bias_ref, layer))
        normed_ref[0, 0] = normed
        scaled_ref[0, 0] = scaled.astype(BF16)
        inverse_ref[0, 0] = inverse
        parts = up.shape[1] // width
        sum_next = mid
        ahead = dot(normed, up[:, :width])
        for part in range(parts):
            at = slice(part * width, (part + 1) * width)
            now = ahead
            if part + 1 < parts:
                ahead = dot(normed, up[:, (part + 1) * width : (part + 2) * width])
            act, slope = gelu_both(now)
            act = act.astype(BF16)
            act_ref[0, :, at] = act
            slope_ref[0, :, at] = slope.astype(BF16)
            sum_next = sum_next + dot(act, down[at, :])
        hidden[rows, :] = sum_next

        @pl.when(layer == layers - 1)
        def _():
            position = lax.broadcasted_iota(jnp.int32, (TILE, 1), 0) + i * TILE
            valid = (position < length_here[0:1, 0:1]).astype(F32)
            out_ref[...] = (sum_next * valid).astype(BF16)

        @pl.when((i == FFN_TILES - 1) & (layer < layers - 1))
        def _():
            for which in range(1, 4):
                weight_copies(which, layer + 1).start()

    @pl.when(t == layers * FORWARD - 1)
    def _():
        move(QKV_STEPS, "wait")


def forward(stream, cotangent, length, embed, first_gain, first_bias, second_gain, second_bias, triple, merge, up, down):
    tokens, width = stream.shape
    layers, _, units = up.shape
    blocks = tokens // BLOCK
    tiles = blocks * (blocks + 1) // 2

    def row_tile(layer, j):
        late = j >= QKV_STEPS + PAIRS
        kind = jnp.where(late, 0, 1)
        return layer, kind, jnp.where(late, j - QKV_STEPS - PAIRS, jnp.minimum(j, QKV_STEPS - 1)), 0

    def query_tile(layer, j):
        return layer, jnp.minimum(j, QKV_STEPS - 1), 0

    def head(j):
        return jnp.clip(j - QKV_STEPS, 0, PAIRS - 1)

    def ffn_tile(layer, j):
        return layer, jnp.maximum(j - QKV_STEPS - PAIRS, 0), 0

    vector = whole((layers, width))
    rows = pl.BlockSpec((1, 1, TILE, width), row_tile)
    dma = pltpu.SemaphoreType.DMA
    return pl.pallas_call(
        functools.partial(forward_kernel, layers),
        grid=(layers, FORWARD),
        in_specs=[ANY, ANY, pl.BlockSpec(memory_space=pltpu.SMEM), whole(embed.shape), vector, vector, vector, vector, ANY, ANY, ANY, ANY],
        out_specs=[
            rows, rows, pl.BlockSpec((1, 1, TILE, 1), row_tile),
            pl.BlockSpec((1, TILE, width), query_tile),
            pl.BlockSpec((1, tokens, LANES), lambda layer, j: (layer, 0, head(j))),
            pl.BlockSpec((1, 1, 8, tokens), lambda layer, j: (layer, head(j), 0, 0)),
            pl.BlockSpec((1, 2, tiles, BLOCK, 2 * BLOCK), lambda layer, j: (layer, head(j), 0, 0, 0)),
            pl.BlockSpec((1, TILE, units), ffn_tile), pl.BlockSpec((1, TILE, units), ffn_tile),
            ANY,
            pl.BlockSpec((TILE, width), lambda layer, j: (jnp.where(layer == layers - 1, ffn_tile(layer, j)[1], 0), 0)),
            ANY, whole((8, LANES)),
        ],
        out_shape=[
            sds((layers, 2, tokens, width), BF16),
            sds((layers, 2, tokens, width), BF16),
            sds((layers, 2, tokens, 1), F32),
            sds((layers, tokens, width), BF16),
            sds((layers, tokens, width), BF16),
            sds((layers, PAIRS, 8, tokens), F32),
            sds((layers, 2 * PAIRS, tiles, BLOCK, 2 * BLOCK), BF16),
            sds((layers, tokens, units), BF16),
            sds((layers, tokens, units), BF16),
            sds((layers, blocks, 2, BLOCK, 2 * width), BF16),
            sds((tokens, width), BF16),
            sds((tokens, width), BF16),
            sds((8, LANES), jnp.int32),
        ],
        scratch_shapes=[
            pltpu.VMEM((tokens, width), F32),
            pltpu.VMEM((tokens, width), BF16),
            pltpu.VMEM((8, LANES), jnp.int32),
            pltpu.VMEM((8, LANES), jnp.int32),
            pltpu.VMEM((tokens, width), BF16),
            pltpu.VMEM((blocks, 2, BLOCK, 2 * width), BF16),
            pltpu.VMEM((2 * tokens, 2 * LANES), BF16),
            pltpu.VMEM((tokens, width), BF16),
            pltpu.VMEM(triple.shape[1:], BF16),
            pltpu.VMEM(merge.shape[1:], BF16),
            pltpu.VMEM(up.shape[1:], BF16),
            pltpu.VMEM(down.shape[1:], BF16),
            dma((4,)), dma, dma((QKV_STEPS,)), dma((QKV_STEPS,)), pltpu.SemaphoreType.REGULAR,
            dma((QKV_STEPS + 2,)), dma((QKV_STEPS + 2,)), dma((QKV_STEPS + 2,)),
        ],
        compiler_params=params(0),
        name="forward",
    )(stream, cotangent, length, embed, first_gain, first_bias, second_gain, second_bias, triple, merge, up, down)


FFN_STEPS = 4
STEPS = FFN_STEPS + PAIRS + 3
PIECES = STEPS - 1
STAGES = 5
ROWS = 16
SHARE = 48
SMALL = 16


def left_part(width):
    return 2 * width // 3


def back_kernel(
    layers, hosted,
    cot_ref, done_ref, length_ref, act_ref, slope_ref, normeds_ref, scaleds_ref, inverses_ref, mixes_ref, up_ref, down_ref,
    merges_ref,
    first_gain_ref, second_gain_ref, query_ref, key_ref, value_ref, total_ref, exp_ref, triples_ref,
    *refs,
):
    outs = refs[: 4 if hosted else 1]
    (
        small_ref, input_ref, output_ref,
        normed_ref, scaled_ref, inverse_ref, mixed_ref, weights, grad, total, grads, pending, landing, exps,
        staged, left0, left1, left2, left3, right0, right1, right2, right3, right4, got0,
        got_left1, got_left2, got_left3, got_left4, got_right1, got_right2, got_right3, got_late,
        final, small, small_got,
        load_sem, exp_sem, cot_sem, kv_send, kv_recv, core_send, core_recv, left_send, left_recv, right_send, right_recv,
        late_send, late_recv, out_sem, small_send, small_recv, swap_send, swap_recv, here_sem,
    ) = refs[len(outs) :]
    low = grads.at[0]
    turn, j = pl.program_id(0), pl.program_id(1)
    t = turn * STEPS + j
    layer = jnp.maximum(layers - 1 - turn, 0)
    row, core, x, z0, z1, own_pass = bits()
    tokens, width = grad.shape
    blocks = tokens // BLOCK
    pair = 2 * BLOCK
    busy = turn < layers
    core_mate = {"rows": row + 1 - 2 * core}
    mates = [
        core_mate, {"rows": row + 2 - 4 * x}, {"rows": row + 4 - 8 * z0}, {"rows": row + 8 - 16 * z1},
        {"pass": 1 - own_pass},
    ]
    diagonal = {"pass": 1 - own_pass, "rows": row + 1 - 2 * core}
    swapped = own_pass != core

    @pl.when(t == 0)
    def _():
        barrier = pltpu.get_barrier_semaphore()
        greeted = mates if hosted else mates[:1]
        for mate in greeted:
            pl.semaphore_signal(barrier, inc=1, device_id=mate, device_id_type=MESH)

        @pl.when(swapped)
        def _():
            pl.semaphore_signal(barrier, inc=1, device_id=diagonal, device_id_type=MESH)

        pl.semaphore_wait(barrier, len(greeted) + jnp.where(swapped, 1, 0))
        load = pltpu.make_async_copy(cot_ref, low, cot_sem)
        load.start()
        load.wait()
        position = lax.broadcasted_iota(jnp.int32, (tokens, 1), 0)
        valid = (position < length_ref[0:1, 0:1]).astype(F32)
        masked = low[...].astype(F32) * valid
        grad[...] = masked
        low[...] = masked.astype(BF16)
        small[...] = jnp.zeros_like(small)


    def swaps(i, act):
        if isinstance(i, int):
            source, target = done_ref, output_ref
        else:
            rows = pl.ds(pl.multiple_of((i - 1) * TILE, TILE), TILE)
            source, target = low.at[rows, :], input_ref.at[rows, :]

        @pl.when(swapped)
        def _():
            getattr(send(source, target, swap_send.at[i], swap_recv.at[i], diagonal), act)()

        @pl.when(jnp.logical_not(swapped))
        def _():
            getattr(pltpu.make_async_copy(source, target, here_sem.at[i]), act)()


    def load(what, of_layer):
        def weight_part(n):
            return triples_ref.at[of_layer, :, n * width : (n + 1) * width]

        source, target, sem = (
            (normeds_ref.at[of_layer, 0], normed_ref, 0), (scaleds_ref.at[of_layer, 0], scaled_ref, 1),
            (inverses_ref.at[of_layer, 0], inverse_ref, 2), (mixes_ref.at[of_layer], mixed_ref, 3),
            (normeds_ref.at[of_layer, 1], normed_ref, 0), (scaleds_ref.at[of_layer, 1], scaled_ref, 1),
            (inverses_ref.at[of_layer, 1], inverse_ref, 2), (merges_ref.at[of_layer], weights.at[0], 4),
            (weight_part(0), weights.at[1], 5), (weight_part(1), weights.at[0], 4), (weight_part(2), weights.at[1], 5),
        )[what]
        return pltpu.make_async_copy(source, target, load_sem.at[sem])

    def fetch(*which, of_layer=layer, when=True):
        @pl.when(when)
        def _():
            for what in which:
                load(what, of_layer).start()

    def have(*which):
        for what in which:
            load(what, layer).wait()

    more = layer > 0
    fetch(0, 1, 2, 3, 7, when=t == 0)


    def exp_copy(head):
        at = lax.rem(lax.div(head, 2), 2), lax.rem(head, 2)
        return pltpu.make_async_copy(exp_ref.at[layer, head], exps.at[at], exp_sem.at[at])

    def put(slot, r, value):
        staged[slot, r % 2, (r // 2) % 2, (r // 4) % 2, (r // 8) % 2] = value

    @pl.when(busy & (j < FFN_STEPS))
    def _():
        @pl.when(j == 0)
        def _():
            total[...] = jnp.zeros_like(total)

        grad_low = low[...]
        down_grad = dot(act_ref[0], grad_low, TN).astype(BF16)
        for q in range(4):
            for i in range(4):
                first = q * 4 * SHARE + i * SHARE
                staged[i, q % 2, q // 2, lax.rem(j, 2), lax.div(j, 2)] = down_grad[first : first + SHARE]
        grad_act = dot(grad_low, down_ref[0], NT)
        grad_pre = (slope_ref[0].astype(F32) * grad_act).astype(BF16)

        @pl.when(j == 0)
        def _():
            have(0)

        up_grad = dot(normed_ref[...], grad_pre, TN).astype(BF16)
        for r in range(ROWS):
            put(4 + lax.rem(j, 2), r, up_grad[r * SHARE : (r + 1) * SHARE])
        total[...] += dot(grad_pre, up_ref[0], NT)

        @pl.when(j == FFN_STEPS - 1)
        def _():
            exp_copy(jnp.int32(0)).start()
            exp_copy(jnp.int32(1)).start()
            have(1, 2, 3, 7)

            def rows(i, sums):
                at = pl.ds(pl.multiple_of(i * TILE, TILE), TILE)
                part = total[at, :]
                scaled = scaled_ref[at, :].astype(F32)
                mid = grad[at, :] + norm_back(part, scaled, inverse_ref[at, :], pick(second_gain_ref, layer))
                grad[at, :] = mid
                low_mid = mid.astype(BF16)
                grads[1, at, :] = low_mid
                grads[0, at, :] = dot(low_mid, weights[0], NT).astype(BF16)
                return (
                    sums[0] + jnp.sum(part * scaled, 0, keepdims=True),
                    sums[1] + jnp.sum(part, 0, keepdims=True),
                )

            empty = jnp.zeros((1, width), F32)
            gain_sum, bias_sum = lax.fori_loop(0, tokens // TILE, rows, (empty, empty))
            small[pl.ds(4 + 4 * layer, 1), :] = gain_sum
            small[pl.ds(5 + 4 * layer, 1), :] = bias_sum
            merge_grad = dot(mixed_ref[...], grads[1], TN).astype(BF16)
            for r in range(ROWS):
                put(6, r, merge_grad[r * SHARE : (r + 1) * SHARE])
            fetch(4, 5, 6, 8, 9)


    def kv_copy(p):
        return send(
            pending.at[lax.rem(p, 2)], landing.at[lax.rem(p, 2)], kv_send.at[lax.rem(p, 2)], kv_recv.at[lax.rem(p, 2)], core_mate,
        )

    def take(p):
        kv_copy(p).wait()
        lanes = pl.ds(pl.multiple_of(p * LANES, LANES), LANES)
        for which in range(2):
            grads[1 + which, :, lanes] = (
                grads[1 + which, :, lanes].astype(F32) + landing[lax.rem(p, 2), which].astype(F32)
            ).astype(BF16)

    @pl.when(busy & (j >= FFN_STEPS) & (j < FFN_STEPS + PAIRS))
    def _():
        p = j - FFN_STEPS
        lanes = pl.ds(pl.multiple_of(p * LANES, LANES), LANES)
        lane = lax.broadcasted_iota(jnp.int32, (tokens, LANES), 1)
        out_grad = grads[0, :, lanes].astype(F32)
        product = out_grad * mixed_ref[:, lanes].astype(F32)
        query = query_ref[0]
        inverses = total_ref[0, 0].T
        weighted = out_grad * jnp.where(lane < HEAD_DIM, inverses[:, :1], inverses[:, 1:2])
        weighted_across = weighted.T.astype(BF16)
        weighted = weighted.astype(BF16)
        query_across = query.astype(F32).T.astype(BF16)
        across = lax.broadcasted_iota(jnp.int32, (LANES, tokens), 0)
        scaled, scaled_across, inner, chosen_across = [], [], [], []
        for head in range(2):
            mine = lane // HEAD_DIM == head
            mine_across = across // HEAD_DIM == head
            scaled.append(jnp.where(mine, weighted, jnp.zeros_like(weighted)))
            scaled_across.append(jnp.where(mine_across, weighted_across, jnp.zeros_like(weighted_across)))
            chosen_across.append(jnp.where(mine_across, query_across, jnp.zeros_like(query_across)))
            inner.append(jnp.sum(jnp.where(mine, product, 0.0), -1, keepdims=True) * inverses[:, head : head + 1])

        def probs_grad(head, block):
            return dot(scaled[head][block * BLOCK :], value_ref[0, block * pair : (block + 1) * pair, :], NT)

        def score_grad(head, block, grad_prob):
            start = tile_index(blocks, block, block)
            prob = exps[lax.rem(p, 2), head, start : start + blocks - block].reshape(tokens - block * BLOCK, pair)
            return prob, (prob.astype(F32) * (grad_prob - inner[head][block * BLOCK :])).astype(BF16)

        sums = {}

        def products(head, block, prob, score):
            first = block * BLOCK
            pairs = dot(chosen_across[head][:, first:], score), dot(scaled_across[head][:, first:], prob)
            grad_query = dot(score, key_ref[0, block * pair : (block + 1) * pair, :])
            mine_lanes = slice(head * LANES, (head + 1) * LANES)
            if block == 0:
                total[:, mine_lanes] = grad_query
            else:
                total[first:, mine_lanes] += grad_query
            if head == 0:
                sums[block] = pairs
                return
            at = pl.ds(first, BLOCK)
            for which in range(2):
                both = (sums[block][which] + pairs[which]).T
                zero, one = both[:BLOCK], both[BLOCK:]
                grads[1 + which, at, lanes] = jnp.where(core == 0, zero, one).astype(BF16)
                pending[lax.rem(p, 2), which, at, :] = jnp.where(core == 0, one, zero).astype(BF16)

        exp_copy(2 * p).wait()
        exp_copy(2 * p + 1).wait()

        @pl.when(p < PAIRS - 1)
        def _():
            exp_copy(2 * p + 2).start()
            exp_copy(2 * p + 3).start()

        items = [(head, block) for block in range(blocks) for head in range(2)]
        ahead = probs_grad(*items[0])
        behind = None
        for n, item in enumerate(items):
            now = ahead
            if n + 1 < len(items):
                ahead = probs_grad(*items[n + 1])
            both = score_grad(*item, now)
            if behind is not None:
                products(*behind)
            behind = (*item, *both)
        products(*behind)

        grads[0, :, lanes] = (
            jnp.where(lane < HEAD_DIM, total[:, :LANES], total[:, LANES : 2 * LANES]) * SCALE
        ).astype(BF16)

        @pl.when(p > 0)
        def _():
            take(p - 1)

        kv_copy(p).start()


    @pl.when(busy & (j == FFN_STEPS + PAIRS))
    def _():
        take(jnp.int32(PAIRS - 1))
        have(4, 8)
        total[...] = dot(grads[0], weights[1], NT)
        fetch(10)
        fetch(3, of_layer=layer - 1, when=more)
        have(9)
        total[...] += dot(grads[1], weights[0], NT)
        fetch(7, of_layer=layer - 1, when=more)

    @pl.when(busy & (j >= FFN_STEPS + PAIRS))
    def _():
        n = j - FFN_STEPS - PAIRS

        triple_grad = dot(normed_ref[...], grads[n], TN).astype(BF16)
        for r in range(ROWS):
            put(4 + n, r, triple_grad[r * SHARE : (r + 1) * SHARE])

        fetch(0, of_layer=layer - 1, when=more & (n == 2))

        @pl.when(n == 1)
        def _():
            have(5, 6, 10)

            def rows(i, sums):
                at = pl.ds(pl.multiple_of(i * TILE, TILE), TILE)
                part = total[at, :] + dot(grads[2, at, :], weights[1], NT)
                scaled = scaled_ref[at, :].astype(F32)
                hidden = grad[at, :] + norm_back(part, scaled, inverse_ref[at, :], pick(first_gain_ref, layer))
                grad[at, :] = hidden
                low[at, :] = hidden.astype(BF16)
                return (
                    sums[0] + jnp.sum(part * scaled, 0, keepdims=True),
                    sums[1] + jnp.sum(part, 0, keepdims=True),
                    sums[2] + jnp.sum(hidden, 0, keepdims=True),
                )

            empty = jnp.zeros((1, width), F32)
            gain_sum, bias_sum, hidden_sum = lax.fori_loop(0, tokens // TILE, rows, (empty, empty, empty))
            small[pl.ds(2 + 4 * layer, 1), :] = gain_sum
            small[pl.ds(3 + 4 * layer, 1), :] = bias_sum

            @pl.when(layer == 0)
            def _():
                small[pl.ds(core, 1), :] = hidden_sum

            fetch(1, 2, of_layer=layer - 1, when=more)


    last = layers * STEPS - 1
    split = left_part(width)

    def piece(ago):
        before = j < ago
        return turn - jnp.where(before, 1, 0), j - ago + jnp.where(before, STEPS, 0)

    def slot(v):
        _, i = v
        return jnp.where(
            i < 4, 4 + lax.rem(i, 2), jnp.where(i < 8, i - 4, jnp.where(i == 8, 6, i - FFN_STEPS - PAIRS + 4))
        )

    def whether(ago):
        made, i = piece(ago)
        return (made >= 0) & (made < layers) & (i != FFN_STEPS + PAIRS - 1)

    def order(v):
        made, i = v
        return made * PIECES + i - jnp.where(i >= FFN_STEPS + PAIRS, 1, 0)

    def turns(v, count):
        return lax.rem(order(v), count)

    def add(a, b):
        return a + b

    def core_stage(v):
        h = turns(v, 2)
        return send(staged.at[slot(v), 1 - core], got0.at[h], core_send.at[h], core_recv.at[h], mates[0])

    def left_stage(s, v):
        h, d = turns(v, 2), turns(v, 4)
        src = (left0.at[h, 1 - x], left1.at[h, 1 - z0], left2.at[h, 1 - z1], left3.at[h])[s - 1]
        dst = (got_left1, got_left2, got_left3, got_left4)[s - 1].at[d]
        return send(src, dst, left_send.at[s - 1, h], left_recv.at[s - 1, d], mates[s])

    def right_stage(s, v):
        h, d = turns(v, 2), turns(v, 4)
        src = (right0.at[h, 1 - own_pass], right1.at[h, 1 - z0], right2.at[h, 1 - z1])[s - 1]
        dst = (got_right1, got_right2, got_right3)[s - 1].at[d]
        return send(src, dst, right_send.at[s - 1, h], right_recv.at[s - 1, d], (mates[4], mates[2], mates[3])[s - 1])

    def late_stage(s, v):
        k = order(v)
        src = (right3, right4)[s - 4].at[turns(v, 2)]
        return send(src, got_late.at[k], late_send.at[s - 4, k], late_recv.at[s - 4, k], (mates[1], mates[4])[s - 4])

    keeps = x == own_pass

    def late_start(s, v):
        @pl.when(keeps == (s == 5))
        def _():
            late_stage(s, v).start()

    def late_wait(s, v, receive):
        @pl.when(keeps == (s == 5))
        def _():
            late_stage(s, v).wait_send()

        @pl.when(keeps != (s == 5))
        def _():
            late_stage(s, v).wait_recv()
            receive()

    def out_copies(v, act):
        h = turns(v, 4)
        made, i = v
        at_layer = layers - 1 - made
        triple_out, merge_out, up_out, down_out = outs

        def columns(n):
            return pl.ds(pl.multiple_of(n * width, width), width)

        def go(target):
            getattr(pltpu.make_async_copy(final.at[h], target, out_sem.at[h]), act)()

        @pl.when(i < 4)
        def _():
            go(up_out.at[at_layer, :, columns(i)])

        @pl.when((i >= 4) & (i < 8))
        def _():
            go(down_out.at[at_layer, pl.ds(pl.multiple_of((i - 4) * SHARE, SHARE), SHARE), :])

        @pl.when(i == 8)
        def _():
            go(merge_out.at[at_layer])

        @pl.when(i >= FFN_STEPS + PAIRS)
        def _():
            go(triple_out.at[at_layer, :, columns(i - FFN_STEPS - PAIRS)])


    if hosted:
        @pl.when(whether(12))
        def _():
            out_copies(piece(12), "wait")

        @pl.when(whether(11))
        def _():
            v = piece(11)
            h, d = turns(v, 2), turns(v, 4)

            def receive():
                right4[h] = got_late[order(v)]

            late_wait(5, v, receive)
            final[d, :, split:] = right4[h].astype(F32)
            out_copies(v, "start")

        @pl.when(whether(9))
        def _():
            v = piece(9)
            h, d = turns(v, 2), turns(v, 4)

            def receive():
                right4[h] = add(right3[h], got_late[order(v)])

            late_wait(4, v, receive)
            late_start(5, v)
            left_stage(4, v).wait()
            final[d, :, :split] = left3[h].astype(F32) + got_left4[d].astype(F32)

        @pl.when(whether(7))
        def _():
            v = piece(7)
            h, d = turns(v, 2), turns(v, 4)
            right_stage(3, v).wait()
            right3[h] = add(right2[h, z1], got_right3[d])
            late_start(4, v)
            left_stage(3, v).wait()
            left3[h] = add(left2[h, z1], got_left3[d])
            left_stage(4, v).start()

        @pl.when(whether(5))
        def _():
            v = piece(5)
            h, d = turns(v, 2), turns(v, 4)
            right_stage(2, v).wait()
            right2[h] = add(right1[h, z0], got_right2[d])
            right_stage(3, v).start()
            left_stage(2, v).wait()
            left2[h] = add(left1[h, z0], got_left2[d])
            left_stage(3, v).start()

        @pl.when(whether(3))
        def _():
            v = piece(3)
            h, d = turns(v, 2), turns(v, 4)
            right_stage(1, v).wait()
            right1[h] = add(right0[h, own_pass], got_right1[d])
            right_stage(2, v).start()
            left_stage(1, v).wait()
            left1[h] = add(left0[h, x], got_left1[d])
            left_stage(2, v).start()

        @pl.when(whether(1))
        def _():
            v = piece(1)
            h = turns(v, 2)
            core_stage(v).wait()
            right0[h] = add(staged[slot(v), core, :, :, :, :, split:], got0[h, :, :, :, :, split:])
            right_stage(1, v).start()
            left0[h] = add(staged[slot(v), core, :, :, :, :, :split], got0[h, :, :, :, :, :split])
            left_stage(1, v).start()

        @pl.when(whether(0))
        def _():
            core_stage(piece(0)).start()

        for s in range(STAGES + 1):
            def small_copy(s):
                return send(small, small_got.at[s], small_send.at[s], small_recv.at[s], mates[s - 1])

            @pl.when(t == last - 1 + s)
            def _():
                if s:
                    small_copy(s - 1).wait()
                    small[...] += small_got[s - 1]
                if s < STAGES:
                    small_copy(s).start()
    else:
        def piece_copy(v):
            return pltpu.make_async_copy(staged.at[slot(v)], outs[0].at[v[0] * STEPS + v[1]], out_sem.at[turns(v, 2)])

        @pl.when(whether(1))
        def _():
            piece_copy(piece(1)).wait()

        @pl.when(whether(0))
        def _():
            piece_copy(piece(0)).start()

    @pl.when(t == 0)
    def _():
        swaps(0, "start")

    for i in range(tokens // TILE):
        @pl.when(t == last - 1 + i)
        def _():
            swaps(jnp.int32(1 + i), "start")

    @pl.when(t == (layers + 1) * STEPS - 1)
    def _():
        for i in range(1 + tokens // TILE):
            swaps(jnp.int32(i) if i else 0, "wait")
        small_ref[...] = small[...]


def back(cotangent, done, length, act, slope, normeds, scaleds, inverses, mixed, up, down, merge, first_gain, second_gain, query, kv,
         total, exps, weight, hosted):
    layers, tokens, width = query.shape
    tiles = exps.shape[2]
    piece = (2, 2, 2, 2, SHARE, width)
    left = (2, 2, 2, SHARE, left_part(width))
    right = (2, 2, 2, SHARE, width - left_part(width))
    count = layers * PIECES
    moved = 1 + tokens // TILE

    def at(turn, j):
        return jnp.maximum(layers - 1 - turn, 0), jnp.where(turn < layers, j, STEPS - 1)

    def tile(*step):
        layer, j = at(*step)
        return layer, jnp.minimum(j, FFN_STEPS - 1)

    def pair(*step):
        layer, j = at(*step)
        return layer, jnp.clip(j - FFN_STEPS, 0, PAIRS - 1)

    def spec(shape, place):
        return pl.BlockSpec(shape, lambda turn, j: place(turn, j))

    def across(*step):
        layer, n = tile(*step)
        return layer, 0, n

    def down_rows(*step):
        layer, n = tile(*step)
        return layer, n, 0

    def lanes(*step):
        layer, n = pair(*step)
        return layer, 0, n

    def value_lanes(*step):
        layer, n = pair(*step)
        return layer, 0, n + PAIRS

    def totals(*step):
        return (*pair(*step), 0, 0)

    units = spec((1, tokens, width), across)
    in_specs = [
        ANY, ANY, whole(length.shape), units, units,
        ANY, ANY, ANY, ANY,
        spec((1, width, width), across), spec((1, width, width), down_rows),
        ANY,
        whole((layers, width)), whole((layers, width)),
        spec((1, tokens, LANES), lanes), spec((1, 2 * tokens, LANES), lanes), spec((1, 2 * tokens, LANES), value_lanes),
        spec((1, 1, 8, tokens), totals),
        ANY, ANY,
    ]
    if hosted:
        shapes = [
            sds((layers, SHARE, 3 * width), F32), sds((layers, SHARE, width), F32),
            sds((layers, SHARE, FFN_STEPS * width), F32), sds((layers, 4 * SHARE, width), F32),
        ]
    else:
        shapes = [sds((layers * STEPS,) + piece, BF16)]
    dma = pltpu.SemaphoreType.DMA

    def some(*shape):
        return pltpu.VMEM(shape, BF16)

    return pl.pallas_call(
        functools.partial(back_kernel, layers, hosted),
        grid=(layers + 1, STEPS),
        in_specs=in_specs,
        out_specs=[ANY] * len(shapes) + [whole((SMALL, width)), ANY, ANY],
        out_shape=shapes + [
            sds((SMALL, width), F32), sds((tokens, width), BF16), sds((tokens, width), BF16),
        ],
        scratch_shapes=[
            some(tokens, width), some(tokens, width), pltpu.VMEM((tokens, 1), F32), some(tokens, width),
            some(2, width, width),
            pltpu.VMEM((tokens, width), F32),
            pltpu.VMEM((tokens, width), F32),
            some(3, tokens, width),
            some(2, 2, tokens, LANES),
            some(2, 2, tokens, LANES),
            some(2, 2, tiles, BLOCK, 2 * BLOCK),
            some(7, *piece),
            some(2, *left), some(2, *left[1:]), some(2, *left[2:]), some(2, *left[3:]),
            some(2, *right), some(2, *right[1:]), some(2, *right[2:]), some(2, *right[3:]), some(2, *right[3:]),
            some(2, *piece[1:]),
            some(4, *left[1:]), some(4, *left[2:]), some(4, *left[3:]), some(4, *left[3:]),
            some(4, *right[1:]), some(4, *right[2:]), some(4, *right[3:]), some(count, *right[3:]),
            pltpu.VMEM((4, SHARE, width), F32),
            pltpu.VMEM((SMALL, width), F32),
            pltpu.VMEM((STAGES, SMALL, width), F32),
            dma((6,)), dma((2, 2)), dma, dma((2,)), dma((2,)), dma((2,)), dma((2,)), dma((4, 2)), dma((4, 4)), dma((3, 2)), dma((3, 4)),
            dma((2, count)), dma((2, count)), dma((4,)),
            dma((STAGES,)), dma((STAGES,)), dma((moved,)), dma((moved,)), dma((moved,)),
        ],
        compiler_params=params(1),
        name="back",
    )(cotangent, done, length, act, slope, normeds, scaleds, inverses, mixed, up, down, merge, first_gain, second_gain, query, kv, kv,
      total, exps, weight)


def local(
    stream, lengths, pass_embed, first_gain, first_bias, triple_weight, merge_weight,
    second_gain, second_bias, up_weight, down_weight, cotangent,
):
    row_count = lax.axis_size("rows")
    own_row = lax.axis_index("rows")
    tokens, width = stream.shape[2], stream.shape[3]
    layers = triple_weight.shape[0]
    hosted = row_count == ROWS

    (normeds, scaleds, inverses, query, mixed, total, exps, act, slope, kv, done, cotangent, length) = forward(
        stream.reshape(tokens, width), cotangent.reshape(tokens, width), lengths, pass_embed,
        first_gain, first_bias, second_gain, second_bias, triple_weight, merge_weight, up_weight, down_weight,
    )
    *weight_grads, small, input_grad, output = back(
        cotangent, done, length, act, slope, normeds, scaleds, inverses, mixed, up_weight, down_weight, merge_weight,
        first_gain, second_gain, query, kv.reshape(layers, 2 * tokens, 2 * width), total, exps, triple_weight, hosted,
    )
    input_grad = input_grad.reshape(stream.shape)
    output = output.reshape(stream.shape)
    if hosted:
        triple_grad, merge_grad, up_grad, down_grad = weight_grads
    else:
        pieces = weight_grads[0].transpose(0, 4, 3, 2, 1, 5, 6).reshape(layers, STEPS, -1, width)[::-1]

        def columns(first, last):
            return pieces[:, first:last].transpose(0, 2, 1, 3).reshape(layers, -1, (last - first) * width)

        def reduce(gradient):
            share = lax.psum_scatter(gradient, "rows", scatter_dimension=1, tiled=True)
            return lax.psum(share, "pass").astype(F32)

        down_grad = pieces[:, 4:8].reshape(layers, 4, ROWS, SHARE, width).transpose(0, 2, 1, 3, 4)
        triple_grad, merge_grad, up_grad, down_grad = map(
            reduce, (columns(10, 13), columns(8, 9), columns(0, 4), down_grad.reshape(layers, -1, width))
        )
        small = lax.psum(small, ("pass", "rows"))
    share = width // row_count
    small = lax.dynamic_slice_in_dim(small, own_row * share, share, 1)
    by_layer = small[2 : 2 + 4 * layers].reshape(layers, 4, share)
    return (
        output, input_grad, small[:2], by_layer[:, 0], by_layer[:, 1], triple_grad, merge_grad,
        by_layer[:, 2], by_layer[:, 3], up_grad, down_grad,
    )


def solution(mesh):
    token = P("pass", "rows", None, None)
    matrix = P(None, "rows", None)
    rows = P(None, "rows")
    in_specs = (token, P("rows")) + (P(),) * 9 + (token,)
    out_specs = (token, token, rows, rows, rows, matrix, matrix, rows, rows, matrix, matrix)
    return jax.shard_map(local, mesh=mesh, in_specs=in_specs, out_specs=out_specs, check_vma=False)
```
